32 devices in a mesh: gran: 8 (over z, x), band: 4 (over y, core).
Axes of the slice: x: 2, y: 2, z: 4, core: 2. Of those that a mesh axis runs over, the one named last changes fastest.
Arguments:
- prior_grids: float32 [128, 12, 2, 4096], P('gran', 'band'), may hold values from -1.5 to 1.5
- pif_rhs: float32 [128, 12, 2, 4096], P('gran', 'band'), may hold values from -8 to 8
- pif_diagonal: float32 [128, 12, 2, 4096], P('gran', 'band'), may hold values from 0.5 to 2
- pif_cross: float32 [128, 12, 4096], P('gran', 'band'), may hold values from -0.7 to 0.7
- pif_coupling: bfloat16 [128, 8, 12, 4096], P('gran', None, 'band'), may hold values from 0.25 to 2
- neighbour_offset: int32 [128, 8], P('gran'), may hold values from -4 to 4, as said below
- neighbour_count: int32 [128], P('gran'), may hold values from 1 to 8, as said below
- tile_route: int32 [128, 2], replicated, may hold values from 0 to 7, all different within a row; in each aligned block of 16 rows (0 to 15, 16 to 31, ...) at most 8 rows name the same one
- tile_window: int32 [128, 2, 2], replicated, may hold values from 0 to 1760
- tile_pixels: bfloat16 [8, 12, 256, 256], P('gran', 'band'), may hold values from 0.049804688 to 1
Outputs:
- balanced_grids: float32 [128, 12, 2, 4096], P('gran', 'band')
- corrected_tiles: bfloat16 [8, 12, 256, 256], P('gran', 'band')
The draws below stay inside these ranges and needn't reach their ends.
Inputs may be any that keep to these rules, and one draw needn't show every extreme that they name: `neighbour_offset`: A granule's slots below its count hold a nonzero offset to another granule; the other slots hold 0. In every aligned block of 16 granules the granule of count 8 has an offset of magnitude 4 in its first slot. `neighbour_count`: every aligned block of 16 granules holds a granule with 8 neighbours. `tile_route`: each granule names two different tiles; every tile is named; among the 16 granules of one device no tile is named more than 8 times.
All inputs are finite; a program needn't handle non-finite values.
Results may differ from the reference program's by a relative error of at most 0.0036.
The reference program's roundings to bfloat16 on the way count: a program that leaves them out, or rounds other values in their place, can miss the bound.
Values may be sent and summed in bfloat16 or wider, within the bound.
No kernel may reach another device: no remote copies, remote signals or barrier semaphores. Data moves between devices by JAX's collectives and lax.ppermute only.
A program may use at most 128 MiB of HBM per device.

```python
import math
import jax
import jax.numpy as jnp
import numpy as np
from jax import lax

BANDS = 12
KN = 64
KNOTS = 4096
PATCH = 8
DEG = 8
REACH = 4
SWEEPS = 3
SP = 32
PIX = 256
G_DEV = 16
GRANULES = 128
TILES = 8
MOST = 8


def neighbour_graph(key):
    key = jax.random.fold_in(key, 7301)
    key_degree, key_hub, key_reach, key_sign = jax.random.split(key, 4)
    granule_index = jnp.arange(GRANULES, dtype=jnp.int32)
    block_total = GRANULES // G_DEV
    degrees = jax.random.randint(key_degree, (GRANULES,), 1, 4, dtype=jnp.int32)
    hub_place = jax.random.randint(key_hub, (block_total,), 0, G_DEV, dtype=jnp.int32)
    is_hub = granule_index % G_DEV == jnp.repeat(hub_place, G_DEV)
    degrees = jnp.where(is_hub, DEG, degrees)
    slot_index = jnp.arange(DEG, dtype=jnp.int32)[None, :]
    reach_size = jax.random.randint(key_reach, (GRANULES, DEG), 1, REACH + 1, dtype=jnp.int32)
    reach_size = jnp.where(is_hub[:, None] & (slot_index == 0), REACH, reach_size)
    direction = jax.random.randint(key_sign, (GRANULES, DEG), 0, 2, dtype=jnp.int32) * 2 - 1
    offsets = reach_size * direction
    target = granule_index[:, None] + offsets
    offsets = jnp.where((target < 0) | (target >= GRANULES), -offsets, offsets)
    offsets = jnp.where(slot_index < degrees[:, None], offsets, 0)
    return (offsets, degrees)


def draw_neighbour_offset(key, part):
    return neighbour_graph(key)[0]


def draw_neighbour_count(key, part):
    return neighbour_graph(key)[1]


def draw_pif_rhs(key, part):
    key_base = jax.random.fold_in(jax.random.fold_in(key, 911), 0)
    band_scale = 0.6 * 3.0 ** (jnp.arange(BANDS, dtype=jnp.float32) / (BANDS - 1))
    shape_all = (GRANULES, BANDS, 2, KNOTS)
    base_value = jnp.clip(jax.random.normal(key_base, shape_all, jnp.float32), -4.0, 4.0)
    return base_value * band_scale[None, :, None, None]


def set_ends(array, own_key, low, top_value):
    longest = array.shape.index(max(array.shape))
    spots = []
    for shift in (0, 1):
        where = [jax.random.randint(jax.random.fold_in(own_key, axis), (), 0, length) for axis, length in enumerate(array.shape)]
        where[longest] = (where[longest] + shift) % array.shape[longest]
        spots.append(tuple(where))
    return array.at[spots[0]].set(low).at[spots[1]].set(top_value)


def steps_of(stream_key, dims, cuts, least, largest):
    def one(axis_at, blocks):
        draws = jax.random.uniform(jax.random.fold_in(jax.random.fold_in(stream_key, 6), axis_at), (blocks,), jnp.float32, least / len(cuts), largest / len(cuts))
        return jnp.repeat(jnp.exp(draws), dims[axis_at] // blocks).reshape((-1,) + (1,) * (len(dims) - axis_at - 1))

    factor_of = one(*cuts[0])
    for cut in cuts[1:]:
        factor_of = factor_of * one(*cut)
    return factor_of


def assign_block(key, own, number, rows, count, top, bound, lean):
    sequence = jax.random.permutation(key, count)
    crowded, ordinary = load_shares(count, rows * top, bound, lean, True), load_shares(count, rows * top, bound, lean, False)
    places = jnp.arange(count)

    def named(sizes, offset_by):
        used = int((sizes > 0).sum())
        fixed = max(1, used // 4)
        passed = fixed + (places - fixed + offset_by * (used - fixed)) % max(1, count - fixed)
        return jnp.zeros((count,), jnp.int32).at[sequence[jnp.where(places < fixed, places, passed)]].set(jnp.asarray(sizes, jnp.int32))

    sizes = jnp.where(number % 4 == 0, named(crowded, number // 4), named(ordinary, number - number // 4 - 1))
    mixed = jax.random.permutation(jax.random.fold_in(own, 3), count)
    donor, taker = mixed[0:count // 2 * 2:2], mixed[1:count // 2 * 2:2]
    room = jnp.minimum(sizes[donor] - 1, bound - sizes[taker]) // 2
    room = jnp.where((donor == sequence[0]) | (taker == sequence[0]) | (sizes[taker] == 0), 0, jnp.maximum(room, 0))
    passed = jax.random.randint(jax.random.fold_in(own, 4), (count // 2,), 0, 1 << 20) % (room + 1)
    sizes = sizes.at[donor].add(-passed).at[taker].add(passed)
    items = jnp.searchsorted(jnp.cumsum(sizes), jnp.arange(rows * top), side="right").astype(jnp.int32)
    listing = items.reshape(top, rows).T
    listing = listing[jax.random.permutation(jax.random.fold_in(own, 1), rows)]
    offset_by = jax.random.randint(jax.random.fold_in(own, 2), (rows, 1), 0, top)
    return jnp.take_along_axis(listing, (jnp.arange(top)[None, :] + offset_by) % top, axis=1)


def load_shares(amount, total, reach, slope, full):
    weights = [(1 << 20) // math.isqrt(standing ** slope) + 1 for standing in range(1, amount + 1)]
    largest = reach if full else min(reach, max(-(-total // amount), total * weights[0] // sum(weights)))
    least = 1 if total - largest >= amount - 1 else 0
    counts, rest = [largest] + [least] * (amount - 1), total - largest - least * (amount - 1)
    while rest > 0:
        movable = [i for i in range(1, amount) if counts[i] < largest] or [i for i in range(1, amount) if counts[i] < reach]
        mass, remaining = sum([weights[i] for i in movable]), rest
        for i in movable:
            extra = min(reach - counts[i], max(1, remaining * weights[i] // mass), rest)
            counts[i] = counts[i] + extra
            rest = rest - extra
    return np.array(counts)


def bell_draw(stream_key, dims, deviation, reach, cuts=(), held_as=jnp.bfloat16):
    array = deviation * jax.random.normal(stream_key, dims, jnp.float32)
    if cuts:
        array = array * steps_of(stream_key, dims, cuts, -0.22, 0.18)
    return jnp.clip(array, -reach, reach).astype(held_as)


def setup_inputs(seed: int = 0) -> dict:
    arg_keys = jax.random.split(jax.random.key(seed), 11)
    prior_grids = bell_draw(arg_keys[0], (GRANULES, BANDS, 2, KNOTS), 0.3, 1.5, ((0, 8), (1, 4)), jnp.float32)
    pif_rhs = draw_pif_rhs(jax.random.fold_in(arg_keys[10], 71), 0)
    pif_diagonal = jnp.clip(jnp.exp(math.log(2.0) - 1.3862944 * jax.random.uniform(arg_keys[2], (GRANULES, BANDS, 2, KNOTS), jnp.float32) ** steps_of(arg_keys[2], (GRANULES, BANDS, 2, KNOTS), ((0, 8), (1, 4)), -0.2, 0.2)), 0.5, 2.0)
    pif_cross = jnp.clip(jax.random.uniform(arg_keys[3], (GRANULES, BANDS, KNOTS), jnp.float32, -0.7, 0.7) * steps_of(arg_keys[3], (GRANULES, BANDS, KNOTS), ((0, 8), (1, 4)), -0.4, 0.0), -0.7, 0.7)
    pif_coupling = jnp.clip(jnp.exp(math.log(2.0) - 2.0794415 * jax.random.uniform(arg_keys[4], (GRANULES, DEG, BANDS, KNOTS), jnp.float32) ** steps_of(arg_keys[4], (GRANULES, DEG, BANDS, KNOTS), ((0, 8), (2, 4)), -0.2, 0.2)), 0.25, 2.0).astype(jnp.bfloat16)
    neighbour_offset = draw_neighbour_offset(jax.random.fold_in(arg_keys[10], 71), 0)
    neighbour_count = draw_neighbour_count(jax.random.fold_in(arg_keys[10], 71), 0)
    tile_route_keys = jax.random.split(jax.random.fold_in(arg_keys[7], 1), GRANULES // G_DEV)
    tile_route_turns = jax.random.permutation(jax.random.fold_in(arg_keys[7], 3), GRANULES // G_DEV)
    tile_route = jax.vmap(lambda own, number: assign_block(jax.random.fold_in(arg_keys[7], 2), own, number, G_DEV, TILES, 2, MOST, 2))(tile_route_keys, tile_route_turns).reshape((GRANULES, 2))
    tile_window = set_ends(jax.random.randint(arg_keys[8], (GRANULES, 2, 2), 0, (KN - 1) * SP - PIX + 1), jax.random.fold_in(arg_keys[8], 1), 0, (KN - 1) * SP - PIX).astype(jnp.int32)
    tile_pixels = jnp.clip(jnp.exp(math.log(1.0) - 2.9996462 * jax.random.uniform(arg_keys[9], (TILES, BANDS, PIX, PIX), jnp.float32) ** steps_of(arg_keys[9], (TILES, BANDS, PIX, PIX), ((0, 8), (1, 4)), -0.2, 0.2)), 0.049804688, 1.0).astype(jnp.bfloat16)
    return dict(prior_grids=prior_grids, pif_rhs=pif_rhs, pif_diagonal=pif_diagonal, pif_cross=pif_cross, pif_coupling=pif_coupling, neighbour_offset=neighbour_offset, neighbour_count=neighbour_count, tile_route=tile_route, tile_window=tile_window, tile_pixels=tile_pixels)


cubic_sharpness = -0.5
robust_scale = 0.3

def cubic_taps(fraction):
    sharpness = cubic_sharpness

    def near_tap(distance):
        return (sharpness + 2.0) * distance ** 3 - (sharpness + 3.0) * distance ** 2 + 1.0

    def far_tap(distance):
        return sharpness * distance ** 3 - 5.0 * sharpness * distance ** 2 + 8.0 * sharpness * distance - 4.0 * sharpness
    return (far_tap(1.0 + fraction), near_tap(fraction), near_tap(1.0 - fraction), far_tap(2.0 - fraction))

def interp_matrix(start_pixel, length, first_knot, extent):
    pixel_index = start_pixel + jnp.arange(length, dtype=jnp.int32)
    base_knot = pixel_index // SP
    fraction = (pixel_index - base_knot * SP).astype(jnp.float32) / SP
    columns = jnp.arange(extent, dtype=jnp.int32)
    result = jnp.zeros((length, extent), jnp.float32)
    for shift_value, tap_weight in zip((-1, 0, 1, 2), cubic_taps(fraction)):
        knot_index = jnp.clip(base_knot + shift_value, 0, KN - 1) - first_knot
        result = result + tap_weight[:, None] * (knot_index[:, None] == columns[None, :]).astype(jnp.float32)
    return result.astype(jnp.bfloat16)

def patch_total(values):
    leading = values.shape[:-1]
    blocks = KN // PATCH
    blocked = values.reshape(leading + (blocks, PATCH, blocks, PATCH))
    return lax.optimization_barrier(jnp.sum(blocked, axis=(-3, -1))).reshape(leading + (blocks * blocks,))

def patch_spread(values):
    leading = values.shape[:-1]
    blocks = KN // PATCH
    blocked = values.reshape(leading + (blocks, 1, blocks, 1))
    return jnp.broadcast_to(blocked, leading + (blocks, PATCH, blocks, PATCH)).reshape(leading + (KN * KN,))

def solve_pairs(pif_diagonal, pif_cross, diagonal_add, drive_term):
    gain_pivot = pif_diagonal[:, :, 0] + diagonal_add
    offset_pivot = pif_diagonal[:, :, 1] + diagonal_add
    cross_term = pif_cross * jnp.sqrt(pif_diagonal[:, :, 0] * pif_diagonal[:, :, 1])
    determinant = gain_pivot * offset_pivot - cross_term * cross_term
    gain_part = (offset_pivot * drive_term[:, :, 0] - cross_term * drive_term[:, :, 1]) / determinant
    offset_part = (gain_pivot * drive_term[:, :, 1] - cross_term * drive_term[:, :, 0]) / determinant
    return jnp.stack([gain_part, offset_part], axis=2)

def reference(prior_grids, pif_rhs, pif_diagonal, pif_cross, pif_coupling, neighbour_offset, neighbour_count, tile_route, tile_window, tile_pixels):
    granule_index = jnp.arange(GRANULES, dtype=jnp.int32)
    neighbour = granule_index[:, None] + neighbour_offset
    slot_weight = (jnp.arange(DEG, dtype=jnp.int32)[None, :] < neighbour_count[:, None]).astype(jnp.float32)
    knot_grids = prior_grids
    for sweep_index in range(SWEEPS):
        response = knot_grids[:, :, 0] + knot_grids[:, :, 1]
        diagonal_add = jnp.zeros((GRANULES, BANDS, KNOTS), jnp.float32)
        drive_term = pif_rhs
        for slot_index in range(DEG):
            partner = neighbour[:, slot_index]
            difference = response - response[partner]
            disparity = patch_total(lax.optimization_barrier(jnp.sum(difference * difference, axis=1)))
            robust = slot_weight[:, slot_index, None] / (1.0 + disparity / (robust_scale * BANDS * PATCH * PATCH))
            effective = patch_spread(robust)[:, None, :] * pif_coupling[:, slot_index].astype(jnp.float32)
            diagonal_add = diagonal_add + effective
            drive_term = drive_term + effective[:, :, None, :] * knot_grids[partner]
        knot_grids = solve_pairs(pif_diagonal, pif_cross, diagonal_add, drive_term)
    shaped = knot_grids.astype(jnp.bfloat16).reshape(GRANULES, BANDS, 2, KN, KN)

    def contribute(entry_index, field_sum):
        granule = entry_index // 2
        route_slot = entry_index % 2
        tile_index = tile_route[granule, route_slot]
        row_start = tile_window[granule, route_slot, 0].astype(jnp.int32)
        col_start = tile_window[granule, route_slot, 1].astype(jnp.int32)
        row_weights = interp_matrix(row_start, PIX, 0, KN).astype(jnp.float32)
        col_weights = interp_matrix(col_start, PIX, 0, KN).astype(jnp.float32)
        knot_values = shaped[granule].astype(jnp.float32)
        rowpass = jnp.einsum('pk,bckl->bcpl', row_weights, knot_values, precision=lax.Precision.HIGHEST)
        rowpass = lax.optimization_barrier(rowpass.astype(jnp.bfloat16)).astype(jnp.float32)
        contribution = jnp.einsum('bcpl,ql->bcpq', rowpass, col_weights, precision=lax.Precision.HIGHEST)
        return field_sum.at[tile_index].add(contribution)
    field_sum = lax.fori_loop(0, 2 * GRANULES, contribute, jnp.zeros((TILES, BANDS, 2, PIX, PIX), jnp.float32))
    covers = lax.optimization_barrier(jnp.sum((tile_route.reshape(-1)[:, None] == jnp.arange(TILES, dtype=jnp.int32)[None, :]).astype(jnp.int32), axis=0))
    covers = covers.astype(jnp.float32)[:, None, None, None]
    pixels = tile_pixels.astype(jnp.float32)
    corrected = pixels * (1.0 + field_sum[:, :, 0] / covers) + field_sum[:, :, 1] / covers
    return (knot_grids, corrected.astype(jnp.bfloat16))
```

```python
import functools
import jax
import jax.numpy as jnp
from jax import lax
from jax.experimental import pallas as pl
from jax.experimental.pallas import tpu as pltpu
from jax.sharding import PartitionSpec as P

BANDS = 12
KN = 64
PATCH = 8
REACH = 4
SWEEPS = 3
SP = 32
LANES = 128
SPAN = 16

robust_scale = 0.3

ON_CHIP = pl.BlockSpec(memory_space=pltpu.VMEM)
SCALARS = pl.BlockSpec(memory_space=pltpu.SMEM)
f32 = jnp.float32
bf16 = jnp.bfloat16


def held(array):
    return pltpu.with_memory_space_constraint(array, pltpu.VMEM)


def scalars(array):
    return pltpu.with_memory_space_constraint(array, pltpu.SMEM)


def call(body, inputs, outputs, scratch=(), aliases=None, limit=24):
    operands, specs = [], []
    for kind, array in inputs:
        operands.append(scalars(array) if kind == "s" else held(array))
        specs.append(SCALARS if kind == "s" else ON_CHIP)
    return pl.pallas_call(
        body,
        in_specs=specs,
        out_specs=tuple(ON_CHIP for _ in outputs),
        out_shape=tuple(pltpu.VMEM(shape, dtype) for shape, dtype in outputs),
        scratch_shapes=list(scratch),
        input_output_aliases=aliases or {},
        compiler_params=pltpu.CompilerParams(vmem_limit_bytes=limit * 2**20),
    )(*operands)


def put_edges(side_ref, load, near_ref, far_ref, granules):
    odd = side_ref[0]
    last = granules - REACH
    for ref, base in ((near_ref, (1 - odd) * last), (far_ref, odd * last)):

        def step(g, carry, ref=ref, base=base):
            for b in range(ref.shape[1]):
                for j in range(4):
                    both = jnp.concatenate([load(base + g, b, j, 0), load(base + g, b, j, 1)], axis=0)
                    ref[g, b, 16 * j : 16 * j + 16, :] = both.astype(bf16)
            return carry

        lax.fori_loop(0, REACH, step, 0)


def first_edges(side_ref, grids_ref, near_ref, far_ref):
    def load(g, b, j, c):
        return grids_ref[g, b, pl.ds(2 * j + c, 8, stride=8), :]

    put_edges(side_ref, load, near_ref, far_ref, grids_ref.shape[0])


def arrange(grids_ref, rhs_ref, diag_ref, cross_ref, coupling_ref, ext_ref, rhs_out, diag_out, cross_out, coupling_out, wide):
    granules, bands = grids_ref.shape[:2]
    slots = coupling_out.shape[1]

    def step(i, carry):
        for b in range(bands):
            for j in range(4):
                d = []
                for c in range(2):
                    rows = pl.ds(2 * j + c, 8, stride=8)
                    to = slice(16 * j + 8 * c, 16 * j + 8 * c + 8)
                    ext_ref[i + REACH, b, to, :] = grids_ref[i, b, rows, :]
                    rhs_out[i, b, to, :] = rhs_ref[i, b, rows, :]
                    value = diag_ref[i, b, rows, :]
                    diag_out[i, b, to, :] = value
                    d.append(value)
                pick = cross_ref[b, i // 8, pl.ds(8 * j + i % 8, 8, stride=32), :]
                cross_out[i, b, 8 * j : 8 * j + 8, :] = pick * jnp.sqrt(d[0] * d[1])
            wide[b] = coupling_ref[i, b].astype(f32)
            for s in range(slots):
                for j in (0, 2):
                    pair = [wide[b, pl.ds(8 * (j + k) + s, 8, stride=32), :] for k in (0, 1)]
                    coupling_out[i, s, b, 8 * j : 8 * j + 16, :] = jnp.concatenate(pair, axis=0).astype(bf16)
        return carry

    lax.fori_loop(0, granules, step, 0)


def lane_sums():
    row = lax.broadcasted_iota(jnp.int32, (LANES, LANES), 0)
    col = lax.broadcasted_iota(jnp.int32, (LANES, LANES), 1)
    return ((row % KN) // PATCH == col % PATCH).astype(f32).astype(bf16)


def lane_spread():
    row = lax.broadcasted_iota(jnp.int32, (LANES, LANES), 0)
    col = lax.broadcasted_iota(jnp.int32, (LANES, LANES), 1)
    return ((col % KN) // PATCH == row % PATCH).astype(f32).astype(bf16)


def disparities(side_ref, offset_ref, count_ref, near_ref, far_ref, ext_in, ext_ref, out_ref, gathered):
    del ext_in
    granules = ext_ref.shape[0] - 2 * REACH
    bands = ext_ref.shape[1]
    slots = gathered.shape[0] * 8 // granules
    odd = side_ref[0]
    right = granules + REACH
    for ref, base in ((near_ref, (1 - odd) * right), (far_ref, odd * right)):

        def widen(g, carry, ref=ref, base=base):
            for b in range(bands):
                ext_ref[base + g, b] = ref[g, b].astype(f32)
            return carry

        lax.fori_loop(0, REACH, widen, 0)
    gathered[...] = jnp.zeros_like(gathered)

    def response(g):
        return [
            ext_ref[g, b, 16 * j : 16 * j + 8, :] + ext_ref[g, b, 16 * j + 8 : 16 * j + 16, :]
            for b in range(bands)
            for j in range(4)
        ]

    def granule(i, carry):
        own = response(i + REACH)
        row = pl.multiple_of((i % 8) * 8, 8)

        def slot(s, carry):
            other = response(i + REACH + offset_ref[i * slots + s])
            total = None
            for a, o in zip(own, other):
                d = a - o
                total = d * d if total is None else total + d * d
            gathered[(i // 8) * slots + s, pl.ds(row, 8), :] = total
            return carry

        lax.fori_loop(0, count_ref[i], slot, 0)
        return carry

    lax.fori_loop(0, granules, granule, 0)
    groups = gathered.shape[0]
    sums = jnp.dot(
        gathered[...].reshape(groups * 64, LANES).astype(bf16), lane_sums(), preferred_element_type=f32
    )
    lane = lax.broadcasted_iota(jnp.int32, (64, LANES), 1) // PATCH
    packed = jnp.zeros((64, LANES), f32)
    for k in range(groups):
        packed = jnp.where(lane == k, sums[64 * k : 64 * k + 64], packed)
    out_ref[...] = packed


def balance(offset_ref, count_ref, own_ref, a_ref, b_ref, c_ref, ext_ref, rhs_ref, diag_ref, cross_ref, coupling_ref, weights, store):
    granules, bands = rhs_ref.shape[:2]
    slots = coupling_ref.shape[1]
    groups = weights.shape[0]
    total = (own_ref[...] + a_ref[...]) + (b_ref[...] + c_ref[...])
    robust = 1.0 / (1.0 + total * (1.0 / (robust_scale * BANDS * PATCH * PATCH)))
    lane = lax.broadcasted_iota(jnp.int32, (64, LANES), 1) // PATCH
    high = robust.astype(bf16).astype(f32)
    low = robust - high
    both = jnp.concatenate([high, low], axis=1)
    lane = jnp.concatenate([lane, lane], axis=1)
    spread = lane_spread()
    spread = jnp.concatenate([spread, spread], axis=0)
    stacked = jnp.concatenate(
        [jnp.where(lane == k, both, 0.0).astype(bf16) for k in range(groups)], axis=0
    )
    weights[...] = jnp.dot(stacked, spread, preferred_element_type=f32).reshape(groups, 64, LANES)

    def granule(i, carry):
        row = pl.multiple_of((i % 8) * 8, 8)
        parts = [(b, j) for b in range(bands) for j in range(4)]
        rhs = tuple(
            rhs_ref[i, b, 16 * j + 8 * c : 16 * j + 8 * c + 8, :] for b, j in parts for c in range(2)
        )

        def slot(s, sums):
            sigma, drive = sums
            weight = weights[(i // 8) * slots + s, pl.ds(row, 8), :]
            n = i + REACH + offset_ref[i * slots + s]
            new_sigma, new_drive = [], []
            for b in range(bands):
                coupling = coupling_ref[i, s, b].astype(f32)
                for j in range(4):
                    k = 4 * b + j
                    effective = weight * coupling[8 * j : 8 * j + 8]
                    new_sigma.append(sigma[k] + effective)
                    for c in range(2):
                        grid = ext_ref[n, b, 16 * j + 8 * c : 16 * j + 8 * c + 8, :]
                        new_drive.append(drive[2 * k + c] + effective * grid)
            return tuple(new_sigma), tuple(new_drive)

        zero = jnp.zeros((8, LANES), f32)
        sigma, drive = lax.fori_loop(0, count_ref[i], slot, ((zero,) * len(parts), rhs))
        for k, (b, j) in enumerate(parts):
            first = diag_ref[i, b, 16 * j : 16 * j + 8, :] + sigma[k]
            second = diag_ref[i, b, 16 * j + 8 : 16 * j + 16, :] + sigma[k]
            cross = cross_ref[i, b, 8 * j : 8 * j + 8, :]
            inverse = 1.0 / (first * second - cross * cross)
            gain, offset = drive[2 * k], drive[2 * k + 1]
            store(i, b, j, 0, (second * gain - cross * offset) * inverse)
            store(i, b, j, 1, (first * offset - cross * gain) * inverse)
        return carry

    lax.fori_loop(0, granules, granule, 0)


def middle_sweep(side_ref, *refs):
    inputs, (new_ref, near_ref, far_ref, weights) = refs[:11], refs[11:]

    def store(i, b, j, c, value):
        new_ref[i + REACH, b, 16 * j + 8 * c : 16 * j + 8 * c + 8, :] = value

    def load(g, b, j, c):
        return new_ref[g + REACH, b, 16 * j + 8 * c : 16 * j + 8 * c + 8, :]

    balance(*inputs, weights, store)
    put_edges(side_ref, load, near_ref, far_ref, new_ref.shape[0] - 2 * REACH)


def last_sweep(place_ref, *refs):
    inputs, (out_ref, send_ref, weights, windows) = refs[:11], refs[11:]
    granules, bands = out_ref.shape[:2]

    def store(i, b, j, c, value):
        out_ref[i, b, pl.ds(2 * j + c, 8, stride=8), :] = value

    balance(*inputs, weights, store)
    windows[...] = jnp.zeros_like(windows)
    lane = lax.broadcasted_iota(jnp.int32, (8, LANES), 1) // SPAN

    def entry(e, carry):
        i = e // 2
        owner, rank, top, left = (place_ref[4 * e + k] for k in range(4))
        here = lane == rank
        shift = rank * SPAN - left
        turns = [lax.rem(shift - KN * half + 2 * LANES, LANES) for half in (0, 1)]
        for b in range(bands):
            for c in range(2):
                rows = out_ref[i, b, pl.ds(2 * top + c, 8, stride=2), :]
                for half in (0, 1):
                    to = slice(16 * (2 * b + c) + 8 * half, 16 * (2 * b + c) + 8 * half + 8)
                    moved = pltpu.roll(rows, turns[half], 1)
                    windows[owner, to, :] = jnp.where(here, moved, windows[owner, to, :])
        return carry

    lax.fori_loop(0, 2 * granules, entry, 0)
    send_ref[...] = windows[...].astype(bf16)


def cubic(distance):
    near = (1.5 * distance - 2.5) * distance * distance + 1.0
    far = ((2.5 - 0.5 * distance) * distance - 4.0) * distance + 2.0
    return jnp.where(distance <= 1.0, near, jnp.where(distance < 2.0, far, 0.0))


def interp_weights(table_ref, rows_out, cols_out):
    pixels, lanes = rows_out.shape

    def step(t, carry):
        at = pl.ds(pl.multiple_of(t * LANES, LANES), LANES)
        for n, ref in ((0, rows_out), (3, cols_out)):
            start, knot, beyond = (table_ref[n + k : n + k + 1, at] for k in range(3))
            for r in range(0, pixels, 16):
                pixel = (lax.broadcasted_iota(jnp.int32, (16, LANES), 0) + r).astype(f32)
                place = pixel * (1.0 / SP) + start
                value = cubic(jnp.abs(place - knot)) + cubic(jnp.abs(place - beyond))
                ref[r : r + 16, at] = value.astype(bf16)
        return carry

    lax.fori_loop(0, lanes // LANES, step, 0)


def compose(covers_ref, received_ref, row_ref, col_ref, pixels_ref, out_ref, passed):
    senders = received_ref.shape[0]
    bands = out_ref.shape[1]
    lane = lax.broadcasted_iota(jnp.int32, (16, LANES), 1) // SPAN
    masks = [(lane == r).astype(f32).astype(bf16) for r in range(LANES // SPAN)]

    def sender(n, carry):
        at = pl.ds(pl.multiple_of(n * LANES, LANES), LANES)
        blocks = []
        for k in range(2 * bands):
            window = received_ref[n, 16 * k : 16 * k + 16, :]
            blocks.append(jnp.concatenate([window * mask for mask in masks], axis=0))
        rows = jnp.dot(row_ref[:, at], jnp.concatenate(blocks, axis=1), preferred_element_type=f32)
        for k in range(2 * bands):
            passed[k, :, at] = rows[:, LANES * k : LANES * k + LANES].astype(bf16)
        return carry

    lax.fori_loop(0, senders, sender, 0)
    scale = 1.0 / covers_ref[0].astype(f32)
    for b in range(bands):
        fields = [
            lax.dot_general(
                passed[2 * b + c], col_ref[...], (((1,), (1,)), ((), ())), preferred_element_type=f32
            )
            * scale
            for c in range(2)
        ]
        pixels = pixels_ref[0, b].astype(f32)
        out_ref[0, b] = (pixels * (1.0 + fields[0]) + fields[1]).astype(bf16)


def per_device(
    prior_grids,
    pif_rhs,
    pif_diagonal,
    pif_cross,
    pif_coupling,
    neighbour_offset,
    neighbour_count,
    tile_route,
    tile_window,
    tile_pixels,
):
    granules, bands = prior_grids.shape[:2]
    slots = pif_coupling.shape[1]
    own_index = lax.axis_index("gran")
    device_total = lax.axis_size("gran")
    band_total = lax.axis_size("band")
    groups = slots * granules // 8

    def by_lane_tile(array):
        cut = array.reshape(array.shape[:2] + (array.shape[2], 32, LANES)).transpose(0, 1, 3, 2, 4)
        return cut.reshape(array.shape[:2] + (32 * array.shape[2], LANES))

    grids = by_lane_tile(prior_grids)
    rhs = by_lane_tile(pif_rhs)
    diagonal = by_lane_tile(pif_diagonal)
    cross = by_lane_tile(pif_cross.transpose(1, 0, 2).reshape(bands, granules // 8, 8, KN * KN))
    coupling = by_lane_tile(pif_coupling.transpose(0, 2, 1, 3))
    side = (own_index % 2).astype(jnp.int32).reshape(1)
    offsets = neighbour_offset.reshape(-1)
    edge = (REACH, bands, 64, LANES)
    own = (granules, bands, 64, LANES)
    ext = (granules + 2 * REACH, bands, 64, LANES)

    near_pairs = [(i, i ^ 1) for i in range(device_total)]
    far_pairs = [
        pair for i in range(1, device_total - 1, 2) for pair in ((i, i + 1), (i + 1, i))
    ]

    def exchange(near, far):
        far = lax.ppermute(far, "gran", far_pairs)
        near = lax.ppermute(near, "gran", near_pairs)
        return near, far

    near, far = call(first_edges, [("s", side), ("v", grids)], [(edge, bf16), (edge, bf16)])
    near, far = exchange(near, far)
    extended, rhs, diagonal, cross, coupling = call(
        arrange,
        [("v", grids), ("v", rhs), ("v", diagonal), ("v", cross), ("v", coupling)],
        [
            (ext, f32),
            (own, f32),
            (own, f32),
            ((granules, bands, 32, LANES), f32),
            ((granules, slots, bands, 32, LANES), bf16),
        ],
        [pltpu.VMEM((bands, 32 * slots, LANES), f32)],
    )

    entries = 2 * granules
    capacity = max(2, 4 * granules // device_total)
    route_table = tile_route.reshape(device_total, entries)
    window_table = tile_window.reshape(device_total, entries, 2)
    order = jnp.arange(entries, dtype=jnp.int32)
    same_tile = route_table[:, :, None] == route_table[:, None, :]
    ranks = jnp.sum((same_tile & (order[None, :] < order[:, None])[None]).astype(jnp.int32), axis=2)

    def first_pair(start):
        return jnp.clip(start // SP - 1, 0, KN - SPAN) // 2

    def first_knot(start):
        return jnp.clip(start // SP - 1, 0, KN - SPAN)

    my_routes = lax.dynamic_index_in_dim(route_table, own_index, 0, keepdims=False)
    my_ranks = lax.dynamic_index_in_dim(ranks, own_index, 0, keepdims=False)
    my_windows = lax.dynamic_index_in_dim(window_table, own_index, 0, keepdims=False)
    places = jnp.stack(
        [my_routes, my_ranks, first_pair(my_windows[:, 0]), first_knot(my_windows[:, 1])], axis=1
    ).reshape(-1)

    seats = LANES // SPAN
    matched = (route_table == own_index)[:, None, :] & (
        ranks[:, None, :] == jnp.arange(seats, dtype=jnp.int32)[None, :, None]
    )
    live = jnp.any(matched, axis=2)
    starts = jnp.sum(jnp.where(matched[..., None], window_table[:, None], 0), axis=2)
    step = jnp.arange(SPAN, dtype=jnp.int32)
    row_knots = 2 * (first_pair(starts[..., 0])[..., None] + step % 8) + step // 8
    col_knots = first_knot(starts[..., 1])[..., None] + step
    table = []
    for start, knots in ((starts[..., 0], row_knots), (starts[..., 1], col_knots)):
        table.append(jnp.broadcast_to(start[..., None], knots.shape).astype(f32) / SP)
        table.append(jnp.where(live[..., None], knots, 4 * KN).astype(f32))
        beyond = jnp.where(knots == 0, -1, jnp.where(knots == KN - 1, KN, 4 * KN))
        table.append(jnp.where(live[..., None], beyond, 4 * KN).astype(f32))
    table = jnp.stack(table + table[:2]).reshape(8, device_total * LANES)
    pixel_count = tile_pixels.shape[2]
    weight_shape = (pixel_count, device_total * LANES)
    row_weights, col_weights = call(
        interp_weights, [("v", table)], [(weight_shape, bf16), (weight_shape, bf16)]
    )

    for sweep in range(SWEEPS):
        extended, partial = call(
            disparities,
            [("s", side), ("s", offsets), ("s", neighbour_count), ("v", near), ("v", far), ("v", extended)],
            [(ext, f32), ((64, LANES), f32)],
            [pltpu.VMEM((groups, 64, LANES), f32)],
            aliases={5: 0},
        )
        shares = [
            lax.ppermute(partial, "band", [(i, i ^ flip) for i in range(band_total)])
            for flip in range(1, band_total)
        ]
        inputs = [("s", offsets), ("s", neighbour_count), ("v", partial)]
        inputs += [("v", share) for share in shares]
        inputs += [("v", extended), ("v", rhs), ("v", diagonal), ("v", cross), ("v", coupling)]
        weights = pltpu.VMEM((groups, 64, LANES), f32)
        if sweep < SWEEPS - 1:
            extended, near, far = call(
                middle_sweep,
                [("s", side)] + inputs,
                [(ext, f32), (edge, bf16), (edge, bf16)],
                [weights],
            )
            near, far = exchange(near, far)
        else:
            windows = (device_total, 2 * bands * SPAN, LANES)
            balanced, payload = call(
                last_sweep,
                [("s", places)] + inputs,
                [(own, f32), (windows, bf16)],
                [weights, pltpu.VMEM(windows, f32)],
            )
    received = lax.all_to_all(payload, "gran", split_axis=0, concat_axis=0, tiled=True)
    covers = jnp.sum((tile_route == own_index).astype(jnp.int32)).reshape(1)
    (corrected,) = call(
        compose,
        [("s", covers), ("v", received), ("v", row_weights), ("v", col_weights), ("v", tile_pixels)],
        [(tile_pixels.shape, bf16)],
        [pltpu.VMEM((2 * bands, pixel_count, device_total * LANES), bf16)],
    )
    balanced = balanced.reshape(granules, bands, 32, 2, LANES).transpose(0, 1, 3, 2, 4)
    return (balanced.reshape(prior_grids.shape), corrected)


def solution(mesh):
    placed = (
        P("gran", "band", None, None),
        P("gran", "band", None, None),
        P("gran", "band", None, None),
        P("gran", "band", None),
        P("gran", None, "band", None),
        P("gran", None),
        P("gran"),
        P(),
        P(),
        P("gran", "band", None, None),
    )
    return jax.shard_map(
        per_device,
        mesh=mesh,
        in_specs=placed,
        out_specs=(P("gran", "band", None, None), P("gran", "band", None, None)),
        check_vma=False,
    )
```

```python
import functools
import jax
import jax.numpy as jnp
from jax import lax
from jax.experimental import pallas as pl
from jax.experimental.pallas import tpu as pltpu
from jax.sharding import PartitionSpec as P

BANDS = 12
KN = 64
PATCH = 8
REACH = 4
SWEEPS = 3
SP = 32
LANES = 128
SPAN = 16

robust_scale = 0.3

ON_CHIP = pl.BlockSpec(memory_space=pltpu.VMEM)
ANYWHERE = pl.BlockSpec(memory_space=pl.ANY)
f32 = jnp.float32
bf16 = jnp.bfloat16


def call(body, inputs, outputs, scratch=(), aliases=None, limit=16):
    operands = [
        pltpu.with_memory_space_constraint(array, pltpu.VMEM) if kind == "v" else array
        for kind, array in inputs
    ]
    return pl.pallas_call(
        body,
        in_specs=[ON_CHIP if kind == "v" else ANYWHERE for kind, _ in inputs],
        out_specs=tuple(ON_CHIP if kind == "v" else ANYWHERE for kind, _, _ in outputs),
        out_shape=tuple(
            pltpu.VMEM(shape, dtype) if kind == "v" else jax.ShapeDtypeStruct(shape, dtype)
            for kind, shape, dtype in outputs
        ),
        scratch_shapes=list(scratch),
        input_output_aliases=aliases or {},
        compiler_params=pltpu.CompilerParams(vmem_limit_bytes=limit * 2**20),
    )(*operands)


def parity():
    return lax.rem(lax.axis_index("gran"), 2)


def first_edges(grids_ref, near_ref, far_ref, raw, sems):
    odd = parity()
    last = grids_ref.shape[0] - REACH
    sides = ((far_ref, odd * last), (near_ref, (1 - odd) * last))
    copies = [
        pltpu.make_async_copy(grids_ref.at[pl.ds(base, REACH)], raw.at[k], sems.at[k])
        for k, (_, base) in enumerate(sides)
    ]
    for copy in copies:
        copy.start()
    for k, (ref, _) in enumerate(sides):
        copies[k].wait()
        for g in range(REACH):
            for b in range(ref.shape[1]):
                for j in range(4):
                    both = [raw[k, g, b, pl.ds(2 * j + c, 8, stride=8), :] for c in range(2)]
                    ref[g, b, 16 * j : 16 * j + 16, :] = jnp.concatenate(both, axis=0).astype(bf16)


def arrange(grids_ref, rhs_ref, diag_ref, cross_ref, coupling_ref, ext_ref, rhs_out, diag_out, cross_out, coupling_out, grids_raw, cross_raw, coupling_raw, wide, sems):
    granules, bands = grids_ref.shape[:2]
    slots = coupling_out.shape[1]
    chunks = sems.shape[1]
    size = granules // chunks
    whole = pltpu.make_async_copy(cross_ref, cross_raw, sems.at[4, 0])
    whole.start()
    copies = []
    for n in range(chunks):
        part = pl.ds(n * size, size)
        moves = ((coupling_ref, coupling_raw), (diag_ref, diag_out), (grids_ref, grids_raw), (rhs_ref, rhs_out))
        copies.append(
            [
                pltpu.make_async_copy(source.at[part], target.at[part], sems.at[k, n])
                for k, (source, target) in enumerate(moves)
            ]
        )
        for copy in copies[n]:
            copy.start()
    whole.wait()

    def step(i, carry):
        for b in range(bands):
            wide[b] = coupling_raw[i, b].astype(f32)
        for b in range(bands):
            for j in range(4):
                d = []
                for c in range(2):
                    rows = pl.ds(2 * j + c, 8, stride=8)
                    to = slice(16 * j + 8 * c, 16 * j + 8 * c + 8)
                    ext_ref[i + REACH, b, to, :] = grids_raw[i, b, rows, :]
                    d.append(diag_out[i, b, rows, :])
                pick = cross_raw[b, i // 8, pl.ds(8 * j + i % 8, 8, stride=32), :]
                cross_out[i, b, 8 * j : 8 * j + 8, :] = pick * jnp.sqrt(d[0] * d[1])
        for b in range(bands):
            for s in range(slots):
                for j in (0, 2):
                    pair = [wide[b, pl.ds(8 * (j + k) + s, 8, stride=32), :] for k in (0, 1)]
                    coupling_out[i, s, b, 8 * j : 8 * j + 16, :] = jnp.concatenate(pair, axis=0).astype(bf16)
        return carry

    for n in range(chunks):
        for copy in copies[n]:
            copy.wait()
        lax.fori_loop(n * size, (n + 1) * size, step, 0)


def lane_sums():
    row = lax.broadcasted_iota(jnp.int32, (LANES, LANES), 0)
    col = lax.broadcasted_iota(jnp.int32, (LANES, LANES), 1)
    return ((row % KN) // PATCH == col % PATCH).astype(f32).astype(bf16)


def lane_spread():
    row = lax.broadcasted_iota(jnp.int32, (LANES, LANES), 0)
    col = lax.broadcasted_iota(jnp.int32, (LANES, LANES), 1)
    return ((col % KN) // PATCH == row % PATCH).astype(f32).astype(bf16)


def read_graph(offset_ref, count_ref, graph):
    slots, granules = offset_ref.shape
    slot = lax.broadcasted_iota(jnp.int32, offset_ref.shape, 0)
    codes = jnp.sum(jnp.left_shift(offset_ref[...] + REACH, 4 * slot), axis=0, keepdims=True)
    counts = count_ref[...]
    for i in range(granules):
        graph[0, i] = codes[0, i]
        graph[1, i] = counts[0, i]


def neighbour(graph, i, s):
    return i + jnp.bitwise_and(jnp.right_shift(graph[0, i], 4 * s), 15)


def group_mask(interior, slots):
    row = lax.broadcasted_iota(jnp.int32, (64, LANES), 0) // 32
    lane = lax.broadcasted_iota(jnp.int32, (64, LANES), 1) // PATCH
    return lane - slots * (1 - row if interior else row)


def disparities(interior, offset_ref, count_ref, ext_ref, gathered, graph):
    bands = ext_ref.shape[1]
    granules = ext_ref.shape[0] - 2 * REACH
    slots = gathered.shape[0]
    gathered[...] = jnp.zeros_like(gathered)
    read_graph(offset_ref, count_ref, graph)

    def response(g):
        return [
            ext_ref[g, b, 16 * j : 16 * j + 8, :] + ext_ref[g, b, 16 * j + 8 : 16 * j + 16, :]
            for b in range(bands)
            for j in range(4)
        ]

    for i in range(granules):
        if (REACH <= i < granules - REACH) != interior:
            continue
        own = response(i + REACH)

        def slot(s, carry, i=i, own=own):
            total = None
            for a, o in zip(own, response(neighbour(graph, i, s))):
                d = a - o
                total = d * d if total is None else total + d * d
            gathered[s, 8 * (i % 8) : 8 * (i % 8) + 8, :] = total
            return carry

        lax.fori_loop(0, graph[1, i], slot, 0)
    sums = jnp.dot(
        gathered[...].reshape(slots * 64, LANES).astype(bf16), lane_sums(), preferred_element_type=f32
    )
    place = group_mask(interior, slots)
    packed = jnp.zeros((64, LANES), f32)
    for s in range(slots):
        packed = jnp.where(place == s, sums[64 * s : 64 * s + 64], packed)
    return packed


def interior_disparities(offset_ref, count_ref, ext_ref, out_ref, gathered, graph):
    out_ref[...] = disparities(True, offset_ref, count_ref, ext_ref, gathered, graph)


def edge_disparities(offset_ref, count_ref, near_ref, far_ref, inner_ref, ext_in, ext_ref, out_ref, gathered, graph):
    del ext_in
    odd = parity()
    right = ext_ref.shape[0] - REACH
    for ref, base in ((near_ref, (1 - odd) * right), (far_ref, odd * right)):
        for g in range(REACH):
            for b in range(ref.shape[1]):
                ext_ref[base + g, b] = ref[g, b].astype(f32)
    out_ref[...] = inner_ref[...] + disparities(False, offset_ref, count_ref, ext_ref, gathered, graph)


def spread_weights(shares, interior, weights):
    slots = weights.shape[0]
    total = (shares[0][...] + shares[1][...]) + (shares[2][...] + shares[3][...])
    robust = 1.0 / (1.0 + total * (1.0 / (robust_scale * BANDS * PATCH * PATCH)))
    high = robust.astype(bf16).astype(f32)
    both = jnp.concatenate([high, robust - high], axis=1)
    place = group_mask(interior, slots)
    place = jnp.concatenate([place, place], axis=1)
    spread = lane_spread()
    spread = jnp.concatenate([spread, spread], axis=0)
    stacked = jnp.concatenate(
        [jnp.where(place == s, both, 0.0).astype(bf16) for s in range(slots)], axis=0
    )
    weights[...] = jnp.dot(stacked, spread, preferred_element_type=f32).reshape(slots, 64, LANES)


def balance(i, ext_ref, rhs_ref, diag_ref, cross_ref, coupling_ref, weights, graph, store):
    bands = rhs_ref.shape[1]
    row = pl.multiple_of(lax.rem(i, 8) * 8, 8)
    parts = [(b, j) for b in range(bands) for j in range(4)]
    rhs = tuple(rhs_ref[i, b, pl.ds(2 * j + c, 8, stride=8), :] for b, j in parts for c in range(2))

    def slot(s, sums):
        sigma, drive = sums
        weight = weights[s, pl.ds(row, 8), :]
        n = neighbour(graph, i, s)
        new_sigma, new_drive = [], []
        for b in range(bands):
            coupling = coupling_ref[i, s, b].astype(f32)
            for j in range(4):
                k = 4 * b + j
                effective = weight * coupling[8 * j : 8 * j + 8]
                new_sigma.append(sigma[k] + effective)
                for c in range(2):
                    grid = ext_ref[n, b, 16 * j + 8 * c : 16 * j + 8 * c + 8, :]
                    new_drive.append(drive[2 * k + c] + effective * grid)
        return tuple(new_sigma), tuple(new_drive)

    zero = jnp.zeros((8, LANES), f32)
    sigma, drive = lax.fori_loop(0, graph[1, i], slot, ((zero,) * len(parts), rhs))
    for k, (b, j) in enumerate(parts):
        first, second = (
            diag_ref[i, b, pl.ds(2 * j + c, 8, stride=8), :] + sigma[k] for c in range(2)
        )
        cross = cross_ref[i, b, 8 * j : 8 * j + 8, :]
        inverse = 1.0 / (first * second - cross * cross)
        gain, offset = drive[2 * k], drive[2 * k + 1]
        store(
            b,
            j,
            (second * gain - cross * offset) * inverse,
            (first * offset - cross * gain) * inverse,
        )


def edge_sweep(offset_ref, count_ref, *refs):
    shares, state, (new_ref, near_ref, far_ref, weights, graph) = refs[:4], refs[4:9], refs[9:]
    read_graph(offset_ref, count_ref, graph)
    spread_weights(shares, False, weights)
    odd = parity()
    last = new_ref.shape[0] - 3 * REACH
    for ref, base in ((far_ref, odd * last), (near_ref, (1 - odd) * last)):

        def step(g, carry, ref=ref, base=base):
            def store(b, j, gain, offset):
                both = jnp.concatenate([gain, offset], axis=0)
                new_ref[base + g + REACH, b, 16 * j : 16 * j + 16, :] = both
                ref[g, b, 16 * j : 16 * j + 16, :] = both.astype(bf16)

            balance(base + g, *state, weights, graph, store)
            return carry

        lax.fori_loop(0, REACH, step, 0)


def interior_sweep(offset_ref, count_ref, *refs):
    shares, state, (_, new_ref, weights, graph) = refs[:4], refs[4:9], refs[9:]
    read_graph(offset_ref, count_ref, graph)
    spread_weights(shares, True, weights)

    def step(i, carry):
        def store(b, j, gain, offset):
            both = jnp.concatenate([gain, offset], axis=0)
            new_ref[i + REACH, b, 16 * j : 16 * j + 16, :] = both

        balance(i, *state, weights, graph, store)
        return carry

    lax.fori_loop(REACH, new_ref.shape[0] - 3 * REACH, step, 0)


def own_columns(ref, at, granules):
    first = lax.axis_index("gran") * granules
    base = pl.multiple_of((first // LANES) * LANES, LANES)
    turn = jnp.bitwise_and(LANES - lax.rem(first, LANES), LANES - 1)
    return pltpu.roll(ref[at + (pl.ds(base, LANES),)], turn, 1)


def last_sweep(offset_ref, count_ref, *refs):
    shares, state, (route_ref, window_ref) = refs[:4], refs[4:9], refs[9:11]
    out_ref, send_ref, solved, windows, weights, graph, ranks, sems = refs[11:]
    granules, bands = solved.shape[:2]
    read_graph(offset_ref, count_ref, graph)
    windows[...] = jnp.zeros_like(windows)
    for owner in range(windows.shape[0]):
        ranks[owner] = 0
    chunks = sems.shape[0]
    size = granules // chunks
    copies = []
    for interior in (True, False):
        spread_weights(shares, interior, weights)

        def step(t, carry, interior=interior):
            i = t if interior else jnp.where(t < REACH, t, t + granules - 2 * REACH)

            def store(b, j, gain, offset):
                solved[i, b, pl.ds(2 * j, 8, stride=8), :] = gain
                solved[i, b, pl.ds(2 * j + 1, 8, stride=8), :] = offset

            balance(i, *state, weights, graph, store)
            return carry

        lax.fori_loop(*((REACH, granules - REACH) if interior else (0, 2 * REACH)), step, 0)
        for n in range(chunks):
            if (REACH <= n * size < granules - REACH) == interior:
                part = pl.ds(n * size, size)
                copies.append(pltpu.make_async_copy(solved.at[part], out_ref.at[part], sems.at[n]))
                copies[-1].start()
    lane = lax.broadcasted_iota(jnp.int32, (8, LANES), 1) // SPAN
    routes = own_columns(route_ref, (slice(None),), granules)
    tops, lefts = [], []
    for r in range(2):
        starts = own_columns(window_ref, (r, slice(None)), granules)
        knots = jnp.clip(jnp.right_shift(starts, 5) - 1, 0, KN - SPAN)
        tops.append(jnp.right_shift(knots, 1))
        lefts.append(knots)
    for i in range(granules):
        for r in range(2):
            owner = routes[r, i]
            rank = ranks[owner]
            ranks[owner] = rank + 1
            top = tops[r][0, i]
            turn = rank * SPAN - lefts[r][1, i] + LANES
            here = lane == rank
            for b in range(bands):
                for c in range(2):
                    rows = solved[i, b, pl.ds(2 * top + c, 8, stride=2), :]
                    for half in (0, 1):
                        at = 16 * (2 * b + c) + 8 * half
                        moved = pltpu.roll(rows, jnp.bitwise_and(turn + KN * half, LANES - 1), 1)
                        pltpu.store(windows.at[owner, at : at + 8, :], moved, mask=here)
    send_ref[...] = windows[...].astype(bf16)
    for copy in copies:
        copy.wait()


def cubic(distance):
    near = (1.5 * distance - 2.5) * distance * distance + 1.0
    far = ((2.5 - 0.5 * distance) * distance - 4.0) * distance + 2.0
    return jnp.where(distance <= 1.0, near, jnp.where(distance < 2.0, far, 0.0))


def interp_weights(route_ref, window_ref, rows_out, cols_out):
    pixels, lanes = rows_out.shape
    senders = lanes // LANES
    granules = route_ref.shape[1] // senders
    own = lax.axis_index("gran")
    lane = lax.broadcasted_iota(jnp.int32, (8, LANES), 1)
    seat, step = lane // SPAN, lane % SPAN

    def sender(n, carry):
        first = n * granules
        base = pl.multiple_of((first // LANES) * LANES, LANES)
        turn = jnp.bitwise_and(LANES - lax.rem(first, LANES), LANES - 1)
        at = pl.ds(base, LANES)
        routes = pltpu.roll(route_ref[:, at], turn, 1)
        starts = [pltpu.roll(window_ref[r, :, at], turn, 1) for r in range(2)]
        rank = jnp.int32(0)
        place = [jnp.full((8, LANES), -1, jnp.int32) for _ in range(2)]
        for i in range(granules):
            for r in range(2):
                hit = routes[r, i] == own
                here = seat == jnp.where(hit, rank, -1)
                rank = rank + hit.astype(jnp.int32)
                for k in range(2):
                    place[k] = jnp.where(here, starts[r][k, i], place[k])
        to = pl.ds(pl.multiple_of(n * LANES, LANES), LANES)
        for k, ref in ((0, rows_out), (1, cols_out)):
            first_knot = jnp.clip(jnp.right_shift(place[k], 5) - 1, 0, KN - SPAN)
            if k == 0:
                knot = 2 * jnp.right_shift(first_knot, 1) + 2 * (step % 8) + step // 8
            else:
                knot = first_knot + step
            beyond = jnp.where(knot == 0, -1, jnp.where(knot == KN - 1, KN, 4 * KN))
            dead = place[k] < 0
            knot = jnp.where(dead, 4 * KN, knot).astype(f32)
            beyond = jnp.where(dead, 4 * KN, beyond).astype(f32)
            start = place[k].astype(f32) * (1.0 / SP)
            knot, beyond = start - knot, start - beyond
            pixel = lax.broadcasted_iota(jnp.int32, (8, LANES), 0).astype(f32) * (1.0 / SP)
            for r in range(0, pixels, 16):
                values = []
                for q in (r, r + 8):
                    at_pixel = pixel + q * (1.0 / SP)
                    values.append(cubic(jnp.abs(at_pixel + knot)) + cubic(jnp.abs(at_pixel + beyond)))
                ref[r : r + 16, to] = jnp.concatenate(values, axis=0).astype(bf16)
        return carry

    lax.fori_loop(0, senders, sender, 0)


def compose(route_ref, received_ref, row_ref, col_ref, pixels_ref, out_ref, passed, result, sems):
    senders = received_ref.shape[0]
    bands = result.shape[0]
    lane = lax.broadcasted_iota(jnp.int32, (16, LANES), 1) // SPAN
    masks = [(lane == r).astype(f32).astype(bf16) for r in range(LANES // SPAN)]
    named = (route_ref[...] == lax.axis_index("gran")).astype(f32)
    scale = 1.0 / jnp.sum(named, keepdims=True)

    def sender(n, carry):
        at = pl.ds(pl.multiple_of(n * LANES, LANES), LANES)
        blocks = []
        for k in range(2 * bands):
            window = received_ref[n, 16 * k : 16 * k + 16, :]
            blocks.append(jnp.concatenate([window * mask for mask in masks], axis=0))
        rows = jnp.dot(row_ref[:, at], jnp.concatenate(blocks, axis=1), preferred_element_type=f32)
        for k in range(2 * bands):
            passed[k, :, at] = rows[:, LANES * k : LANES * k + LANES].astype(bf16)
        return carry

    lax.fori_loop(0, senders, sender, 0)
    copies = []
    for b in range(bands):
        fields = [
            lax.dot_general(
                passed[2 * b + c], col_ref[...], (((1,), (1,)), ((), ())), preferred_element_type=f32
            )
            * scale
            for c in range(2)
        ]
        pixels = pixels_ref[0, b].astype(f32)
        result[b] = (pixels * (1.0 + fields[0]) + fields[1]).astype(bf16)
        copies.append(pltpu.make_async_copy(result.at[b], out_ref.at[0, b], sems.at[b]))
        copies[b].start()
    for copy in copies:
        copy.wait()


def per_device(
    prior_grids,
    pif_rhs,
    pif_diagonal,
    pif_cross,
    pif_coupling,
    neighbour_offset,
    neighbour_count,
    tile_route,
    tile_window,
    tile_pixels,
):
    granules, bands = prior_grids.shape[:2]
    slots = pif_coupling.shape[1]
    pixel_count = tile_pixels.shape[2]
    device_total = lax.axis_size("gran")
    band_total = lax.axis_size("band")

    def by_lane_tile(array):
        cut = array.reshape(array.shape[:2] + (array.shape[2], 32, LANES)).transpose(0, 1, 3, 2, 4)
        return cut.reshape(array.shape[:2] + (32 * array.shape[2], LANES))

    grids = by_lane_tile(prior_grids)
    rhs = by_lane_tile(pif_rhs)
    diagonal = by_lane_tile(pif_diagonal)
    cross = by_lane_tile(pif_cross.transpose(1, 0, 2).reshape(bands, granules // 8, 8, KN * KN))
    coupling = by_lane_tile(pif_coupling.transpose(0, 2, 1, 3))
    graph = [("v", neighbour_offset.T), ("v", neighbour_count[None, :])]
    tiles = [("v", tile_route.T), ("v", tile_window.transpose(1, 2, 0))]
    edge = (REACH, bands, 64, LANES)
    own = (granules, bands, 64, LANES)
    ext = (granules + 2 * REACH, bands, 64, LANES)
    packed = ("v", (64, LANES), f32)
    chunks = 4

    near_pairs = [(i, i ^ 1) for i in range(device_total)]
    far_pairs = [
        pair for i in range(1, device_total - 1, 2) for pair in ((i, i + 1), (i + 1, i))
    ]

    def exchange(near, far):
        far = lax.ppermute(far, "gran", far_pairs)
        near = lax.ppermute(near, "gran", near_pairs)
        return near, far

    near, far = call(
        first_edges,
        [("a", grids)],
        [("v", edge, bf16), ("v", edge, bf16)],
        [pltpu.VMEM((2,) + edge, f32), pltpu.SemaphoreType.DMA((2,))],
    )
    near, far = exchange(near, far)
    extended, rhs, diagonal, cross, coupling = call(
        arrange,
        [("a", grids), ("a", rhs), ("a", diagonal), ("a", cross), ("a", coupling)],
        [
            ("v", ext, f32),
            ("v", own, f32),
            ("v", own, f32),
            ("v", (granules, bands, 32, LANES), f32),
            ("v", (granules, slots, bands, 32, LANES), bf16),
        ],
        [
            pltpu.VMEM(own, f32),
            pltpu.VMEM(cross.shape, f32),
            pltpu.VMEM(coupling.shape, bf16),
            pltpu.VMEM((bands, 32 * slots, LANES), f32),
            pltpu.SemaphoreType.DMA((5, chunks)),
        ],
    )
    gathered = pltpu.VMEM((slots, 64, LANES), f32)
    weights = pltpu.VMEM((slots, 64, LANES), f32)
    scalars = pltpu.SMEM((2, granules), jnp.int32)

    for sweep in range(SWEEPS):
        (inner,) = call(
            interior_disparities, graph + [("v", extended)], [packed], [gathered, scalars]
        )
        if sweep == 1:
            weight_shape = (pixel_count, device_total * LANES)
            row_weights, col_weights = call(
                interp_weights, tiles, [("v", weight_shape, bf16), ("v", weight_shape, bf16)]
            )
        extended, partial = call(
            edge_disparities,
            graph + [("v", near), ("v", far), ("v", inner), ("v", extended)],
            [("v", ext, f32), packed],
            [gathered, scalars],
            aliases={5: 0},
        )
        shares = [partial] + [
            lax.ppermute(partial, "band", [(i, i ^ flip) for i in range(band_total)])
            for flip in range(1, band_total)
        ]
        inputs = graph + [("v", share) for share in shares]
        inputs += [("v", extended), ("v", rhs), ("v", diagonal), ("v", cross), ("v", coupling)]
        if sweep < SWEEPS - 1:
            updated, near, far = call(
                edge_sweep,
                inputs,
                [("v", ext, f32), ("v", edge, bf16), ("v", edge, bf16)],
                [weights, scalars],
            )
            near, far = exchange(near, far)
            (extended,) = call(
                interior_sweep,
                inputs + [("v", updated)],
                [("v", ext, f32)],
                [weights, scalars],
                aliases={len(inputs): 0},
            )
        else:
            windows = (device_total, 2 * bands * SPAN, LANES)
            balanced, payload = call(
                last_sweep,
                inputs + tiles,
                [("a", own, f32), ("v", windows, bf16)],
                [
                    pltpu.VMEM(own, f32),
                    pltpu.VMEM(windows, f32),
                    weights,
                    scalars,
                    pltpu.SMEM((device_total,), jnp.int32),
                    pltpu.SemaphoreType.DMA((chunks,)),
                ],
            )
    received = lax.all_to_all(payload, "gran", split_axis=0, concat_axis=0, tiled=True)
    (corrected,) = call(
        compose,
        [tiles[0], ("v", received), ("v", row_weights), ("v", col_weights), ("v", tile_pixels)],
        [("a", tile_pixels.shape, bf16)],
        [
            pltpu.VMEM((2 * bands, pixel_count, device_total * LANES), bf16),
            pltpu.VMEM(tile_pixels.shape[1:], bf16),
            pltpu.SemaphoreType.DMA((bands,)),
        ],
        limit=32,
    )
    balanced = balanced.reshape(granules, bands, 32, 2, LANES).transpose(0, 1, 3, 2, 4)
    return (balanced.reshape(prior_grids.shape), corrected)


def solution(mesh):
    placed = (
        P("gran", "band", None, None),
        P("gran", "band", None, None),
        P("gran", "band", None, None),
        P("gran", "band", None),
        P("gran", None, "band", None),
        P("gran", None),
        P("gran"),
        P(),
        P(),
        P("gran", "band", None, None),
    )
    return jax.shard_map(
        per_device,
        mesh=mesh,
        in_specs=placed,
        out_specs=(P("gran", "band", None, None), P("gran", "band", None, None)),
        check_vma=False,
    )
```

```python
import functools
import jax
import jax.numpy as jnp
from jax import lax
from jax.experimental import pallas as pl
from jax.experimental.pallas import tpu as pltpu
from jax.sharding import PartitionSpec as P

BANDS = 12
KN = 64
PATCH = 8
REACH = 4
SWEEPS = 3
SP = 32
LANES = 128
SPAN = 16

robust_scale = 0.3

ON_CHIP = pl.BlockSpec(memory_space=pltpu.VMEM)
ANYWHERE = pl.BlockSpec(memory_space=pl.ANY)
f32 = jnp.float32
bf16 = jnp.bfloat16


def call(body, inputs, outputs, scratch=(), aliases=None, limit=16):
    operands = [
        pltpu.with_memory_space_constraint(array, pltpu.VMEM if kind == "v" else pltpu.HBM)
        for kind, array in inputs
    ]
    return pl.pallas_call(
        body,
        in_specs=[ON_CHIP if kind == "v" else ANYWHERE for kind, _ in inputs],
        out_specs=tuple(ON_CHIP if kind == "v" else ANYWHERE for kind, _, _ in outputs),
        out_shape=tuple(
            (pltpu.VMEM if kind == "v" else pltpu.HBM)(shape, dtype)
            for kind, shape, dtype in outputs
        ),
        scratch_shapes=list(scratch),
        input_output_aliases=aliases or {},
        compiler_params=pltpu.CompilerParams(vmem_limit_bytes=limit * 2**20),
    )(*operands)


def parity():
    return lax.rem(lax.axis_index("gran"), 2)


def first_edges(grids_ref, near_ref, far_ref, raw, sems):
    odd = parity()
    last = grids_ref.shape[0] - REACH
    sides = ((far_ref, odd * last), (near_ref, (1 - odd) * last))
    copies = [
        pltpu.make_async_copy(grids_ref.at[pl.ds(base, REACH)], raw.at[k], sems.at[k])
        for k, (_, base) in enumerate(sides)
    ]
    for copy in copies:
        copy.start()
    for k, (ref, _) in enumerate(sides):
        copies[k].wait()
        for g in range(REACH):
            for b in range(ref.shape[1]):
                for j in range(4):
                    both = [raw[k, g, b, pl.ds(2 * j + c, 8, stride=8), :] for c in range(2)]
                    ref[g, b, 16 * j : 16 * j + 16, :] = jnp.concatenate(both, axis=0).astype(bf16)


def arrange_grids(grids_ref, ext_ref, raw, sems):
    granules, bands = grids_ref.shape[:2]
    chunks = sems.shape[0]
    size = granules // chunks
    copies = []
    for n in range(chunks):
        part = pl.ds(n * size, size)
        copies.append(pltpu.make_async_copy(grids_ref.at[part], raw.at[part], sems.at[n]))
        copies[n].start()

    def step(i, carry):
        for b in range(bands):
            for q in range(8):
                ext_ref[i + REACH, b, 8 * q : 8 * q + 8, :] = raw[i, b, pl.ds(q, 8, stride=8), :]
        return carry

    for n in range(chunks):
        copies[n].wait()
        lax.fori_loop(n * size, (n + 1) * size, step, 0)


def arrange(rhs_ref, diag_ref, cross_ref, coupling_ref, rhs_out, diag_out, cross_out, coupling_out, cross_raw, coupling_raw, wide, sems):
    granules, bands = rhs_ref.shape[:2]
    slots = coupling_out.shape[1]
    chunks = sems.shape[1]
    size = granules // chunks
    copies = []
    for n in range(chunks):
        part = pl.ds(n * size, size)
        moves = ((coupling_ref, coupling_raw), (diag_ref, diag_out))
        copies.append(
            [
                pltpu.make_async_copy(source.at[part], target.at[part], sems.at[k, n])
                for k, (source, target) in enumerate(moves)
            ]
        )
        for copy in copies[n]:
            copy.start()
        if n == 0:
            whole = pltpu.make_async_copy(cross_ref, cross_raw, sems.at[2, 0])
            whole.start()
    rest = pltpu.make_async_copy(rhs_ref, rhs_out, sems.at[2, 1])
    rest.start()

    def step(i, carry):
        for b in range(bands):
            wide[b] = coupling_raw[i, b].astype(f32)
        for b in range(bands):
            for j in range(4):
                d = [diag_out[i, b, pl.ds(2 * j + c, 8, stride=8), :] for c in range(2)]
                pick = cross_raw[b, i // 8, pl.ds(8 * j + i % 8, 8, stride=32), :]
                cross_out[i, b, 8 * j : 8 * j + 8, :] = pick * jnp.sqrt(d[0] * d[1])
        for b in range(bands):
            for s in range(slots):
                for j in (0, 2):
                    pair = [wide[b, pl.ds(8 * (j + k) + s, 8, stride=32), :] for k in (0, 1)]
                    coupling_out[i, s, b, 8 * j : 8 * j + 16, :] = jnp.concatenate(pair, axis=0).astype(bf16)
        return carry

    for n in range(chunks):
        for copy in copies[n]:
            copy.wait()
        if n == 0:
            whole.wait()
        lax.fori_loop(n * size, (n + 1) * size, step, 0)
    rest.wait()


def lane_sums():
    row = lax.broadcasted_iota(jnp.int32, (LANES, LANES), 0)
    col = lax.broadcasted_iota(jnp.int32, (LANES, LANES), 1)
    return ((row % KN) // PATCH == col % PATCH).astype(f32).astype(bf16)


def lane_spread():
    row = lax.broadcasted_iota(jnp.int32, (LANES, LANES), 0)
    col = lax.broadcasted_iota(jnp.int32, (LANES, LANES), 1)
    return ((col % KN) // PATCH == row % PATCH).astype(f32).astype(bf16)


def read_graph(offset_ref, count_ref, graph):
    slots, granules = offset_ref.shape
    slot = lax.broadcasted_iota(jnp.int32, offset_ref.shape, 0)
    codes = jnp.sum(jnp.left_shift(offset_ref[...] + REACH, 4 * slot), axis=0, keepdims=True)
    counts = count_ref[...]
    for i in range(granules):
        graph[0, i] = codes[0, i]
        graph[1, i] = counts[0, i]


def neighbour(graph, i, s):
    return i + jnp.bitwise_and(jnp.right_shift(graph[0, i], 4 * s), 15)


def group_mask(interior, slots):
    row = lax.broadcasted_iota(jnp.int32, (64, LANES), 0) // 32
    lane = lax.broadcasted_iota(jnp.int32, (64, LANES), 1) // PATCH
    return lane - slots * (1 - row if interior else row)


def disparities(interior, offset_ref, count_ref, ext_ref, gathered, graph):
    bands = ext_ref.shape[1]
    granules = ext_ref.shape[0] - 2 * REACH
    slots = gathered.shape[0]
    gathered[...] = jnp.zeros_like(gathered)
    read_graph(offset_ref, count_ref, graph)

    def response(g):
        return [
            ext_ref[g, b, 16 * j : 16 * j + 8, :] + ext_ref[g, b, 16 * j + 8 : 16 * j + 16, :]
            for b in range(bands)
            for j in range(4)
        ]

    for i in range(granules):
        if (REACH <= i < granules - REACH) != interior:
            continue
        own = response(i + REACH)

        def slot(s, carry, i=i, own=own):
            total = None
            for a, o in zip(own, response(neighbour(graph, i, s))):
                d = a - o
                total = d * d if total is None else total + d * d
            gathered[s, 8 * (i % 8) : 8 * (i % 8) + 8, :] = total
            return carry

        lax.fori_loop(0, graph[1, i], slot, 0)
    sums = jnp.dot(
        gathered[...].reshape(slots * 64, LANES).astype(bf16), lane_sums(), preferred_element_type=f32
    )
    place = group_mask(interior, slots)
    packed = jnp.zeros((64, LANES), f32)
    for s in range(slots):
        packed = jnp.where(place == s, sums[64 * s : 64 * s + 64], packed)
    return packed


def interior_disparities(offset_ref, count_ref, ext_ref, out_ref, gathered, graph):
    out_ref[...] = disparities(True, offset_ref, count_ref, ext_ref, gathered, graph)


def edge_disparities(offset_ref, count_ref, near_ref, far_ref, *refs):
    ext_ref, out_ref, gathered, graph = refs[-4:]
    odd = parity()
    right = ext_ref.shape[0] - REACH
    for ref, base in ((near_ref, (1 - odd) * right), (far_ref, odd * right)):
        for g in range(REACH):
            for b in range(ref.shape[1]):
                ext_ref[base + g, b] = ref[g, b].astype(f32)
    packed = disparities(False, offset_ref, count_ref, ext_ref, gathered, graph)
    out_ref[...] = packed + refs[1][...] if len(refs) == 6 else packed


def spread_weights(shares, interior, weights):
    slots = weights.shape[0]
    total = (shares[0][...] + shares[1][...]) + (shares[2][...] + shares[3][...])
    robust = 1.0 / (1.0 + total * (1.0 / (robust_scale * BANDS * PATCH * PATCH)))
    high = robust.astype(bf16).astype(f32)
    both = jnp.concatenate([high, robust - high], axis=1)
    place = group_mask(interior, slots)
    place = jnp.concatenate([place, place], axis=1)
    spread = lane_spread()
    spread = jnp.concatenate([spread, spread], axis=0)
    stacked = jnp.concatenate(
        [jnp.where(place == s, both, 0.0).astype(bf16) for s in range(slots)], axis=0
    )
    weights[...] = jnp.dot(stacked, spread, preferred_element_type=f32).reshape(slots, 64, LANES)


def balance(i, ext_ref, rhs_ref, diag_ref, cross_ref, coupling_ref, weights, graph, store):
    bands = rhs_ref.shape[1]
    row = pl.multiple_of(lax.rem(i, 8) * 8, 8)
    parts = [(b, j) for b in range(bands) for j in range(4)]
    rhs = tuple(rhs_ref[i, b, pl.ds(2 * j + c, 8, stride=8), :] for b, j in parts for c in range(2))

    def slot(s, sums):
        sigma, drive = sums
        weight = weights[s, pl.ds(row, 8), :]
        n = neighbour(graph, i, s)
        new_sigma, new_drive = [], []
        for b in range(bands):
            coupling = coupling_ref[i, s, b].astype(f32)
            for j in range(4):
                k = 4 * b + j
                effective = weight * coupling[8 * j : 8 * j + 8]
                new_sigma.append(sigma[k] + effective)
                for c in range(2):
                    grid = ext_ref[n, b, 16 * j + 8 * c : 16 * j + 8 * c + 8, :]
                    new_drive.append(drive[2 * k + c] + effective * grid)
        return tuple(new_sigma), tuple(new_drive)

    zero = jnp.zeros((8, LANES), f32)
    sigma, drive = lax.fori_loop(0, graph[1, i], slot, ((zero,) * len(parts), rhs))
    for k, (b, j) in enumerate(parts):
        first, second = (
            diag_ref[i, b, pl.ds(2 * j + c, 8, stride=8), :] + sigma[k] for c in range(2)
        )
        cross = cross_ref[i, b, 8 * j : 8 * j + 8, :]
        inverse = 1.0 / (first * second - cross * cross)
        gain, offset = drive[2 * k], drive[2 * k + 1]
        store(
            b,
            j,
            (second * gain - cross * offset) * inverse,
            (first * offset - cross * gain) * inverse,
        )


def edge_sweep(offset_ref, count_ref, *refs):
    shares, state, (new_ref, near_ref, far_ref, weights, graph) = refs[:4], refs[4:9], refs[9:]
    read_graph(offset_ref, count_ref, graph)
    spread_weights(shares, False, weights)
    odd = parity()
    last = new_ref.shape[0] - 3 * REACH
    for ref, base in ((far_ref, odd * last), (near_ref, (1 - odd) * last)):

        def step(g, carry, ref=ref, base=base):
            def store(b, j, gain, offset):
                both = jnp.concatenate([gain, offset], axis=0)
                new_ref[base + g + REACH, b, 16 * j : 16 * j + 16, :] = both
                ref[g, b, 16 * j : 16 * j + 16, :] = both.astype(bf16)

            balance(base + g, *state, weights, graph, store)
            return carry

        lax.fori_loop(0, REACH, step, 0)


def interior_sweep(offset_ref, count_ref, *refs):
    shares, state, (_, new_ref, weights, graph) = refs[:4], refs[4:9], refs[9:]
    read_graph(offset_ref, count_ref, graph)
    spread_weights(shares, True, weights)

    def step(i, carry):
        def store(b, j, gain, offset):
            both = jnp.concatenate([gain, offset], axis=0)
            new_ref[i + REACH, b, 16 * j : 16 * j + 16, :] = both

        balance(i, *state, weights, graph, store)
        return carry

    lax.fori_loop(REACH, new_ref.shape[0] - 3 * REACH, step, 0)


def own_columns(ref, at, granules):
    first = lax.axis_index("gran") * granules
    base = pl.multiple_of((first // LANES) * LANES, LANES)
    turn = jnp.bitwise_and(LANES - lax.rem(first, LANES), LANES - 1)
    return pltpu.roll(ref[at + (pl.ds(base, LANES),)], turn, 1)


def visits(granules, interior):
    inner = list(range(REACH, granules - REACH))
    return inner if interior else [i for i in range(granules) if i not in inner]


def last_sweep(interior, offset_ref, count_ref, *refs):
    shares, state, (route_ref, window_ref) = refs[:4], refs[4:9], refs[9:11]
    weights, graph, ranks, solved, sems = refs[-5:]
    if interior:
        out_ref, windows = refs[11:13]
    else:
        out_ref, send_ref, windows = refs[13:16]
    granules, bands = solved.shape[:2]
    inner = visits(granules, True)
    read_graph(offset_ref, count_ref, graph)
    if interior:
        windows[...] = jnp.zeros_like(windows)
    for owner in range(windows.shape[0]):
        ranks[owner] = 0
    spread_weights(shares, interior, weights)

    def step(t, carry):
        i = t if interior else jnp.where(t < REACH, t, t + granules - 2 * REACH)

        def store(b, j, gain, offset):
            solved[i, b, pl.ds(2 * j, 8, stride=8), :] = gain
            solved[i, b, pl.ds(2 * j + 1, 8, stride=8), :] = offset

        balance(i, *state, weights, graph, store)
        return carry

    lax.fori_loop(*((REACH, granules - REACH) if interior else (0, 2 * REACH)), step, 0)
    parts = ((REACH, granules - 2 * REACH),) if interior else ((0, REACH), (granules - REACH, REACH))
    copies = []
    for n, (first, size) in enumerate(parts):
        part = pl.ds(first, size)
        copies.append(pltpu.make_async_copy(solved.at[part], out_ref.at[part], sems.at[n]))
        copies[n].start()
    lane = lax.broadcasted_iota(jnp.int32, (8, LANES), 1) // SPAN
    routes = own_columns(route_ref, (slice(None),), granules)
    if not interior:
        for i in inner:
            for r in range(2):
                owner = routes[r, i]
                ranks[owner] = ranks[owner] + 1
    tops, lefts = [], []
    for r in range(2):
        starts = own_columns(window_ref, (r, slice(None)), granules)
        knots = jnp.clip(jnp.right_shift(starts, 5) - 1, 0, KN - SPAN)
        tops.append(jnp.right_shift(knots, 1))
        lefts.append(knots)
    for i in visits(granules, interior):
        for r in range(2):
            owner = routes[r, i]
            rank = ranks[owner]
            ranks[owner] = rank + 1
            top = tops[r][0, i]
            turn = rank * SPAN - lefts[r][1, i] + LANES
            here = lane == rank
            for b in range(bands):
                for c in range(2):
                    rows = solved[i, b, pl.ds(2 * top + c, 8, stride=2), :]
                    for half in (0, 1):
                        at = 16 * (2 * b + c) + 8 * half
                        moved = pltpu.roll(rows, jnp.bitwise_and(turn + KN * half, LANES - 1), 1)
                        pltpu.store(windows.at[owner, at : at + 8, :], moved, mask=here)
    if not interior:
        send_ref[...] = windows[...].astype(bf16)
    for copy in copies:
        copy.wait()


def cubic(distance):
    near = (1.5 * distance - 2.5) * distance * distance + 1.0
    far = ((2.5 - 0.5 * distance) * distance - 4.0) * distance + 2.0
    return jnp.where(distance <= 1.0, near, jnp.where(distance < 2.0, far, 0.0))


def interp_weights(route_ref, window_ref, rows_out, cols_out):
    pixels, lanes = rows_out.shape
    senders = lanes // LANES
    granules = route_ref.shape[1] // senders
    own = lax.axis_index("gran")
    lane = lax.broadcasted_iota(jnp.int32, (8, LANES), 1)
    seat, step = lane // SPAN, lane % SPAN

    def sender(n, carry):
        first = n * granules
        base = pl.multiple_of((first // LANES) * LANES, LANES)
        turn = jnp.bitwise_and(LANES - lax.rem(first, LANES), LANES - 1)
        at = pl.ds(base, LANES)
        routes = pltpu.roll(route_ref[:, at], turn, 1)
        starts = [pltpu.roll(window_ref[r, :, at], turn, 1) for r in range(2)]
        rank = jnp.int32(0)
        place = [jnp.full((8, LANES), -1, jnp.int32) for _ in range(2)]
        for i in visits(granules, True) + visits(granules, False):
            for r in range(2):
                hit = routes[r, i] == own
                here = seat == jnp.where(hit, rank, -1)
                rank = rank + hit.astype(jnp.int32)
                for k in range(2):
                    place[k] = jnp.where(here, starts[r][k, i], place[k])
        to = pl.ds(pl.multiple_of(n * LANES, LANES), LANES)
        for k, ref in ((0, rows_out), (1, cols_out)):
            first_knot = jnp.clip(jnp.right_shift(place[k], 5) - 1, 0, KN - SPAN)
            if k == 0:
                knot = 2 * jnp.right_shift(first_knot, 1) + 2 * (step % 8) + step // 8
            else:
                knot = first_knot + step
            beyond = jnp.where(knot == 0, -1, jnp.where(knot == KN - 1, KN, 4 * KN))
            dead = place[k] < 0
            knot = jnp.where(dead, 4 * KN, knot).astype(f32)
            beyond = jnp.where(dead, 4 * KN, beyond).astype(f32)
            start = place[k].astype(f32) * (1.0 / SP)
            knot, beyond = start - knot, start - beyond
            pixel = lax.broadcasted_iota(jnp.int32, (8, LANES), 0).astype(f32) * (1.0 / SP)
            for r in range(0, pixels, 16):
                values = []
                for q in (r, r + 8):
                    at_pixel = pixel + q * (1.0 / SP)
                    values.append(cubic(jnp.abs(at_pixel + knot)) + cubic(jnp.abs(at_pixel + beyond)))
                ref[r : r + 16, to] = jnp.concatenate(values, axis=0).astype(bf16)
        return carry

    lax.fori_loop(0, senders, sender, 0)


def compose(route_ref, received_ref, row_ref, col_ref, pixels_ref, out_ref, passed, result, sems):
    senders = received_ref.shape[0]
    bands = result.shape[0]
    lane = lax.broadcasted_iota(jnp.int32, (16, LANES), 1) // SPAN
    masks = [(lane == r).astype(f32).astype(bf16) for r in range(LANES // SPAN)]
    named = (route_ref[...] == lax.axis_index("gran")).astype(f32)
    scale = 1.0 / jnp.sum(named, keepdims=True)

    def sender(n, carry):
        at = pl.ds(pl.multiple_of(n * LANES, LANES), LANES)
        blocks = []
        for k in range(2 * bands):
            window = received_ref[n, 16 * k : 16 * k + 16, :]
            blocks.append(jnp.concatenate([window * mask for mask in masks], axis=0))
        rows = jnp.dot(row_ref[:, at], jnp.concatenate(blocks, axis=1), preferred_element_type=f32)
        for k in range(2 * bands):
            passed[k, :, at] = rows[:, LANES * k : LANES * k + LANES].astype(bf16)
        return carry

    lax.fori_loop(0, senders, sender, 0)
    copies = []
    for b in range(bands):
        fields = [
            lax.dot_general(
                passed[2 * b + c], col_ref[...], (((1,), (1,)), ((), ())), preferred_element_type=f32
            )
            * scale
            for c in range(2)
        ]
        pixels = pixels_ref[0, b].astype(f32)
        result[b] = (pixels * (1.0 + fields[0]) + fields[1]).astype(bf16)
        copies.append(pltpu.make_async_copy(result.at[b], out_ref.at[0, b], sems.at[b]))
        copies[b].start()
    for copy in copies:
        copy.wait()


def per_device(
    prior_grids,
    pif_rhs,
    pif_diagonal,
    pif_cross,
    pif_coupling,
    neighbour_offset,
    neighbour_count,
    tile_route,
    tile_window,
    tile_pixels,
):
    granules, bands = prior_grids.shape[:2]
    slots = pif_coupling.shape[1]
    pixel_count = tile_pixels.shape[2]
    device_total = lax.axis_size("gran")
    band_total = lax.axis_size("band")

    def by_lane_tile(array):
        cut = array.reshape(array.shape[:2] + (array.shape[2], 32, LANES)).transpose(0, 1, 3, 2, 4)
        return cut.reshape(array.shape[:2] + (32 * array.shape[2], LANES))

    grids = by_lane_tile(prior_grids)
    rhs = by_lane_tile(pif_rhs)
    diagonal = by_lane_tile(pif_diagonal)
    cross = by_lane_tile(pif_cross.transpose(1, 0, 2).reshape(bands, granules // 8, 8, KN * KN))
    coupling = by_lane_tile(pif_coupling.transpose(0, 2, 1, 3))
    graph = [("v", neighbour_offset.T), ("v", neighbour_count[None, :])]
    tiles = [("v", tile_route.T), ("v", tile_window.transpose(1, 2, 0))]
    edge = (REACH, bands, 64, LANES)
    own = (granules, bands, 64, LANES)
    ext = (granules + 2 * REACH, bands, 64, LANES)
    packed = ("v", (64, LANES), f32)
    chunks = 4

    near_pairs = [(i, i ^ 1) for i in range(device_total)]
    far_pairs = [
        pair for i in range(1, device_total - 1, 2) for pair in ((i, i + 1), (i + 1, i))
    ]

    def exchange(near, far):
        far = lax.ppermute(far, "gran", far_pairs)
        near = lax.ppermute(near, "gran", near_pairs)
        return near, far

    near, far = call(
        first_edges,
        [("h", grids)],
        [("v", edge, bf16), ("v", edge, bf16)],
        [pltpu.VMEM((2,) + edge, f32), pltpu.SemaphoreType.DMA((2,))],
    )
    near, far = exchange(near, far)
    (extended,) = call(
        arrange_grids,
        [("h", grids)],
        [("v", ext, f32)],
        [pltpu.VMEM(own, f32), pltpu.SemaphoreType.DMA((chunks,))],
    )
    rhs, diagonal, cross, coupling = call(
        arrange,
        [("h", rhs), ("h", diagonal), ("h", cross), ("h", coupling)],
        [
            ("v", own, f32),
            ("v", own, f32),
            ("v", (granules, bands, 32, LANES), f32),
            ("v", (granules, slots, bands, 32, LANES), bf16),
        ],
        [
            pltpu.VMEM(cross.shape, f32),
            pltpu.VMEM(coupling.shape, bf16),
            pltpu.VMEM((bands, 32 * slots, LANES), f32),
            pltpu.SemaphoreType.DMA((3, chunks)),
        ],
    )
    gathered = pltpu.VMEM((slots, 64, LANES), f32)
    weights = pltpu.VMEM((slots, 64, LANES), f32)
    scalars = pltpu.SMEM((2, granules), jnp.int32)

    def over_band(partial):
        return [("v", partial)] + [
            ("v", lax.ppermute(partial, "band", [(i, i ^ flip) for i in range(band_total)]))
            for flip in range(1, band_total)
        ]

    for sweep in range(SWEEPS):
        last = sweep == SWEEPS - 1
        (inner,) = call(
            interior_disparities, graph + [("v", extended)], [packed], [gathered, scalars]
        )
        if last:
            inner_shares = over_band(inner)
        if sweep == 1:
            weight_shape = (pixel_count, device_total * LANES)
            routes, starts, _ = lax.optimization_barrier((tiles[0][1], tiles[1][1], inner))
            row_weights, col_weights = call(
                interp_weights,
                [("v", routes), ("v", starts)],
                [("v", weight_shape, bf16), ("v", weight_shape, bf16)],
            )
            inner, row_weights, col_weights = lax.optimization_barrier(
                (inner, row_weights, col_weights)
            )
        inputs = graph + [("v", near), ("v", far), ("v", extended)]
        inputs += [] if last else [("v", inner)]
        extended, partial = call(
            edge_disparities,
            inputs,
            [("v", ext, f32), packed],
            [gathered, scalars],
            aliases={4: 0},
        )
        shares = over_band(partial)
        state = [("v", extended), ("v", rhs), ("v", diagonal), ("v", cross), ("v", coupling)]
        if not last:
            inputs = graph + shares + state
            updated, near, far = call(
                edge_sweep,
                inputs,
                [("v", ext, f32), ("v", edge, bf16), ("v", edge, bf16)],
                [weights, scalars],
            )
            near, far = exchange(near, far)
            (extended,) = call(
                interior_sweep,
                inputs + [("v", updated)],
                [("v", ext, f32)],
                [weights, scalars],
                aliases={len(inputs): 0},
            )
    windows = (device_total, 2 * bands * SPAN, LANES)
    scratch = [
        weights,
        scalars,
        pltpu.SMEM((device_total,), jnp.int32),
        pltpu.VMEM(own, f32),
        pltpu.SemaphoreType.DMA((2,)),
    ]
    inputs = graph + inner_shares + state + tiles
    balanced, gathered_windows = call(
        functools.partial(last_sweep, True),
        inputs,
        [("h", own, f32), ("v", windows, f32)],
        scratch,
    )
    inputs = graph + shares + state + tiles + [("h", balanced), ("v", gathered_windows)]
    balanced, payload, _ = call(
        functools.partial(last_sweep, False),
        inputs,
        [("h", own, f32), ("v", windows, bf16), ("v", windows, f32)],
        scratch,
        aliases={len(inputs) - 2: 0, len(inputs) - 1: 2},
    )
    received = lax.all_to_all(payload, "gran", split_axis=0, concat_axis=0, tiled=True)
    (corrected,) = call(
        compose,
        [tiles[0], ("v", received), ("v", row_weights), ("v", col_weights), ("v", tile_pixels)],
        [("h", tile_pixels.shape, bf16)],
        [
            pltpu.VMEM((2 * bands, pixel_count, device_total * LANES), bf16),
            pltpu.VMEM(tile_pixels.shape[1:], bf16),
            pltpu.SemaphoreType.DMA((bands,)),
        ],
        limit=32,
    )
    balanced = balanced.reshape(granules, bands, 32, 2, LANES).transpose(0, 1, 3, 2, 4)
    return (balanced.reshape(prior_grids.shape), corrected)


def solution(mesh):
    placed = (
        P("gran", "band", None, None),
        P("gran", "band", None, None),
        P("gran", "band", None, None),
        P("gran", "band", None),
        P("gran", None, "band", None),
        P("gran", None),
        P("gran"),
        P(),
        P(),
        P("gran", "band", None, None),
    )
    return jax.shard_map(
        per_device,
        mesh=mesh,
        in_specs=placed,
        out_specs=(P("gran", "band", None, None), P("gran", "band", None, None)),
        check_vma=False,
    )
```

```python
import functools
import jax
import jax.numpy as jnp
from jax import lax
from jax.experimental import pallas as pl
from jax.experimental.pallas import tpu as pltpu
from jax.sharding import PartitionSpec as P

BANDS = 12
KN = 64
PATCH = 8
REACH = 4
SWEEPS = 3
SP = 32
LANES = 128
SPAN = 16

robust_scale = 0.3

ON_CHIP = pl.BlockSpec(memory_space=pltpu.VMEM)
ANYWHERE = pl.BlockSpec(memory_space=pl.ANY)
f32 = jnp.float32
bf16 = jnp.bfloat16


def call(body, inputs, outputs, scratch=(), aliases=None, limit=16):
    operands = [
        pltpu.with_memory_space_constraint(array, pltpu.VMEM if kind == "v" else pltpu.HBM)
        for kind, array in inputs
    ]
    return pl.pallas_call(
        body,
        in_specs=[ON_CHIP if kind == "v" else ANYWHERE for kind, _ in inputs],
        out_specs=tuple(ON_CHIP if kind == "v" else ANYWHERE for kind, _, _ in outputs),
        out_shape=tuple(
            (pltpu.VMEM if kind == "v" else pltpu.HBM)(shape, dtype)
            for kind, shape, dtype in outputs
        ),
        scratch_shapes=list(scratch),
        input_output_aliases=aliases or {},
        compiler_params=pltpu.CompilerParams(vmem_limit_bytes=limit * 2**20),
    )(*operands)


def parity():
    return lax.rem(lax.axis_index("gran"), 2)


def first_edges(grids_ref, near_ref, far_ref, raw, sems):
    odd = parity()
    last = grids_ref.shape[0] - REACH
    sides = ((far_ref, odd * last), (near_ref, (1 - odd) * last))
    copies = [
        [pltpu.make_async_copy(grids_ref.at[base + g], raw.at[k, g], sems.at[k, g]) for g in range(REACH)]
        for k, (_, base) in enumerate(sides)
    ]
    for copy in copies[0] + copies[1]:
        copy.start()
    for k, (ref, _) in enumerate(sides):
        for g in range(REACH):
            copies[k][g].wait()
            for b in range(ref.shape[1]):
                for j in range(4):
                    both = [raw[k, g, b, pl.ds(2 * j + c, 8, stride=8), :] for c in range(2)]
                    ref[g, b, 16 * j : 16 * j + 16, :] = jnp.concatenate(both, axis=0).astype(bf16)


def arrange_grids(grids_ref, ext_ref, raw, sems):
    granules, bands = grids_ref.shape[:2]
    chunks = sems.shape[0]
    size = granules // chunks
    copies = []
    for n in range(chunks):
        part = pl.ds(n * size, size)
        copies.append(pltpu.make_async_copy(grids_ref.at[part], raw.at[part], sems.at[n]))
        copies[n].start()

    def step(i, carry):
        for b in range(bands):
            for q in range(8):
                ext_ref[i + REACH, b, 8 * q : 8 * q + 8, :] = raw[i, b, pl.ds(q, 8, stride=8), :]
        return carry

    for n in range(chunks):
        copies[n].wait()
        lax.fori_loop(n * size, (n + 1) * size, step, 0)


def visits(granules, interior):
    inner = list(range(REACH, granules - REACH))
    return inner if interior else [i for i in range(granules) if i not in inner]


def arrange(interior, rhs_ref, diag_ref, cross_ref, coupling_ref, rhs_out, diag_out, cross_out, coupling_out, cross_raw, coupling_raw, wide, sems):
    granules, bands = rhs_ref.shape[:2]
    slots = coupling_out.shape[1]
    own = visits(granules, interior)
    size = REACH
    chunks = len(own) // size
    copies = []
    for n in range(chunks):
        source, target = pl.ds(own[n * size], size), pl.ds(n * size, size)
        moves = ((coupling_ref, coupling_raw), (diag_ref, diag_out), (rhs_ref, rhs_out))
        copies.append(
            [
                pltpu.make_async_copy(here.at[source], there.at[target], sems.at[k, n])
                for k, (here, there) in enumerate(moves)
            ]
        )
        for copy in copies[n][:2]:
            copy.start()
        if n == 0:
            whole = pltpu.make_async_copy(cross_ref, cross_raw, sems.at[3, 0])
            whole.start()
    for n in range(chunks):
        copies[n][2].start()
    for n in range(chunks):
        for copy in copies[n][:2]:
            copy.wait()
        if n == 0:
            whole.wait()

        def step(g, carry, n=n):
            at = n * size + g
            i = own[n * size] + g
            for b in range(bands):
                wide[b] = coupling_raw[at, b].astype(f32)
            for b in range(bands):
                for j in range(4):
                    d = [diag_out[at, b, pl.ds(2 * j + c, 8, stride=8), :] for c in range(2)]
                    pick = cross_raw[b, i // 8, pl.ds(8 * j + i % 8, 8, stride=32), :]
                    cross_out[at, b, 8 * j : 8 * j + 8, :] = pick * jnp.sqrt(d[0] * d[1])
            for b in range(bands):
                for s in range(slots):
                    for j in (0, 2):
                        pair = [wide[b, pl.ds(8 * (j + k) + s, 8, stride=32), :] for k in (0, 1)]
                        coupling_out[at, s, b, 8 * j : 8 * j + 16, :] = jnp.concatenate(pair, axis=0).astype(bf16)
            return carry

        lax.fori_loop(0, size, step, 0)
    for n in range(chunks):
        copies[n][2].wait()


def lane_sums():
    row = lax.broadcasted_iota(jnp.int32, (LANES, LANES), 0)
    col = lax.broadcasted_iota(jnp.int32, (LANES, LANES), 1)
    return ((row % KN) // PATCH == col % PATCH).astype(f32).astype(bf16)


def lane_spread():
    row = lax.broadcasted_iota(jnp.int32, (LANES, LANES), 0)
    col = lax.broadcasted_iota(jnp.int32, (LANES, LANES), 1)
    return ((col % KN) // PATCH == row % PATCH).astype(f32).astype(bf16)


def read_graph(offset_ref, count_ref, graph):
    slots, granules = offset_ref.shape
    slot = lax.broadcasted_iota(jnp.int32, offset_ref.shape, 0)
    codes = jnp.sum(jnp.left_shift(offset_ref[...] + REACH, 4 * slot), axis=0, keepdims=True)
    counts = count_ref[...]
    for i in range(granules):
        graph[0, i] = codes[0, i]
        graph[1, i] = counts[0, i]


def neighbour(graph, i, s):
    return i + jnp.bitwise_and(jnp.right_shift(graph[0, i], 4 * s), 15)


def group_mask(interior, slots):
    row = lax.broadcasted_iota(jnp.int32, (64, LANES), 0) // 32
    lane = lax.broadcasted_iota(jnp.int32, (64, LANES), 1) // PATCH
    return lane - slots * (1 - row if interior else row)


def disparities(interior, offset_ref, count_ref, ext_ref, gathered, graph):
    bands = ext_ref.shape[1]
    granules = ext_ref.shape[0] - 2 * REACH
    slots = gathered.shape[0]
    gathered[...] = jnp.zeros_like(gathered)
    read_graph(offset_ref, count_ref, graph)

    def response(g):
        return [
            ext_ref[g, b, 16 * j : 16 * j + 8, :] + ext_ref[g, b, 16 * j + 8 : 16 * j + 16, :]
            for b in range(bands)
            for j in range(4)
        ]

    for i in range(granules):
        if (REACH <= i < granules - REACH) != interior:
            continue
        own = response(i + REACH)

        def slot(s, carry, i=i, own=own):
            total = None
            for a, o in zip(own, response(neighbour(graph, i, s))):
                d = a - o
                total = d * d if total is None else total + d * d
            gathered[s, 8 * (i % 8) : 8 * (i % 8) + 8, :] = total
            return carry

        lax.fori_loop(0, graph[1, i], slot, 0)
    sums = jnp.dot(
        gathered[...].reshape(slots * 64, LANES).astype(bf16), lane_sums(), preferred_element_type=f32
    )
    place = group_mask(interior, slots)
    packed = jnp.zeros((64, LANES), f32)
    for s in range(slots):
        packed = jnp.where(place == s, sums[64 * s : 64 * s + 64], packed)
    return packed


def interior_disparities(offset_ref, count_ref, ext_ref, out_ref, gathered, graph):
    out_ref[...] = disparities(True, offset_ref, count_ref, ext_ref, gathered, graph)


def edge_disparities(offset_ref, count_ref, near_ref, far_ref, *refs):
    ext_ref, out_ref, gathered, graph = refs[-4:]
    odd = parity()
    right = ext_ref.shape[0] - REACH
    for ref, base in ((near_ref, (1 - odd) * right), (far_ref, odd * right)):
        for g in range(REACH):
            for b in range(ref.shape[1]):
                ext_ref[base + g, b] = ref[g, b].astype(f32)
    packed = disparities(False, offset_ref, count_ref, ext_ref, gathered, graph)
    out_ref[...] = packed + refs[1][...] if len(refs) == 6 else packed


def spread_weights(shares, interior, weights):
    slots = weights.shape[0]
    total = (shares[0][...] + shares[1][...]) + (shares[2][...] + shares[3][...])
    robust = 1.0 / (1.0 + total * (1.0 / (robust_scale * BANDS * PATCH * PATCH)))
    high = robust.astype(bf16).astype(f32)
    both = jnp.concatenate([high, robust - high], axis=1)
    place = group_mask(interior, slots)
    place = jnp.concatenate([place, place], axis=1)
    spread = lane_spread()
    spread = jnp.concatenate([spread, spread], axis=0)
    stacked = jnp.concatenate(
        [jnp.where(place == s, both, 0.0).astype(bf16) for s in range(slots)], axis=0
    )
    weights[...] = jnp.dot(stacked, spread, preferred_element_type=f32).reshape(slots, 64, LANES)


def balance(i, at, ext_ref, rhs_ref, diag_ref, cross_ref, coupling_ref, weights, graph, store):
    bands = rhs_ref.shape[1]
    row = pl.multiple_of(lax.rem(i, 8) * 8, 8)
    parts = [(b, j) for b in range(bands) for j in range(4)]
    rhs = tuple(rhs_ref[at, b, pl.ds(2 * j + c, 8, stride=8), :] for b, j in parts for c in range(2))

    def slot(s, sums):
        sigma, drive = sums
        weight = weights[s, pl.ds(row, 8), :]
        n = neighbour(graph, i, s)
        new_sigma, new_drive = [], []
        for b in range(bands):
            coupling = coupling_ref[at, s, b].astype(f32)
            for j in range(4):
                k = 4 * b + j
                effective = weight * coupling[8 * j : 8 * j + 8]
                new_sigma.append(sigma[k] + effective)
                for c in range(2):
                    grid = ext_ref[n, b, 16 * j + 8 * c : 16 * j + 8 * c + 8, :]
                    new_drive.append(drive[2 * k + c] + effective * grid)
        return tuple(new_sigma), tuple(new_drive)

    zero = jnp.zeros((8, LANES), f32)
    sigma, drive = lax.fori_loop(0, graph[1, i], slot, ((zero,) * len(parts), rhs))
    for k, (b, j) in enumerate(parts):
        first, second = (
            diag_ref[at, b, pl.ds(2 * j + c, 8, stride=8), :] + sigma[k] for c in range(2)
        )
        cross = cross_ref[at, b, 8 * j : 8 * j + 8, :]
        inverse = 1.0 / (first * second - cross * cross)
        gain, offset = drive[2 * k], drive[2 * k + 1]
        store(
            b,
            j,
            (second * gain - cross * offset) * inverse,
            (first * offset - cross * gain) * inverse,
        )


def edge_sweep(offset_ref, count_ref, *refs):
    shares, state, (new_ref, near_ref, far_ref, weights, graph) = refs[:4], refs[4:9], refs[9:]
    read_graph(offset_ref, count_ref, graph)
    spread_weights(shares, False, weights)
    odd = parity()
    last = new_ref.shape[0] - 3 * REACH
    for ref, base in ((far_ref, odd * last), (near_ref, (1 - odd) * last)):

        def step(g, carry, ref=ref, base=base):
            def store(b, j, gain, offset):
                both = jnp.concatenate([gain, offset], axis=0)
                new_ref[base + g + REACH, b, 16 * j : 16 * j + 16, :] = both
                ref[g, b, 16 * j : 16 * j + 16, :] = both.astype(bf16)

            balance(base + g, lax.div(base, 2 * REACH) * REACH + g, *state, weights, graph, store)
            return carry

        lax.fori_loop(0, REACH, step, 0)


def interior_sweep(offset_ref, count_ref, *refs):
    shares, state, (_, new_ref, weights, graph) = refs[:4], refs[4:9], refs[9:]
    read_graph(offset_ref, count_ref, graph)
    spread_weights(shares, True, weights)

    def step(i, carry):
        def store(b, j, gain, offset):
            both = jnp.concatenate([gain, offset], axis=0)
            new_ref[i + REACH, b, 16 * j : 16 * j + 16, :] = both

        balance(i, i - REACH, *state, weights, graph, store)
        return carry

    lax.fori_loop(REACH, new_ref.shape[0] - 3 * REACH, step, 0)


def own_columns(ref, at, granules):
    first = lax.axis_index("gran") * granules
    base = pl.multiple_of((first // LANES) * LANES, LANES)
    turn = jnp.bitwise_and(LANES - lax.rem(first, LANES), LANES - 1)
    return pltpu.roll(ref[at + (pl.ds(base, LANES),)], turn, 1)


def last_sweep(interior, offset_ref, count_ref, *refs):
    shares, state, (route_ref, window_ref) = refs[:4], refs[4:9], refs[9:11]
    weights, graph, ranks, solved, sems = refs[-5:]
    if interior:
        out_ref, windows = refs[11:13]
    else:
        out_ref, send_ref, windows = refs[13:16]
    granules, bands = solved.shape[:2]
    inner = visits(granules, True)
    read_graph(offset_ref, count_ref, graph)
    if interior:
        windows[...] = jnp.zeros_like(windows)
    for owner in range(windows.shape[0]):
        ranks[owner] = 0
    spread_weights(shares, interior, weights)

    def step(t, carry):
        i = t if interior else jnp.where(t < REACH, t, t + granules - 2 * REACH)

        def store(b, j, gain, offset):
            solved[i, b, pl.ds(2 * j, 8, stride=8), :] = gain
            solved[i, b, pl.ds(2 * j + 1, 8, stride=8), :] = offset

        balance(i, t - REACH if interior else t, *state, weights, graph, store)
        return carry

    lax.fori_loop(*((REACH, granules - REACH) if interior else (0, 2 * REACH)), step, 0)
    parts = ((REACH, granules - 2 * REACH),) if interior else ((0, REACH), (granules - REACH, REACH))
    copies = []
    for n, (first, size) in enumerate(parts):
        part = pl.ds(first, size)
        copies.append(pltpu.make_async_copy(solved.at[part], out_ref.at[part], sems.at[n]))
        copies[n].start()
    lane = lax.broadcasted_iota(jnp.int32, (8, LANES), 1) // SPAN
    routes = own_columns(route_ref, (slice(None),), granules)
    if not interior:
        for i in inner:
            for r in range(2):
                owner = routes[r, i]
                ranks[owner] = ranks[owner] + 1
    tops, lefts = [], []
    for r in range(2):
        starts = own_columns(window_ref, (r, slice(None)), granules)
        knots = jnp.clip(jnp.right_shift(starts, 5) - 1, 0, KN - SPAN)
        tops.append(jnp.right_shift(knots, 1))
        lefts.append(knots)
    for i in visits(granules, interior):
        for r in range(2):
            owner = routes[r, i]
            rank = ranks[owner]
            ranks[owner] = rank + 1
            top = tops[r][0, i]
            turn = rank * SPAN - lefts[r][1, i] + LANES
            here = lane == rank
            for b in range(bands):
                for c in range(2):
                    rows = solved[i, b, pl.ds(2 * top + c, 8, stride=2), :]
                    for half in (0, 1):
                        at = 16 * (2 * b + c) + 8 * half
                        moved = pltpu.roll(rows, jnp.bitwise_and(turn + KN * half, LANES - 1), 1)
                        pltpu.store(windows.at[owner, at : at + 8, :], moved, mask=here)
    if not interior:
        send_ref[...] = windows[...].astype(bf16)
    for copy in copies:
        copy.wait()


def cubic(distance):
    near = (1.5 * distance - 2.5) * distance * distance + 1.0
    far = ((2.5 - 0.5 * distance) * distance - 4.0) * distance + 2.0
    return jnp.where(distance <= 1.0, near, jnp.where(distance < 2.0, far, 0.0))


def interp_weights(axis, route_ref, window_ref, out_ref):
    pixels, lanes = out_ref.shape
    senders = lanes // LANES
    granules = route_ref.shape[1] // senders
    own = lax.axis_index("gran")
    lane = lax.broadcasted_iota(jnp.int32, (8, LANES), 1)
    seat, step = lane // SPAN, lane % SPAN

    def sender(n, carry):
        first = n * granules
        base = pl.multiple_of((first // LANES) * LANES, LANES)
        turn = jnp.bitwise_and(LANES - lax.rem(first, LANES), LANES - 1)
        at = pl.ds(base, LANES)
        routes = pltpu.roll(route_ref[:, at], turn, 1)
        starts = [pltpu.roll(window_ref[r, :, at], turn, 1) for r in range(2)]
        rank = jnp.int32(0)
        place = jnp.full((8, LANES), -1, jnp.int32)
        for i in visits(granules, True) + visits(granules, False):
            for r in range(2):
                hit = routes[r, i] == own
                here = seat == jnp.where(hit, rank, -1)
                rank = rank + hit.astype(jnp.int32)
                place = jnp.where(here, starts[r][axis, i], place)
        to = pl.ds(pl.multiple_of(n * LANES, LANES), LANES)
        first_knot = jnp.clip(jnp.right_shift(place, 5) - 1, 0, KN - SPAN)
        if axis == 0:
            knot = 2 * jnp.right_shift(first_knot, 1) + 2 * (step % 8) + step // 8
        else:
            knot = first_knot + step
        beyond = jnp.where(knot == 0, -1, jnp.where(knot == KN - 1, KN, 4 * KN))
        dead = place < 0
        knot = jnp.where(dead, 4 * KN, knot).astype(f32)
        beyond = jnp.where(dead, 4 * KN, beyond).astype(f32)
        start = place.astype(f32) * (1.0 / SP)
        knot, beyond = start - knot, start - beyond
        pixel = lax.broadcasted_iota(jnp.int32, (8, LANES), 0).astype(f32) * (1.0 / SP)
        for r in range(0, pixels, 16):
            values = []
            for q in (r, r + 8):
                at_pixel = pixel + q * (1.0 / SP)
                values.append(cubic(jnp.abs(at_pixel + knot)) + cubic(jnp.abs(at_pixel + beyond)))
            out_ref[r : r + 16, to] = jnp.concatenate(values, axis=0).astype(bf16)
        return carry

    lax.fori_loop(0, senders, sender, 0)


def compose(route_ref, received_ref, row_ref, col_ref, pixels_ref, out_ref, passed, result, sems):
    senders = received_ref.shape[0]
    bands = result.shape[0]
    lane = lax.broadcasted_iota(jnp.int32, (16, LANES), 1) // SPAN
    masks = [(lane == r).astype(f32).astype(bf16) for r in range(LANES // SPAN)]
    named = (route_ref[...] == lax.axis_index("gran")).astype(f32)
    scale = 1.0 / jnp.sum(named, keepdims=True)

    def sender(n, carry):
        at = pl.ds(pl.multiple_of(n * LANES, LANES), LANES)
        blocks = []
        for k in range(2 * bands):
            window = received_ref[n, 16 * k : 16 * k + 16, :]
            blocks.append(jnp.concatenate([window * mask for mask in masks], axis=0))
        rows = jnp.dot(row_ref[:, at], jnp.concatenate(blocks, axis=1), preferred_element_type=f32)
        for k in range(2 * bands):
            passed[k, :, at] = rows[:, LANES * k : LANES * k + LANES].astype(bf16)
        return carry

    steps = min(8, senders)

    def several(n, carry):
        for k in range(steps):
            sender(n * steps + k, carry)
        return carry

    lax.fori_loop(0, senders // steps, several, 0)
    copies = []
    for b in range(bands):
        fields = [
            lax.dot_general(
                passed[2 * b + c], col_ref[...], (((1,), (1,)), ((), ())), preferred_element_type=f32
            )
            * scale
            for c in range(2)
        ]
        pixels = pixels_ref[0, b].astype(f32)
        result[b] = (pixels * (1.0 + fields[0]) + fields[1]).astype(bf16)
        copies.append(pltpu.make_async_copy(result.at[b], out_ref.at[0, b], sems.at[b]))
        copies[b].start()
    for copy in copies:
        copy.wait()


def per_device(
    prior_grids,
    pif_rhs,
    pif_diagonal,
    pif_cross,
    pif_coupling,
    neighbour_offset,
    neighbour_count,
    tile_route,
    tile_window,
    tile_pixels,
):
    granules, bands = prior_grids.shape[:2]
    slots = pif_coupling.shape[1]
    pixel_count = tile_pixels.shape[2]
    device_total = lax.axis_size("gran")
    band_total = lax.axis_size("band")

    def by_lane_tile(array):
        cut = array.reshape(array.shape[:2] + (array.shape[2], 32, LANES)).transpose(0, 1, 3, 2, 4)
        return cut.reshape(array.shape[:2] + (32 * array.shape[2], LANES))

    grids = by_lane_tile(prior_grids)
    rhs = by_lane_tile(pif_rhs)
    diagonal = by_lane_tile(pif_diagonal)
    cross = by_lane_tile(pif_cross.transpose(1, 0, 2).reshape(bands, granules // 8, 8, KN * KN))
    coupling = by_lane_tile(pif_coupling.transpose(0, 2, 1, 3))
    graph = [("v", neighbour_offset.T), ("v", neighbour_count[None, :])]
    tiles = [("v", tile_route.T), ("v", tile_window.transpose(1, 2, 0))]
    edge = (REACH, bands, 64, LANES)
    own = (granules, bands, 64, LANES)
    ext = (granules + 2 * REACH, bands, 64, LANES)
    packed = ("v", (64, LANES), f32)
    chunks = 4

    near_pairs = [(i, i ^ 1) for i in range(device_total)]
    far_pairs = [
        pair for i in range(1, device_total - 1, 2) for pair in ((i, i + 1), (i + 1, i))
    ]

    def exchange(near, far):
        far = lax.ppermute(far, "gran", far_pairs)
        near = lax.ppermute(near, "gran", near_pairs)
        return near, far

    near, far = call(
        first_edges,
        [("h", grids)],
        [("v", edge, bf16), ("v", edge, bf16)],
        [pltpu.VMEM((2,) + edge, f32), pltpu.SemaphoreType.DMA((2, REACH))],
    )
    near, far = exchange(near, far)
    (extended,) = call(
        arrange_grids,
        [("h", grids)],
        [("v", ext, f32)],
        [pltpu.VMEM(own, f32), pltpu.SemaphoreType.DMA((chunks,))],
    )
    sources = [rhs, diagonal, cross, coupling]

    def arranged(interior, sources):
        part = len(visits(granules, interior))
        some = (part, bands, 64, LANES)
        return call(
            functools.partial(arrange, interior),
            [("h", source) for source in sources],
            [
                ("v", some, f32),
                ("v", some, f32),
                ("v", (part, bands, 32, LANES), f32),
                ("v", (part, slots, bands, 32, LANES), bf16),
            ],
            [
                pltpu.VMEM(cross.shape, f32),
                pltpu.VMEM((part,) + coupling.shape[1:], bf16),
                pltpu.VMEM((bands, 32 * slots, LANES), f32),
                pltpu.SemaphoreType.DMA((4, chunks)),
            ],
        )

    def interpolation(axis, after):
        weight_shape = (pixel_count, device_total * LANES)
        routes, starts, _ = lax.optimization_barrier((tiles[0][1], tiles[1][1], after))
        return call(
            functools.partial(interp_weights, axis),
            [("v", routes), ("v", starts)],
            [("v", weight_shape, bf16)],
        )[0]

    gathered = pltpu.VMEM((slots, 64, LANES), f32)
    weights = pltpu.VMEM((slots, 64, LANES), f32)
    scalars = pltpu.SMEM((2, granules), jnp.int32)

    def over_band(partial):
        return [("v", partial)] + [
            ("v", lax.ppermute(partial, "band", [(i, i ^ flip) for i in range(band_total)]))
            for flip in range(1, band_total)
        ]

    for sweep in range(SWEEPS):
        last = sweep == SWEEPS - 1
        (inner,) = call(
            interior_disparities, graph + [("v", extended)], [packed], [gathered, scalars]
        )
        if sweep == 0:
            inner, *edge_state = lax.optimization_barrier((inner, *arranged(False, sources)))
        if sweep == 1:
            inner, row_weights = lax.optimization_barrier((inner, interpolation(0, inner)))
        if last:
            inner_shares = over_band(inner)
        inputs = graph + [("v", near), ("v", far), ("v", extended)]
        inputs += [] if last else [("v", inner)]
        extended, partial = call(
            edge_disparities,
            inputs,
            [("v", ext, f32), packed],
            [gathered, scalars],
            aliases={4: 0},
        )
        shares = over_band(partial)
        if sweep == 0:
            *later, _ = lax.optimization_barrier((*sources, partial))
            partial, *inner_state = lax.optimization_barrier((partial, *arranged(True, later)))
            shares[0] = ("v", partial)
        if sweep == 1:
            partial, col_weights = lax.optimization_barrier((partial, interpolation(1, partial)))
            shares[0] = ("v", partial)
        edge_state_now = [("v", extended)] + [("v", array) for array in edge_state]
        inner_state_now = [("v", extended)] + [("v", array) for array in inner_state]
        if not last:
            inputs = graph + shares + edge_state_now
            updated, near, far = call(
                edge_sweep,
                inputs,
                [("v", ext, f32), ("v", edge, bf16), ("v", edge, bf16)],
                [weights, scalars],
            )
            near, far = exchange(near, far)
            inputs = graph + shares + inner_state_now
            (extended,) = call(
                interior_sweep,
                inputs + [("v", updated)],
                [("v", ext, f32)],
                [weights, scalars],
                aliases={len(inputs): 0},
            )
    windows = (device_total, 2 * bands * SPAN, LANES)
    scratch = [
        weights,
        scalars,
        pltpu.SMEM((device_total,), jnp.int32),
        pltpu.VMEM(own, f32),
        pltpu.SemaphoreType.DMA((2,)),
    ]
    inputs = graph + inner_shares + inner_state_now + tiles
    balanced, gathered_windows = call(
        functools.partial(last_sweep, True),
        inputs,
        [("h", own, f32), ("v", windows, f32)],
        scratch,
    )
    inputs = graph + shares + edge_state_now + tiles + [("h", balanced), ("v", gathered_windows)]
    balanced, payload, _ = call(
        functools.partial(last_sweep, False),
        inputs,
        [("h", own, f32), ("v", windows, bf16), ("v", windows, f32)],
        scratch,
        aliases={len(inputs) - 2: 0, len(inputs) - 1: 2},
    )
    received = lax.all_to_all(payload, "gran", split_axis=0, concat_axis=0, tiled=True)
    (corrected,) = call(
        compose,
        [tiles[0], ("v", received), ("v", row_weights), ("v", col_weights), ("v", tile_pixels)],
        [("h", tile_pixels.shape, bf16)],
        [
            pltpu.VMEM((2 * bands, pixel_count, device_total * LANES), bf16),
            pltpu.VMEM(tile_pixels.shape[1:], bf16),
            pltpu.SemaphoreType.DMA((bands,)),
        ],
        limit=32,
    )
    balanced = balanced.reshape(granules, bands, 32, 2, LANES).transpose(0, 1, 3, 2, 4)
    return (balanced.reshape(prior_grids.shape), corrected)


def solution(mesh):
    placed = (
        P("gran", "band", None, None),
        P("gran", "band", None, None),
        P("gran", "band", None, None),
        P("gran", "band", None),
        P("gran", None, "band", None),
        P("gran", None),
        P("gran"),
        P(),
        P(),
        P("gran", "band", None, None),
    )
    return jax.shard_map(
        per_device,
        mesh=mesh,
        in_specs=placed,
        out_specs=(P("gran", "band", None, None), P("gran", "band", None, None)),
        check_vma=False,
    )
```

```python
import functools
import jax
import jax.numpy as jnp
from jax import lax
from jax.experimental import pallas as pl
from jax.experimental.pallas import tpu as pltpu
from jax.sharding import PartitionSpec as P

BANDS = 12
KN = 64
PATCH = 8
REACH = 4
SWEEPS = 3
SP = 32
LANES = 128
SPAN = 16

robust_scale = 0.3

ON_CHIP = pl.BlockSpec(memory_space=pltpu.VMEM)
ANYWHERE = pl.BlockSpec(memory_space=pl.ANY)
f32 = jnp.float32
bf16 = jnp.bfloat16


def call(body, inputs, outputs, scratch=(), aliases=None, limit=16):
    operands = [
        pltpu.with_memory_space_constraint(array, pltpu.VMEM if kind == "v" else pltpu.HBM)
        for kind, array in inputs
    ]
    return pl.pallas_call(
        body,
        in_specs=[ON_CHIP if kind == "v" else ANYWHERE for kind, _ in inputs],
        out_specs=tuple(ON_CHIP if kind == "v" else ANYWHERE for kind, _, _ in outputs),
        out_shape=tuple(
            (pltpu.VMEM if kind == "v" else pltpu.HBM)(shape, dtype)
            for kind, shape, dtype in outputs
        ),
        scratch_shapes=list(scratch),
        input_output_aliases=aliases or {},
        compiler_params=pltpu.CompilerParams(vmem_limit_bytes=limit * 2**20),
    )(*operands)


def parity():
    return lax.rem(lax.axis_index("gran"), 2)


def first_edges(grids_ref, near_ref, far_ref, raw, sems):
    odd = parity()
    last = grids_ref.shape[0] - REACH
    sides = ((far_ref, odd * last), (near_ref, (1 - odd) * last))
    copies = [
        [pltpu.make_async_copy(grids_ref.at[base + g], raw.at[k, g], sems.at[k, g]) for g in range(REACH)]
        for k, (_, base) in enumerate(sides)
    ]
    for copy in copies[0] + copies[1]:
        copy.start()
    for k, (ref, _) in enumerate(sides):
        for g in range(REACH):
            copies[k][g].wait()
            for b in range(ref.shape[1]):
                for j in range(4):
                    both = [raw[k, g, b, pl.ds(2 * j + c, 8, stride=8), :] for c in range(2)]
                    ref[g, b, 16 * j : 16 * j + 16, :] = jnp.concatenate(both, axis=0).astype(bf16)


def arrange_grids(grids_ref, ext_ref, raw, sems):
    granules, bands = grids_ref.shape[:2]
    chunks = sems.shape[0]
    size = granules // chunks
    copies = []
    for n in range(chunks):
        part = pl.ds(n * size, size)
        copies.append(pltpu.make_async_copy(grids_ref.at[part], raw.at[part], sems.at[n]))
        copies[n].start()

    def step(i, carry):
        for b in range(bands):
            for q in range(8):
                ext_ref[i + REACH, b, 8 * q : 8 * q + 8, :] = raw[i, b, pl.ds(q, 8, stride=8), :]
        return carry

    for n in range(chunks):
        copies[n].wait()
        lax.fori_loop(n * size, (n + 1) * size, step, 0)


def visits(granules, interior):
    inner = list(range(REACH, granules - REACH))
    return inner if interior else [i for i in range(granules) if i not in inner]


def arrange(interior, rhs_ref, diag_ref, cross_ref, coupling_ref, rhs_out, diag_out, cross_out, coupling_out, cross_raw, coupling_raw, sems):
    granules, bands = rhs_ref.shape[:2]
    own = visits(granules, interior)
    size = REACH
    chunks = len(own) // size
    copies = []
    for n in range(chunks):
        source, target = pl.ds(own[n * size], size), pl.ds(n * size, size)
        moves = ((coupling_ref, coupling_raw), (diag_ref, diag_out), (rhs_ref, rhs_out))
        copies.append(
            [
                pltpu.make_async_copy(here.at[source], there.at[target], sems.at[k, n])
                for k, (here, there) in enumerate(moves)
            ]
        )
        for copy in copies[n][:2]:
            copy.start()
        if n == 0:
            whole = pltpu.make_async_copy(cross_ref, cross_raw, sems.at[3, 0])
            whole.start()
    for n in range(chunks):
        copies[n][2].start()
    for n in range(chunks):
        for copy in copies[n][:2]:
            copy.wait()
        if n == 0:
            whole.wait()

        def step(g, carry, n=n):
            at = n * size + g
            i = own[n * size] + g
            for b in range(bands):
                coupling_out[at, b] = coupling_raw[at, b].astype(f32)
                for j in range(4):
                    d = [diag_out[at, b, pl.ds(2 * j + c, 8, stride=8), :] for c in range(2)]
                    pick = cross_raw[b, i // 8, pl.ds(8 * j + i % 8, 8, stride=32), :]
                    cross_out[at, b, 8 * j : 8 * j + 8, :] = pick * jnp.sqrt(d[0] * d[1])
            return carry

        lax.fori_loop(0, size, step, 0)
    for n in range(chunks):
        copies[n][2].wait()


def lane_sums():
    row = lax.broadcasted_iota(jnp.int32, (LANES, LANES), 0)
    col = lax.broadcasted_iota(jnp.int32, (LANES, LANES), 1)
    return ((row % KN) // PATCH == col % PATCH).astype(f32).astype(bf16)


def lane_spread():
    row = lax.broadcasted_iota(jnp.int32, (LANES, LANES), 0)
    col = lax.broadcasted_iota(jnp.int32, (LANES, LANES), 1)
    return ((col % KN) // PATCH == row % PATCH).astype(f32).astype(bf16)


def read_graph(offset_ref, count_ref, graph):
    slots, granules = offset_ref.shape
    slot = lax.broadcasted_iota(jnp.int32, offset_ref.shape, 0)
    codes = jnp.sum(jnp.left_shift(offset_ref[...] + REACH, 4 * slot), axis=0, keepdims=True)
    counts = count_ref[...]
    for i in range(granules):
        graph[0, i] = codes[0, i]
        graph[1, i] = counts[0, i]


def neighbour(graph, i, s):
    return i + jnp.bitwise_and(jnp.right_shift(graph[0, i], 4 * s), 15)


def group_mask(interior, slots):
    row = lax.broadcasted_iota(jnp.int32, (64, LANES), 0) // 32
    lane = lax.broadcasted_iota(jnp.int32, (64, LANES), 1) // PATCH
    return lane - slots * (1 - row if interior else row)


def disparities(interior, offset_ref, count_ref, ext_ref, gathered, graph):
    bands = ext_ref.shape[1]
    granules = ext_ref.shape[0] - 2 * REACH
    slots = gathered.shape[0]
    gathered[...] = jnp.zeros_like(gathered)
    read_graph(offset_ref, count_ref, graph)

    def response(g):
        return [
            ext_ref[g, b, 16 * j : 16 * j + 8, :] + ext_ref[g, b, 16 * j + 8 : 16 * j + 16, :]
            for b in range(bands)
            for j in range(4)
        ]

    for i in range(granules):
        if (REACH <= i < granules - REACH) != interior:
            continue
        own = response(i + REACH)

        def slot(s, carry, i=i, own=own):
            total = None
            for a, o in zip(own, response(neighbour(graph, i, s))):
                d = a - o
                total = d * d if total is None else total + d * d
            gathered[s, 8 * (i % 8) : 8 * (i % 8) + 8, :] = total
            return carry

        lax.fori_loop(0, graph[1, i], slot, 0)
    sums = jnp.dot(
        gathered[...].reshape(slots * 64, LANES).astype(bf16), lane_sums(), preferred_element_type=f32
    )
    place = group_mask(interior, slots)
    packed = jnp.zeros((64, LANES), f32)
    for s in range(slots):
        packed = jnp.where(place == s, sums[64 * s : 64 * s + 64], packed)
    return packed


def interior_disparities(offset_ref, count_ref, ext_ref, out_ref, gathered, graph):
    out_ref[...] = disparities(True, offset_ref, count_ref, ext_ref, gathered, graph)


def edge_disparities(offset_ref, count_ref, near_ref, far_ref, *refs):
    ext_ref, out_ref, gathered, graph = refs[-4:]
    odd = parity()
    right = ext_ref.shape[0] - REACH
    for ref, base in ((near_ref, (1 - odd) * right), (far_ref, odd * right)):
        for g in range(REACH):
            for b in range(ref.shape[1]):
                ext_ref[base + g, b] = ref[g, b].astype(f32)
    packed = disparities(False, offset_ref, count_ref, ext_ref, gathered, graph)
    out_ref[...] = packed + refs[1][...] if len(refs) == 6 else packed


def spread_weights(shares, interior, weights):
    slots = weights.shape[0]
    total = (shares[0][...] + shares[1][...]) + (shares[2][...] + shares[3][...])
    robust = 1.0 / (1.0 + total * (1.0 / (robust_scale * BANDS * PATCH * PATCH)))
    high = robust.astype(bf16).astype(f32)
    both = jnp.concatenate([high, robust - high], axis=1)
    place = group_mask(interior, slots)
    place = jnp.concatenate([place, place], axis=1)
    spread = lane_spread()
    spread = jnp.concatenate([spread, spread], axis=0)
    stacked = jnp.concatenate(
        [jnp.where(place == s, both, 0.0).astype(bf16) for s in range(slots)], axis=0
    )
    weights[...] = jnp.dot(stacked, spread, preferred_element_type=f32).reshape(slots, 64, LANES)


def balance(i, at, ext_ref, rhs_ref, diag_ref, cross_ref, coupling_ref, weights, graph, store):
    bands = rhs_ref.shape[1]
    row = pl.multiple_of(lax.rem(i, 8) * 8, 8)
    parts = [(b, j) for b in range(bands) for j in range(4)]
    rhs = tuple(rhs_ref[at, b, pl.ds(2 * j + c, 8, stride=8), :] for b, j in parts for c in range(2))

    def slot(s, sums):
        sigma, drive = sums
        weight = weights[s, pl.ds(row, 8), :]
        n = neighbour(graph, i, s)
        new_sigma, new_drive = [], []
        for b in range(bands):
            for j in range(4):
                k = 4 * b + j
                effective = weight * coupling_ref[at, b, pl.ds(8 * j + s, 8, stride=32), :]
                new_sigma.append(sigma[k] + effective)
                for c in range(2):
                    grid = ext_ref[n, b, 16 * j + 8 * c : 16 * j + 8 * c + 8, :]
                    new_drive.append(drive[2 * k + c] + effective * grid)
        return tuple(new_sigma), tuple(new_drive)

    zero = jnp.zeros((8, LANES), f32)
    sigma, drive = lax.fori_loop(0, graph[1, i], slot, ((zero,) * len(parts), rhs))
    for k, (b, j) in enumerate(parts):
        first, second = (
            diag_ref[at, b, pl.ds(2 * j + c, 8, stride=8), :] + sigma[k] for c in range(2)
        )
        cross = cross_ref[at, b, 8 * j : 8 * j + 8, :]
        inverse = 1.0 / (first * second - cross * cross)
        gain, offset = drive[2 * k], drive[2 * k + 1]
        store(
            b,
            j,
            (second * gain - cross * offset) * inverse,
            (first * offset - cross * gain) * inverse,
        )


def edge_sweep(offset_ref, count_ref, *refs):
    shares, state, (new_ref, near_ref, far_ref, weights, graph) = refs[:4], refs[4:9], refs[9:]
    read_graph(offset_ref, count_ref, graph)
    spread_weights(shares, False, weights)
    odd = parity()
    last = new_ref.shape[0] - 3 * REACH
    for ref, base in ((far_ref, odd * last), (near_ref, (1 - odd) * last)):

        def step(g, carry, ref=ref, base=base):
            def store(b, j, gain, offset):
                both = jnp.concatenate([gain, offset], axis=0)
                new_ref[base + g + REACH, b, 16 * j : 16 * j + 16, :] = both
                ref[g, b, 16 * j : 16 * j + 16, :] = both.astype(bf16)

            balance(base + g, lax.div(base, 2 * REACH) * REACH + g, *state, weights, graph, store)
            return carry

        lax.fori_loop(0, REACH, step, 0)


def interior_sweep(offset_ref, count_ref, *refs):
    shares, state, (_, new_ref, weights, graph) = refs[:4], refs[4:9], refs[9:]
    read_graph(offset_ref, count_ref, graph)
    spread_weights(shares, True, weights)

    def step(i, carry):
        def store(b, j, gain, offset):
            both = jnp.concatenate([gain, offset], axis=0)
            new_ref[i + REACH, b, 16 * j : 16 * j + 16, :] = both

        balance(i, i - REACH, *state, weights, graph, store)
        return carry

    lax.fori_loop(REACH, new_ref.shape[0] - 3 * REACH, step, 0)


def own_columns(ref, at, granules):
    first = lax.axis_index("gran") * granules
    base = pl.multiple_of((first // LANES) * LANES, LANES)
    turn = jnp.bitwise_and(LANES - lax.rem(first, LANES), LANES - 1)
    return pltpu.roll(ref[at + (pl.ds(base, LANES),)], turn, 1)


def last_sweep(interior, offset_ref, count_ref, *refs):
    shares, state, place_ref = refs[:4], refs[4:9], refs[9]
    weights, graph, solved, sems = refs[-4:]
    if interior:
        out_ref, windows = refs[10:12]
    else:
        out_ref, send_ref, windows = refs[12:15]
    granules, bands = solved.shape[:2]
    read_graph(offset_ref, count_ref, graph)
    if interior:
        windows[...] = jnp.zeros_like(windows)
    spread_weights(shares, interior, weights)

    def step(t, carry):
        i = t if interior else jnp.where(t < REACH, t, t + granules - 2 * REACH)

        def store(b, j, gain, offset):
            solved[i, b, pl.ds(2 * j, 8, stride=8), :] = gain
            solved[i, b, pl.ds(2 * j + 1, 8, stride=8), :] = offset

        balance(i, t - REACH if interior else t, *state, weights, graph, store)
        return carry

    lax.fori_loop(*((REACH, granules - REACH) if interior else (0, 2 * REACH)), step, 0)
    parts = ((REACH, granules - 2 * REACH),) if interior else ((0, REACH), (granules - REACH, REACH))
    copies = []
    for n, (first, size) in enumerate(parts):
        part = pl.ds(first, size)
        copies.append(pltpu.make_async_copy(solved.at[part], out_ref.at[part], sems.at[n]))
        copies[n].start()
    lane = lax.broadcasted_iota(jnp.int32, (8, LANES), 1) // SPAN
    places = place_ref[...]
    for i in visits(granules, interior):
        for r in range(2):
            owner, rank, top, turn = (places[k, r * granules + i] for k in range(4))
            here = lane == rank
            for b in range(bands):
                for c in range(2):
                    rows = solved[i, b, pl.ds(2 * top + c, 8, stride=2), :]
                    for half in (0, 1):
                        at = 16 * (2 * b + c) + 8 * half
                        moved = pltpu.roll(rows, jnp.bitwise_and(turn + KN * half, LANES - 1), 1)
                        pltpu.store(windows.at[owner, at : at + 8, :], moved, mask=here)
    if not interior:
        send_ref[...] = windows[...].astype(bf16)
    for copy in copies:
        copy.wait()


def earlier(first, second, granules):
    def edge(i):
        return ((i < REACH) | (i >= granules - REACH)).astype(jnp.int32)

    def rank(entry):
        return (edge(entry[1]) * 2 + entry[0]) * granules + entry[1]

    return rank(first) < rank(second)


def spread_columns(row):
    return jnp.transpose(jnp.broadcast_to(row, (LANES, LANES)))


def tile_places(route_ref, window_ref, rows_out, cols_out, place_ref):
    pixels, lanes = rows_out.shape
    senders = lanes // LANES
    granules = route_ref.shape[1] // senders
    own = lax.axis_index("gran")
    lane_row = lax.broadcasted_iota(jnp.int32, (1, LANES), 1)

    def both_routes(rows):
        return jnp.where(lane_row < granules, rows[0:1], pltpu.roll(rows, granules, 1)[1:2])

    routes = own_columns(route_ref, (slice(None),), granules)
    starts = [own_columns(window_ref, (r, slice(None)), granules) for r in range(2)]
    named = both_routes(routes).astype(f32)
    col = lax.broadcasted_iota(jnp.int32, (LANES, LANES), 1)
    row = lax.broadcasted_iota(jnp.int32, (LANES, LANES), 0)
    before = earlier((row // granules, row % granules), (col // granules, col % granules), granules)
    before = before & (row < 2 * granules) & (spread_columns(named) == named)
    rank = jnp.sum(before.astype(f32), axis=0, keepdims=True).astype(jnp.int32)
    knots = [
        jnp.clip(jnp.right_shift(both_routes(jnp.concatenate([s[k : k + 1] for s in starts])), 5) - 1, 0, KN - SPAN)
        for k in range(2)
    ]
    turn = rank * SPAN - knots[1] + LANES
    place_ref[...] = jnp.concatenate(
        [named.astype(jnp.int32), rank, jnp.right_shift(knots[0], 1), turn] * 2, axis=0
    )

    wide = 2 * LANES
    col = lax.broadcasted_iota(jnp.int32, (wide, wide), 1)
    row = lax.broadcasted_iota(jnp.int32, (wide, wide), 0)
    route = [at // LANES for at in (row, col)]
    place = [at % LANES for at in (row, col)]
    before = earlier((route[0], place[0] % granules), (route[1], place[1] % granules), granules)
    before = before & (place[0] // granules == place[1] // granules)
    before = before.astype(f32).astype(bf16)
    seat = (lax.broadcasted_iota(jnp.int32, (LANES, LANES), 1) // SPAN).astype(f32)
    lane = lax.broadcasted_iota(jnp.int32, (8, LANES), 1)
    step = lane % SPAN
    pixel = lax.broadcasted_iota(jnp.int32, (8, LANES), 0).astype(f32) * (1.0 / SP)
    part = LANES // granules
    for t in range(route_ref.shape[1] // LANES):
        at = slice(t * LANES, (t + 1) * LANES)
        hits = [(route_ref[r : r + 1, at] == own).astype(f32) for r in range(2)]
        hits = jnp.broadcast_to(jnp.concatenate(hits, axis=1), (8, wide))
        ranks = jnp.dot(hits.astype(bf16), before, preferred_element_type=f32)
        ranks = jnp.where(hits > 0.5, ranks, -1.0)
        chosen, values = [], []
        for r in range(2):
            chosen.append((spread_columns(ranks[0:1, r * LANES : (r + 1) * LANES]) == seat).astype(f32).astype(bf16))
            sender = lax.broadcasted_iota(jnp.int32, (part, LANES), 0)
            within = lax.broadcasted_iota(jnp.int32, (part, LANES), 1) // granules == sender
            kinds = []
            for k in range(2):
                start = window_ref[r, k : k + 1, at]
                kinds += [jnp.right_shift(start, 5), jnp.bitwise_and(start, SP - 1)]
            kinds.append(jnp.ones((1, LANES), jnp.int32))
            values.append(jnp.concatenate([jnp.where(within, kind, 0).astype(f32) for kind in kinds], axis=0))
        found = jnp.dot(
            jnp.concatenate(values, axis=1).astype(bf16),
            jnp.concatenate(chosen, axis=0),
            preferred_element_type=f32,
        )
        for n in range(part):
            live = found[4 * part + n : 4 * part + n + 1] > 0.5
            for k, ref in ((0, rows_out), (1, cols_out)):
                base = found[2 * k * part + n : 2 * k * part + n + 1]
                rest = found[(2 * k + 1) * part + n : (2 * k + 1) * part + n + 1]
                first = jnp.clip(base.astype(jnp.int32) - 1, 0, KN - SPAN)
                if k == 0:
                    knot = 2 * jnp.right_shift(first, 1) + 2 * (step % 8) + step // 8
                else:
                    knot = first + step
                border = (knot == 0) | (knot == KN - 1)
                cube = jnp.where(border, 1.0, 1.5)
                square = jnp.where(border, -1.5, -2.5)
                single = jnp.where(border, -0.5, 0.0)
                away = jnp.where(live, base + rest * (1.0 / SP) - knot.astype(f32), 4.0 * KN)
                away = away + pixel
                to = pl.ds((t * part + n) * LANES, LANES)
                for q in range(0, pixels, 16):
                    pair = []
                    for p in (q, q + 8):
                        d = jnp.abs(away + p * (1.0 / SP))
                        near = ((cube * d + square) * d + single) * d + 1.0
                        far = ((2.5 - 0.5 * d) * d - 4.0) * d + 2.0
                        pair.append(jnp.where(d <= 1.0, near, jnp.where(d < 2.0, far, 0.0)))
                    ref[q : q + 16, to] = jnp.concatenate(pair, axis=0).astype(bf16)


def compose(route_ref, received_ref, row_ref, col_ref, pixels_ref, out_ref, passed, result, sems):
    senders = received_ref.shape[0]
    bands = result.shape[0]
    lane = lax.broadcasted_iota(jnp.int32, (16, LANES), 1) // SPAN
    masks = [(lane == r).astype(f32).astype(bf16) for r in range(LANES // SPAN)]
    named = (route_ref[...] == lax.axis_index("gran")).astype(f32)
    scale = 1.0 / jnp.sum(named, keepdims=True)

    def sender(n, carry):
        at = pl.ds(pl.multiple_of(n * LANES, LANES), LANES)
        blocks = []
        for k in range(2 * bands):
            window = received_ref[n, 16 * k : 16 * k + 16, :]
            blocks.append(jnp.concatenate([window * mask for mask in masks], axis=0))
        rows = jnp.dot(row_ref[:, at], jnp.concatenate(blocks, axis=1), preferred_element_type=f32)
        for k in range(2 * bands):
            passed[k, :, at] = rows[:, LANES * k : LANES * k + LANES].astype(bf16)
        return carry

    steps = min(8, senders)

    def several(n, carry):
        for k in range(steps):
            sender(n * steps + k, carry)
        return carry

    lax.fori_loop(0, senders // steps, several, 0)
    copies = []
    for b in range(bands):
        fields = [
            lax.dot_general(
                passed[2 * b + c], col_ref[...], (((1,), (1,)), ((), ())), preferred_element_type=f32
            )
            * scale
            for c in range(2)
        ]
        pixels = pixels_ref[0, b].astype(f32)
        result[b] = (pixels * (1.0 + fields[0]) + fields[1]).astype(bf16)
        copies.append(pltpu.make_async_copy(result.at[b], out_ref.at[0, b], sems.at[b]))
        copies[b].start()
    for copy in copies:
        copy.wait()


def per_device(
    prior_grids,
    pif_rhs,
    pif_diagonal,
    pif_cross,
    pif_coupling,
    neighbour_offset,
    neighbour_count,
    tile_route,
    tile_window,
    tile_pixels,
):
    granules, bands = prior_grids.shape[:2]
    slots = pif_coupling.shape[1]
    pixel_count = tile_pixels.shape[2]
    device_total = lax.axis_size("gran")
    band_total = lax.axis_size("band")

    def by_lane_tile(array):
        cut = array.reshape(array.shape[:2] + (array.shape[2], 32, LANES)).transpose(0, 1, 3, 2, 4)
        return cut.reshape(array.shape[:2] + (32 * array.shape[2], LANES))

    grids = by_lane_tile(prior_grids)
    rhs = by_lane_tile(pif_rhs)
    diagonal = by_lane_tile(pif_diagonal)
    cross = by_lane_tile(pif_cross.transpose(1, 0, 2).reshape(bands, granules // 8, 8, KN * KN))
    coupling = by_lane_tile(pif_coupling.transpose(0, 2, 1, 3))
    graph = [("v", neighbour_offset.T), ("v", neighbour_count[None, :])]
    tiles = [("v", tile_route.T), ("v", tile_window.transpose(1, 2, 0))]
    edge = (REACH, bands, 64, LANES)
    own = (granules, bands, 64, LANES)
    ext = (granules + 2 * REACH, bands, 64, LANES)
    packed = ("v", (64, LANES), f32)
    chunks = 4

    near_pairs = [(i, i ^ 1) for i in range(device_total)]
    far_pairs = [
        pair for i in range(1, device_total - 1, 2) for pair in ((i, i + 1), (i + 1, i))
    ]

    def exchange(near, far):
        far = lax.ppermute(far, "gran", far_pairs)
        near = lax.ppermute(near, "gran", near_pairs)
        return near, far

    near, far = call(
        first_edges,
        [("h", grids)],
        [("v", edge, bf16), ("v", edge, bf16)],
        [pltpu.VMEM((2,) + edge, f32), pltpu.SemaphoreType.DMA((2, REACH))],
    )
    near, far = exchange(near, far)
    (extended,) = call(
        arrange_grids,
        [("h", grids)],
        [("v", ext, f32)],
        [pltpu.VMEM(own, f32), pltpu.SemaphoreType.DMA((chunks,))],
    )
    sources = [rhs, diagonal, cross, coupling]

    def arranged(interior, sources):
        part = len(visits(granules, interior))
        some = (part, bands, 64, LANES)
        return call(
            functools.partial(arrange, interior),
            [("h", source) for source in sources],
            [
                ("v", some, f32),
                ("v", some, f32),
                ("v", (part, bands, 32, LANES), f32),
                ("v", (part,) + coupling.shape[1:], f32),
            ],
            [
                pltpu.VMEM(cross.shape, f32),
                pltpu.VMEM((part,) + coupling.shape[1:], bf16),
                pltpu.SemaphoreType.DMA((4, chunks)),
            ],
        )

    gathered = pltpu.VMEM((slots, 64, LANES), f32)
    weights = pltpu.VMEM((slots, 64, LANES), f32)
    scalars = pltpu.SMEM((2, granules), jnp.int32)

    def over_band(partial):
        return [("v", partial)] + [
            ("v", lax.ppermute(partial, "band", [(i, i ^ flip) for i in range(band_total)]))
            for flip in range(1, band_total)
        ]

    for sweep in range(SWEEPS):
        last = sweep == SWEEPS - 1
        (inner,) = call(
            interior_disparities, graph + [("v", extended)], [packed], [gathered, scalars]
        )
        if sweep == 0:
            inner, *edge_state = lax.optimization_barrier((inner, *arranged(False, sources)))
        if sweep == 1:
            routes, starts, _ = lax.optimization_barrier((tiles[0][1], tiles[1][1], inner))
            weight_shape = ("v", (pixel_count, device_total * LANES), bf16)
            made = call(
                tile_places,
                [("v", routes), ("v", starts)],
                [weight_shape, weight_shape, ("v", (8, LANES), jnp.int32)],
            )
            inner, row_weights, col_weights, places = lax.optimization_barrier((inner, *made))
        if last:
            inner_shares = over_band(inner)
        inputs = graph + [("v", near), ("v", far), ("v", extended)]
        inputs += [] if last else [("v", inner)]
        extended, partial = call(
            edge_disparities,
            inputs,
            [("v", ext, f32), packed],
            [gathered, scalars],
            aliases={4: 0},
        )
        shares = over_band(partial)
        if sweep == 0:
            *later, _ = lax.optimization_barrier((*sources, partial))
            partial, *inner_state = lax.optimization_barrier((partial, *arranged(True, later)))
            shares[0] = ("v", partial)
        edge_state_now = [("v", extended)] + [("v", array) for array in edge_state]
        inner_state_now = [("v", extended)] + [("v", array) for array in inner_state]
        if not last:
            inputs = graph + shares + edge_state_now
            updated, near, far = call(
                edge_sweep,
                inputs,
                [("v", ext, f32), ("v", edge, bf16), ("v", edge, bf16)],
                [weights, scalars],
            )
            near, far = exchange(near, far)
            inputs = graph + shares + inner_state_now
            (extended,) = call(
                interior_sweep,
                inputs + [("v", updated)],
                [("v", ext, f32)],
                [weights, scalars],
                aliases={len(inputs): 0},
            )
    windows = (device_total, 2 * bands * SPAN, LANES)
    scratch = [
        weights,
        scalars,
        pltpu.VMEM(own, f32),
        pltpu.SemaphoreType.DMA((2,)),
    ]
    inputs = graph + inner_shares + inner_state_now + [("v", places)]
    balanced, gathered_windows = call(
        functools.partial(last_sweep, True),
        inputs,
        [("h", own, f32), ("v", windows, f32)],
        scratch,
    )
    inputs = graph + shares + edge_state_now + [("v", places)] + [("h", balanced), ("v", gathered_windows)]
    balanced, payload, _ = call(
        functools.partial(last_sweep, False),
        inputs,
        [("h", own, f32), ("v", windows, bf16), ("v", windows, f32)],
        scratch,
        aliases={len(inputs) - 2: 0, len(inputs) - 1: 2},
    )
    received = lax.all_to_all(payload, "gran", split_axis=0, concat_axis=0, tiled=True)
    (corrected,) = call(
        compose,
        [tiles[0], ("v", received), ("v", row_weights), ("v", col_weights), ("v", tile_pixels)],
        [("h", tile_pixels.shape, bf16)],
        [
            pltpu.VMEM((2 * bands, pixel_count, device_total * LANES), bf16),
            pltpu.VMEM(tile_pixels.shape[1:], bf16),
            pltpu.SemaphoreType.DMA((bands,)),
        ],
        limit=32,
    )
    balanced = balanced.reshape(granules, bands, 32, 2, LANES).transpose(0, 1, 3, 2, 4)
    return (balanced.reshape(prior_grids.shape), corrected)


def solution(mesh):
    placed = (
        P("gran", "band", None, None),
        P("gran", "band", None, None),
        P("gran", "band", None, None),
        P("gran", "band", None),
        P("gran", None, "band", None),
        P("gran", None),
        P("gran"),
        P(),
        P(),
        P("gran", "band", None, None),
    )
    return jax.shard_map(
        per_device,
        mesh=mesh,
        in_specs=placed,
        out_specs=(P("gran", "band", None, None), P("gran", "band", None, None)),
        check_vma=False,
    )
```

```python
import functools
import jax
import jax.numpy as jnp
from jax import lax
from jax.experimental import pallas as pl
from jax.experimental.pallas import tpu as pltpu
from jax.sharding import PartitionSpec as P

BANDS = 12
KN = 64
PATCH = 8
REACH = 4
SWEEPS = 3
SP = 32
LANES = 128
SPAN = 16

robust_scale = 0.3

ON_CHIP = pl.BlockSpec(memory_space=pltpu.VMEM)
ANYWHERE = pl.BlockSpec(memory_space=pl.ANY)
f32 = jnp.float32
bf16 = jnp.bfloat16


def call(body, inputs, outputs, scratch=(), aliases=None, limit=16):
    operands = [
        pltpu.with_memory_space_constraint(array, pltpu.VMEM if kind == "v" else pltpu.HBM)
        for kind, array in inputs
    ]
    return pl.pallas_call(
        body,
        in_specs=[ON_CHIP if kind == "v" else ANYWHERE for kind, _ in inputs],
        out_specs=tuple(ON_CHIP if kind == "v" else ANYWHERE for kind, _, _ in outputs),
        out_shape=tuple(
            (pltpu.VMEM if kind == "v" else pltpu.HBM)(shape, dtype)
            for kind, shape, dtype in outputs
        ),
        scratch_shapes=list(scratch),
        input_output_aliases=aliases or {},
        compiler_params=pltpu.CompilerParams(vmem_limit_bytes=limit * 2**20),
    )(*operands)


def parity():
    return lax.rem(lax.axis_index("gran"), 2)


def first_edges(grids_ref, near_ref, far_ref, raw, sems):
    odd = parity()
    last = grids_ref.shape[0] - REACH
    sides = ((far_ref, odd * last), (near_ref, (1 - odd) * last))
    copies = [
        [pltpu.make_async_copy(grids_ref.at[base + g], raw.at[k, g], sems.at[k, g]) for g in range(REACH)]
        for k, (_, base) in enumerate(sides)
    ]
    for copy in copies[0] + copies[1]:
        copy.start()
    for k, (ref, _) in enumerate(sides):
        for g in range(REACH):
            copies[k][g].wait()
            for b in range(ref.shape[1]):
                for j in range(4):
                    both = [raw[k, g, b, pl.ds(2 * j + c, 8, stride=8), :] for c in range(2)]
                    ref[g, b, 16 * j : 16 * j + 16, :] = jnp.concatenate(both, axis=0).astype(bf16)


def arrange_grids(grids_ref, ext_ref, raw, sems):
    granules, bands = grids_ref.shape[:2]
    chunks = sems.shape[0]
    size = granules // chunks
    copies = []
    for n in range(chunks):
        part = pl.ds(n * size, size)
        copies.append(pltpu.make_async_copy(grids_ref.at[part], raw.at[part], sems.at[n]))
        copies[n].start()

    def step(i, carry):
        for b in range(bands):
            for q in range(8):
                ext_ref[i + REACH, b, 8 * q : 8 * q + 8, :] = raw[i, b, pl.ds(q, 8, stride=8), :]
        return carry

    for n in range(chunks):
        copies[n].wait()
        lax.fori_loop(n * size, (n + 1) * size, step, 0)


def visits(granules, interior):
    inner = list(range(REACH, granules - REACH))
    return inner if interior else [i for i in range(granules) if i not in inner]


def arrange(interior, offset_ref, count_ref, rhs_ref, diag_ref, cross_ref, coupling_ref, rhs_out, diag_out, cross_out, coupling_out, cross_raw, coupling_raw, wide, graph, sems):
    granules, bands = rhs_ref.shape[:2]
    own = visits(granules, interior)
    size = REACH
    chunks = len(own) // size
    copies = []
    for n in range(chunks):
        source, target = pl.ds(own[n * size], size), pl.ds(n * size, size)
        moves = ((coupling_ref, coupling_raw), (diag_ref, diag_out), (rhs_ref, rhs_out))
        copies.append(
            [
                pltpu.make_async_copy(here.at[source], there.at[target], sems.at[k, n])
                for k, (here, there) in enumerate(moves)
            ]
        )
        for copy in copies[n][:2]:
            copy.start()
        if n == 0:
            whole = pltpu.make_async_copy(cross_ref, cross_raw, sems.at[3, 0])
            whole.start()
    for n in range(chunks):
        copies[n][2].start()
    read_graph(offset_ref, count_ref, graph)
    for n in range(chunks):
        for copy in copies[n][:2]:
            copy.wait()
        if n == 0:
            whole.wait()

        def step(g, carry, n=n):
            at = n * size + g
            i = own[n * size] + g
            for b in range(bands):
                wide[b] = coupling_raw[at, b].astype(f32)
                for j in range(4):
                    d = [diag_out[at, b, pl.ds(2 * j + c, 8, stride=8), :] for c in range(2)]
                    pick = cross_raw[b, i // 8, pl.ds(8 * j + i % 8, 8, stride=32), :]
                    cross_out[at, b, 8 * j : 8 * j + 8, :] = pick * jnp.sqrt(d[0] * d[1])

            def slot(s, carry):
                for b in range(bands):
                    for j in range(4):
                        pick = wide[b, pl.ds(8 * j + s, 8, stride=32), :]
                        coupling_out[at, s, b, 8 * j : 8 * j + 8, :] = pick
                return carry

            return lax.fori_loop(0, graph[1, i], slot, carry)

        lax.fori_loop(0, size, step, 0)
    for n in range(chunks):
        copies[n][2].wait()


def lane_sums():
    row = lax.broadcasted_iota(jnp.int32, (LANES, LANES), 0)
    col = lax.broadcasted_iota(jnp.int32, (LANES, LANES), 1)
    return ((row % KN) // PATCH == col % PATCH).astype(f32).astype(bf16)


def lane_spread():
    row = lax.broadcasted_iota(jnp.int32, (LANES, LANES), 0)
    col = lax.broadcasted_iota(jnp.int32, (LANES, LANES), 1)
    return ((col % KN) // PATCH == row % PATCH).astype(f32).astype(bf16)


def read_graph(offset_ref, count_ref, graph):
    slots, granules = offset_ref.shape
    slot = lax.broadcasted_iota(jnp.int32, offset_ref.shape, 0)
    codes = jnp.sum(jnp.left_shift(offset_ref[...] + REACH, 4 * slot), axis=0, keepdims=True)
    counts = count_ref[...]
    for i in range(granules):
        graph[0, i] = codes[0, i]
        graph[1, i] = counts[0, i]


def neighbour(graph, i, s):
    return i + jnp.bitwise_and(jnp.right_shift(graph[0, i], 4 * s), 15)


def group_mask(interior, slots):
    row = lax.broadcasted_iota(jnp.int32, (64, LANES), 0) // 32
    lane = lax.broadcasted_iota(jnp.int32, (64, LANES), 1) // PATCH
    return lane - slots * (1 - row if interior else row)


def disparities(interior, offset_ref, count_ref, ext_ref, gathered, graph):
    bands = ext_ref.shape[1]
    granules = ext_ref.shape[0] - 2 * REACH
    slots = gathered.shape[0]
    gathered[...] = jnp.zeros_like(gathered)
    read_graph(offset_ref, count_ref, graph)

    def response(g):
        return [
            ext_ref[g, b, 16 * j : 16 * j + 8, :] + ext_ref[g, b, 16 * j + 8 : 16 * j + 16, :]
            for b in range(bands)
            for j in range(4)
        ]

    for i in range(granules):
        if (REACH <= i < granules - REACH) != interior:
            continue
        own = response(i + REACH)

        def slot(s, carry, i=i, own=own):
            total = None
            for a, o in zip(own, response(neighbour(graph, i, s))):
                d = a - o
                total = d * d if total is None else total + d * d
            gathered[s, 8 * (i % 8) : 8 * (i % 8) + 8, :] = total
            return carry

        lax.fori_loop(0, graph[1, i], slot, 0)
    sums = jnp.dot(
        gathered[...].reshape(slots * 64, LANES).astype(bf16), lane_sums(), preferred_element_type=f32
    )
    place = group_mask(interior, slots)
    packed = jnp.zeros((64, LANES), f32)
    for s in range(slots):
        packed = jnp.where(place == s, sums[64 * s : 64 * s + 64], packed)
    return packed


def interior_disparities(offset_ref, count_ref, ext_ref, out_ref, gathered, graph):
    out_ref[...] = disparities(True, offset_ref, count_ref, ext_ref, gathered, graph)


def edge_disparities(offset_ref, count_ref, near_ref, far_ref, *refs):
    ext_ref, out_ref, gathered, graph = refs[-4:]
    odd = parity()
    right = ext_ref.shape[0] - REACH
    for ref, base in ((near_ref, (1 - odd) * right), (far_ref, odd * right)):
        for g in range(REACH):
            for b in range(ref.shape[1]):
                ext_ref[base + g, b] = ref[g, b].astype(f32)
    packed = disparities(False, offset_ref, count_ref, ext_ref, gathered, graph)
    out_ref[...] = packed + refs[1][...] if len(refs) == 6 else packed


def spread_weights(shares, interior, weights):
    slots = weights.shape[0]
    total = (shares[0][...] + shares[1][...]) + (shares[2][...] + shares[3][...])
    robust = 1.0 / (1.0 + total * (1.0 / (robust_scale * BANDS * PATCH * PATCH)))
    high = robust.astype(bf16).astype(f32)
    both = jnp.concatenate([high, robust - high], axis=1)
    place = group_mask(interior, slots)
    place = jnp.concatenate([place, place], axis=1)
    spread = lane_spread()
    spread = jnp.concatenate([spread, spread], axis=0)
    stacked = jnp.concatenate(
        [jnp.where(place == s, both, 0.0).astype(bf16) for s in range(slots)], axis=0
    )
    weights[...] = jnp.dot(stacked, spread, preferred_element_type=f32).reshape(slots, 64, LANES)


def balance(i, at, ext_ref, rhs_ref, diag_ref, cross_ref, coupling_ref, weights, graph, store):
    bands = rhs_ref.shape[1]
    row = pl.multiple_of(lax.rem(i, 8) * 8, 8)
    parts = [(b, j) for b in range(bands) for j in range(4)]
    rhs = tuple(rhs_ref[at, b, pl.ds(2 * j + c, 8, stride=8), :] for b, j in parts for c in range(2))

    def slot(s, sums):
        sigma, drive = sums
        weight = weights[s, pl.ds(row, 8), :]
        n = neighbour(graph, i, s)
        new_sigma, new_drive = [], []
        for b in range(bands):
            for j in range(4):
                k = 4 * b + j
                effective = weight * coupling_ref[at, s, b, 8 * j : 8 * j + 8, :]
                new_sigma.append(sigma[k] + effective)
                for c in range(2):
                    grid = ext_ref[n, b, 16 * j + 8 * c : 16 * j + 8 * c + 8, :]
                    new_drive.append(drive[2 * k + c] + effective * grid)
        return tuple(new_sigma), tuple(new_drive)

    zero = jnp.zeros((8, LANES), f32)
    sigma, drive = lax.fori_loop(0, graph[1, i], slot, ((zero,) * len(parts), rhs))
    for k, (b, j) in enumerate(parts):
        first, second = (
            diag_ref[at, b, pl.ds(2 * j + c, 8, stride=8), :] + sigma[k] for c in range(2)
        )
        cross = cross_ref[at, b, 8 * j : 8 * j + 8, :]
        inverse = 1.0 / (first * second - cross * cross)
        gain, offset = drive[2 * k], drive[2 * k + 1]
        store(
            b,
            j,
            (second * gain - cross * offset) * inverse,
            (first * offset - cross * gain) * inverse,
        )


def edge_sweep(offset_ref, count_ref, *refs):
    shares, state, (new_ref, near_ref, far_ref, weights, graph) = refs[:4], refs[4:9], refs[9:]
    read_graph(offset_ref, count_ref, graph)
    spread_weights(shares, False, weights)
    odd = parity()
    last = new_ref.shape[0] - 3 * REACH
    for ref, base in ((far_ref, odd * last), (near_ref, (1 - odd) * last)):

        def step(g, carry, ref=ref, base=base):
            def store(b, j, gain, offset):
                both = jnp.concatenate([gain, offset], axis=0)
                new_ref[base + g + REACH, b, 16 * j : 16 * j + 16, :] = both
                ref[g, b, 16 * j : 16 * j + 16, :] = both.astype(bf16)

            balance(base + g, lax.div(base, 2 * REACH) * REACH + g, *state, weights, graph, store)
            return carry

        lax.fori_loop(0, REACH, step, 0)


def interior_sweep(offset_ref, count_ref, *refs):
    shares, state, (_, new_ref, weights, graph) = refs[:4], refs[4:9], refs[9:]
    read_graph(offset_ref, count_ref, graph)
    spread_weights(shares, True, weights)

    def step(i, carry):
        def store(b, j, gain, offset):
            both = jnp.concatenate([gain, offset], axis=0)
            new_ref[i + REACH, b, 16 * j : 16 * j + 16, :] = both

        balance(i, i - REACH, *state, weights, graph, store)
        return carry

    lax.fori_loop(REACH, new_ref.shape[0] - 3 * REACH, step, 0)


def own_columns(ref, at, granules):
    first = lax.axis_index("gran") * granules
    base = pl.multiple_of((first // LANES) * LANES, LANES)
    turn = jnp.bitwise_and(LANES - lax.rem(first, LANES), LANES - 1)
    return pltpu.roll(ref[at + (pl.ds(base, LANES),)], turn, 1)


def last_sweep(interior, offset_ref, count_ref, *refs):
    shares, state, place_ref = refs[:4], refs[4:9], refs[9]
    weights, graph, solved, sems = refs[-4:]
    if interior:
        out_ref, windows = refs[10:12]
    else:
        out_ref, send_ref, windows = refs[12:15]
    granules, bands = solved.shape[:2]
    read_graph(offset_ref, count_ref, graph)
    if interior:
        windows[...] = jnp.zeros_like(windows)
    spread_weights(shares, interior, weights)

    def step(t, carry):
        i = t if interior else jnp.where(t < REACH, t, t + granules - 2 * REACH)

        def store(b, j, gain, offset):
            solved[i, b, pl.ds(2 * j, 8, stride=8), :] = gain
            solved[i, b, pl.ds(2 * j + 1, 8, stride=8), :] = offset

        balance(i, t - REACH if interior else t, *state, weights, graph, store)
        return carry

    lax.fori_loop(*((REACH, granules - REACH) if interior else (0, 2 * REACH)), step, 0)
    parts = ((REACH, granules - 2 * REACH),) if interior else ((0, REACH), (granules - REACH, REACH))
    copies = []
    for n, (first, size) in enumerate(parts):
        part = pl.ds(first, size)
        copies.append(pltpu.make_async_copy(solved.at[part], out_ref.at[part], sems.at[n]))
        copies[n].start()
    lane = lax.broadcasted_iota(jnp.int32, (8, LANES), 1) // SPAN
    places = place_ref[...]
    for i in visits(granules, interior):
        for r in range(2):
            owner, rank, top, turn = (places[k, r * granules + i] for k in range(4))
            here = lane == rank
            for b in range(bands):
                for c in range(2):
                    rows = solved[i, b, pl.ds(2 * top + c, 8, stride=2), :]
                    for half in (0, 1):
                        at = 16 * (2 * b + c) + 8 * half
                        moved = pltpu.roll(rows, jnp.bitwise_and(turn + KN * half, LANES - 1), 1)
                        pltpu.store(windows.at[owner, at : at + 8, :], moved, mask=here)
    if not interior:
        send_ref[...] = windows[...].astype(bf16)
    for copy in copies:
        copy.wait()


def earlier(first, second, granules):
    def edge(i):
        return ((i < REACH) | (i >= granules - REACH)).astype(jnp.int32)

    def rank(entry):
        return (edge(entry[1]) * 2 + entry[0]) * granules + entry[1]

    return rank(first) < rank(second)


def spread_columns(row):
    return jnp.transpose(jnp.broadcast_to(row, (LANES, LANES)))


def tile_places(route_ref, window_ref, rows_out, cols_out, place_ref):
    pixels, lanes = rows_out.shape
    senders = lanes // LANES
    granules = route_ref.shape[1] // senders
    own = lax.axis_index("gran")
    lane_row = lax.broadcasted_iota(jnp.int32, (1, LANES), 1)

    def both_routes(rows):
        return jnp.where(lane_row < granules, rows[0:1], pltpu.roll(rows, granules, 1)[1:2])

    routes = own_columns(route_ref, (slice(None),), granules)
    starts = [own_columns(window_ref, (r, slice(None)), granules) for r in range(2)]
    named = both_routes(routes).astype(f32)
    col = lax.broadcasted_iota(jnp.int32, (LANES, LANES), 1)
    row = lax.broadcasted_iota(jnp.int32, (LANES, LANES), 0)
    before = earlier((row // granules, row % granules), (col // granules, col % granules), granules)
    before = before & (row < 2 * granules) & (spread_columns(named) == named)
    rank = jnp.sum(before.astype(f32), axis=0, keepdims=True).astype(jnp.int32)
    knots = [
        jnp.clip(jnp.right_shift(both_routes(jnp.concatenate([s[k : k + 1] for s in starts])), 5) - 1, 0, KN - SPAN)
        for k in range(2)
    ]
    turn = rank * SPAN - knots[1] + LANES
    place_ref[...] = jnp.concatenate(
        [named.astype(jnp.int32), rank, jnp.right_shift(knots[0], 1), turn] * 2, axis=0
    )

    wide = 2 * LANES
    col = lax.broadcasted_iota(jnp.int32, (wide, wide), 1)
    row = lax.broadcasted_iota(jnp.int32, (wide, wide), 0)
    route = [at // LANES for at in (row, col)]
    place = [at % LANES for at in (row, col)]
    before = earlier((route[0], place[0] % granules), (route[1], place[1] % granules), granules)
    before = before & (place[0] // granules == place[1] // granules)
    before = before.astype(f32).astype(bf16)
    seat = (lax.broadcasted_iota(jnp.int32, (LANES, LANES), 1) // SPAN).astype(f32)
    lane = lax.broadcasted_iota(jnp.int32, (8, LANES), 1)
    step = lane % SPAN
    pixel = lax.broadcasted_iota(jnp.int32, (8, LANES), 0).astype(f32) * (1.0 / SP)
    part = LANES // granules
    for t in range(route_ref.shape[1] // LANES):
        at = slice(t * LANES, (t + 1) * LANES)
        hits = [(route_ref[r : r + 1, at] == own).astype(f32) for r in range(2)]
        hits = jnp.broadcast_to(jnp.concatenate(hits, axis=1), (8, wide))
        ranks = jnp.dot(hits.astype(bf16), before, preferred_element_type=f32)
        ranks = jnp.where(hits > 0.5, ranks, -1.0)
        chosen, values = [], []
        for r in range(2):
            chosen.append((spread_columns(ranks[0:1, r * LANES : (r + 1) * LANES]) == seat).astype(f32).astype(bf16))
            sender = lax.broadcasted_iota(jnp.int32, (part, LANES), 0)
            within = lax.broadcasted_iota(jnp.int32, (part, LANES), 1) // granules == sender
            kinds = []
            for k in range(2):
                start = window_ref[r, k : k + 1, at]
                kinds += [jnp.right_shift(start, 5), jnp.bitwise_and(start, SP - 1)]
            kinds.append(jnp.ones((1, LANES), jnp.int32))
            values.append(jnp.concatenate([jnp.where(within, kind, 0).astype(f32) for kind in kinds], axis=0))
        found = jnp.dot(
            jnp.concatenate(values, axis=1).astype(bf16),
            jnp.concatenate(chosen, axis=0),
            preferred_element_type=f32,
        )
        for n in range(part):
            live = found[4 * part + n : 4 * part + n + 1] > 0.5
            for k, ref in ((0, rows_out), (1, cols_out)):
                base = found[2 * k * part + n : 2 * k * part + n + 1]
                rest = found[(2 * k + 1) * part + n : (2 * k + 1) * part + n + 1]
                first = jnp.clip(base.astype(jnp.int32) - 1, 0, KN - SPAN)
                if k == 0:
                    knot = 2 * jnp.right_shift(first, 1) + 2 * (step % 8) + step // 8
                else:
                    knot = first + step
                border = (knot == 0) | (knot == KN - 1)
                cube = jnp.where(border, 1.0, 1.5)
                square = jnp.where(border, -1.5, -2.5)
                single = jnp.where(border, -0.5, 0.0)
                away = jnp.where(live, base + rest * (1.0 / SP) - knot.astype(f32), 4.0 * KN)
                away = away + pixel
                to = pl.ds((t * part + n) * LANES, LANES)
                for q in range(0, pixels, 16):
                    pair = []
                    for p in (q, q + 8):
                        d = jnp.abs(away + p * (1.0 / SP))
                        near = ((cube * d + square) * d + single) * d + 1.0
                        far = ((2.5 - 0.5 * d) * d - 4.0) * d + 2.0
                        pair.append(jnp.where(d <= 1.0, near, jnp.where(d < 2.0, far, 0.0)))
                    ref[q : q + 16, to] = jnp.concatenate(pair, axis=0).astype(bf16)


def compose(route_ref, received_ref, row_ref, col_ref, pixels_ref, out_ref, passed, result, sems):
    senders = received_ref.shape[0]
    bands = result.shape[0]
    lane = lax.broadcasted_iota(jnp.int32, (16, LANES), 1) // SPAN
    masks = [(lane == r).astype(f32).astype(bf16) for r in range(LANES // SPAN)]
    named = (route_ref[...] == lax.axis_index("gran")).astype(f32)
    scale = 1.0 / jnp.sum(named, keepdims=True)

    def sender(n, carry):
        at = pl.ds(pl.multiple_of(n * LANES, LANES), LANES)
        blocks = []
        for k in range(2 * bands):
            window = received_ref[n, 16 * k : 16 * k + 16, :]
            blocks.append(jnp.concatenate([window * mask for mask in masks], axis=0))
        rows = jnp.dot(row_ref[:, at], jnp.concatenate(blocks, axis=1), preferred_element_type=f32)
        for k in range(2 * bands):
            passed[k, :, at] = rows[:, LANES * k : LANES * k + LANES].astype(bf16)
        return carry

    steps = min(8, senders)

    def several(n, carry):
        for k in range(steps):
            sender(n * steps + k, carry)
        return carry

    lax.fori_loop(0, senders // steps, several, 0)
    copies = []
    for b in range(bands):
        fields = [
            lax.dot_general(
                passed[2 * b + c], col_ref[...], (((1,), (1,)), ((), ())), preferred_element_type=f32
            )
            * scale
            for c in range(2)
        ]
        pixels = pixels_ref[0, b].astype(f32)
        result[b] = (pixels * (1.0 + fields[0]) + fields[1]).astype(bf16)
        copies.append(pltpu.make_async_copy(result.at[b], out_ref.at[0, b], sems.at[b]))
        copies[b].start()
    for copy in copies:
        copy.wait()


def per_device(
    prior_grids,
    pif_rhs,
    pif_diagonal,
    pif_cross,
    pif_coupling,
    neighbour_offset,
    neighbour_count,
    tile_route,
    tile_window,
    tile_pixels,
):
    granules, bands = prior_grids.shape[:2]
    slots = pif_coupling.shape[1]
    pixel_count = tile_pixels.shape[2]
    device_total = lax.axis_size("gran")
    band_total = lax.axis_size("band")

    def by_lane_tile(array):
        cut = array.reshape(array.shape[:2] + (array.shape[2], 32, LANES)).transpose(0, 1, 3, 2, 4)
        return cut.reshape(array.shape[:2] + (32 * array.shape[2], LANES))

    grids = by_lane_tile(prior_grids)
    rhs = by_lane_tile(pif_rhs)
    diagonal = by_lane_tile(pif_diagonal)
    cross = by_lane_tile(pif_cross.transpose(1, 0, 2).reshape(bands, granules // 8, 8, KN * KN))
    coupling = by_lane_tile(pif_coupling.transpose(0, 2, 1, 3))
    graph = [("v", neighbour_offset.T), ("v", neighbour_count[None, :])]
    tiles = [("v", tile_route.T), ("v", tile_window.transpose(1, 2, 0))]
    edge = (REACH, bands, 64, LANES)
    own = (granules, bands, 64, LANES)
    ext = (granules + 2 * REACH, bands, 64, LANES)
    packed = ("v", (64, LANES), f32)
    chunks = 4

    near_pairs = [(i, i ^ 1) for i in range(device_total)]
    far_pairs = [
        pair for i in range(1, device_total - 1, 2) for pair in ((i, i + 1), (i + 1, i))
    ]

    def exchange(near, far):
        far = lax.ppermute(far, "gran", far_pairs)
        near = lax.ppermute(near, "gran", near_pairs)
        return near, far

    near, far = call(
        first_edges,
        [("h", grids)],
        [("v", edge, bf16), ("v", edge, bf16)],
        [pltpu.VMEM((2,) + edge, f32), pltpu.SemaphoreType.DMA((2, REACH))],
    )
    near, far = exchange(near, far)
    (extended,) = call(
        arrange_grids,
        [("h", grids)],
        [("v", ext, f32)],
        [pltpu.VMEM(own, f32), pltpu.SemaphoreType.DMA((chunks,))],
    )
    sources = [rhs, diagonal, cross, coupling]

    def arranged(interior, sources):
        part = len(visits(granules, interior))
        some = (part, bands, 64, LANES)
        return call(
            functools.partial(arrange, interior),
            graph + [("h", source) for source in sources],
            [
                ("v", some, f32),
                ("v", some, f32),
                ("v", (part, bands, 32, LANES), f32),
                ("v", (part, slots, bands, 32, LANES), f32),
            ],
            [
                pltpu.VMEM(cross.shape, f32),
                pltpu.VMEM((part,) + coupling.shape[1:], bf16),
                pltpu.VMEM(coupling.shape[1:], f32),
                pltpu.SMEM((2, granules), jnp.int32),
                pltpu.SemaphoreType.DMA((4, chunks)),
            ],
        )

    gathered = pltpu.VMEM((slots, 64, LANES), f32)
    weights = pltpu.VMEM((slots, 64, LANES), f32)
    scalars = pltpu.SMEM((2, granules), jnp.int32)

    def over_band(partial):
        return [("v", partial)] + [
            ("v", lax.ppermute(partial, "band", [(i, i ^ flip) for i in range(band_total)]))
            for flip in range(1, band_total)
        ]

    for sweep in range(SWEEPS):
        last = sweep == SWEEPS - 1
        (inner,) = call(
            interior_disparities, graph + [("v", extended)], [packed], [gathered, scalars]
        )
        if sweep == 0:
            inner, *edge_state = lax.optimization_barrier((inner, *arranged(False, sources)))
        if last:
            inner_shares = over_band(inner)
        inputs = graph + [("v", near), ("v", far), ("v", extended)]
        inputs += [] if last else [("v", inner)]
        extended, partial = call(
            edge_disparities,
            inputs,
            [("v", ext, f32), packed],
            [gathered, scalars],
            aliases={4: 0},
        )
        shares = over_band(partial)
        if sweep == 1:
            routes, starts, _ = lax.optimization_barrier((tiles[0][1], tiles[1][1], partial))
            weight_shape = ("v", (pixel_count, device_total * LANES), bf16)
            made = call(
                tile_places,
                [("v", routes), ("v", starts)],
                [weight_shape, weight_shape, ("v", (8, LANES), jnp.int32)],
            )
            partial, row_weights, col_weights, places = lax.optimization_barrier((partial, *made))
            shares[0] = ("v", partial)
        edge_state_now = [("v", extended)] + [("v", array) for array in edge_state]
        if not last:
            inputs = graph + shares + edge_state_now
            updated, near, far = call(
                edge_sweep,
                inputs,
                [("v", ext, f32), ("v", edge, bf16), ("v", edge, bf16)],
                [weights, scalars],
            )
            near, far = exchange(near, far)
            if sweep == 0:
                *later, updated = lax.optimization_barrier((*sources, updated))
                inner_state = [("v", array) for array in arranged(True, later)]
            inputs = graph + shares + [("v", extended)] + inner_state
            (extended,) = call(
                interior_sweep,
                inputs + [("v", updated)],
                [("v", ext, f32)],
                [weights, scalars],
                aliases={len(inputs): 0},
            )
    windows = (device_total, 2 * bands * SPAN, LANES)
    scratch = [
        weights,
        scalars,
        pltpu.VMEM(own, f32),
        pltpu.SemaphoreType.DMA((2,)),
    ]
    inputs = graph + inner_shares + [("v", extended)] + inner_state + [("v", places)]
    balanced, gathered_windows = call(
        functools.partial(last_sweep, True),
        inputs,
        [("h", own, f32), ("v", windows, f32)],
        scratch,
    )
    inputs = graph + shares + edge_state_now + [("v", places)] + [("h", balanced), ("v", gathered_windows)]
    balanced, payload, _ = call(
        functools.partial(last_sweep, False),
        inputs,
        [("h", own, f32), ("v", windows, bf16), ("v", windows, f32)],
        scratch,
        aliases={len(inputs) - 2: 0, len(inputs) - 1: 2},
    )
    received = lax.all_to_all(payload, "gran", split_axis=0, concat_axis=0, tiled=True)
    (corrected,) = call(
        compose,
        [tiles[0], ("v", received), ("v", row_weights), ("v", col_weights), ("v", tile_pixels)],
        [("h", tile_pixels.shape, bf16)],
        [
            pltpu.VMEM((2 * bands, pixel_count, device_total * LANES), bf16),
            pltpu.VMEM(tile_pixels.shape[1:], bf16),
            pltpu.SemaphoreType.DMA((bands,)),
        ],
        limit=32,
    )
    balanced = balanced.reshape(granules, bands, 32, 2, LANES).transpose(0, 1, 3, 2, 4)
    return (balanced.reshape(prior_grids.shape), corrected)


def solution(mesh):
    placed = (
        P("gran", "band", None, None),
        P("gran", "band", None, None),
        P("gran", "band", None, None),
        P("gran", "band", None),
        P("gran", None, "band", None),
        P("gran", None),
        P("gran"),
        P(),
        P(),
        P("gran", "band", None, None),
    )
    return jax.shard_map(
        per_device,
        mesh=mesh,
        in_specs=placed,
        out_specs=(P("gran", "band", None, None), P("gran", "band", None, None)),
        check_vma=False,
    )
```

```python
import functools
import jax
import jax.numpy as jnp
from jax import lax
from jax.experimental import pallas as pl
from jax.experimental.pallas import tpu as pltpu
from jax.sharding import PartitionSpec as P

BANDS = 12
KN = 64
PATCH = 8
REACH = 4
SWEEPS = 3
SP = 32
LANES = 128
SPAN = 16

robust_scale = 0.3

ON_CHIP = pl.BlockSpec(memory_space=pltpu.VMEM)
ANYWHERE = pl.BlockSpec(memory_space=pl.ANY)
f32 = jnp.float32
bf16 = jnp.bfloat16


def call(body, inputs, outputs, scratch=(), aliases=None, limit=16):
    operands = [
        pltpu.with_memory_space_constraint(array, pltpu.VMEM if kind == "v" else pltpu.HBM)
        for kind, array in inputs
    ]
    return pl.pallas_call(
        body,
        in_specs=[ON_CHIP if kind == "v" else ANYWHERE for kind, _ in inputs],
        out_specs=tuple(ON_CHIP if kind == "v" else ANYWHERE for kind, _, _ in outputs),
        out_shape=tuple(
            (pltpu.VMEM if kind == "v" else pltpu.HBM)(shape, dtype)
            for kind, shape, dtype in outputs
        ),
        scratch_shapes=list(scratch),
        input_output_aliases=aliases or {},
        compiler_params=pltpu.CompilerParams(vmem_limit_bytes=limit * 2**20),
    )(*operands)


def parity():
    return lax.rem(lax.axis_index("gran"), 2)


def first_edges(grids_ref, near_ref, far_ref, raw, sems):
    odd = parity()
    last = grids_ref.shape[0] - REACH
    sides = ((far_ref, odd * last), (near_ref, (1 - odd) * last))
    copies = [
        [pltpu.make_async_copy(grids_ref.at[base + g], raw.at[k, g], sems.at[k, g]) for g in range(REACH)]
        for k, (_, base) in enumerate(sides)
    ]
    for copy in copies[0] + copies[1]:
        copy.start()
    for k, (ref, _) in enumerate(sides):
        for g in range(REACH):
            copies[k][g].wait()
            for b in range(ref.shape[1]):
                for j in range(4):
                    both = [raw[k, g, b, pl.ds(2 * j + c, 8, stride=8), :] for c in range(2)]
                    ref[g, b, 16 * j : 16 * j + 16, :] = jnp.concatenate(both, axis=0).astype(bf16)


def arrange_grids(grids_ref, ext_ref, raw, sems):
    granules, bands = grids_ref.shape[:2]
    chunks = sems.shape[0]
    size = granules // chunks
    copies = []
    for n in range(chunks):
        part = pl.ds(n * size, size)
        copies.append(pltpu.make_async_copy(grids_ref.at[part], raw.at[part], sems.at[n]))
        copies[n].start()

    def step(i, carry):
        for b in range(bands):
            for q in range(8):
                ext_ref[i + REACH, b, 8 * q : 8 * q + 8, :] = raw[i, b, pl.ds(q, 8, stride=8), :]
        return carry

    for n in range(chunks):
        copies[n].wait()
        lax.fori_loop(n * size, (n + 1) * size, step, 0)


def visits(granules, interior):
    inner = list(range(REACH, granules - REACH))
    return inner if interior else [i for i in range(granules) if i not in inner]


def arrange(interior, offset_ref, count_ref, rhs_ref, diag_ref, cross_ref, coupling_ref, rhs_out, diag_out, cross_out, coupling_out, cross_raw, coupling_raw, wide, graph, sems):
    granules, bands = rhs_ref.shape[:2]
    own = visits(granules, interior)
    size = REACH
    chunks = len(own) // size
    copies = []
    for n in range(chunks):
        source, target = pl.ds(own[n * size], size), pl.ds(n * size, size)
        moves = ((coupling_ref, coupling_raw), (diag_ref, diag_out), (rhs_ref, rhs_out))
        copies.append(
            [
                pltpu.make_async_copy(here.at[source], there.at[target], sems.at[k, n])
                for k, (here, there) in enumerate(moves)
            ]
        )
        for copy in copies[n][:2]:
            copy.start()
        if n == 0:
            whole = pltpu.make_async_copy(cross_ref, cross_raw, sems.at[3, 0])
            whole.start()
    for n in range(chunks):
        copies[n][2].start()
    read_graph(offset_ref, count_ref, graph)
    for n in range(chunks):
        for copy in copies[n][:2]:
            copy.wait()
        if n == 0:
            whole.wait()

        def step(g, carry, n=n):
            at = n * size + g
            i = own[n * size] + g
            for b in range(bands):
                wide[b] = coupling_raw[at, b].astype(f32)
                for j in range(4):
                    d = [diag_out[at, b, pl.ds(2 * j + c, 8, stride=8), :] for c in range(2)]
                    pick = cross_raw[b, i // 8, pl.ds(8 * j + i % 8, 8, stride=32), :]
                    cross_out[at, b, 8 * j : 8 * j + 8, :] = pick * jnp.sqrt(d[0] * d[1])

            def slot(s, carry):
                for b in range(bands):
                    for j in range(4):
                        pick = wide[b, pl.ds(8 * j + s, 8, stride=32), :]
                        coupling_out[at, s, b, 8 * j : 8 * j + 8, :] = pick
                return carry

            return lax.fori_loop(0, graph[1, i], slot, carry)

        lax.fori_loop(0, size, step, 0)
    for n in range(chunks):
        copies[n][2].wait()


def lane_sums():
    row = lax.broadcasted_iota(jnp.int32, (LANES, LANES), 0)
    col = lax.broadcasted_iota(jnp.int32, (LANES, LANES), 1)
    return ((row % KN) // PATCH == col % PATCH).astype(f32).astype(bf16)


def lane_spread():
    row = lax.broadcasted_iota(jnp.int32, (LANES, LANES), 0)
    col = lax.broadcasted_iota(jnp.int32, (LANES, LANES), 1)
    return ((col % KN) // PATCH == row % PATCH).astype(f32).astype(bf16)


def read_graph(offset_ref, count_ref, graph):
    slots, granules = offset_ref.shape
    slot = lax.broadcasted_iota(jnp.int32, offset_ref.shape, 0)
    codes = jnp.sum(jnp.left_shift(offset_ref[...] + REACH, 4 * slot), axis=0, keepdims=True)
    counts = count_ref[...]
    for i in range(granules):
        graph[0, i] = codes[0, i]
        graph[1, i] = counts[0, i]


def neighbour(graph, i, s):
    return i + jnp.bitwise_and(jnp.right_shift(graph[0, i], 4 * s), 15)


def group_mask(interior, slots):
    row = lax.broadcasted_iota(jnp.int32, (64, LANES), 0) // 32
    lane = lax.broadcasted_iota(jnp.int32, (64, LANES), 1) // PATCH
    return lane - slots * (1 - row if interior else row)


def disparities(interior, offset_ref, count_ref, ext_ref, gathered, graph):
    bands = ext_ref.shape[1]
    granules = ext_ref.shape[0] - 2 * REACH
    slots = gathered.shape[0]
    gathered[...] = jnp.zeros_like(gathered)
    read_graph(offset_ref, count_ref, graph)

    def response(g):
        return [
            ext_ref[g, b, 16 * j : 16 * j + 8, :] + ext_ref[g, b, 16 * j + 8 : 16 * j + 16, :]
            for b in range(bands)
            for j in range(4)
        ]

    for i in range(granules):
        if (REACH <= i < granules - REACH) != interior:
            continue
        own = response(i + REACH)

        def slot(s, carry, i=i, own=own):
            total = None
            for a, o in zip(own, response(neighbour(graph, i, s))):
                d = a - o
                total = d * d if total is None else total + d * d
            gathered[s, 8 * (i % 8) : 8 * (i % 8) + 8, :] = total
            return carry

        lax.fori_loop(0, graph[1, i], slot, 0)
    sums = jnp.dot(
        gathered[...].reshape(slots * 64, LANES).astype(bf16), lane_sums(), preferred_element_type=f32
    )
    place = group_mask(interior, slots)
    packed = jnp.zeros((64, LANES), f32)
    for s in range(slots):
        packed = jnp.where(place == s, sums[64 * s : 64 * s + 64], packed)
    return packed


def interior_disparities(offset_ref, count_ref, ext_ref, out_ref, gathered, graph):
    out_ref[...] = disparities(True, offset_ref, count_ref, ext_ref, gathered, graph)


def edge_disparities(offset_ref, count_ref, near_ref, far_ref, *refs):
    ext_ref, out_ref, gathered, graph = refs[-4:]
    odd = parity()
    right = ext_ref.shape[0] - REACH
    for ref, base in ((near_ref, (1 - odd) * right), (far_ref, odd * right)):
        for g in range(REACH):
            for b in range(ref.shape[1]):
                ext_ref[base + g, b] = ref[g, b].astype(f32)
    packed = disparities(False, offset_ref, count_ref, ext_ref, gathered, graph)
    out_ref[...] = packed + refs[1][...] if len(refs) == 6 else packed


def spread_weights(shares, interior, weights):
    slots = weights.shape[0]
    total = (shares[0][...] + shares[1][...]) + (shares[2][...] + shares[3][...])
    robust = 1.0 / (1.0 + total * (1.0 / (robust_scale * BANDS * PATCH * PATCH)))
    high = robust.astype(bf16).astype(f32)
    both = jnp.concatenate([high, robust - high], axis=1)
    place = group_mask(interior, slots)
    place = jnp.concatenate([place, place], axis=1)
    spread = lane_spread()
    spread = jnp.concatenate([spread, spread], axis=0)
    stacked = jnp.concatenate(
        [jnp.where(place == s, both, 0.0).astype(bf16) for s in range(slots)], axis=0
    )
    weights[...] = jnp.dot(stacked, spread, preferred_element_type=f32).reshape(slots, 64, LANES)


def balance(i, at, ext_ref, rhs_ref, diag_ref, cross_ref, coupling_ref, weights, graph, store):
    bands = rhs_ref.shape[1]
    row = pl.multiple_of(lax.rem(i, 8) * 8, 8)
    parts = [(b, j) for b in range(bands) for j in range(4)]
    rhs = tuple(rhs_ref[at, b, pl.ds(2 * j + c, 8, stride=8), :] for b, j in parts for c in range(2))

    def slot(s, sums):
        sigma, drive = sums
        weight = weights[s, pl.ds(row, 8), :]
        n = neighbour(graph, i, s)
        new_sigma, new_drive = [], []
        for b in range(bands):
            for j in range(4):
                k = 4 * b + j
                effective = weight * coupling_ref[at, s, b, 8 * j : 8 * j + 8, :]
                new_sigma.append(sigma[k] + effective)
                for c in range(2):
                    grid = ext_ref[n, b, 16 * j + 8 * c : 16 * j + 8 * c + 8, :]
                    new_drive.append(drive[2 * k + c] + effective * grid)
        return tuple(new_sigma), tuple(new_drive)

    zero = jnp.zeros((8, LANES), f32)
    sigma, drive = lax.fori_loop(1, graph[1, i], slot, slot(0, ((zero,) * len(parts), rhs)))
    for k, (b, j) in enumerate(parts):
        first, second = (
            diag_ref[at, b, pl.ds(2 * j + c, 8, stride=8), :] + sigma[k] for c in range(2)
        )
        cross = cross_ref[at, b, 8 * j : 8 * j + 8, :]
        inverse = 1.0 / (first * second - cross * cross)
        gain, offset = drive[2 * k], drive[2 * k + 1]
        store(
            b,
            j,
            (second * gain - cross * offset) * inverse,
            (first * offset - cross * gain) * inverse,
        )


def edge_sweep(offset_ref, count_ref, *refs):
    shares, state, (new_ref, near_ref, far_ref, weights, graph) = refs[:4], refs[4:9], refs[9:]
    read_graph(offset_ref, count_ref, graph)
    spread_weights(shares, False, weights)
    odd = parity()
    last = new_ref.shape[0] - 3 * REACH
    for ref, base in ((far_ref, odd * last), (near_ref, (1 - odd) * last)):

        def step(g, carry, ref=ref, base=base):
            def store(b, j, gain, offset):
                both = jnp.concatenate([gain, offset], axis=0)
                new_ref[base + g + REACH, b, 16 * j : 16 * j + 16, :] = both
                ref[g, b, 16 * j : 16 * j + 16, :] = both.astype(bf16)

            balance(base + g, lax.div(base, 2 * REACH) * REACH + g, *state, weights, graph, store)
            return carry

        lax.fori_loop(0, REACH, step, 0)


def interior_sweep(offset_ref, count_ref, *refs):
    shares, state, (_, new_ref, weights, graph) = refs[:4], refs[4:9], refs[9:]
    read_graph(offset_ref, count_ref, graph)
    spread_weights(shares, True, weights)

    def step(i, carry):
        def store(b, j, gain, offset):
            both = jnp.concatenate([gain, offset], axis=0)
            new_ref[i + REACH, b, 16 * j : 16 * j + 16, :] = both

        balance(i, i - REACH, *state, weights, graph, store)
        return carry

    lax.fori_loop(REACH, new_ref.shape[0] - 3 * REACH, step, 0)


def own_columns(ref, at, granules):
    first = lax.axis_index("gran") * granules
    base = pl.multiple_of((first // LANES) * LANES, LANES)
    turn = jnp.bitwise_and(LANES - lax.rem(first, LANES), LANES - 1)
    return pltpu.roll(ref[at + (pl.ds(base, LANES),)], turn, 1)


def last_sweep(interior, offset_ref, count_ref, *refs):
    shares, state, place_ref = refs[:4], refs[4:9], refs[9]
    weights, graph = refs[-2:]
    if interior:
        solved, windows = refs[10:12]
    else:
        solved, send_ref, windows = refs[12:15]
    granules, bands = solved.shape[:2]
    read_graph(offset_ref, count_ref, graph)
    if interior:
        windows[...] = jnp.zeros_like(windows)
    spread_weights(shares, interior, weights)

    def step(t, carry):
        i = t if interior else jnp.where(t < REACH, t, t + granules - 2 * REACH)

        def store(b, j, gain, offset):
            solved[i, b, pl.ds(2 * j, 8, stride=8), :] = gain
            solved[i, b, pl.ds(2 * j + 1, 8, stride=8), :] = offset

        balance(i, t - REACH if interior else t, *state, weights, graph, store)
        return carry

    lax.fori_loop(*((REACH, granules - REACH) if interior else (0, 2 * REACH)), step, 0)
    lane = lax.broadcasted_iota(jnp.int32, (8, LANES), 1) // SPAN
    seats = LANES // SPAN
    places = place_ref[...]
    for i in visits(granules, interior):
        for r in range(2):
            owner, rank, top, turn = (places[k, r * granules + i] for k in range(4))
            here = [lane == jnp.bitwise_and(rank + half * (KN // SPAN), seats - 1) for half in (0, 1)]
            for b in range(bands):
                for c in range(2):
                    rows = solved[i, b, pl.ds(2 * top + c, 8, stride=2), :]
                    moved = pltpu.roll(rows, jnp.bitwise_and(turn, LANES - 1), 1)
                    for half in (0, 1):
                        at = 16 * (2 * b + c) + 8 * half
                        pltpu.store(windows.at[owner, at : at + 8, :], moved, mask=here[half])
    if not interior:
        for owner in range(windows.shape[0]):
            for at in range(0, windows.shape[1], 16):
                odd = pltpu.roll(windows[owner, at + 8 : at + 16, :], KN, 1)
                both = jnp.concatenate([windows[owner, at : at + 8, :], odd], axis=0)
                send_ref[owner, at : at + 16, :] = both.astype(bf16)


def copy_out(solved, out_ref, sem):
    copy = pltpu.make_async_copy(solved, out_ref, sem)
    copy.start()
    copy.wait()


def earlier(first, second, granules):
    def edge(i):
        return ((i < REACH) | (i >= granules - REACH)).astype(jnp.int32)

    def rank(entry):
        return (edge(entry[1]) * 2 + entry[0]) * granules + entry[1]

    return rank(first) < rank(second)


def spread_columns(row):
    return jnp.transpose(jnp.broadcast_to(row, (LANES, LANES)))


def tile_places(route_ref, window_ref, rows_out, cols_out, place_ref):
    pixels, lanes = rows_out.shape
    senders = lanes // LANES
    granules = route_ref.shape[1] // senders
    own = lax.axis_index("gran")
    lane_row = lax.broadcasted_iota(jnp.int32, (1, LANES), 1)

    def both_routes(rows):
        return jnp.where(lane_row < granules, rows[0:1], pltpu.roll(rows, granules, 1)[1:2])

    routes = own_columns(route_ref, (slice(None),), granules)
    starts = [own_columns(window_ref, (r, slice(None)), granules) for r in range(2)]
    named = both_routes(routes).astype(f32)
    col = lax.broadcasted_iota(jnp.int32, (LANES, LANES), 1)
    row = lax.broadcasted_iota(jnp.int32, (LANES, LANES), 0)
    before = earlier((row // granules, row % granules), (col // granules, col % granules), granules)
    before = before & (row < 2 * granules) & (spread_columns(named) == named)
    rank = jnp.sum(before.astype(f32), axis=0, keepdims=True).astype(jnp.int32)
    knots = [
        jnp.clip(jnp.right_shift(both_routes(jnp.concatenate([s[k : k + 1] for s in starts])), 5) - 1, 0, KN - SPAN)
        for k in range(2)
    ]
    turn = rank * SPAN - knots[1] + LANES
    place_ref[...] = jnp.concatenate(
        [named.astype(jnp.int32), rank, jnp.right_shift(knots[0], 1), turn] * 2, axis=0
    )

    wide = 2 * LANES
    col = lax.broadcasted_iota(jnp.int32, (wide, wide), 1)
    row = lax.broadcasted_iota(jnp.int32, (wide, wide), 0)
    route = [at // LANES for at in (row, col)]
    place = [at % LANES for at in (row, col)]
    before = earlier((route[0], place[0] % granules), (route[1], place[1] % granules), granules)
    before = before & (place[0] // granules == place[1] // granules)
    before = before.astype(f32).astype(bf16)
    seat = (lax.broadcasted_iota(jnp.int32, (LANES, LANES), 1) // SPAN).astype(f32)
    lane = lax.broadcasted_iota(jnp.int32, (8, LANES), 1)
    step = lane % SPAN
    pixel = lax.broadcasted_iota(jnp.int32, (8, LANES), 0).astype(f32) * (1.0 / SP)
    part = LANES // granules
    for t in range(route_ref.shape[1] // LANES):
        at = slice(t * LANES, (t + 1) * LANES)
        hits = [(route_ref[r : r + 1, at] == own).astype(f32) for r in range(2)]
        hits = jnp.broadcast_to(jnp.concatenate(hits, axis=1), (8, wide))
        ranks = jnp.dot(hits.astype(bf16), before, preferred_element_type=f32)
        ranks = jnp.where(hits > 0.5, ranks, -1.0)
        chosen, values = [], []
        for r in range(2):
            chosen.append((spread_columns(ranks[0:1, r * LANES : (r + 1) * LANES]) == seat).astype(f32).astype(bf16))
            sender = lax.broadcasted_iota(jnp.int32, (part, LANES), 0)
            within = lax.broadcasted_iota(jnp.int32, (part, LANES), 1) // granules == sender
            kinds = []
            for k in range(2):
                start = window_ref[r, k : k + 1, at]
                kinds += [jnp.right_shift(start, 5), jnp.bitwise_and(start, SP - 1)]
            kinds.append(jnp.ones((1, LANES), jnp.int32))
            values.append(jnp.concatenate([jnp.where(within, kind, 0).astype(f32) for kind in kinds], axis=0))
        found = jnp.dot(
            jnp.concatenate(values, axis=1).astype(bf16),
            jnp.concatenate(chosen, axis=0),
            preferred_element_type=f32,
        )
        for n in range(part):
            live = found[4 * part + n : 4 * part + n + 1] > 0.5
            for k, ref in ((0, rows_out), (1, cols_out)):
                base = found[2 * k * part + n : 2 * k * part + n + 1]
                rest = found[(2 * k + 1) * part + n : (2 * k + 1) * part + n + 1]
                first = jnp.clip(base.astype(jnp.int32) - 1, 0, KN - SPAN)
                if k == 0:
                    knot = 2 * jnp.right_shift(first, 1) + 2 * (step % 8) + step // 8
                else:
                    knot = first + step
                border = (knot == 0) | (knot == KN - 1)
                cube = jnp.where(border, 1.0, 1.5)
                square = jnp.where(border, -1.5, -2.5)
                single = jnp.where(border, -0.5, 0.0)
                away = jnp.where(live, base + rest * (1.0 / SP) - knot.astype(f32), 4.0 * KN)
                away = away + pixel
                to = pl.ds((t * part + n) * LANES, LANES)
                for q in range(0, pixels, 16):
                    pair = []
                    for p in (q, q + 8):
                        d = jnp.abs(away + p * (1.0 / SP))
                        near = ((cube * d + square) * d + single) * d + 1.0
                        far = ((2.5 - 0.5 * d) * d - 4.0) * d + 2.0
                        pair.append(jnp.where(d <= 1.0, near, jnp.where(d < 2.0, far, 0.0)))
                    ref[q : q + 16, to] = jnp.concatenate(pair, axis=0).astype(bf16)


def compose(route_ref, received_ref, row_ref, col_ref, pixels_ref, out_ref, passed, result, sems):
    senders = received_ref.shape[0]
    bands = result.shape[0]
    lane = lax.broadcasted_iota(jnp.int32, (16, LANES), 1) // SPAN
    masks = [(lane == r).astype(f32).astype(bf16) for r in range(LANES // SPAN)]
    named = (route_ref[...] == lax.axis_index("gran")).astype(f32)
    scale = 1.0 / jnp.sum(named, keepdims=True)

    def sender(n, carry):
        at = pl.ds(pl.multiple_of(n * LANES, LANES), LANES)
        blocks = []
        for k in range(2 * bands):
            window = received_ref[n, 16 * k : 16 * k + 16, :]
            blocks.append(jnp.concatenate([window * mask for mask in masks], axis=0))
        rows = jnp.dot(row_ref[:, at], jnp.concatenate(blocks, axis=1), preferred_element_type=f32)
        for k in range(2 * bands):
            passed[k, :, at] = rows[:, LANES * k : LANES * k + LANES].astype(bf16)
        return carry

    steps = min(8, senders)

    def several(n, carry):
        for k in range(steps):
            sender(n * steps + k, carry)
        return carry

    lax.fori_loop(0, senders // steps, several, 0)
    copies = []
    for b in range(bands):
        fields = [
            lax.dot_general(
                passed[2 * b + c], col_ref[...], (((1,), (1,)), ((), ())), preferred_element_type=f32
            )
            * scale
            for c in range(2)
        ]
        pixels = pixels_ref[0, b].astype(f32)
        result[b] = (pixels * (1.0 + fields[0]) + fields[1]).astype(bf16)
        copies.append(pltpu.make_async_copy(result.at[b], out_ref.at[0, b], sems.at[b]))
        copies[b].start()
    for copy in copies:
        copy.wait()


def per_device(
    prior_grids,
    pif_rhs,
    pif_diagonal,
    pif_cross,
    pif_coupling,
    neighbour_offset,
    neighbour_count,
    tile_route,
    tile_window,
    tile_pixels,
):
    granules, bands = prior_grids.shape[:2]
    slots = pif_coupling.shape[1]
    pixel_count = tile_pixels.shape[2]
    device_total = lax.axis_size("gran")
    band_total = lax.axis_size("band")

    def by_lane_tile(array):
        cut = array.reshape(array.shape[:2] + (array.shape[2], 32, LANES)).transpose(0, 1, 3, 2, 4)
        return cut.reshape(array.shape[:2] + (32 * array.shape[2], LANES))

    grids = by_lane_tile(prior_grids)
    rhs = by_lane_tile(pif_rhs)
    diagonal = by_lane_tile(pif_diagonal)
    cross = by_lane_tile(pif_cross.transpose(1, 0, 2).reshape(bands, granules // 8, 8, KN * KN))
    coupling = by_lane_tile(pif_coupling.transpose(0, 2, 1, 3))
    graph = [("v", neighbour_offset.T), ("v", neighbour_count[None, :])]
    tiles = [("v", tile_route.T), ("v", tile_window.transpose(1, 2, 0))]
    edge = (REACH, bands, 64, LANES)
    own = (granules, bands, 64, LANES)
    ext = (granules + 2 * REACH, bands, 64, LANES)
    packed = ("v", (64, LANES), f32)
    chunks = 4

    near_pairs = [(i, i ^ 1) for i in range(device_total)]
    far_pairs = [
        pair for i in range(1, device_total - 1, 2) for pair in ((i, i + 1), (i + 1, i))
    ]

    def exchange(near, far):
        far = lax.ppermute(far, "gran", far_pairs)
        near = lax.ppermute(near, "gran", near_pairs)
        return near, far

    near, far = call(
        first_edges,
        [("h", grids)],
        [("v", edge, bf16), ("v", edge, bf16)],
        [pltpu.VMEM((2,) + edge, f32), pltpu.SemaphoreType.DMA((2, REACH))],
    )
    near, far = exchange(near, far)
    (extended,) = call(
        arrange_grids,
        [("h", grids)],
        [("v", ext, f32)],
        [pltpu.VMEM(own, f32), pltpu.SemaphoreType.DMA((chunks,))],
    )
    sources = [rhs, diagonal, cross, coupling]

    def arranged(interior, sources):
        part = len(visits(granules, interior))
        some = (part, bands, 64, LANES)
        return call(
            functools.partial(arrange, interior),
            graph + [("h", source) for source in sources],
            [
                ("v", some, f32),
                ("v", some, f32),
                ("v", (part, bands, 32, LANES), f32),
                ("v", (part, slots, bands, 32, LANES), f32),
            ],
            [
                pltpu.VMEM(cross.shape, f32),
                pltpu.VMEM((part,) + coupling.shape[1:], bf16),
                pltpu.VMEM(coupling.shape[1:], f32),
                pltpu.SMEM((2, granules), jnp.int32),
                pltpu.SemaphoreType.DMA((4, chunks)),
            ],
        )

    gathered = pltpu.VMEM((slots, 64, LANES), f32)
    weights = pltpu.VMEM((slots, 64, LANES), f32)
    scalars = pltpu.SMEM((2, granules), jnp.int32)

    def over_band(partial):
        return [("v", partial)] + [
            ("v", lax.ppermute(partial, "band", [(i, i ^ flip) for i in range(band_total)]))
            for flip in range(1, band_total)
        ]

    for sweep in range(SWEEPS):
        last = sweep == SWEEPS - 1
        (inner,) = call(
            interior_disparities, graph + [("v", extended)], [packed], [gathered, scalars]
        )
        if sweep == 0:
            inner, *edge_state = lax.optimization_barrier((inner, *arranged(False, sources)))
        if last:
            inner_shares = over_band(inner)
        inputs = graph + [("v", near), ("v", far), ("v", extended)]
        inputs += [] if last else [("v", inner)]
        extended, partial = call(
            edge_disparities,
            inputs,
            [("v", ext, f32), packed],
            [gathered, scalars],
            aliases={4: 0},
        )
        shares = over_band(partial)
        if sweep == 1:
            routes, starts, _ = lax.optimization_barrier((tiles[0][1], tiles[1][1], partial))
            weight_shape = ("v", (pixel_count, device_total * LANES), bf16)
            made = call(
                tile_places,
                [("v", routes), ("v", starts)],
                [weight_shape, weight_shape, ("v", (8, LANES), jnp.int32)],
            )
            partial, row_weights, col_weights, places = lax.optimization_barrier((partial, *made))
            shares[0] = ("v", partial)
        edge_state_now = [("v", extended)] + [("v", array) for array in edge_state]
        if not last:
            inputs = graph + shares + edge_state_now
            updated, near, far = call(
                edge_sweep,
                inputs,
                [("v", ext, f32), ("v", edge, bf16), ("v", edge, bf16)],
                [weights, scalars],
            )
            near, far = exchange(near, far)
            if sweep == 0:
                *later, updated = lax.optimization_barrier((*sources, updated))
                inner_state = [("v", array) for array in arranged(True, later)]
            inputs = graph + shares + [("v", extended)] + inner_state
            (extended,) = call(
                interior_sweep,
                inputs + [("v", updated)],
                [("v", ext, f32)],
                [weights, scalars],
                aliases={len(inputs): 0},
            )
    windows = (device_total, 2 * bands * SPAN, LANES)
    scratch = [weights, scalars]
    inputs = graph + inner_shares + [("v", extended)] + inner_state + [("v", places)]
    balanced, gathered_windows = call(
        functools.partial(last_sweep, True),
        inputs,
        [("v", own, f32), ("v", windows, f32)],
        scratch,
    )
    inputs = graph + shares + edge_state_now + [("v", places)] + [("v", balanced), ("v", gathered_windows)]
    balanced, payload, _ = call(
        functools.partial(last_sweep, False),
        inputs,
        [("v", own, f32), ("v", windows, bf16), ("v", windows, f32)],
        scratch,
        aliases={len(inputs) - 2: 0, len(inputs) - 1: 2},
    )
    received = lax.all_to_all(payload, "gran", split_axis=0, concat_axis=0, tiled=True)
    (balanced,) = call(copy_out, [("v", balanced)], [("h", own, f32)], [pltpu.SemaphoreType.DMA])
    (corrected,) = call(
        compose,
        [tiles[0], ("v", received), ("v", row_weights), ("v", col_weights), ("v", tile_pixels)],
        [("h", tile_pixels.shape, bf16)],
        [
            pltpu.VMEM((2 * bands, pixel_count, device_total * LANES), bf16),
            pltpu.VMEM(tile_pixels.shape[1:], bf16),
            pltpu.SemaphoreType.DMA((bands,)),
        ],
        limit=32,
    )
    balanced = balanced.reshape(granules, bands, 32, 2, LANES).transpose(0, 1, 3, 2, 4)
    return (balanced.reshape(prior_grids.shape), corrected)


def solution(mesh):
    placed = (
        P("gran", "band", None, None),
        P("gran", "band", None, None),
        P("gran", "band", None, None),
        P("gran", "band", None),
        P("gran", None, "band", None),
        P("gran", None),
        P("gran"),
        P(),
        P(),
        P("gran", "band", None, None),
    )
    return jax.shard_map(
        per_device,
        mesh=mesh,
        in_specs=placed,
        out_specs=(P("gran", "band", None, None), P("gran", "band", None, None)),
        check_vma=False,
    )
```

```python
import functools
import jax
import jax.numpy as jnp
from jax import lax
from jax.experimental import pallas as pl
from jax.experimental.pallas import tpu as pltpu
from jax.sharding import PartitionSpec as P

BANDS = 12
KN = 64
PATCH = 8
REACH = 4
SWEEPS = 3
SP = 32
LANES = 128
SPAN = 16

robust_scale = 0.3

ON_CHIP = pl.BlockSpec(memory_space=pltpu.VMEM)
ANYWHERE = pl.BlockSpec(memory_space=pl.ANY)
f32 = jnp.float32
bf16 = jnp.bfloat16


def call(body, inputs, outputs, scratch=(), aliases=None, limit=16):
    operands = [
        pltpu.with_memory_space_constraint(array, pltpu.VMEM if kind == "v" else pltpu.HBM)
        for kind, array in inputs
    ]
    return pl.pallas_call(
        body,
        in_specs=[ON_CHIP if kind == "v" else ANYWHERE for kind, _ in inputs],
        out_specs=tuple(ON_CHIP if kind == "v" else ANYWHERE for kind, _, _ in outputs),
        out_shape=tuple(
            (pltpu.VMEM if kind == "v" else pltpu.HBM)(shape, dtype)
            for kind, shape, dtype in outputs
        ),
        scratch_shapes=list(scratch),
        input_output_aliases=aliases or {},
        compiler_params=pltpu.CompilerParams(vmem_limit_bytes=limit * 2**20),
    )(*operands)


def parity():
    return lax.rem(lax.axis_index("gran"), 2)


def first_edges(grids_ref, near_ref, far_ref, raw, sems):
    odd = parity()
    last = grids_ref.shape[0] - REACH
    sides = ((far_ref, odd * last), (near_ref, (1 - odd) * last))
    copies = [
        [pltpu.make_async_copy(grids_ref.at[base + g], raw.at[k, g], sems.at[k, g]) for g in range(REACH)]
        for k, (_, base) in enumerate(sides)
    ]
    for copy in copies[0] + copies[1]:
        copy.start()
    for k, (ref, _) in enumerate(sides):
        for g in range(REACH):
            copies[k][g].wait()
            for b in range(ref.shape[1]):
                for j in range(4):
                    both = [raw[k, g, b, pl.ds(2 * j + c, 8, stride=8), :] for c in range(2)]
                    ref[g, b, 16 * j : 16 * j + 16, :] = jnp.concatenate(both, axis=0).astype(bf16)


def arrange_grids(grids_ref, ext_ref, raw, sems):
    granules, bands = grids_ref.shape[:2]
    chunks = sems.shape[0]
    size = granules // chunks
    copies = []
    for n in range(chunks):
        part = pl.ds(n * size, size)
        copies.append(pltpu.make_async_copy(grids_ref.at[part], raw.at[part], sems.at[n]))
        copies[n].start()

    def step(i, carry):
        for b in range(bands):
            for q in range(8):
                ext_ref[i + REACH, b, 8 * q : 8 * q + 8, :] = raw[i, b, pl.ds(q, 8, stride=8), :]
        return carry

    for n in range(chunks):
        copies[n].wait()
        lax.fori_loop(n * size, (n + 1) * size, step, 0)


def visits(granules, interior):
    inner = list(range(REACH, granules - REACH))
    return inner if interior else [i for i in range(granules) if i not in inner]


def arrange(interior, offset_ref, count_ref, rhs_ref, diag_ref, cross_ref, coupling_ref, rhs_out, diag_out, cross_out, coupling_out, cross_raw, coupling_raw, wide, graph, sems):
    granules, bands = rhs_ref.shape[:2]
    own = visits(granules, interior)
    size = REACH
    chunks = len(own) // size
    copies = []
    for n in range(chunks):
        source, target = pl.ds(own[n * size], size), pl.ds(n * size, size)
        moves = ((coupling_ref, coupling_raw), (diag_ref, diag_out), (rhs_ref, rhs_out))
        copies.append(
            [
                pltpu.make_async_copy(here.at[source], there.at[target], sems.at[k, n])
                for k, (here, there) in enumerate(moves)
            ]
        )
        for copy in copies[n][:2]:
            copy.start()
        if n == 0:
            whole = pltpu.make_async_copy(cross_ref, cross_raw, sems.at[3, 0])
            whole.start()
    for n in range(chunks):
        copies[n][2].start()
    read_graph(offset_ref, count_ref, graph)
    for n in range(chunks):
        for copy in copies[n][:2]:
            copy.wait()
        if n == 0:
            whole.wait()

        def step(g, carry, n=n):
            at = n * size + g
            i = own[n * size] + g
            for b in range(bands):
                wide[b] = coupling_raw[at, b].astype(f32)
                for j in range(4):
                    d = [diag_out[at, b, pl.ds(2 * j + c, 8, stride=8), :] for c in range(2)]
                    pick = cross_raw[b, i // 8, pl.ds(8 * j + i % 8, 8, stride=32), :]
                    cross_out[at, b, 8 * j : 8 * j + 8, :] = pick * jnp.sqrt(d[0] * d[1])

            def slot(s, carry):
                for b in range(bands):
                    for j in range(4):
                        pick = wide[b, pl.ds(8 * j + s, 8, stride=32), :]
                        coupling_out[at, s, b, 8 * j : 8 * j + 8, :] = pick
                return carry

            return lax.fori_loop(0, graph[1, i], slot, carry)

        lax.fori_loop(0, size, step, 0)
    for n in range(chunks):
        copies[n][2].wait()


def lane_sums():
    row = lax.broadcasted_iota(jnp.int32, (LANES, LANES), 0)
    col = lax.broadcasted_iota(jnp.int32, (LANES, LANES), 1)
    return ((row % KN) // PATCH == col % PATCH).astype(f32).astype(bf16)


def lane_spread():
    row = lax.broadcasted_iota(jnp.int32, (LANES, LANES), 0)
    col = lax.broadcasted_iota(jnp.int32, (LANES, LANES), 1)
    return ((col % KN) // PATCH == row % PATCH).astype(f32).astype(bf16)


def read_graph(offset_ref, count_ref, graph):
    slots, granules = offset_ref.shape
    slot = lax.broadcasted_iota(jnp.int32, offset_ref.shape, 0)
    codes = jnp.sum(jnp.left_shift(offset_ref[...] + REACH, 4 * slot), axis=0, keepdims=True)
    counts = count_ref[...]
    for i in range(granules):
        graph[0, i] = codes[0, i]
        graph[1, i] = counts[0, i]


def neighbour(graph, i, s):
    return i + jnp.bitwise_and(jnp.right_shift(graph[0, i], 4 * s), 15)


def group_mask(interior, slots):
    row = lax.broadcasted_iota(jnp.int32, (64, LANES), 0) // 32
    lane = lax.broadcasted_iota(jnp.int32, (64, LANES), 1) // PATCH
    return lane - slots * (1 - row if interior else row)


def disparities(interior, offset_ref, count_ref, ext_ref, gathered, graph):
    bands = ext_ref.shape[1]
    granules = ext_ref.shape[0] - 2 * REACH
    slots = gathered.shape[0]
    gathered[...] = jnp.zeros_like(gathered)
    read_graph(offset_ref, count_ref, graph)

    def response(g):
        return [
            ext_ref[g, b, 16 * j : 16 * j + 8, :] + ext_ref[g, b, 16 * j + 8 : 16 * j + 16, :]
            for b in range(bands)
            for j in range(4)
        ]

    for i in range(granules):
        if (REACH <= i < granules - REACH) != interior:
            continue
        own = response(i + REACH)

        def slot(s, carry, i=i, own=own):
            total = None
            for a, o in zip(own, response(neighbour(graph, i, s))):
                d = a - o
                total = d * d if total is None else total + d * d
            gathered[s, 8 * (i % 8) : 8 * (i % 8) + 8, :] = total
            return carry

        lax.fori_loop(0, graph[1, i], slot, 0)
    sums = jnp.dot(
        gathered[...].reshape(slots * 64, LANES).astype(bf16), lane_sums(), preferred_element_type=f32
    )
    place = group_mask(interior, slots)
    packed = jnp.zeros((64, LANES), f32)
    for s in range(slots):
        packed = jnp.where(place == s, sums[64 * s : 64 * s + 64], packed)
    return packed


def interior_disparities(offset_ref, count_ref, ext_ref, out_ref, gathered, graph):
    out_ref[...] = disparities(True, offset_ref, count_ref, ext_ref, gathered, graph)


def edge_disparities(offset_ref, count_ref, near_ref, far_ref, *refs):
    ext_ref, out_ref, gathered, graph = refs[-4:]
    odd = parity()
    right = ext_ref.shape[0] - REACH
    for ref, base in ((near_ref, (1 - odd) * right), (far_ref, odd * right)):
        for g in range(REACH):
            for b in range(ref.shape[1]):
                ext_ref[base + g, b] = ref[g, b].astype(f32)
    packed = disparities(False, offset_ref, count_ref, ext_ref, gathered, graph)
    out_ref[...] = packed + refs[1][...] if len(refs) == 6 else packed


def spread_weights(shares, interior, weights):
    slots = weights.shape[0]
    total = (shares[0][...] + shares[1][...]) + (shares[2][...] + shares[3][...])
    robust = 1.0 / (1.0 + total * (1.0 / (robust_scale * BANDS * PATCH * PATCH)))
    high = robust.astype(bf16).astype(f32)
    both = jnp.concatenate([high, robust - high], axis=1)
    place = group_mask(interior, slots)
    place = jnp.concatenate([place, place], axis=1)
    spread = lane_spread()
    spread = jnp.concatenate([spread, spread], axis=0)
    stacked = jnp.concatenate(
        [jnp.where(place == s, both, 0.0).astype(bf16) for s in range(slots)], axis=0
    )
    weights[...] = jnp.dot(stacked, spread, preferred_element_type=f32).reshape(slots, 64, LANES)


def balance(i, at, ext_ref, rhs_ref, diag_ref, cross_ref, coupling_ref, weights, graph, store):
    bands = rhs_ref.shape[1]
    row = pl.multiple_of(lax.rem(i, 8) * 8, 8)
    parts = [(b, j) for b in range(bands) for j in range(4)]
    rhs = tuple(rhs_ref[at, b, pl.ds(2 * j + c, 8, stride=8), :] for b, j in parts for c in range(2))

    def slot(s, sums):
        sigma, drive = sums
        weight = weights[s, pl.ds(row, 8), :]
        n = neighbour(graph, i, s)
        new_sigma, new_drive = [], []
        for b in range(bands):
            for j in range(4):
                k = 4 * b + j
                effective = weight * coupling_ref[at, s, b, 8 * j : 8 * j + 8, :]
                new_sigma.append(sigma[k] + effective)
                for c in range(2):
                    grid = ext_ref[n, b, 16 * j + 8 * c : 16 * j + 8 * c + 8, :]
                    new_drive.append(drive[2 * k + c] + effective * grid)
        return tuple(new_sigma), tuple(new_drive)

    zero = jnp.zeros((8, LANES), f32)
    sigma, drive = lax.fori_loop(1, graph[1, i], slot, slot(0, ((zero,) * len(parts), rhs)))
    for k, (b, j) in enumerate(parts):
        first, second = (
            diag_ref[at, b, pl.ds(2 * j + c, 8, stride=8), :] + sigma[k] for c in range(2)
        )
        cross = cross_ref[at, b, 8 * j : 8 * j + 8, :]
        inverse = 1.0 / (first * second - cross * cross)
        gain, offset = drive[2 * k], drive[2 * k + 1]
        store(
            b,
            j,
            (second * gain - cross * offset) * inverse,
            (first * offset - cross * gain) * inverse,
        )


def edge_sweep(offset_ref, count_ref, *refs):
    shares, state, (new_ref, near_ref, far_ref, weights, graph) = refs[:4], refs[4:9], refs[9:]
    read_graph(offset_ref, count_ref, graph)
    spread_weights(shares, False, weights)
    odd = parity()
    last = new_ref.shape[0] - 3 * REACH
    for ref, base in ((far_ref, odd * last), (near_ref, (1 - odd) * last)):

        def step(g, carry, ref=ref, base=base):
            def store(b, j, gain, offset):
                both = jnp.concatenate([gain, offset], axis=0)
                new_ref[base + g + REACH, b, 16 * j : 16 * j + 16, :] = both
                ref[g, b, 16 * j : 16 * j + 16, :] = both.astype(bf16)

            balance(base + g, lax.div(base, 2 * REACH) * REACH + g, *state, weights, graph, store)
            return carry

        lax.fori_loop(0, REACH, step, 0)


def interior_sweep(offset_ref, count_ref, *refs):
    shares, state, (_, new_ref, weights, graph) = refs[:4], refs[4:9], refs[9:]
    read_graph(offset_ref, count_ref, graph)
    spread_weights(shares, True, weights)

    def step(i, carry):
        def store(b, j, gain, offset):
            both = jnp.concatenate([gain, offset], axis=0)
            new_ref[i + REACH, b, 16 * j : 16 * j + 16, :] = both

        balance(i, i - REACH, *state, weights, graph, store)
        return carry

    lax.fori_loop(REACH, new_ref.shape[0] - 3 * REACH, step, 0)


def own_columns(ref, at, granules):
    first = lax.axis_index("gran") * granules
    base = pl.multiple_of((first // LANES) * LANES, LANES)
    turn = jnp.bitwise_and(LANES - lax.rem(first, LANES), LANES - 1)
    return pltpu.roll(ref[at + (pl.ds(base, LANES),)], turn, 1)


def last_sweep(interior, offset_ref, count_ref, *refs):
    shares, state, place_ref = refs[:4], refs[4:9], refs[9]
    weights, graph = refs[-2:]
    if interior:
        solved, windows = refs[10:12]
    else:
        solved, send_ref, windows = refs[12:15]
    granules, bands = solved.shape[:2]
    read_graph(offset_ref, count_ref, graph)
    if interior:
        windows[...] = jnp.zeros_like(windows)
    spread_weights(shares, interior, weights)

    def step(t, carry):
        i = t if interior else jnp.where(t < REACH, t, t + granules - 2 * REACH)

        def store(b, j, gain, offset):
            solved[i, b, pl.ds(2 * j, 8, stride=8), :] = gain
            solved[i, b, pl.ds(2 * j + 1, 8, stride=8), :] = offset

        balance(i, t - REACH if interior else t, *state, weights, graph, store)
        return carry

    lax.fori_loop(*((REACH, granules - REACH) if interior else (0, 2 * REACH)), step, 0)
    lane = lax.broadcasted_iota(jnp.int32, (8, LANES), 1) // SPAN
    seats = LANES // SPAN
    places = place_ref[...]
    for i in visits(granules, interior):
        for r in range(2):
            owner, rank, top, turn = (places[k, r * granules + i] for k in range(4))
            here = [lane == jnp.bitwise_and(rank + half * (KN // SPAN), seats - 1) for half in (0, 1)]
            for b in range(bands):
                for c in range(2):
                    rows = solved[i, b, pl.ds(2 * top + c, 8, stride=2), :]
                    moved = pltpu.roll(rows, jnp.bitwise_and(turn, LANES - 1), 1)
                    for half in (0, 1):
                        at = 16 * (2 * b + c) + 8 * half
                        pltpu.store(windows.at[owner, at : at + 8, :], moved, mask=here[half])
    if not interior:
        for owner in range(windows.shape[0]):
            for at in range(0, windows.shape[1], 16):
                odd = pltpu.roll(windows[owner, at + 8 : at + 16, :], KN, 1)
                both = jnp.concatenate([windows[owner, at : at + 8, :], odd], axis=0)
                send_ref[owner, at : at + 16, :] = both.astype(bf16)


def earlier(first, second, granules):
    def edge(i):
        return ((i < REACH) | (i >= granules - REACH)).astype(jnp.int32)

    def rank(entry):
        return (edge(entry[1]) * 2 + entry[0]) * granules + entry[1]

    return rank(first) < rank(second)


def spread_columns(row):
    return jnp.transpose(jnp.broadcast_to(row, (LANES, LANES)))


def tile_places(route_ref, window_ref, rows_out, cols_out, place_ref):
    pixels, lanes = rows_out.shape
    senders = lanes // LANES
    granules = route_ref.shape[1] // senders
    own = lax.axis_index("gran")
    lane_row = lax.broadcasted_iota(jnp.int32, (1, LANES), 1)

    def both_routes(rows):
        return jnp.where(lane_row < granules, rows[0:1], pltpu.roll(rows, granules, 1)[1:2])

    routes = own_columns(route_ref, (slice(None),), granules)
    starts = [own_columns(window_ref, (r, slice(None)), granules) for r in range(2)]
    named = both_routes(routes).astype(f32)
    col = lax.broadcasted_iota(jnp.int32, (LANES, LANES), 1)
    row = lax.broadcasted_iota(jnp.int32, (LANES, LANES), 0)
    before = earlier((row // granules, row % granules), (col // granules, col % granules), granules)
    before = before & (row < 2 * granules) & (spread_columns(named) == named)
    rank = jnp.sum(before.astype(f32), axis=0, keepdims=True).astype(jnp.int32)
    knots = [
        jnp.clip(jnp.right_shift(both_routes(jnp.concatenate([s[k : k + 1] for s in starts])), 5) - 1, 0, KN - SPAN)
        for k in range(2)
    ]
    turn = rank * SPAN - knots[1] + LANES
    place_ref[...] = jnp.concatenate(
        [named.astype(jnp.int32), rank, jnp.right_shift(knots[0], 1), turn] * 2, axis=0
    )

    wide = 2 * LANES
    col = lax.broadcasted_iota(jnp.int32, (wide, wide), 1)
    row = lax.broadcasted_iota(jnp.int32, (wide, wide), 0)
    route = [at // LANES for at in (row, col)]
    place = [at % LANES for at in (row, col)]
    before = earlier((route[0], place[0] % granules), (route[1], place[1] % granules), granules)
    before = before & (place[0] // granules == place[1] // granules)
    before = before.astype(f32).astype(bf16)
    seat = (lax.broadcasted_iota(jnp.int32, (LANES, LANES), 1) // SPAN).astype(f32)
    lane = lax.broadcasted_iota(jnp.int32, (8, LANES), 1)
    step = lane % SPAN
    pixel = lax.broadcasted_iota(jnp.int32, (8, LANES), 0).astype(f32) * (1.0 / SP)
    part = LANES // granules
    for t in range(route_ref.shape[1] // LANES):
        at = slice(t * LANES, (t + 1) * LANES)
        hits = [(route_ref[r : r + 1, at] == own).astype(f32) for r in range(2)]
        hits = jnp.broadcast_to(jnp.concatenate(hits, axis=1), (8, wide))
        ranks = jnp.dot(hits.astype(bf16), before, preferred_element_type=f32)
        ranks = jnp.where(hits > 0.5, ranks, -1.0)
        chosen, values = [], []
        for r in range(2):
            chosen.append((spread_columns(ranks[0:1, r * LANES : (r + 1) * LANES]) == seat).astype(f32).astype(bf16))
            sender = lax.broadcasted_iota(jnp.int32, (part, LANES), 0)
            within = lax.broadcasted_iota(jnp.int32, (part, LANES), 1) // granules == sender
            kinds = []
            for k in range(2):
                start = window_ref[r, k : k + 1, at]
                kinds += [jnp.right_shift(start, 5), jnp.bitwise_and(start, SP - 1)]
            kinds.append(jnp.ones((1, LANES), jnp.int32))
            values.append(jnp.concatenate([jnp.where(within, kind, 0).astype(f32) for kind in kinds], axis=0))
        found = jnp.dot(
            jnp.concatenate(values, axis=1).astype(bf16),
            jnp.concatenate(chosen, axis=0),
            preferred_element_type=f32,
        )
        for n in range(part):
            live = found[4 * part + n : 4 * part + n + 1] > 0.5
            for k, ref in ((0, rows_out), (1, cols_out)):
                base = found[2 * k * part + n : 2 * k * part + n + 1]
                rest = found[(2 * k + 1) * part + n : (2 * k + 1) * part + n + 1]
                first = jnp.clip(base.astype(jnp.int32) - 1, 0, KN - SPAN)
                if k == 0:
                    knot = 2 * jnp.right_shift(first, 1) + 2 * (step % 8) + step // 8
                else:
                    knot = first + step
                border = (knot == 0) | (knot == KN - 1)
                cube = jnp.where(border, 1.0, 1.5)
                square = jnp.where(border, -1.5, -2.5)
                single = jnp.where(border, -0.5, 0.0)
                away = jnp.where(live, base + rest * (1.0 / SP) - knot.astype(f32), 4.0 * KN)
                away = away + pixel
                to = pl.ds((t * part + n) * LANES, LANES)
                for q in range(0, pixels, 16):
                    pair = []
                    for p in (q, q + 8):
                        d = jnp.abs(away + p * (1.0 / SP))
                        near = ((cube * d + square) * d + single) * d + 1.0
                        far = ((2.5 - 0.5 * d) * d - 4.0) * d + 2.0
                        pair.append(jnp.where(d <= 1.0, near, jnp.where(d < 2.0, far, 0.0)))
                    ref[q : q + 16, to] = jnp.concatenate(pair, axis=0).astype(bf16)


def compose(route_ref, received_ref, row_ref, col_ref, pixels_ref, solved, out_ref, grids_out, passed, result, sems):
    copies = [pltpu.make_async_copy(solved, grids_out, sems.at[result.shape[0]])]
    copies[0].start()
    senders = received_ref.shape[0]
    bands = result.shape[0]
    lane = lax.broadcasted_iota(jnp.int32, (16, LANES), 1) // SPAN
    masks = [(lane == r).astype(f32).astype(bf16) for r in range(LANES // SPAN)]
    named = (route_ref[...] == lax.axis_index("gran")).astype(f32)
    scale = 1.0 / jnp.sum(named, keepdims=True)

    def sender(n, carry):
        at = pl.ds(pl.multiple_of(n * LANES, LANES), LANES)
        blocks = []
        for k in range(2 * bands):
            window = received_ref[n, 16 * k : 16 * k + 16, :]
            blocks.append(jnp.concatenate([window * mask for mask in masks], axis=0))
        rows = jnp.dot(row_ref[:, at], jnp.concatenate(blocks, axis=1), preferred_element_type=f32)
        for k in range(2 * bands):
            passed[k, :, at] = rows[:, LANES * k : LANES * k + LANES].astype(bf16)
        return carry

    steps = min(8, senders)

    def several(n, carry):
        for k in range(steps):
            sender(n * steps + k, carry)
        return carry

    lax.fori_loop(0, senders // steps, several, 0)
    for b in range(bands):
        fields = [
            lax.dot_general(
                passed[2 * b + c], col_ref[...], (((1,), (1,)), ((), ())), preferred_element_type=f32
            )
            * scale
            for c in range(2)
        ]
        pixels = pixels_ref[0, b].astype(f32)
        result[b] = (pixels * (1.0 + fields[0]) + fields[1]).astype(bf16)
        copies.append(pltpu.make_async_copy(result.at[b], out_ref.at[0, b], sems.at[b]))
        copies[-1].start()
    for copy in copies:
        copy.wait()


def per_device(
    prior_grids,
    pif_rhs,
    pif_diagonal,
    pif_cross,
    pif_coupling,
    neighbour_offset,
    neighbour_count,
    tile_route,
    tile_window,
    tile_pixels,
):
    granules, bands = prior_grids.shape[:2]
    slots = pif_coupling.shape[1]
    pixel_count = tile_pixels.shape[2]
    device_total = lax.axis_size("gran")
    band_total = lax.axis_size("band")

    def by_lane_tile(array):
        cut = array.reshape(array.shape[:2] + (array.shape[2], 32, LANES)).transpose(0, 1, 3, 2, 4)
        return cut.reshape(array.shape[:2] + (32 * array.shape[2], LANES))

    grids = by_lane_tile(prior_grids)
    rhs = by_lane_tile(pif_rhs)
    diagonal = by_lane_tile(pif_diagonal)
    cross = by_lane_tile(pif_cross.transpose(1, 0, 2).reshape(bands, granules // 8, 8, KN * KN))
    coupling = by_lane_tile(pif_coupling.transpose(0, 2, 1, 3))
    graph = [("v", neighbour_offset.T), ("v", neighbour_count[None, :])]
    tiles = [("v", tile_route.T), ("v", tile_window.transpose(1, 2, 0))]
    edge = (REACH, bands, 64, LANES)
    own = (granules, bands, 64, LANES)
    ext = (granules + 2 * REACH, bands, 64, LANES)
    packed = ("v", (64, LANES), f32)
    chunks = 4

    near_pairs = [(i, i ^ 1) for i in range(device_total)]
    far_pairs = [
        pair for i in range(1, device_total - 1, 2) for pair in ((i, i + 1), (i + 1, i))
    ]

    def exchange(near, far):
        far = lax.ppermute(far, "gran", far_pairs)
        near = lax.ppermute(near, "gran", near_pairs)
        return near, far

    near, far = call(
        first_edges,
        [("h", grids)],
        [("v", edge, bf16), ("v", edge, bf16)],
        [pltpu.VMEM((2,) + edge, f32), pltpu.SemaphoreType.DMA((2, REACH))],
    )
    near, far = exchange(near, far)
    (extended,) = call(
        arrange_grids,
        [("h", grids)],
        [("v", ext, f32)],
        [pltpu.VMEM(own, f32), pltpu.SemaphoreType.DMA((chunks,))],
    )
    sources = [rhs, diagonal, cross, coupling]

    def arranged(interior, sources):
        part = len(visits(granules, interior))
        some = (part, bands, 64, LANES)
        return call(
            functools.partial(arrange, interior),
            graph + [("h", source) for source in sources],
            [
                ("v", some, f32),
                ("v", some, f32),
                ("v", (part, bands, 32, LANES), f32),
                ("v", (part, slots, bands, 32, LANES), f32),
            ],
            [
                pltpu.VMEM(cross.shape, f32),
                pltpu.VMEM((part,) + coupling.shape[1:], bf16),
                pltpu.VMEM(coupling.shape[1:], f32),
                pltpu.SMEM((2, granules), jnp.int32),
                pltpu.SemaphoreType.DMA((4, chunks)),
            ],
        )

    gathered = pltpu.VMEM((slots, 64, LANES), f32)
    weights = pltpu.VMEM((slots, 64, LANES), f32)
    scalars = pltpu.SMEM((2, granules), jnp.int32)

    def over_band(partial):
        return [("v", partial)] + [
            ("v", lax.ppermute(partial, "band", [(i, i ^ flip) for i in range(band_total)]))
            for flip in range(1, band_total)
        ]

    for sweep in range(SWEEPS):
        last = sweep == SWEEPS - 1
        (inner,) = call(
            interior_disparities, graph + [("v", extended)], [packed], [gathered, scalars]
        )
        if sweep == 0:
            inner, *edge_state = lax.optimization_barrier((inner, *arranged(False, sources)))
        if last:
            inner_shares = over_band(inner)
        inputs = graph + [("v", near), ("v", far), ("v", extended)]
        inputs += [] if last else [("v", inner)]
        extended, partial = call(
            edge_disparities,
            inputs,
            [("v", ext, f32), packed],
            [gathered, scalars],
            aliases={4: 0},
        )
        shares = over_band(partial)
        if sweep == 1:
            routes, starts, _ = lax.optimization_barrier((tiles[0][1], tiles[1][1], partial))
            weight_shape = ("v", (pixel_count, device_total * LANES), bf16)
            made = call(
                tile_places,
                [("v", routes), ("v", starts)],
                [weight_shape, weight_shape, ("v", (8, LANES), jnp.int32)],
            )
            partial, row_weights, col_weights, places = lax.optimization_barrier((partial, *made))
            shares[0] = ("v", partial)
        edge_state_now = [("v", extended)] + [("v", array) for array in edge_state]
        if not last:
            inputs = graph + shares + edge_state_now
            updated, near, far = call(
                edge_sweep,
                inputs,
                [("v", ext, f32), ("v", edge, bf16), ("v", edge, bf16)],
                [weights, scalars],
            )
            near, far = exchange(near, far)
            if sweep == 0:
                *later, updated = lax.optimization_barrier((*sources, updated))
                inner_state = [("v", array) for array in arranged(True, later)]
            inputs = graph + shares + [("v", extended)] + inner_state
            (extended,) = call(
                interior_sweep,
                inputs + [("v", updated)],
                [("v", ext, f32)],
                [weights, scalars],
                aliases={len(inputs): 0},
            )
    windows = (device_total, 2 * bands * SPAN, LANES)
    scratch = [weights, scalars]
    inputs = graph + inner_shares + [("v", extended)] + inner_state + [("v", places)]
    balanced, gathered_windows = call(
        functools.partial(last_sweep, True),
        inputs,
        [("v", own, f32), ("v", windows, f32)],
        scratch,
    )
    inputs = graph + shares + edge_state_now + [("v", places)] + [("v", balanced), ("v", gathered_windows)]
    balanced, payload, _ = call(
        functools.partial(last_sweep, False),
        inputs,
        [("v", own, f32), ("v", windows, bf16), ("v", windows, f32)],
        scratch,
        aliases={len(inputs) - 2: 0, len(inputs) - 1: 2},
    )
    received = lax.all_to_all(payload, "gran", split_axis=0, concat_axis=0, tiled=True)
    inputs = [tiles[0], ("v", received), ("v", row_weights), ("v", col_weights), ("v", tile_pixels)]
    corrected, balanced = call(
        compose,
        inputs + [("v", balanced)],
        [("h", tile_pixels.shape, bf16), ("h", own, f32)],
        [
            pltpu.VMEM((2 * bands, pixel_count, device_total * LANES), bf16),
            pltpu.VMEM(tile_pixels.shape[1:], bf16),
            pltpu.SemaphoreType.DMA((bands + 1,)),
        ],
        limit=32,
    )
    balanced = balanced.reshape(granules, bands, 32, 2, LANES).transpose(0, 1, 3, 2, 4)
    return (balanced.reshape(prior_grids.shape), corrected)


def solution(mesh):
    placed = (
        P("gran", "band", None, None),
        P("gran", "band", None, None),
        P("gran", "band", None, None),
        P("gran", "band", None),
        P("gran", None, "band", None),
        P("gran", None),
        P("gran"),
        P(),
        P(),
        P("gran", "band", None, None),
    )
    return jax.shard_map(
        per_device,
        mesh=mesh,
        in_specs=placed,
        out_specs=(P("gran", "band", None, None), P("gran", "band", None, None)),
        check_vma=False,
    )
```

```python
import functools
import jax
import jax.numpy as jnp
from jax import lax
from jax.experimental import pallas as pl
from jax.experimental.pallas import tpu as pltpu
from jax.sharding import PartitionSpec as P

BANDS = 12
KN = 64
PATCH = 8
REACH = 4
SWEEPS = 3
SP = 32
LANES = 128
SPAN = 16

robust_scale = 0.3

ON_CHIP = pl.BlockSpec(memory_space=pltpu.VMEM)
ANYWHERE = pl.BlockSpec(memory_space=pl.ANY)
f32 = jnp.float32
bf16 = jnp.bfloat16


def call(body, inputs, outputs, scratch=(), aliases=None, limit=16):
    operands = [
        pltpu.with_memory_space_constraint(array, pltpu.VMEM if kind == "v" else pltpu.HBM)
        for kind, array in inputs
    ]
    return pl.pallas_call(
        body,
        in_specs=[ON_CHIP if kind == "v" else ANYWHERE for kind, _ in inputs],
        out_specs=tuple(ON_CHIP if kind == "v" else ANYWHERE for kind, _, _ in outputs),
        out_shape=tuple(
            (pltpu.VMEM if kind == "v" else pltpu.HBM)(shape, dtype)
            for kind, shape, dtype in outputs
        ),
        scratch_shapes=list(scratch),
        input_output_aliases=aliases or {},
        compiler_params=pltpu.CompilerParams(vmem_limit_bytes=limit * 2**20),
    )(*operands)


def parity():
    return lax.rem(lax.axis_index("gran"), 2)


def first_edges(grids_ref, near_ref, far_ref, raw, sems):
    odd = parity()
    last = grids_ref.shape[0] - REACH
    sides = ((far_ref, odd * last), (near_ref, (1 - odd) * last))
    copies = [
        [pltpu.make_async_copy(grids_ref.at[base + g], raw.at[k, g], sems.at[k, g]) for g in range(REACH)]
        for k, (_, base) in enumerate(sides)
    ]
    for copy in copies[0] + copies[1]:
        copy.start()
    for k, (ref, _) in enumerate(sides):
        for g in range(REACH):
            copies[k][g].wait()
            for b in range(ref.shape[1]):
                for j in range(4):
                    both = [raw[k, g, b, pl.ds(2 * j + c, 8, stride=8), :] for c in range(2)]
                    ref[g, b, 16 * j : 16 * j + 16, :] = jnp.concatenate(both, axis=0).astype(bf16)


def arrange_grids(grids_ref, ext_ref, raw, sems):
    granules, bands = grids_ref.shape[:2]
    chunks = sems.shape[0]
    size = granules // chunks
    copies = []
    for n in range(chunks):
        part = pl.ds(n * size, size)
        copies.append(pltpu.make_async_copy(grids_ref.at[part], raw.at[part], sems.at[n]))
        copies[n].start()

    def step(i, carry):
        for b in range(bands):
            for q in range(8):
                ext_ref[i + REACH, b, 8 * q : 8 * q + 8, :] = raw[i, b, pl.ds(q, 8, stride=8), :]
        return carry

    for n in range(chunks):
        copies[n].wait()
        lax.fori_loop(n * size, (n + 1) * size, step, 0)


def visits(granules, interior):
    inner = list(range(REACH, granules - REACH))
    return inner if interior else [i for i in range(granules) if i not in inner]


def arrange(interior, offset_ref, count_ref, rhs_ref, diag_ref, cross_ref, coupling_ref, rhs_out, diag_out, cross_out, coupling_out, cross_raw, coupling_raw, wide, graph, sems):
    granules, bands = rhs_ref.shape[:2]
    own = visits(granules, interior)
    size = REACH
    chunks = len(own) // size
    copies = []
    for n in range(chunks):
        source, target = pl.ds(own[n * size], size), pl.ds(n * size, size)
        moves = ((coupling_ref, coupling_raw), (diag_ref, diag_out), (rhs_ref, rhs_out))
        copies.append(
            [
                pltpu.make_async_copy(here.at[source], there.at[target], sems.at[k, n])
                for k, (here, there) in enumerate(moves)
            ]
        )
        for copy in copies[n][:2]:
            copy.start()
        if n == 0:
            whole = pltpu.make_async_copy(cross_ref, cross_raw, sems.at[3, 0])
            whole.start()
    for n in range(chunks):
        copies[n][2].start()
    read_graph(offset_ref, count_ref, graph)
    for n in range(chunks):
        for copy in copies[n][:2]:
            copy.wait()
        if n == 0:
            whole.wait()

        def step(g, carry, n=n):
            at = n * size + g
            i = own[n * size] + g
            for b in range(bands):
                wide[b] = coupling_raw[at, b].astype(f32)
                for j in range(4):
                    d = [diag_out[at, b, pl.ds(2 * j + c, 8, stride=8), :] for c in range(2)]
                    pick = cross_raw[b, i // 8, pl.ds(8 * j + i % 8, 8, stride=32), :]
                    cross_out[at, b, 8 * j : 8 * j + 8, :] = pick * jnp.sqrt(d[0] * d[1])

            def slot(s, carry):
                for b in range(bands):
                    for j in range(4):
                        pick = wide[b, pl.ds(8 * j + s, 8, stride=32), :]
                        coupling_out[at, s, b, 8 * j : 8 * j + 8, :] = pick
                return carry

            return lax.fori_loop(0, graph[1, i], slot, carry)

        lax.fori_loop(0, size, step, 0)
    for n in range(chunks):
        copies[n][2].wait()


def lane_sums():
    row = lax.broadcasted_iota(jnp.int32, (LANES, LANES), 0)
    col = lax.broadcasted_iota(jnp.int32, (LANES, LANES), 1)
    return ((row % KN) // PATCH == col % PATCH).astype(f32).astype(bf16)


def lane_spread():
    row = lax.broadcasted_iota(jnp.int32, (LANES, LANES), 0)
    col = lax.broadcasted_iota(jnp.int32, (LANES, LANES), 1)
    return ((col % KN) // PATCH == row % PATCH).astype(f32).astype(bf16)


def read_graph(offset_ref, count_ref, graph):
    slots, granules = offset_ref.shape
    slot = lax.broadcasted_iota(jnp.int32, offset_ref.shape, 0)
    codes = jnp.sum(jnp.left_shift(offset_ref[...] + REACH, 4 * slot), axis=0, keepdims=True)
    counts = count_ref[...]
    for i in range(granules):
        graph[0, i] = codes[0, i]
        graph[1, i] = counts[0, i]


def neighbour(graph, i, s):
    return i + jnp.bitwise_and(jnp.right_shift(graph[0, i], 4 * s), 15)


def group_mask(interior, slots):
    row = lax.broadcasted_iota(jnp.int32, (64, LANES), 0) // 32
    lane = lax.broadcasted_iota(jnp.int32, (64, LANES), 1) // PATCH
    return lane - slots * (1 - row if interior else row)


def disparities(interior, offset_ref, count_ref, ext_ref, gathered, graph):
    bands = ext_ref.shape[1]
    granules = ext_ref.shape[0] - 2 * REACH
    slots = gathered.shape[0]
    gathered[...] = jnp.zeros_like(gathered)
    read_graph(offset_ref, count_ref, graph)

    def response(g):
        return [
            ext_ref[g, b, 16 * j : 16 * j + 8, :] + ext_ref[g, b, 16 * j + 8 : 16 * j + 16, :]
            for b in range(bands)
            for j in range(4)
        ]

    for i in range(granules):
        if (REACH <= i < granules - REACH) != interior:
            continue
        own = response(i + REACH)

        def slot(s, carry, i=i, own=own):
            total = None
            for a, o in zip(own, response(neighbour(graph, i, s))):
                d = a - o
                total = d * d if total is None else total + d * d
            gathered[s, 8 * (i % 8) : 8 * (i % 8) + 8, :] = total
            return carry

        lax.fori_loop(0, graph[1, i], slot, 0)
    sums = jnp.dot(
        gathered[...].reshape(slots * 64, LANES).astype(bf16), lane_sums(), preferred_element_type=f32
    )
    place = group_mask(interior, slots)
    packed = jnp.zeros((64, LANES), f32)
    for s in range(slots):
        packed = jnp.where(place == s, sums[64 * s : 64 * s + 64], packed)
    return packed


def interior_disparities(offset_ref, count_ref, ext_ref, out_ref, gathered, graph):
    out_ref[...] = disparities(True, offset_ref, count_ref, ext_ref, gathered, graph)


def edge_disparities(offset_ref, count_ref, near_ref, far_ref, *refs):
    ext_ref, out_ref, gathered, graph = refs[-4:]
    odd = parity()
    right = ext_ref.shape[0] - REACH
    for ref, base in ((near_ref, (1 - odd) * right), (far_ref, odd * right)):
        for g in range(REACH):
            for b in range(ref.shape[1]):
                ext_ref[base + g, b] = ref[g, b].astype(f32)
    packed = disparities(False, offset_ref, count_ref, ext_ref, gathered, graph)
    out_ref[...] = packed + refs[1][...] if len(refs) == 6 else packed


def add(one_ref, other_ref, out_ref):
    out_ref[...] = one_ref[...] + other_ref[...]


def spread_weights(shares, interior, weights):
    slots = weights.shape[0]
    total = shares[0][...] + shares[1][...]
    robust = 1.0 / (1.0 + total * (1.0 / (robust_scale * BANDS * PATCH * PATCH)))
    high = robust.astype(bf16).astype(f32)
    both = jnp.concatenate([high, robust - high], axis=1)
    place = group_mask(interior, slots)
    place = jnp.concatenate([place, place], axis=1)
    spread = lane_spread()
    spread = jnp.concatenate([spread, spread], axis=0)
    stacked = jnp.concatenate(
        [jnp.where(place == s, both, 0.0).astype(bf16) for s in range(slots)], axis=0
    )
    weights[...] = jnp.dot(stacked, spread, preferred_element_type=f32).reshape(slots, 64, LANES)


def balance(i, at, ext_ref, rhs_ref, diag_ref, cross_ref, coupling_ref, weights, graph, store):
    bands = rhs_ref.shape[1]
    row = pl.multiple_of(lax.rem(i, 8) * 8, 8)
    parts = [(b, j) for b in range(bands) for j in range(4)]
    rhs = tuple(rhs_ref[at, b, pl.ds(2 * j + c, 8, stride=8), :] for b, j in parts for c in range(2))

    def slot(s, sums):
        sigma, drive = sums
        weight = weights[s, pl.ds(row, 8), :]
        n = neighbour(graph, i, s)
        new_sigma, new_drive = [], []
        for b in range(bands):
            for j in range(4):
                k = 4 * b + j
                effective = weight * coupling_ref[at, s, b, 8 * j : 8 * j + 8, :]
                new_sigma.append(sigma[k] + effective)
                for c in range(2):
                    grid = ext_ref[n, b, 16 * j + 8 * c : 16 * j + 8 * c + 8, :]
                    new_drive.append(drive[2 * k + c] + effective * grid)
        return tuple(new_sigma), tuple(new_drive)

    zero = jnp.zeros((8, LANES), f32)
    sigma, drive = lax.fori_loop(1, graph[1, i], slot, slot(0, ((zero,) * len(parts), rhs)))
    for k, (b, j) in enumerate(parts):
        first, second = (
            diag_ref[at, b, pl.ds(2 * j + c, 8, stride=8), :] + sigma[k] for c in range(2)
        )
        cross = cross_ref[at, b, 8 * j : 8 * j + 8, :]
        inverse = 1.0 / (first * second - cross * cross)
        gain, offset = drive[2 * k], drive[2 * k + 1]
        store(
            b,
            j,
            (second * gain - cross * offset) * inverse,
            (first * offset - cross * gain) * inverse,
        )


def edge_sweep(offset_ref, count_ref, *refs):
    shares, state, (new_ref, near_ref, far_ref, weights, graph) = refs[:2], refs[2:7], refs[7:]
    read_graph(offset_ref, count_ref, graph)
    spread_weights(shares, False, weights)
    odd = parity()
    last = new_ref.shape[0] - 3 * REACH
    for ref, base in ((far_ref, odd * last), (near_ref, (1 - odd) * last)):

        def step(g, carry, ref=ref, base=base):
            def store(b, j, gain, offset):
                both = jnp.concatenate([gain, offset], axis=0)
                new_ref[base + g + REACH, b, 16 * j : 16 * j + 16, :] = both
                ref[g, b, 16 * j : 16 * j + 16, :] = both.astype(bf16)

            balance(base + g, lax.div(base, 2 * REACH) * REACH + g, *state, weights, graph, store)
            return carry

        lax.fori_loop(0, REACH, step, 0)


def interior_sweep(offset_ref, count_ref, *refs):
    shares, state, (_, new_ref, weights, graph) = refs[:2], refs[2:7], refs[7:]
    read_graph(offset_ref, count_ref, graph)
    spread_weights(shares, True, weights)

    def step(i, carry):
        def store(b, j, gain, offset):
            both = jnp.concatenate([gain, offset], axis=0)
            new_ref[i + REACH, b, 16 * j : 16 * j + 16, :] = both

        balance(i, i - REACH, *state, weights, graph, store)
        return carry

    lax.fori_loop(REACH, new_ref.shape[0] - 3 * REACH, step, 0)


def own_columns(ref, at, granules):
    first = lax.axis_index("gran") * granules
    base = pl.multiple_of((first // LANES) * LANES, LANES)
    turn = jnp.bitwise_and(LANES - lax.rem(first, LANES), LANES - 1)
    return pltpu.roll(ref[at + (pl.ds(base, LANES),)], turn, 1)


def last_sweep(interior, offset_ref, count_ref, *refs):
    shares, state, place_ref = refs[:2], refs[2:7], refs[7]
    weights, graph = refs[-2:]
    if interior:
        solved, windows = refs[8:10]
    else:
        solved, send_ref, windows = refs[10:13]
    granules, bands = solved.shape[:2]
    read_graph(offset_ref, count_ref, graph)
    if interior:
        windows[...] = jnp.zeros_like(windows)
    spread_weights(shares, interior, weights)

    def step(t, carry):
        i = t if interior else jnp.where(t < REACH, t, t + granules - 2 * REACH)

        def store(b, j, gain, offset):
            solved[i, b, pl.ds(2 * j, 8, stride=8), :] = gain
            solved[i, b, pl.ds(2 * j + 1, 8, stride=8), :] = offset

        balance(i, t - REACH if interior else t, *state, weights, graph, store)
        return carry

    lax.fori_loop(*((REACH, granules - REACH) if interior else (0, 2 * REACH)), step, 0)
    lane = lax.broadcasted_iota(jnp.int32, (8, LANES), 1) // SPAN
    seats = LANES // SPAN
    places = place_ref[...]
    for i in visits(granules, interior):
        for r in range(2):
            owner, rank, top, turn = (places[k, r * granules + i] for k in range(4))
            here = [lane == jnp.bitwise_and(rank + half * (KN // SPAN), seats - 1) for half in (0, 1)]
            for b in range(bands):
                for c in range(2):
                    rows = solved[i, b, pl.ds(2 * top + c, 8, stride=2), :]
                    moved = pltpu.roll(rows, jnp.bitwise_and(turn, LANES - 1), 1)
                    for half in (0, 1):
                        at = 16 * (2 * b + c) + 8 * half
                        pltpu.store(windows.at[owner, at : at + 8, :], moved, mask=here[half])
    if not interior:
        for owner in range(windows.shape[0]):
            for at in range(0, windows.shape[1], 16):
                odd = pltpu.roll(windows[owner, at + 8 : at + 16, :], KN, 1)
                both = jnp.concatenate([windows[owner, at : at + 8, :], odd], axis=0)
                send_ref[owner, at : at + 16, :] = both.astype(bf16)


def earlier(first, second, granules):
    def edge(i):
        return ((i < REACH) | (i >= granules - REACH)).astype(jnp.int32)

    def rank(entry):
        return (edge(entry[1]) * 2 + entry[0]) * granules + entry[1]

    return rank(first) < rank(second)


def spread_columns(row):
    return jnp.transpose(jnp.broadcast_to(row, (LANES, LANES)))


def tile_places(route_ref, window_ref, rows_out, cols_out, place_ref):
    pixels, lanes = rows_out.shape
    senders = lanes // LANES
    granules = route_ref.shape[1] // senders
    own = lax.axis_index("gran")
    lane_row = lax.broadcasted_iota(jnp.int32, (1, LANES), 1)

    def both_routes(rows):
        return jnp.where(lane_row < granules, rows[0:1], pltpu.roll(rows, granules, 1)[1:2])

    routes = own_columns(route_ref, (slice(None),), granules)
    starts = [own_columns(window_ref, (r, slice(None)), granules) for r in range(2)]
    named = both_routes(routes).astype(f32)
    col = lax.broadcasted_iota(jnp.int32, (LANES, LANES), 1)
    row = lax.broadcasted_iota(jnp.int32, (LANES, LANES), 0)
    before = earlier((row // granules, row % granules), (col // granules, col % granules), granules)
    before = before & (row < 2 * granules) & (spread_columns(named) == named)
    rank = jnp.sum(before.astype(f32), axis=0, keepdims=True).astype(jnp.int32)
    knots = [
        jnp.clip(jnp.right_shift(both_routes(jnp.concatenate([s[k : k + 1] for s in starts])), 5) - 1, 0, KN - SPAN)
        for k in range(2)
    ]
    turn = rank * SPAN - knots[1] + LANES
    place_ref[...] = jnp.concatenate(
        [named.astype(jnp.int32), rank, jnp.right_shift(knots[0], 1), turn] * 2, axis=0
    )

    wide = 2 * LANES
    col = lax.broadcasted_iota(jnp.int32, (wide, wide), 1)
    row = lax.broadcasted_iota(jnp.int32, (wide, wide), 0)
    route = [at // LANES for at in (row, col)]
    place = [at % LANES for at in (row, col)]
    before = earlier((route[0], place[0] % granules), (route[1], place[1] % granules), granules)
    before = before & (place[0] // granules == place[1] // granules)
    before = before.astype(f32).astype(bf16)
    seat = (lax.broadcasted_iota(jnp.int32, (LANES, LANES), 1) // SPAN).astype(f32)
    lane = lax.broadcasted_iota(jnp.int32, (8, LANES), 1)
    step = lane % SPAN
    pixel = lax.broadcasted_iota(jnp.int32, (8, LANES), 0).astype(f32) * (1.0 / SP)
    part = LANES // granules
    for t in range(route_ref.shape[1] // LANES):
        at = slice(t * LANES, (t + 1) * LANES)
        hits = [(route_ref[r : r + 1, at] == own).astype(f32) for r in range(2)]
        hits = jnp.broadcast_to(jnp.concatenate(hits, axis=1), (8, wide))
        ranks = jnp.dot(hits.astype(bf16), before, preferred_element_type=f32)
        ranks = jnp.where(hits > 0.5, ranks, -1.0)
        chosen, values = [], []
        for r in range(2):
            chosen.append((spread_columns(ranks[0:1, r * LANES : (r + 1) * LANES]) == seat).astype(f32).astype(bf16))
            sender = lax.broadcasted_iota(jnp.int32, (part, LANES), 0)
            within = lax.broadcasted_iota(jnp.int32, (part, LANES), 1) // granules == sender
            kinds = []
            for k in range(2):
                start = window_ref[r, k : k + 1, at]
                kinds += [jnp.right_shift(start, 5), jnp.bitwise_and(start, SP - 1)]
            kinds.append(jnp.ones((1, LANES), jnp.int32))
            values.append(jnp.concatenate([jnp.where(within, kind, 0).astype(f32) for kind in kinds], axis=0))
        found = jnp.dot(
            jnp.concatenate(values, axis=1).astype(bf16),
            jnp.concatenate(chosen, axis=0),
            preferred_element_type=f32,
        )
        for n in range(part):
            live = found[4 * part + n : 4 * part + n + 1] > 0.5
            for k, ref in ((0, rows_out), (1, cols_out)):
                base = found[2 * k * part + n : 2 * k * part + n + 1]
                rest = found[(2 * k + 1) * part + n : (2 * k + 1) * part + n + 1]
                first = jnp.clip(base.astype(jnp.int32) - 1, 0, KN - SPAN)
                if k == 0:
                    knot = 2 * jnp.right_shift(first, 1) + 2 * (step % 8) + step // 8
                else:
                    knot = first + step
                border = (knot == 0) | (knot == KN - 1)
                cube = jnp.where(border, 1.0, 1.5)
                square = jnp.where(border, -1.5, -2.5)
                single = jnp.where(border, -0.5, 0.0)
                away = jnp.where(live, base + rest * (1.0 / SP) - knot.astype(f32), 4.0 * KN)
                away = away + pixel
                to = pl.ds((t * part + n) * LANES, LANES)
                for q in range(0, pixels, 16):
                    pair = []
                    for p in (q, q + 8):
                        d = jnp.abs(away + p * (1.0 / SP))
                        near = ((cube * d + square) * d + single) * d + 1.0
                        far = ((2.5 - 0.5 * d) * d - 4.0) * d + 2.0
                        pair.append(jnp.where(d <= 1.0, near, jnp.where(d < 2.0, far, 0.0)))
                    ref[q : q + 16, to] = jnp.concatenate(pair, axis=0).astype(bf16)


def compose(route_ref, received_ref, row_ref, col_ref, pixels_ref, solved, out_ref, grids_out, passed, result, sems):
    copies = [pltpu.make_async_copy(solved, grids_out, sems.at[result.shape[0]])]
    copies[0].start()
    senders = received_ref.shape[0]
    bands = result.shape[0]
    lane = lax.broadcasted_iota(jnp.int32, (16, LANES), 1) // SPAN
    masks = [(lane == r).astype(f32).astype(bf16) for r in range(LANES // SPAN)]
    named = (route_ref[...] == lax.axis_index("gran")).astype(f32)
    scale = 1.0 / jnp.sum(named, keepdims=True)

    def sender(n, carry):
        at = pl.ds(pl.multiple_of(n * LANES, LANES), LANES)
        blocks = []
        for k in range(2 * bands):
            window = received_ref[n, 16 * k : 16 * k + 16, :]
            blocks.append(jnp.concatenate([window * mask for mask in masks], axis=0))
        rows = jnp.dot(row_ref[:, at], jnp.concatenate(blocks, axis=1), preferred_element_type=f32)
        for k in range(2 * bands):
            passed[k, :, at] = rows[:, LANES * k : LANES * k + LANES].astype(bf16)
        return carry

    steps = min(8, senders)

    def several(n, carry):
        for k in range(steps):
            sender(n * steps + k, carry)
        return carry

    lax.fori_loop(0, senders // steps, several, 0)
    for b in range(bands):
        fields = [
            lax.dot_general(
                passed[2 * b + c], col_ref[...], (((1,), (1,)), ((), ())), preferred_element_type=f32
            )
            * scale
            for c in range(2)
        ]
        pixels = pixels_ref[0, b].astype(f32)
        result[b] = (pixels * (1.0 + fields[0]) + fields[1]).astype(bf16)
        copies.append(pltpu.make_async_copy(result.at[b], out_ref.at[0, b], sems.at[b]))
        copies[-1].start()
    for copy in copies:
        copy.wait()


def per_device(
    prior_grids,
    pif_rhs,
    pif_diagonal,
    pif_cross,
    pif_coupling,
    neighbour_offset,
    neighbour_count,
    tile_route,
    tile_window,
    tile_pixels,
):
    granules, bands = prior_grids.shape[:2]
    slots = pif_coupling.shape[1]
    pixel_count = tile_pixels.shape[2]
    device_total = lax.axis_size("gran")
    band_total = lax.axis_size("band")

    def by_lane_tile(array):
        cut = array.reshape(array.shape[:2] + (array.shape[2], 32, LANES)).transpose(0, 1, 3, 2, 4)
        return cut.reshape(array.shape[:2] + (32 * array.shape[2], LANES))

    grids = by_lane_tile(prior_grids)
    rhs = by_lane_tile(pif_rhs)
    diagonal = by_lane_tile(pif_diagonal)
    cross = by_lane_tile(pif_cross.transpose(1, 0, 2).reshape(bands, granules // 8, 8, KN * KN))
    coupling = by_lane_tile(pif_coupling.transpose(0, 2, 1, 3))
    graph = [("v", neighbour_offset.T), ("v", neighbour_count[None, :])]
    tiles = [("v", tile_route.T), ("v", tile_window.transpose(1, 2, 0))]
    edge = (REACH, bands, 64, LANES)
    own = (granules, bands, 64, LANES)
    ext = (granules + 2 * REACH, bands, 64, LANES)
    packed = ("v", (64, LANES), f32)
    chunks = 4

    near_pairs = [(i, i ^ 1) for i in range(device_total)]
    far_pairs = [
        pair for i in range(1, device_total - 1, 2) for pair in ((i, i + 1), (i + 1, i))
    ]

    def exchange(near, far):
        far = lax.ppermute(far, "gran", far_pairs)
        near = lax.ppermute(near, "gran", near_pairs)
        return near, far

    near, far = call(
        first_edges,
        [("h", grids)],
        [("v", edge, bf16), ("v", edge, bf16)],
        [pltpu.VMEM((2,) + edge, f32), pltpu.SemaphoreType.DMA((2, REACH))],
    )
    near, far = exchange(near, far)
    (extended,) = call(
        arrange_grids,
        [("h", grids)],
        [("v", ext, f32)],
        [pltpu.VMEM(own, f32), pltpu.SemaphoreType.DMA((chunks,))],
    )
    sources = [rhs, diagonal, cross, coupling]

    def arranged(interior, sources):
        part = len(visits(granules, interior))
        some = (part, bands, 64, LANES)
        return call(
            functools.partial(arrange, interior),
            graph + [("h", source) for source in sources],
            [
                ("v", some, f32),
                ("v", some, f32),
                ("v", (part, bands, 32, LANES), f32),
                ("v", (part, slots, bands, 32, LANES), f32),
            ],
            [
                pltpu.VMEM(cross.shape, f32),
                pltpu.VMEM((part,) + coupling.shape[1:], bf16),
                pltpu.VMEM(coupling.shape[1:], f32),
                pltpu.SMEM((2, granules), jnp.int32),
                pltpu.SemaphoreType.DMA((4, chunks)),
            ],
        )

    gathered = pltpu.VMEM((slots, 64, LANES), f32)
    weights = pltpu.VMEM((slots, 64, LANES), f32)
    scalars = pltpu.SMEM((2, granules), jnp.int32)

    def over_band(partial):
        flip = 1
        other = lax.ppermute(partial, "band", [(i, i ^ flip) for i in range(band_total)])
        while 2 * flip + 1 < band_total:
            flip = 2 * flip + 1
            (partial,) = call(add, [("v", partial), ("v", other)], [packed])
            other = lax.ppermute(partial, "band", [(i, i ^ flip) for i in range(band_total)])
        return [("v", partial), ("v", other)]

    for sweep in range(SWEEPS):
        last = sweep == SWEEPS - 1
        (inner,) = call(
            interior_disparities, graph + [("v", extended)], [packed], [gathered, scalars]
        )
        if sweep == 0:
            inner, *edge_state = lax.optimization_barrier((inner, *arranged(False, sources)))
        if last:
            inner_shares = over_band(inner)
        inputs = graph + [("v", near), ("v", far), ("v", extended)]
        inputs += [] if last else [("v", inner)]
        extended, partial = call(
            edge_disparities,
            inputs,
            [("v", ext, f32), packed],
            [gathered, scalars],
            aliases={4: 0},
        )
        shares = over_band(partial)
        if sweep == 1:
            summed = shares[0][1]
            routes, starts, _ = lax.optimization_barrier((tiles[0][1], tiles[1][1], summed))
            weight_shape = ("v", (pixel_count, device_total * LANES), bf16)
            made = call(
                tile_places,
                [("v", routes), ("v", starts)],
                [weight_shape, weight_shape, ("v", (8, LANES), jnp.int32)],
            )
            summed, row_weights, col_weights, places = lax.optimization_barrier((summed, *made))
            shares[0] = ("v", summed)
        edge_state_now = [("v", extended)] + [("v", array) for array in edge_state]
        if not last:
            inputs = graph + shares + edge_state_now
            updated, near, far = call(
                edge_sweep,
                inputs,
                [("v", ext, f32), ("v", edge, bf16), ("v", edge, bf16)],
                [weights, scalars],
            )
            near, far = exchange(near, far)
            if sweep == 0:
                *later, updated = lax.optimization_barrier((*sources, updated))
                inner_state = [("v", array) for array in arranged(True, later)]
            inputs = graph + shares + [("v", extended)] + inner_state
            (extended,) = call(
                interior_sweep,
                inputs + [("v", updated)],
                [("v", ext, f32)],
                [weights, scalars],
                aliases={len(inputs): 0},
            )
    windows = (device_total, 2 * bands * SPAN, LANES)
    scratch = [weights, scalars]
    inputs = graph + inner_shares + [("v", extended)] + inner_state + [("v", places)]
    balanced, gathered_windows = call(
        functools.partial(last_sweep, True),
        inputs,
        [("v", own, f32), ("v", windows, f32)],
        scratch,
    )
    inputs = graph + shares + edge_state_now + [("v", places)] + [("v", balanced), ("v", gathered_windows)]
    balanced, payload, _ = call(
        functools.partial(last_sweep, False),
        inputs,
        [("v", own, f32), ("v", windows, bf16), ("v", windows, f32)],
        scratch,
        aliases={len(inputs) - 2: 0, len(inputs) - 1: 2},
    )
    received = lax.all_to_all(payload, "gran", split_axis=0, concat_axis=0, tiled=True)
    inputs = [tiles[0], ("v", received), ("v", row_weights), ("v", col_weights), ("v", tile_pixels)]
    corrected, balanced = call(
        compose,
        inputs + [("v", balanced)],
        [("h", tile_pixels.shape, bf16), ("h", own, f32)],
        [
            pltpu.VMEM((2 * bands, pixel_count, device_total * LANES), bf16),
            pltpu.VMEM(tile_pixels.shape[1:], bf16),
            pltpu.SemaphoreType.DMA((bands + 1,)),
        ],
        limit=32,
    )
    balanced = balanced.reshape(granules, bands, 32, 2, LANES).transpose(0, 1, 3, 2, 4)
    return (balanced.reshape(prior_grids.shape), corrected)


def solution(mesh):
    placed = (
        P("gran", "band", None, None),
        P("gran", "band", None, None),
        P("gran", "band", None, None),
        P("gran", "band", None),
        P("gran", None, "band", None),
        P("gran", None),
        P("gran"),
        P(),
        P(),
        P("gran", "band", None, None),
    )
    return jax.shard_map(
        per_device,
        mesh=mesh,
        in_specs=placed,
        out_specs=(P("gran", "band", None, None), P("gran", "band", None, None)),
        check_vma=False,
    )
```

```python
import functools
import jax
import jax.numpy as jnp
from jax import lax
from jax.experimental import pallas as pl
from jax.experimental.pallas import tpu as pltpu
from jax.sharding import PartitionSpec as P

BANDS = 12
KN = 64
PATCH = 8
REACH = 4
SWEEPS = 3
SP = 32
LANES = 128
SPAN = 16
FIRST = 3

robust_scale = 0.3

ON_CHIP = pl.BlockSpec(memory_space=pltpu.VMEM)
ANYWHERE = pl.BlockSpec(memory_space=pl.ANY)
f32 = jnp.float32
bf16 = jnp.bfloat16


def call(body, inputs, outputs, scratch=(), aliases=None, limit=16):
    operands = [
        pltpu.with_memory_space_constraint(array, pltpu.VMEM if kind == "v" else pltpu.HBM)
        for kind, array in inputs
    ]
    return pl.pallas_call(
        body,
        in_specs=[ON_CHIP if kind == "v" else ANYWHERE for kind, _ in inputs],
        out_specs=tuple(ON_CHIP if kind == "v" else ANYWHERE for kind, _, _ in outputs),
        out_shape=tuple(
            (pltpu.VMEM if kind == "v" else pltpu.HBM)(shape, dtype)
            for kind, shape, dtype in outputs
        ),
        scratch_shapes=list(scratch),
        input_output_aliases=aliases or {},
        compiler_params=pltpu.CompilerParams(vmem_limit_bytes=limit * 2**20),
    )(*operands)


def parity():
    return lax.rem(lax.axis_index("gran"), 2)


def first_edges(grids_ref, near_ref, far_ref, raw, sems):
    odd = parity()
    last = grids_ref.shape[0] - REACH
    sides = ((far_ref, odd * last), (near_ref, (1 - odd) * last))
    copies = [
        [pltpu.make_async_copy(grids_ref.at[base + g], raw.at[k, g], sems.at[k, g]) for g in range(REACH)]
        for k, (_, base) in enumerate(sides)
    ]
    for copy in copies[0] + copies[1]:
        copy.start()
    for k, (ref, _) in enumerate(sides):
        for g in range(REACH):
            copies[k][g].wait()
            for b in range(ref.shape[1]):
                for j in range(4):
                    both = [raw[k, g, b, pl.ds(2 * j + c, 8, stride=8), :] for c in range(2)]
                    ref[g, b, 16 * j : 16 * j + 16, :] = jnp.concatenate(both, axis=0).astype(bf16)


def arrange_grids(grids_ref, ext_ref, raw, sems):
    granules, bands = grids_ref.shape[:2]
    chunks = sems.shape[0]
    size = granules // chunks
    copies = []
    for n in range(chunks):
        part = pl.ds(n * size, size)
        copies.append(pltpu.make_async_copy(grids_ref.at[part], raw.at[part], sems.at[n]))
        copies[n].start()

    def step(i, carry):
        for b in range(bands):
            for q in range(8):
                ext_ref[i + REACH, b, 8 * q : 8 * q + 8, :] = raw[i, b, pl.ds(q, 8, stride=8), :]
        return carry

    for n in range(chunks):
        copies[n].wait()
        lax.fori_loop(n * size, (n + 1) * size, step, 0)


def visits(granules, interior):
    inner = list(range(REACH, granules - REACH))
    return inner if interior else [i for i in range(granules) if i not in inner]


def arrange(interior, offset_ref, count_ref, rhs_ref, diag_ref, cross_ref, coupling_ref, rhs_out, diag_out, cross_out, coupling_out, cross_raw, coupling_raw, wide, graph, sems):
    granules, bands = rhs_ref.shape[:2]
    own = visits(granules, interior)
    size = REACH
    chunks = len(own) // size
    copies = []
    for n in range(chunks):
        source, target = pl.ds(own[n * size], size), pl.ds(n * size, size)
        moves = ((coupling_ref, coupling_raw), (diag_ref, diag_out), (rhs_ref, rhs_out))
        copies.append(
            [
                pltpu.make_async_copy(here.at[source], there.at[target], sems.at[k, n])
                for k, (here, there) in enumerate(moves)
            ]
        )
        for copy in copies[n][:2]:
            copy.start()
        if n == 0:
            whole = pltpu.make_async_copy(cross_ref, cross_raw, sems.at[3, 0])
            whole.start()
    for n in range(chunks):
        copies[n][2].start()
    read_graph(offset_ref, count_ref, graph)
    for n in range(chunks):
        for copy in copies[n][:2]:
            copy.wait()
        if n == 0:
            whole.wait()

        def step(g, carry, n=n):
            at = n * size + g
            i = own[n * size] + g
            for b in range(bands):
                wide[b] = coupling_raw[at, b].astype(f32)
                for j in range(4):
                    d = [diag_out[at, b, pl.ds(2 * j + c, 8, stride=8), :] for c in range(2)]
                    pick = cross_raw[b, i // 8, pl.ds(8 * j + i % 8, 8, stride=32), :]
                    cross_out[at, b, 8 * j : 8 * j + 8, :] = pick * jnp.sqrt(d[0] * d[1])

            def slot(s, carry):
                for b in range(bands):
                    for j in range(4):
                        pick = wide[b, pl.ds(8 * j + s, 8, stride=32), :]
                        coupling_out[at, s, b, 8 * j : 8 * j + 8, :] = pick
                return carry

            return lax.fori_loop(0, graph[1, i], slot, carry)

        lax.fori_loop(0, size, step, 0)
    for n in range(chunks):
        copies[n][2].wait()


def lane_sums():
    row = lax.broadcasted_iota(jnp.int32, (LANES, LANES), 0)
    col = lax.broadcasted_iota(jnp.int32, (LANES, LANES), 1)
    return ((row % KN) // PATCH == col % PATCH).astype(f32).astype(bf16)


def lane_spread():
    row = lax.broadcasted_iota(jnp.int32, (LANES, LANES), 0)
    col = lax.broadcasted_iota(jnp.int32, (LANES, LANES), 1)
    return ((col % KN) // PATCH == row % PATCH).astype(f32).astype(bf16)


def read_graph(offset_ref, count_ref, graph):
    slots, granules = offset_ref.shape
    slot = lax.broadcasted_iota(jnp.int32, offset_ref.shape, 0)
    codes = jnp.sum(jnp.left_shift(offset_ref[...] + REACH, 4 * slot), axis=0, keepdims=True)
    counts = count_ref[...]
    for i in range(granules):
        graph[0, i] = codes[0, i]
        graph[1, i] = counts[0, i]


def neighbour(graph, i, s):
    return i + jnp.bitwise_and(jnp.right_shift(graph[0, i], 4 * s), 15)


def group_mask(interior, slots):
    row = lax.broadcasted_iota(jnp.int32, (64, LANES), 0) // 32
    lane = lax.broadcasted_iota(jnp.int32, (64, LANES), 1) // PATCH
    return lane - slots * (1 - row if interior else row)


def disparities(interior, offset_ref, count_ref, ext_ref, gathered, graph):
    bands = ext_ref.shape[1]
    granules = ext_ref.shape[0] - 2 * REACH
    slots = gathered.shape[0]
    gathered[...] = jnp.zeros_like(gathered)
    read_graph(offset_ref, count_ref, graph)

    def response(g):
        return [
            ext_ref[g, b, 16 * j : 16 * j + 8, :] + ext_ref[g, b, 16 * j + 8 : 16 * j + 16, :]
            for b in range(bands)
            for j in range(4)
        ]

    for i in range(granules):
        if (REACH <= i < granules - REACH) != interior:
            continue
        own = response(i + REACH)

        def slot(s, i=i, own=own):
            total = None
            for a, o in zip(own, response(neighbour(graph, i, s))):
                d = a - o
                total = d * d if total is None else total + d * d
            gathered[s, 8 * (i % 8) : 8 * (i % 8) + 8, :] = total

        for s in range(FIRST):
            slot(s)

        @pl.when(graph[1, i] > FIRST)
        def _(slot=slot):
            for s in range(FIRST, slots):
                slot(s)

    sums = jnp.dot(
        gathered[...].reshape(slots * 64, LANES).astype(bf16), lane_sums(), preferred_element_type=f32
    )
    place = group_mask(interior, slots)
    packed = jnp.zeros((64, LANES), f32)
    for s in range(slots):
        packed = jnp.where(place == s, sums[64 * s : 64 * s + 64], packed)
    return packed


def interior_disparities(offset_ref, count_ref, ext_ref, out_ref, send_ref, gathered, graph):
    packed = disparities(True, offset_ref, count_ref, ext_ref, gathered, graph)
    out_ref[...] = packed
    send_ref[...] = packed.astype(bf16)


def edge_disparities(offset_ref, count_ref, near_ref, far_ref, *refs):
    ext_ref, out_ref, send_ref, gathered, graph = refs[-5:]
    odd = parity()
    right = ext_ref.shape[0] - REACH
    for ref, base in ((near_ref, (1 - odd) * right), (far_ref, odd * right)):
        for g in range(REACH):
            for b in range(ref.shape[1]):
                ext_ref[base + g, b] = ref[g, b].astype(f32)
    packed = disparities(False, offset_ref, count_ref, ext_ref, gathered, graph)
    if len(refs) == 7:
        packed = packed + refs[1][...]
    out_ref[...] = packed
    send_ref[...] = packed.astype(bf16)


def spread_weights(shares, interior, weights):
    slots = weights.shape[0]
    total = shares[0][...]
    for share in shares[1:]:
        total = total + share[...].astype(f32)
    robust = 1.0 / (1.0 + total * (1.0 / (robust_scale * BANDS * PATCH * PATCH)))
    high = robust.astype(bf16).astype(f32)
    both = jnp.concatenate([high, robust - high], axis=1)
    place = group_mask(interior, slots)
    place = jnp.concatenate([place, place], axis=1)
    spread = lane_spread()
    spread = jnp.concatenate([spread, spread], axis=0)
    stacked = jnp.concatenate(
        [jnp.where(place == s, both, 0.0).astype(bf16) for s in range(slots)], axis=0
    )
    weights[...] = jnp.dot(stacked, spread, preferred_element_type=f32).reshape(slots, 64, LANES)


def balance(i, at, ext_ref, rhs_ref, diag_ref, cross_ref, coupling_ref, weights, graph, store):
    bands = rhs_ref.shape[1]
    row = pl.multiple_of(lax.rem(i, 8) * 8, 8)
    slots = weights.shape[0]
    parts = [(b, j) for b in range(bands) for j in range(4)]
    rhs = tuple(rhs_ref[at, b, pl.ds(2 * j + c, 8, stride=8), :] for b, j in parts for c in range(2))

    count = graph[1, i]

    def slot(slot_index, sums):
        sigma, drive = sums
        s = jnp.minimum(slot_index, count - 1)
        weight = jnp.where(slot_index < count, weights[s, pl.ds(row, 8), :], 0.0)
        n = neighbour(graph, i, s)
        new_sigma, new_drive = [], []
        for b in range(bands):
            for j in range(4):
                k = 4 * b + j
                effective = weight * coupling_ref[at, s, b, 8 * j : 8 * j + 8, :]
                new_sigma.append(sigma[k] + effective)
                for c in range(2):
                    grid = ext_ref[n, b, 16 * j + 8 * c : 16 * j + 8 * c + 8, :]
                    new_drive.append(drive[2 * k + c] + effective * grid)
        return tuple(new_sigma), tuple(new_drive)

    zero = jnp.zeros((8, LANES), f32)
    sums = ((zero,) * len(parts), rhs)
    for s in range(FIRST):
        sums = slot(s, sums)

    def others(_, sums):
        for s in range(FIRST, slots):
            sums = slot(s, sums)
        return sums

    sigma, drive = lax.fori_loop(0, (count > FIRST).astype(jnp.int32), others, sums)
    for k, (b, j) in enumerate(parts):
        first, second = (
            diag_ref[at, b, pl.ds(2 * j + c, 8, stride=8), :] + sigma[k] for c in range(2)
        )
        cross = cross_ref[at, b, 8 * j : 8 * j + 8, :]
        inverse = 1.0 / (first * second - cross * cross)
        gain, offset = drive[2 * k], drive[2 * k + 1]
        store(
            b,
            j,
            (second * gain - cross * offset) * inverse,
            (first * offset - cross * gain) * inverse,
        )


def edge_sweep(offset_ref, count_ref, *refs):
    shares, state, (new_ref, near_ref, far_ref, weights, graph) = refs[:4], refs[4:9], refs[9:]
    read_graph(offset_ref, count_ref, graph)
    spread_weights(shares, False, weights)
    odd = parity()
    last = new_ref.shape[0] - 3 * REACH
    for ref, base in ((far_ref, odd * last), (near_ref, (1 - odd) * last)):

        def step(g, carry, ref=ref, base=base):
            def store(b, j, gain, offset):
                both = jnp.concatenate([gain, offset], axis=0)
                new_ref[base + g + REACH, b, 16 * j : 16 * j + 16, :] = both
                ref[g, b, 16 * j : 16 * j + 16, :] = both.astype(bf16)

            balance(base + g, lax.div(base, 2 * REACH) * REACH + g, *state, weights, graph, store)
            return carry

        lax.fori_loop(0, REACH, step, 0)


def interior_sweep(offset_ref, count_ref, *refs):
    shares, state, (_, new_ref, weights, graph) = refs[:4], refs[4:9], refs[9:]
    read_graph(offset_ref, count_ref, graph)
    spread_weights(shares, True, weights)

    def step(i, carry):
        def store(b, j, gain, offset):
            both = jnp.concatenate([gain, offset], axis=0)
            new_ref[i + REACH, b, 16 * j : 16 * j + 16, :] = both

        balance(i, i - REACH, *state, weights, graph, store)
        return carry

    lax.fori_loop(REACH, new_ref.shape[0] - 3 * REACH, step, 0)


def own_columns(ref, at, granules):
    first = lax.axis_index("gran") * granules
    base = pl.multiple_of((first // LANES) * LANES, LANES)
    turn = jnp.bitwise_and(LANES - lax.rem(first, LANES), LANES - 1)
    return pltpu.roll(ref[at + (pl.ds(base, LANES),)], turn, 1)


def last_sweep(interior, offset_ref, count_ref, *refs):
    shares, state, place_ref = refs[:4], refs[4:9], refs[9]
    weights, graph = refs[-2:]
    if interior:
        solved, windows = refs[10:12]
    else:
        solved, send_ref, windows = refs[12:15]
    granules, bands = solved.shape[:2]
    read_graph(offset_ref, count_ref, graph)
    if interior:
        windows[...] = jnp.zeros_like(windows)
    spread_weights(shares, interior, weights)

    def step(t, carry):
        i = t if interior else jnp.where(t < REACH, t, t + granules - 2 * REACH)

        def store(b, j, gain, offset):
            solved[i, b, pl.ds(2 * j, 8, stride=8), :] = gain
            solved[i, b, pl.ds(2 * j + 1, 8, stride=8), :] = offset

        balance(i, t - REACH if interior else t, *state, weights, graph, store)
        return carry

    lax.fori_loop(*((REACH, granules - REACH) if interior else (0, 2 * REACH)), step, 0)
    lane = lax.broadcasted_iota(jnp.int32, (8, LANES), 1) // SPAN
    seats = LANES // SPAN
    places = place_ref[...]
    for i in visits(granules, interior):
        for r in range(2):
            owner, rank, top, turn = (places[k, r * granules + i] for k in range(4))
            here = [lane == jnp.bitwise_and(rank + half * (KN // SPAN), seats - 1) for half in (0, 1)]
            for b in range(bands):
                for c in range(2):
                    rows = solved[i, b, pl.ds(2 * top + c, 8, stride=2), :]
                    moved = pltpu.roll(rows, jnp.bitwise_and(turn, LANES - 1), 1)
                    for half in (0, 1):
                        at = 16 * (2 * b + c) + 8 * half
                        pltpu.store(windows.at[owner, at : at + 8, :], moved, mask=here[half])
    if not interior:
        for owner in range(windows.shape[0]):
            for at in range(0, windows.shape[1], 16):
                odd = pltpu.roll(windows[owner, at + 8 : at + 16, :], KN, 1)
                both = jnp.concatenate([windows[owner, at : at + 8, :], odd], axis=0)
                send_ref[owner, at : at + 16, :] = both.astype(bf16)


def earlier(first, second, granules):
    def edge(i):
        return ((i < REACH) | (i >= granules - REACH)).astype(jnp.int32)

    def rank(entry):
        return (edge(entry[1]) * 2 + entry[0]) * granules + entry[1]

    return rank(first) < rank(second)


def spread_columns(row):
    return jnp.transpose(jnp.broadcast_to(row, (LANES, LANES)))


def tile_places(route_ref, window_ref, rows_out, cols_out, place_ref):
    pixels, lanes = rows_out.shape
    senders = lanes // LANES
    granules = route_ref.shape[1] // senders
    own = lax.axis_index("gran")
    lane_row = lax.broadcasted_iota(jnp.int32, (1, LANES), 1)

    def both_routes(rows):
        return jnp.where(lane_row < granules, rows[0:1], pltpu.roll(rows, granules, 1)[1:2])

    routes = own_columns(route_ref, (slice(None),), granules)
    starts = [own_columns(window_ref, (r, slice(None)), granules) for r in range(2)]
    named = both_routes(routes).astype(f32)
    col = lax.broadcasted_iota(jnp.int32, (LANES, LANES), 1)
    row = lax.broadcasted_iota(jnp.int32, (LANES, LANES), 0)
    before = earlier((row // granules, row % granules), (col // granules, col % granules), granules)
    before = before & (row < 2 * granules) & (spread_columns(named) == named)
    rank = jnp.sum(before.astype(f32), axis=0, keepdims=True).astype(jnp.int32)
    knots = [
        jnp.clip(jnp.right_shift(both_routes(jnp.concatenate([s[k : k + 1] for s in starts])), 5) - 1, 0, KN - SPAN)
        for k in range(2)
    ]
    turn = rank * SPAN - knots[1] + LANES
    place_ref[...] = jnp.concatenate(
        [named.astype(jnp.int32), rank, jnp.right_shift(knots[0], 1), turn] * 2, axis=0
    )

    wide = 2 * LANES
    col = lax.broadcasted_iota(jnp.int32, (wide, wide), 1)
    row = lax.broadcasted_iota(jnp.int32, (wide, wide), 0)
    route = [at // LANES for at in (row, col)]
    place = [at % LANES for at in (row, col)]
    before = earlier((route[0], place[0] % granules), (route[1], place[1] % granules), granules)
    before = before & (place[0] // granules == place[1] // granules)
    before = before.astype(f32).astype(bf16)
    seat = (lax.broadcasted_iota(jnp.int32, (LANES, LANES), 1) // SPAN).astype(f32)
    lane = lax.broadcasted_iota(jnp.int32, (8, LANES), 1)
    step = lane % SPAN
    pixel = lax.broadcasted_iota(jnp.int32, (8, LANES), 0).astype(f32) * (1.0 / SP)
    part = LANES // granules
    for t in range(route_ref.shape[1] // LANES):
        at = slice(t * LANES, (t + 1) * LANES)
        hits = [(route_ref[r : r + 1, at] == own).astype(f32) for r in range(2)]
        hits = jnp.broadcast_to(jnp.concatenate(hits, axis=1), (8, wide))
        ranks = jnp.dot(hits.astype(bf16), before, preferred_element_type=f32)
        ranks = jnp.where(hits > 0.5, ranks, -1.0)
        chosen, values = [], []
        for r in range(2):
            chosen.append((spread_columns(ranks[0:1, r * LANES : (r + 1) * LANES]) == seat).astype(f32).astype(bf16))
            sender = lax.broadcasted_iota(jnp.int32, (part, LANES), 0)
            within = lax.broadcasted_iota(jnp.int32, (part, LANES), 1) // granules == sender
            kinds = []
            for k in range(2):
                start = window_ref[r, k : k + 1, at]
                kinds += [jnp.right_shift(start, 5), jnp.bitwise_and(start, SP - 1)]
            kinds.append(jnp.ones((1, LANES), jnp.int32))
            values.append(jnp.concatenate([jnp.where(within, kind, 0).astype(f32) for kind in kinds], axis=0))
        found = jnp.dot(
            jnp.concatenate(values, axis=1).astype(bf16),
            jnp.concatenate(chosen, axis=0),
            preferred_element_type=f32,
        )
        for n in range(part):
            live = found[4 * part + n : 4 * part + n + 1] > 0.5
            for k, ref in ((0, rows_out), (1, cols_out)):
                base = found[2 * k * part + n : 2 * k * part + n + 1]
                rest = found[(2 * k + 1) * part + n : (2 * k + 1) * part + n + 1]
                first = jnp.clip(base.astype(jnp.int32) - 1, 0, KN - SPAN)
                if k == 0:
                    knot = 2 * jnp.right_shift(first, 1) + 2 * (step % 8) + step // 8
                else:
                    knot = first + step
                border = (knot == 0) | (knot == KN - 1)
                cube = jnp.where(border, 1.0, 1.5)
                square = jnp.where(border, -1.5, -2.5)
                single = jnp.where(border, -0.5, 0.0)
                away = jnp.where(live, base + rest * (1.0 / SP) - knot.astype(f32), 4.0 * KN)
                away = away + pixel
                to = pl.ds((t * part + n) * LANES, LANES)
                for q in range(0, pixels, 16):
                    pair = []
                    for p in (q, q + 8):
                        d = jnp.abs(away + p * (1.0 / SP))
                        near = ((cube * d + square) * d + single) * d + 1.0
                        far = ((2.5 - 0.5 * d) * d - 4.0) * d + 2.0
                        pair.append(jnp.where(d <= 1.0, near, jnp.where(d < 2.0, far, 0.0)))
                    ref[q : q + 16, to] = jnp.concatenate(pair, axis=0).astype(bf16)


def compose(route_ref, received_ref, row_ref, col_ref, pixels_ref, solved, out_ref, grids_out, passed, result, sems):
    copies = [pltpu.make_async_copy(solved, grids_out, sems.at[result.shape[0]])]
    copies[0].start()
    senders = received_ref.shape[0]
    bands = result.shape[0]
    lane = lax.broadcasted_iota(jnp.int32, (16, LANES), 1) // SPAN
    masks = [(lane == r).astype(f32).astype(bf16) for r in range(LANES // SPAN)]
    named = (route_ref[...] == lax.axis_index("gran")).astype(f32)
    scale = 1.0 / jnp.sum(named, keepdims=True)

    def sender(n, carry):
        at = pl.ds(pl.multiple_of(n * LANES, LANES), LANES)
        blocks = []
        for k in range(2 * bands):
            window = received_ref[n, 16 * k : 16 * k + 16, :]
            blocks.append(jnp.concatenate([window * mask for mask in masks], axis=0))
        rows = jnp.dot(row_ref[:, at], jnp.concatenate(blocks, axis=1), preferred_element_type=f32)
        for k in range(2 * bands):
            passed[k, :, at] = rows[:, LANES * k : LANES * k + LANES].astype(bf16)
        return carry

    steps = min(8, senders)

    def several(n, carry):
        for k in range(steps):
            sender(n * steps + k, carry)
        return carry

    if senders == steps:
        several(0, 0)
    else:
        lax.fori_loop(0, senders // steps, several, 0)
    for b in range(bands):
        fields = [
            lax.dot_general(
                passed[2 * b + c], col_ref[...], (((1,), (1,)), ((), ())), preferred_element_type=f32
            )
            * scale
            for c in range(2)
        ]
        pixels = pixels_ref[0, b].astype(f32)
        result[b] = (pixels * (1.0 + fields[0]) + fields[1]).astype(bf16)
        copies.append(pltpu.make_async_copy(result.at[b], out_ref.at[0, b], sems.at[b]))
        copies[-1].start()
    for copy in copies:
        copy.wait()


def per_device(
    prior_grids,
    pif_rhs,
    pif_diagonal,
    pif_cross,
    pif_coupling,
    neighbour_offset,
    neighbour_count,
    tile_route,
    tile_window,
    tile_pixels,
):
    granules, bands = prior_grids.shape[:2]
    slots = pif_coupling.shape[1]
    pixel_count = tile_pixels.shape[2]
    device_total = lax.axis_size("gran")
    band_total = lax.axis_size("band")

    def by_lane_tile(array):
        cut = array.reshape(array.shape[:2] + (array.shape[2], 32, LANES)).transpose(0, 1, 3, 2, 4)
        return cut.reshape(array.shape[:2] + (32 * array.shape[2], LANES))

    grids = by_lane_tile(prior_grids)
    rhs = by_lane_tile(pif_rhs)
    diagonal = by_lane_tile(pif_diagonal)
    cross = by_lane_tile(pif_cross.transpose(1, 0, 2).reshape(bands, granules // 8, 8, KN * KN))
    coupling = by_lane_tile(pif_coupling.transpose(0, 2, 1, 3))
    graph = [("v", neighbour_offset.T), ("v", neighbour_count[None, :])]
    tiles = [("v", tile_route.T), ("v", tile_window.transpose(1, 2, 0))]
    edge = (REACH, bands, 64, LANES)
    own = (granules, bands, 64, LANES)
    ext = (granules + 2 * REACH, bands, 64, LANES)
    packed = [("v", (64, LANES), f32), ("v", (64, LANES), bf16)]
    chunks = 4

    near_pairs = [(i, i ^ 1) for i in range(device_total)]
    far_pairs = [
        pair for i in range(1, device_total - 1, 2) for pair in ((i, i + 1), (i + 1, i))
    ]

    def exchange(near, far):
        far = lax.ppermute(far, "gran", far_pairs)
        near = lax.ppermute(near, "gran", near_pairs)
        return near, far

    near, far = call(
        first_edges,
        [("h", grids)],
        [("v", edge, bf16), ("v", edge, bf16)],
        [pltpu.VMEM((2,) + edge, f32), pltpu.SemaphoreType.DMA((2, REACH))],
    )
    near, far = exchange(near, far)
    (extended,) = call(
        arrange_grids,
        [("h", grids)],
        [("v", ext, f32)],
        [pltpu.VMEM(own, f32), pltpu.SemaphoreType.DMA((chunks,))],
    )
    sources = [rhs, diagonal, cross, coupling]

    def arranged(interior, sources):
        part = len(visits(granules, interior))
        some = (part, bands, 64, LANES)
        return call(
            functools.partial(arrange, interior),
            graph + [("h", source) for source in sources],
            [
                ("v", some, f32),
                ("v", some, f32),
                ("v", (part, bands, 32, LANES), f32),
                ("v", (part, slots, bands, 32, LANES), f32),
            ],
            [
                pltpu.VMEM(cross.shape, f32),
                pltpu.VMEM((part,) + coupling.shape[1:], bf16),
                pltpu.VMEM(coupling.shape[1:], f32),
                pltpu.SMEM((2, granules), jnp.int32),
                pltpu.SemaphoreType.DMA((4, chunks)),
            ],
        )

    gathered = pltpu.VMEM((slots, 64, LANES), f32)
    weights = pltpu.VMEM((slots, 64, LANES), f32)
    scalars = pltpu.SMEM((2, granules), jnp.int32)

    def over_band(partial, rounded):
        return [("v", partial)] + [
            ("v", lax.ppermute(rounded, "band", [(i, i ^ flip) for i in range(band_total)]))
            for flip in range(1, band_total)
        ]

    for sweep in range(SWEEPS):
        last = sweep == SWEEPS - 1
        inner, inner_rounded = call(
            interior_disparities, graph + [("v", extended)], packed, [gathered, scalars]
        )
        if sweep == 0:
            inner, *edge_state = lax.optimization_barrier((inner, *arranged(False, sources)))
        if last:
            inner_shares = over_band(inner, inner_rounded)
        inputs = graph + [("v", near), ("v", far), ("v", extended)]
        inputs += [] if last else [("v", inner)]
        extended, partial, rounded = call(
            edge_disparities,
            inputs,
            [("v", ext, f32)] + packed,
            [gathered, scalars],
            aliases={4: 0},
        )
        shares = over_band(partial, rounded)
        if sweep == 1:
            routes, starts, _ = lax.optimization_barrier((tiles[0][1], tiles[1][1], partial))
            weight_shape = ("v", (pixel_count, device_total * LANES), bf16)
            made = call(
                tile_places,
                [("v", routes), ("v", starts)],
                [weight_shape, weight_shape, ("v", (8, LANES), jnp.int32)],
            )
            partial, row_weights, col_weights, places = lax.optimization_barrier((partial, *made))
            shares[0] = ("v", partial)
        edge_state_now = [("v", extended)] + [("v", array) for array in edge_state]
        if not last:
            inputs = graph + shares + edge_state_now
            updated, near, far = call(
                edge_sweep,
                inputs,
                [("v", ext, f32), ("v", edge, bf16), ("v", edge, bf16)],
                [weights, scalars],
            )
            near, far = exchange(near, far)
            if sweep == 0:
                *later, updated = lax.optimization_barrier((*sources, updated))
                inner_state = [("v", array) for array in arranged(True, later)]
            inputs = graph + shares + [("v", extended)] + inner_state
            (extended,) = call(
                interior_sweep,
                inputs + [("v", updated)],
                [("v", ext, f32)],
                [weights, scalars],
                aliases={len(inputs): 0},
            )
    windows = (device_total, 2 * bands * SPAN, LANES)
    scratch = [weights, scalars]
    inputs = graph + inner_shares + [("v", extended)] + inner_state + [("v", places)]
    balanced, gathered_windows = call(
        functools.partial(last_sweep, True),
        inputs,
        [("v", own, f32), ("v", windows, f32)],
        scratch,
    )
    inputs = graph + shares + edge_state_now + [("v", places)] + [("v", balanced), ("v", gathered_windows)]
    balanced, payload, _ = call(
        functools.partial(last_sweep, False),
        inputs,
        [("v", own, f32), ("v", windows, bf16), ("v", windows, f32)],
        scratch,
        aliases={len(inputs) - 2: 0, len(inputs) - 1: 2},
    )
    received = lax.all_to_all(payload, "gran", split_axis=0, concat_axis=0, tiled=True)
    inputs = [tiles[0], ("v", received), ("v", row_weights), ("v", col_weights), ("v", tile_pixels)]
    corrected, balanced = call(
        compose,
        inputs + [("v", balanced)],
        [("h", tile_pixels.shape, bf16), ("h", own, f32)],
        [
            pltpu.VMEM((2 * bands, pixel_count, device_total * LANES), bf16),
            pltpu.VMEM(tile_pixels.shape[1:], bf16),
            pltpu.SemaphoreType.DMA((bands + 1,)),
        ],
        limit=32,
    )
    balanced = balanced.reshape(granules, bands, 32, 2, LANES).transpose(0, 1, 3, 2, 4)
    return (balanced.reshape(prior_grids.shape), corrected)


def solution(mesh):
    placed = (
        P("gran", "band", None, None),
        P("gran", "band", None, None),
        P("gran", "band", None, None),
        P("gran", "band", None),
        P("gran", None, "band", None),
        P("gran", None),
        P("gran"),
        P(),
        P(),
        P("gran", "band", None, None),
    )
    return jax.shard_map(
        per_device,
        mesh=mesh,
        in_specs=placed,
        out_specs=(P("gran", "band", None, None), P("gran", "band", None, None)),
        check_vma=False,
    )
```

```python
import functools
import jax
import jax.numpy as jnp
from jax import lax
from jax.experimental import pallas as pl
from jax.experimental.pallas import tpu as pltpu
from jax.sharding import PartitionSpec as P

BANDS = 12
KN = 64
PATCH = 8
REACH = 4
SWEEPS = 3
SP = 32
LANES = 128
SPAN = 16
FIRST = 3

robust_scale = 0.3

ON_CHIP = pl.BlockSpec(memory_space=pltpu.VMEM)
ANYWHERE = pl.BlockSpec(memory_space=pl.ANY)
f32 = jnp.float32
bf16 = jnp.bfloat16


def call(body, inputs, outputs, scratch=(), aliases=None, limit=16):
    operands = [
        pltpu.with_memory_space_constraint(array, pltpu.VMEM if kind == "v" else pltpu.HBM)
        for kind, array in inputs
    ]
    return pl.pallas_call(
        body,
        in_specs=[ON_CHIP if kind == "v" else ANYWHERE for kind, _ in inputs],
        out_specs=tuple(ON_CHIP if kind == "v" else ANYWHERE for kind, _, _ in outputs),
        out_shape=tuple(
            (pltpu.VMEM if kind == "v" else pltpu.HBM)(shape, dtype)
            for kind, shape, dtype in outputs
        ),
        scratch_shapes=list(scratch),
        input_output_aliases=aliases or {},
        compiler_params=pltpu.CompilerParams(vmem_limit_bytes=limit * 2**20),
    )(*operands)


def parity():
    return lax.rem(lax.axis_index("gran"), 2)


def first_edges(grids_ref, near_ref, far_ref, raw, sems):
    odd = parity()
    last = grids_ref.shape[0] - REACH
    sides = ((far_ref, odd * last), (near_ref, (1 - odd) * last))
    copies = [
        [pltpu.make_async_copy(grids_ref.at[base + g], raw.at[k, g], sems.at[k, g]) for g in range(REACH)]
        for k, (_, base) in enumerate(sides)
    ]
    for copy in copies[0] + copies[1]:
        copy.start()
    for k, (ref, _) in enumerate(sides):
        for g in range(REACH):
            copies[k][g].wait()
            for b in range(ref.shape[1]):
                for j in range(4):
                    both = [raw[k, g, b, pl.ds(2 * j + c, 8, stride=8), :] for c in range(2)]
                    ref[g, b, 16 * j : 16 * j + 16, :] = jnp.concatenate(both, axis=0).astype(bf16)


def arrange_grids(grids_ref, ext_ref, raw, sems):
    granules, bands = grids_ref.shape[:2]
    chunks = sems.shape[0]
    size = granules // chunks
    copies = []
    for n in range(chunks):
        part = pl.ds(n * size, size)
        copies.append(pltpu.make_async_copy(grids_ref.at[part], raw.at[part], sems.at[n]))
        copies[n].start()

    def step(i, carry):
        for b in range(bands):
            for q in range(8):
                ext_ref[i + REACH, b, 8 * q : 8 * q + 8, :] = raw[i, b, pl.ds(q, 8, stride=8), :]
        return carry

    for n in range(chunks):
        copies[n].wait()
        lax.fori_loop(n * size, (n + 1) * size, step, 0)


def visits(granules, interior):
    inner = list(range(REACH, granules - REACH))
    return inner if interior else [i for i in range(granules) if i not in inner]


def arrange(interior, count_ref, rhs_ref, diag_ref, cross_ref, coupling_ref, rhs_out, diag_out, cross_out, coupling_out, rhs_raw, diag_raw, cross_raw, coupling_raw, wide, graph, sems):
    granules, bands = rhs_ref.shape[:2]
    own = visits(granules, interior)
    size = REACH
    chunks = len(own) // size
    copies = []
    for n in range(chunks):
        source, target = pl.ds(own[n * size], size), pl.ds(n * size, size)
        moves = ((coupling_ref, coupling_raw), (diag_ref, diag_raw), (rhs_ref, rhs_raw))
        copies.append(
            [
                pltpu.make_async_copy(here.at[source], there.at[target], sems.at[k, n])
                for k, (here, there) in enumerate(moves)
            ]
        )
        for copy in copies[n]:
            copy.start()
        if n == 0:
            whole = pltpu.make_async_copy(cross_ref, cross_raw, sems.at[3, 0])
            whole.start()
    for i, count in enumerate(visits(granules, interior)):
        graph[i] = count_ref[...][0, count]
    for n in range(chunks):
        for copy in copies[n]:
            copy.wait()
        if n == 0:
            whole.wait()

        def step(g, carry, n=n):
            at = n * size + g
            i = own[n * size] + g
            for b in range(bands):
                wide[b] = coupling_raw[at, b].astype(f32)
                for j in range(4):
                    d = []
                    for c in range(2):
                        rows = pl.ds(2 * j + c, 8, stride=8)
                        to = slice(16 * j + 8 * c, 16 * j + 8 * c + 8)
                        rhs_out[at, b, to, :] = rhs_raw[at, b, rows, :]
                        d.append(diag_raw[at, b, rows, :])
                        diag_out[at, b, to, :] = d[c]
                    pick = cross_raw[b, i // 8, pl.ds(8 * j + i % 8, 8, stride=32), :]
                    cross_out[at, b, 8 * j : 8 * j + 8, :] = pick * jnp.sqrt(d[0] * d[1])

            def slot(s, carry):
                for b in range(bands):
                    for j in range(4):
                        pick = wide[b, pl.ds(8 * j + s, 8, stride=32), :]
                        coupling_out[at, s, b, 8 * j : 8 * j + 8, :] = pick
                return carry

            return lax.fori_loop(0, graph[at], slot, carry)

        lax.fori_loop(0, size, step, 0)


def lane_sums():
    row = lax.broadcasted_iota(jnp.int32, (LANES, LANES), 0)
    col = lax.broadcasted_iota(jnp.int32, (LANES, LANES), 1)
    return ((row % KN) // PATCH == col % PATCH).astype(f32).astype(bf16)


def lane_spread():
    row = lax.broadcasted_iota(jnp.int32, (LANES, LANES), 0)
    col = lax.broadcasted_iota(jnp.int32, (LANES, LANES), 1)
    return ((col % KN) // PATCH == row % PATCH).astype(f32).astype(bf16)


def graph_codes(offset_ref):
    slot = lax.broadcasted_iota(jnp.int32, offset_ref.shape, 0)
    return jnp.sum(jnp.left_shift(offset_ref[...] + REACH, 4 * slot), axis=0, keepdims=True)


def read_graph(offset_ref, graph):
    codes = graph_codes(offset_ref)
    for i in range(offset_ref.shape[1]):
        graph[i] = codes[0, i]


def step_to(code, s):
    return jnp.bitwise_and(jnp.right_shift(code, 4 * s), 15)


def group_mask(interior, slots):
    row = lax.broadcasted_iota(jnp.int32, (64, LANES), 0) // 32
    lane = lax.broadcasted_iota(jnp.int32, (64, LANES), 1) // PATCH
    return lane - slots * (1 - row if interior else row)


def disparities(interior, offset_ref, ext_ref, gathered):
    bands = ext_ref.shape[1]
    granules = ext_ref.shape[0] - 2 * REACH
    slots = gathered.shape[0]
    gathered[...] = jnp.zeros_like(gathered)
    codes = graph_codes(offset_ref)

    def response(g):
        return [
            ext_ref[g, b, 16 * j : 16 * j + 8, :] + ext_ref[g, b, 16 * j + 8 : 16 * j + 16, :]
            for b in range(bands)
            for j in range(4)
        ]

    for i in range(granules):
        if (REACH <= i < granules - REACH) != interior:
            continue
        own = response(i + REACH)
        code = codes[0, i]

        def slot(s, i=i, own=own, code=code):
            total = None
            for a, o in zip(own, response(i + step_to(code, s))):
                d = a - o
                total = d * d if total is None else total + d * d
            gathered[s, 8 * (i % 8) : 8 * (i % 8) + 8, :] = total

        for s in range(FIRST):
            slot(s)

        @pl.when(step_to(code, FIRST) != REACH)
        def _(slot=slot):
            for s in range(FIRST, slots):
                slot(s)

    sums = jnp.dot(
        gathered[...].reshape(slots * 64, LANES).astype(bf16), lane_sums(), preferred_element_type=f32
    )
    place = group_mask(interior, slots)
    packed = jnp.zeros((64, LANES), f32)
    for s in range(slots):
        packed = jnp.where(place == s, sums[64 * s : 64 * s + 64], packed)
    return packed


def interior_disparities(offset_ref, ext_ref, out_ref, *refs):
    packed = disparities(True, offset_ref, ext_ref, refs[-1])
    out_ref[...] = packed
    if len(refs) == 2:
        refs[0][...] = packed.astype(bf16)


def edge_disparities(offset_ref, near_ref, far_ref, *refs):
    ext_ref, out_ref, send_ref, gathered = refs[-4:]
    odd = parity()
    right = ext_ref.shape[0] - REACH
    for ref, base in ((near_ref, (1 - odd) * right), (far_ref, odd * right)):
        for g in range(REACH):
            for b in range(ref.shape[1]):
                ext_ref[base + g, b] = ref[g, b].astype(f32)
    packed = disparities(False, offset_ref, ext_ref, gathered)
    if len(refs) == 6:
        packed = packed + refs[1][...]
    out_ref[...] = packed
    send_ref[...] = packed.astype(bf16)


def spread_weights(shares, interior, weights):
    slots = weights.shape[0]
    total = shares[0][...]
    for share in shares[1:]:
        total = total + share[...].astype(f32)
    robust = 1.0 / (1.0 + total * (1.0 / (robust_scale * BANDS * PATCH * PATCH)))
    high = robust.astype(bf16).astype(f32)
    both = jnp.concatenate([high, robust - high], axis=1)
    place = group_mask(interior, slots)
    place = jnp.concatenate([place, place], axis=1)
    spread = lane_spread()
    spread = jnp.concatenate([spread, spread], axis=0)
    stacked = jnp.concatenate(
        [jnp.where(place == s, both, 0.0).astype(bf16) for s in range(slots)], axis=0
    )
    weights[...] = jnp.dot(stacked, spread, preferred_element_type=f32).reshape(slots, 64, LANES)


def balance(i, at, ext_ref, rhs_ref, diag_ref, cross_ref, coupling_ref, weights, graph, store):
    bands = rhs_ref.shape[1]
    row = pl.multiple_of(lax.rem(i, 8) * 8, 8)
    slots = weights.shape[0]
    parts = [(b, j) for b in range(bands) for j in range(4)]
    rows = [slice(8 * q, 8 * q + 8) for q in range(8)]
    rhs = tuple(rhs_ref[at, b, rows[2 * j + c], :] for b, j in parts for c in range(2))

    code = graph[i]

    def slot(slot_index, sums):
        sigma, drive = sums
        used = step_to(code, slot_index) != REACH
        s = jnp.where(used, slot_index, 0)
        weight = jnp.where(used, weights[s, pl.ds(row, 8), :], 0.0)
        n = i + step_to(code, s)
        new_sigma, new_drive = [], []
        for b in range(bands):
            for j in range(4):
                k = 4 * b + j
                effective = weight * coupling_ref[at, s, b, 8 * j : 8 * j + 8, :]
                new_sigma.append(sigma[k] + effective)
                for c in range(2):
                    grid = ext_ref[n, b, 16 * j + 8 * c : 16 * j + 8 * c + 8, :]
                    new_drive.append(drive[2 * k + c] + effective * grid)
        return tuple(new_sigma), tuple(new_drive)

    zero = jnp.zeros((8, LANES), f32)
    sums = ((zero,) * len(parts), rhs)
    for s in range(FIRST):
        sums = slot(s, sums)

    def others(_, sums):
        for s in range(FIRST, slots):
            sums = slot(s, sums)
        return sums

    sigma, drive = lax.fori_loop(0, (step_to(code, FIRST) != REACH).astype(jnp.int32), others, sums)
    for k, (b, j) in enumerate(parts):
        first, second = (
            diag_ref[at, b, rows[2 * j + c], :] + sigma[k] for c in range(2)
        )
        cross = cross_ref[at, b, 8 * j : 8 * j + 8, :]
        inverse = 1.0 / (first * second - cross * cross)
        gain, offset = drive[2 * k], drive[2 * k + 1]
        store(
            b,
            j,
            (second * gain - cross * offset) * inverse,
            (first * offset - cross * gain) * inverse,
        )


def edge_sweep(offset_ref, *refs):
    shares, state, (new_ref, near_ref, far_ref, weights, graph) = refs[:4], refs[4:9], refs[9:]
    read_graph(offset_ref, graph)
    spread_weights(shares, False, weights)
    odd = parity()
    last = new_ref.shape[0] - 3 * REACH
    for ref, base in ((far_ref, odd * last), (near_ref, (1 - odd) * last)):

        def step(g, carry, ref=ref, base=base):
            def store(b, j, gain, offset):
                both = jnp.concatenate([gain, offset], axis=0)
                new_ref[base + g + REACH, b, 16 * j : 16 * j + 16, :] = both
                ref[g, b, 16 * j : 16 * j + 16, :] = both.astype(bf16)

            balance(base + g, lax.div(base, 2 * REACH) * REACH + g, *state, weights, graph, store)
            return carry

        lax.fori_loop(0, REACH, step, 0)


def interior_sweep(offset_ref, *refs):
    shares, state, (_, new_ref, weights, graph) = refs[:4], refs[4:9], refs[9:]
    read_graph(offset_ref, graph)
    spread_weights(shares, True, weights)

    def step(i, carry):
        def store(b, j, gain, offset):
            both = jnp.concatenate([gain, offset], axis=0)
            new_ref[i + REACH, b, 16 * j : 16 * j + 16, :] = both

        balance(i, i - REACH, *state, weights, graph, store)
        return carry

    lax.fori_loop(REACH, new_ref.shape[0] - 3 * REACH, step, 0)


def own_columns(ref, at, granules):
    first = lax.axis_index("gran") * granules
    base = pl.multiple_of((first // LANES) * LANES, LANES)
    turn = jnp.bitwise_and(LANES - lax.rem(first, LANES), LANES - 1)
    return pltpu.roll(ref[at + (pl.ds(base, LANES),)], turn, 1)


def last_sweep(interior, offset_ref, *refs):
    shares, state, place_ref = refs[:4], refs[4:9], refs[9]
    weights, graph = refs[-2:]
    if interior:
        solved, windows = refs[10:12]
    else:
        solved, send_ref, windows = refs[12:15]
    granules, bands = solved.shape[:2]
    read_graph(offset_ref, graph)
    if interior:
        windows[...] = jnp.zeros_like(windows)
    spread_weights(shares, interior, weights)

    def step(t, carry):
        i = t if interior else jnp.where(t < REACH, t, t + granules - 2 * REACH)

        def store(b, j, gain, offset):
            solved[i, b, pl.ds(2 * j, 8, stride=8), :] = gain
            solved[i, b, pl.ds(2 * j + 1, 8, stride=8), :] = offset

        balance(i, t - REACH if interior else t, *state, weights, graph, store)
        return carry

    lax.fori_loop(*((REACH, granules - REACH) if interior else (0, 2 * REACH)), step, 0)
    lane = lax.broadcasted_iota(jnp.int32, (8, LANES), 1) // SPAN
    seats = LANES // SPAN
    places = place_ref[...]
    for i in visits(granules, interior):
        for r in range(2):
            owner, rank, top, turn = (places[k, r * granules + i] for k in range(4))
            here = [lane == jnp.bitwise_and(rank + half * (KN // SPAN), seats - 1) for half in (0, 1)]
            for b in range(bands):
                for c in range(2):
                    rows = solved[i, b, pl.ds(2 * top + c, 8, stride=2), :]
                    moved = pltpu.roll(rows, jnp.bitwise_and(turn, LANES - 1), 1)
                    for half in (0, 1):
                        at = 16 * (2 * b + c) + 8 * half
                        pltpu.store(windows.at[owner, at : at + 8, :], moved, mask=here[half])
    if not interior:
        for owner in range(windows.shape[0]):
            for at in range(0, windows.shape[1], 16):
                odd = pltpu.roll(windows[owner, at + 8 : at + 16, :], KN, 1)
                both = jnp.concatenate([windows[owner, at : at + 8, :], odd], axis=0)
                send_ref[owner, at : at + 16, :] = both.astype(bf16)


def earlier(first, second, granules):
    def edge(i):
        return ((i < REACH) | (i >= granules - REACH)).astype(jnp.int32)

    def rank(entry):
        return (edge(entry[1]) * 2 + entry[0]) * granules + entry[1]

    return rank(first) < rank(second)


def spread_columns(row):
    return jnp.transpose(jnp.broadcast_to(row, (LANES, LANES)))


def tile_places(route_ref, window_ref, rows_out, cols_out, place_ref):
    pixels, lanes = rows_out.shape
    senders = lanes // LANES
    granules = route_ref.shape[1] // senders
    own = lax.axis_index("gran")
    lane_row = lax.broadcasted_iota(jnp.int32, (1, LANES), 1)

    def both_routes(rows):
        return jnp.where(lane_row < granules, rows[0:1], pltpu.roll(rows, granules, 1)[1:2])

    routes = own_columns(route_ref, (slice(None),), granules)
    starts = [own_columns(window_ref, (r, slice(None)), granules) for r in range(2)]
    named = both_routes(routes).astype(f32)
    col = lax.broadcasted_iota(jnp.int32, (LANES, LANES), 1)
    row = lax.broadcasted_iota(jnp.int32, (LANES, LANES), 0)
    before = earlier((row // granules, row % granules), (col // granules, col % granules), granules)
    before = before & (row < 2 * granules) & (spread_columns(named) == named)
    rank = jnp.sum(before.astype(f32), axis=0, keepdims=True).astype(jnp.int32)
    knots = [
        jnp.clip(jnp.right_shift(both_routes(jnp.concatenate([s[k : k + 1] for s in starts])), 5) - 1, 0, KN - SPAN)
        for k in range(2)
    ]
    turn = rank * SPAN - knots[1] + LANES
    place_ref[...] = jnp.concatenate(
        [named.astype(jnp.int32), rank, jnp.right_shift(knots[0], 1), turn] * 2, axis=0
    )

    wide = 2 * LANES
    col = lax.broadcasted_iota(jnp.int32, (wide, wide), 1)
    row = lax.broadcasted_iota(jnp.int32, (wide, wide), 0)
    route = [at // LANES for at in (row, col)]
    place = [at % LANES for at in (row, col)]
    before = earlier((route[0], place[0] % granules), (route[1], place[1] % granules), granules)
    before = before & (place[0] // granules == place[1] // granules)
    before = before.astype(f32).astype(bf16)
    seat = (lax.broadcasted_iota(jnp.int32, (LANES, LANES), 1) // SPAN).astype(f32)
    lane = lax.broadcasted_iota(jnp.int32, (8, LANES), 1)
    step = lane % SPAN
    pixel = lax.broadcasted_iota(jnp.int32, (8, LANES), 0).astype(f32) * (1.0 / SP)
    part = LANES // granules
    for t in range(route_ref.shape[1] // LANES):
        at = slice(t * LANES, (t + 1) * LANES)
        hits = [(route_ref[r : r + 1, at] == own).astype(f32) for r in range(2)]
        hits = jnp.broadcast_to(jnp.concatenate(hits, axis=1), (8, wide))
        ranks = jnp.dot(hits.astype(bf16), before, preferred_element_type=f32)
        ranks = jnp.where(hits > 0.5, ranks, -1.0)
        chosen, values = [], []
        for r in range(2):
            chosen.append((spread_columns(ranks[0:1, r * LANES : (r + 1) * LANES]) == seat).astype(f32).astype(bf16))
            sender = lax.broadcasted_iota(jnp.int32, (part, LANES), 0)
            within = lax.broadcasted_iota(jnp.int32, (part, LANES), 1) // granules == sender
            kinds = []
            for k in range(2):
                start = window_ref[r, k : k + 1, at]
                kinds += [jnp.right_shift(start, 5), jnp.bitwise_and(start, SP - 1)]
            kinds.append(jnp.ones((1, LANES), jnp.int32))
            values.append(jnp.concatenate([jnp.where(within, kind, 0).astype(f32) for kind in kinds], axis=0))
        found = jnp.dot(
            jnp.concatenate(values, axis=1).astype(bf16),
            jnp.concatenate(chosen, axis=0),
            preferred_element_type=f32,
        )
        for n in range(part):
            live = found[4 * part + n : 4 * part + n + 1] > 0.5
            for k, ref in ((0, rows_out), (1, cols_out)):
                base = found[2 * k * part + n : 2 * k * part + n + 1]
                rest = found[(2 * k + 1) * part + n : (2 * k + 1) * part + n + 1]
                first = jnp.clip(base.astype(jnp.int32) - 1, 0, KN - SPAN)
                if k == 0:
                    knot = 2 * jnp.right_shift(first, 1) + 2 * (step % 8) + step // 8
                else:
                    knot = first + step
                border = (knot == 0) | (knot == KN - 1)
                cube = jnp.where(border, 1.0, 1.5)
                square = jnp.where(border, -1.5, -2.5)
                single = jnp.where(border, -0.5, 0.0)
                away = jnp.where(live, base + rest * (1.0 / SP) - knot.astype(f32), 4.0 * KN)
                away = away + pixel
                to = pl.ds((t * part + n) * LANES, LANES)
                for q in range(0, pixels, 16):
                    pair = []
                    for p in (q, q + 8):
                        d = jnp.abs(away + p * (1.0 / SP))
                        near = ((cube * d + square) * d + single) * d + 1.0
                        far = ((2.5 - 0.5 * d) * d - 4.0) * d + 2.0
                        pair.append(jnp.where(d <= 1.0, near, jnp.where(d < 2.0, far, 0.0)))
                    ref[q : q + 16, to] = jnp.concatenate(pair, axis=0).astype(bf16)


def compose(route_ref, received_ref, row_ref, col_ref, pixels_ref, solved, out_ref, grids_out, passed, result, sems):
    copies = [pltpu.make_async_copy(solved, grids_out, sems.at[result.shape[0]])]
    copies[0].start()
    senders = received_ref.shape[0]
    bands = result.shape[0]
    lane = lax.broadcasted_iota(jnp.int32, (16, LANES), 1) // SPAN
    masks = [(lane == r).astype(f32).astype(bf16) for r in range(LANES // SPAN)]
    named = (route_ref[...] == lax.axis_index("gran")).astype(f32)
    scale = 1.0 / jnp.sum(named, keepdims=True)

    def sender(n, carry):
        at = pl.ds(pl.multiple_of(n * LANES, LANES), LANES)
        blocks = []
        for k in range(2 * bands):
            window = received_ref[n, 16 * k : 16 * k + 16, :]
            blocks.append(jnp.concatenate([window * mask for mask in masks], axis=0))
        rows = jnp.dot(row_ref[:, at], jnp.concatenate(blocks, axis=1), preferred_element_type=f32)
        for k in range(2 * bands):
            passed[k, :, at] = rows[:, LANES * k : LANES * k + LANES].astype(bf16)
        return carry

    steps = min(8, senders)

    def several(n, carry):
        for k in range(steps):
            sender(n * steps + k, carry)
        return carry

    if senders == steps:
        several(0, 0)
    else:
        lax.fori_loop(0, senders // steps, several, 0)
    for b in range(bands):
        fields = [
            lax.dot_general(
                passed[2 * b + c], col_ref[...], (((1,), (1,)), ((), ())), preferred_element_type=f32
            )
            * scale
            for c in range(2)
        ]
        pixels = pixels_ref[0, b].astype(f32)
        result[b] = (pixels * (1.0 + fields[0]) + fields[1]).astype(bf16)
        copies.append(pltpu.make_async_copy(result.at[b], out_ref.at[0, b], sems.at[b]))
        copies[-1].start()
    for copy in copies:
        copy.wait()


def per_device(
    prior_grids,
    pif_rhs,
    pif_diagonal,
    pif_cross,
    pif_coupling,
    neighbour_offset,
    neighbour_count,
    tile_route,
    tile_window,
    tile_pixels,
):
    granules, bands = prior_grids.shape[:2]
    slots = pif_coupling.shape[1]
    pixel_count = tile_pixels.shape[2]
    device_total = lax.axis_size("gran")
    band_total = lax.axis_size("band")

    def by_lane_tile(array):
        cut = array.reshape(array.shape[:2] + (array.shape[2], 32, LANES)).transpose(0, 1, 3, 2, 4)
        return cut.reshape(array.shape[:2] + (32 * array.shape[2], LANES))

    grids = by_lane_tile(prior_grids)
    rhs = by_lane_tile(pif_rhs)
    diagonal = by_lane_tile(pif_diagonal)
    cross = by_lane_tile(pif_cross.transpose(1, 0, 2).reshape(bands, granules // 8, 8, KN * KN))
    coupling = by_lane_tile(pif_coupling.transpose(0, 2, 1, 3))
    graph = [("v", neighbour_offset.T)]
    tiles = [("v", tile_route.T), ("v", tile_window.transpose(1, 2, 0))]
    edge = (REACH, bands, 64, LANES)
    own = (granules, bands, 64, LANES)
    ext = (granules + 2 * REACH, bands, 64, LANES)
    packed = [("v", (64, LANES), f32), ("v", (64, LANES), bf16)]
    chunks = 4

    near_pairs = [(i, i ^ 1) for i in range(device_total)]
    far_pairs = [
        pair for i in range(1, device_total - 1, 2) for pair in ((i, i + 1), (i + 1, i))
    ]

    def exchange(near, far):
        far = lax.ppermute(far, "gran", far_pairs)
        near = lax.ppermute(near, "gran", near_pairs)
        return near, far

    near, far = call(
        first_edges,
        [("h", grids)],
        [("v", edge, bf16), ("v", edge, bf16)],
        [pltpu.VMEM((2,) + edge, f32), pltpu.SemaphoreType.DMA((2, REACH))],
    )
    near, far = exchange(near, far)
    (extended,) = call(
        arrange_grids,
        [("h", grids)],
        [("v", ext, f32)],
        [pltpu.VMEM(own, f32), pltpu.SemaphoreType.DMA((chunks,))],
    )
    sources = [rhs, diagonal, cross, coupling]

    def arranged(interior, sources):
        part = len(visits(granules, interior))
        some = (part, bands, 64, LANES)
        return call(
            functools.partial(arrange, interior),
            [("v", neighbour_count[None, :])] + [("h", source) for source in sources],
            [
                ("v", some, f32),
                ("v", some, f32),
                ("v", (part, bands, 32, LANES), f32),
                ("v", (part, slots, bands, 32, LANES), f32),
            ],
            [
                pltpu.VMEM(some, f32),
                pltpu.VMEM(some, f32),
                pltpu.VMEM(cross.shape, f32),
                pltpu.VMEM((part,) + coupling.shape[1:], bf16),
                pltpu.VMEM(coupling.shape[1:], f32),
                pltpu.SMEM((part,), jnp.int32),
                pltpu.SemaphoreType.DMA((4, chunks)),
            ],
        )

    gathered = pltpu.VMEM((slots, 64, LANES), f32)
    weights = pltpu.VMEM((slots, 64, LANES), f32)
    scalars = pltpu.SMEM((granules,), jnp.int32)

    def over_band(partial, rounded):
        return [("v", partial)] + [
            ("v", lax.ppermute(rounded, "band", [(i, i ^ flip) for i in range(band_total)]))
            for flip in range(1, band_total)
        ]

    for sweep in range(SWEEPS):
        last = sweep == SWEEPS - 1
        inner, *inner_rounded = call(
            interior_disparities,
            graph + [("v", extended)],
            packed if last else packed[:1],
            [gathered],
        )
        if sweep == 0:
            inner, *edge_state = lax.optimization_barrier((inner, *arranged(False, sources)))
        if last:
            inner_shares = over_band(inner, *inner_rounded)
        inputs = graph + [("v", near), ("v", far), ("v", extended)]
        inputs += [] if last else [("v", inner)]
        extended, partial, rounded = call(
            edge_disparities,
            inputs,
            [("v", ext, f32)] + packed,
            [gathered],
            aliases={3: 0},
        )
        shares = over_band(partial, rounded)
        if sweep == 1:
            routes, starts, _ = lax.optimization_barrier((tiles[0][1], tiles[1][1], partial))
            weight_shape = ("v", (pixel_count, device_total * LANES), bf16)
            made = call(
                tile_places,
                [("v", routes), ("v", starts)],
                [weight_shape, weight_shape, ("v", (8, LANES), jnp.int32)],
            )
            partial, row_weights, col_weights, places = lax.optimization_barrier((partial, *made))
            shares[0] = ("v", partial)
        edge_state_now = [("v", extended)] + [("v", array) for array in edge_state]
        if not last:
            inputs = graph + shares + edge_state_now
            updated, near, far = call(
                edge_sweep,
                inputs,
                [("v", ext, f32), ("v", edge, bf16), ("v", edge, bf16)],
                [weights, scalars],
            )
            near, far = exchange(near, far)
            if sweep == 0:
                *later, updated = lax.optimization_barrier((*sources, updated))
                inner_state = [("v", array) for array in arranged(True, later)]
            inputs = graph + shares + [("v", extended)] + inner_state
            (extended,) = call(
                interior_sweep,
                inputs + [("v", updated)],
                [("v", ext, f32)],
                [weights, scalars],
                aliases={len(inputs): 0},
            )
    windows = (device_total, 2 * bands * SPAN, LANES)
    scratch = [weights, scalars]
    inputs = graph + inner_shares + [("v", extended)] + inner_state + [("v", places)]
    balanced, gathered_windows = call(
        functools.partial(last_sweep, True),
        inputs,
        [("v", own, f32), ("v", windows, f32)],
        scratch,
    )
    inputs = graph + shares + edge_state_now + [("v", places)] + [("v", balanced), ("v", gathered_windows)]
    balanced, payload, _ = call(
        functools.partial(last_sweep, False),
        inputs,
        [("v", own, f32), ("v", windows, bf16), ("v", windows, f32)],
        scratch,
        aliases={len(inputs) - 2: 0, len(inputs) - 1: 2},
    )
    received = lax.all_to_all(payload, "gran", split_axis=0, concat_axis=0, tiled=True)
    inputs = [tiles[0], ("v", received), ("v", row_weights), ("v", col_weights), ("v", tile_pixels)]
    corrected, balanced = call(
        compose,
        inputs + [("v", balanced)],
        [("h", tile_pixels.shape, bf16), ("h", own, f32)],
        [
            pltpu.VMEM((2 * bands, pixel_count, device_total * LANES), bf16),
            pltpu.VMEM(tile_pixels.shape[1:], bf16),
            pltpu.SemaphoreType.DMA((bands + 1,)),
        ],
        limit=32,
    )
    balanced = balanced.reshape(granules, bands, 32, 2, LANES).transpose(0, 1, 3, 2, 4)
    return (balanced.reshape(prior_grids.shape), corrected)


def solution(mesh):
    placed = (
        P("gran", "band", None, None),
        P("gran", "band", None, None),
        P("gran", "band", None, None),
        P("gran", "band", None),
        P("gran", None, "band", None),
        P("gran", None),
        P("gran"),
        P(),
        P(),
        P("gran", "band", None, None),
    )
    return jax.shard_map(
        per_device,
        mesh=mesh,
        in_specs=placed,
        out_specs=(P("gran", "band", None, None), P("gran", "band", None, None)),
        check_vma=False,
    )
```

```python
import functools
import jax
import jax.numpy as jnp
from jax import lax
from jax.experimental import pallas as pl
from jax.experimental.pallas import tpu as pltpu
from jax.sharding import PartitionSpec as P

BANDS = 12
KN = 64
PATCH = 8
REACH = 4
SWEEPS = 3
SP = 32
LANES = 128
SPAN = 16
FIRST = 3

robust_scale = 0.3

ON_CHIP = pl.BlockSpec(memory_space=pltpu.VMEM)
ANYWHERE = pl.BlockSpec(memory_space=pl.ANY)
f32 = jnp.float32
bf16 = jnp.bfloat16


def call(body, inputs, outputs, scratch=(), aliases=None, limit=16):
    operands = [
        pltpu.with_memory_space_constraint(array, pltpu.VMEM if kind == "v" else pltpu.HBM)
        for kind, array in inputs
    ]
    return pl.pallas_call(
        body,
        in_specs=[ON_CHIP if kind == "v" else ANYWHERE for kind, _ in inputs],
        out_specs=tuple(ON_CHIP if kind == "v" else ANYWHERE for kind, _, _ in outputs),
        out_shape=tuple(
            (pltpu.VMEM if kind == "v" else pltpu.HBM)(shape, dtype)
            for kind, shape, dtype in outputs
        ),
        scratch_shapes=list(scratch),
        input_output_aliases=aliases or {},
        compiler_params=pltpu.CompilerParams(vmem_limit_bytes=limit * 2**20),
    )(*operands)


def parity():
    return lax.rem(lax.axis_index("gran"), 2)


def first_edges(grids_ref, near_ref, far_ref, raw, sems):
    odd = parity()
    last = grids_ref.shape[0] - REACH
    sides = ((far_ref, odd * last), (near_ref, (1 - odd) * last))
    copies = [
        [pltpu.make_async_copy(grids_ref.at[base + g], raw.at[k, g], sems.at[k, g]) for g in range(REACH)]
        for k, (_, base) in enumerate(sides)
    ]
    for copy in copies[0] + copies[1]:
        copy.start()
    for k, (ref, _) in enumerate(sides):
        for g in range(REACH):
            copies[k][g].wait()
            for b in range(ref.shape[1]):
                for j in range(4):
                    both = [raw[k, g, b, pl.ds(2 * j + c, 8, stride=8), :] for c in range(2)]
                    ref[g, b, 16 * j : 16 * j + 16, :] = jnp.concatenate(both, axis=0).astype(bf16)


def arrange_grids(grids_ref, ext_ref, raw, sems):
    granules, bands = grids_ref.shape[:2]
    chunks = sems.shape[0]
    size = granules // chunks
    copies = []
    for n in range(chunks):
        part = pl.ds(n * size, size)
        copies.append(pltpu.make_async_copy(grids_ref.at[part], raw.at[part], sems.at[n]))
        copies[n].start()

    def step(i, carry):
        for b in range(bands):
            for q in range(8):
                ext_ref[i + REACH, b, 8 * q : 8 * q + 8, :] = raw[i, b, pl.ds(q, 8, stride=8), :]
        return carry

    for n in range(chunks):
        copies[n].wait()
        lax.fori_loop(n * size, (n + 1) * size, step, 0)


def visits(granules, interior):
    inner = list(range(REACH, granules - REACH))
    return inner if interior else [i for i in range(granules) if i not in inner]


def arrange(interior, count_ref, rhs_ref, diag_ref, cross_ref, coupling_ref, rhs_out, diag_out, cross_out, coupling_out, rhs_raw, diag_raw, cross_raw, coupling_raw, wide, graph, sems):
    granules, bands = rhs_ref.shape[:2]
    own = visits(granules, interior)
    size = REACH
    chunks = len(own) // size
    copies = []
    for n in range(chunks):
        source, target = pl.ds(own[n * size], size), pl.ds(n * size, size)
        moves = ((coupling_ref, coupling_raw), (diag_ref, diag_raw), (rhs_ref, rhs_raw))
        copies.append(
            [
                pltpu.make_async_copy(here.at[source], there.at[target], sems.at[k, n])
                for k, (here, there) in enumerate(moves)
            ]
        )
        for copy in copies[n]:
            copy.start()
        if n == 0:
            whole = pltpu.make_async_copy(cross_ref, cross_raw, sems.at[3, 0])
            whole.start()
    for i, count in enumerate(visits(granules, interior)):
        graph[i] = count_ref[...][0, count]
    for n in range(chunks):
        for copy in copies[n]:
            copy.wait()
        if n == 0:
            whole.wait()

        def step(g, carry, n=n):
            at = n * size + g
            i = own[n * size] + g
            for b in range(bands):
                wide[b] = coupling_raw[at, b].astype(f32)
                for j in range(4):
                    d = []
                    for c in range(2):
                        rows = pl.ds(2 * j + c, 8, stride=8)
                        to = slice(16 * j + 8 * c, 16 * j + 8 * c + 8)
                        rhs_out[at, b, to, :] = rhs_raw[at, b, rows, :]
                        d.append(diag_raw[at, b, rows, :])
                        diag_out[at, b, to, :] = d[c]
                    pick = cross_raw[b, i // 8, pl.ds(8 * j + i % 8, 8, stride=32), :]
                    cross_out[at, b, 8 * j : 8 * j + 8, :] = pick * jnp.sqrt(d[0] * d[1])

            def slot(s, carry):
                for b in range(bands):
                    for j in range(4):
                        pick = wide[b, pl.ds(8 * j + s, 8, stride=32), :]
                        coupling_out[at, s, b, 8 * j : 8 * j + 8, :] = pick
                return carry

            return lax.fori_loop(0, graph[at], slot, carry)

        lax.fori_loop(0, size, step, 0)


def lane_sums():
    row = lax.broadcasted_iota(jnp.int32, (LANES, LANES), 0)
    col = lax.broadcasted_iota(jnp.int32, (LANES, LANES), 1)
    return ((row % KN) // PATCH == col % PATCH).astype(f32).astype(bf16)


def lane_spread():
    row = lax.broadcasted_iota(jnp.int32, (LANES, LANES), 0)
    col = lax.broadcasted_iota(jnp.int32, (LANES, LANES), 1)
    return ((col % KN) // PATCH == row % PATCH).astype(f32).astype(bf16)


def read_graph(offset_ref, graph):
    slot = lax.broadcasted_iota(jnp.int32, offset_ref.shape, 0)
    codes = jnp.sum(jnp.left_shift(offset_ref[...] + REACH, 4 * slot), axis=0, keepdims=True)
    for i in range(offset_ref.shape[1]):
        graph[i] = codes[0, i]


def step_to(code, s):
    return jnp.bitwise_and(jnp.right_shift(code, 4 * s), 15)


def group_mask(interior, slots):
    row = lax.broadcasted_iota(jnp.int32, (64, LANES), 0) // 32
    lane = lax.broadcasted_iota(jnp.int32, (64, LANES), 1) // PATCH
    return lane - slots * (1 - row if interior else row)


def disparities(interior, offset_ref, ext_ref, gathered, graph):
    bands = ext_ref.shape[1]
    granules = ext_ref.shape[0] - 2 * REACH
    slots = gathered.shape[0]
    gathered[...] = jnp.zeros_like(gathered)
    read_graph(offset_ref, graph)

    def response(g):
        return [
            ext_ref[g, b, 16 * j : 16 * j + 8, :] + ext_ref[g, b, 16 * j + 8 : 16 * j + 16, :]
            for b in range(bands)
            for j in range(4)
        ]

    for i in range(granules):
        if (REACH <= i < granules - REACH) != interior:
            continue
        own = response(i + REACH)
        code = graph[i]

        def slot(s, i=i, own=own, code=code):
            total = None
            for a, o in zip(own, response(i + step_to(code, s))):
                d = a - o
                total = d * d if total is None else total + d * d
            gathered[s, 8 * (i % 8) : 8 * (i % 8) + 8, :] = total

        for s in range(FIRST):
            slot(s)

        @pl.when(step_to(code, FIRST) != REACH)
        def _(slot=slot):
            for s in range(FIRST, slots):
                slot(s)

    sums = jnp.dot(
        gathered[...].reshape(slots * 64, LANES).astype(bf16), lane_sums(), preferred_element_type=f32
    )
    place = group_mask(interior, slots)
    packed = jnp.zeros((64, LANES), f32)
    for s in range(slots):
        packed = jnp.where(place == s, sums[64 * s : 64 * s + 64], packed)
    return packed


def interior_disparities(offset_ref, ext_ref, out_ref, *refs):
    packed = disparities(True, offset_ref, ext_ref, *refs[-2:])
    out_ref[...] = packed
    if len(refs) == 3:
        refs[0][...] = packed.astype(bf16)


def edge_disparities(offset_ref, near_ref, far_ref, *refs):
    ext_ref, out_ref, send_ref, gathered, graph = refs[-5:]
    odd = parity()
    right = ext_ref.shape[0] - REACH
    for ref, base in ((near_ref, (1 - odd) * right), (far_ref, odd * right)):
        for g in range(REACH):
            for b in range(ref.shape[1]):
                ext_ref[base + g, b] = ref[g, b].astype(f32)
    packed = disparities(False, offset_ref, ext_ref, gathered, graph)
    if len(refs) == 7:
        packed = packed + refs[1][...]
    out_ref[...] = packed
    send_ref[...] = packed.astype(bf16)


def spread_weights(shares, interior, weights):
    slots = weights.shape[0]
    total = shares[0][...]
    for share in shares[1:]:
        total = total + share[...].astype(f32)
    robust = 1.0 / (1.0 + total * (1.0 / (robust_scale * BANDS * PATCH * PATCH)))
    high = robust.astype(bf16).astype(f32)
    both = jnp.concatenate([high, robust - high], axis=1)
    place = group_mask(interior, slots)
    place = jnp.concatenate([place, place], axis=1)
    spread = lane_spread()
    spread = jnp.concatenate([spread, spread], axis=0)
    stacked = jnp.concatenate(
        [jnp.where(place == s, both, 0.0).astype(bf16) for s in range(slots)], axis=0
    )
    weights[...] = jnp.dot(stacked, spread, preferred_element_type=f32).reshape(slots, 64, LANES)


def balance(i, at, ext_ref, rhs_ref, diag_ref, cross_ref, coupling_ref, weights, graph, store):
    bands = rhs_ref.shape[1]
    row = pl.multiple_of(lax.rem(i, 8) * 8, 8)
    slots = weights.shape[0]
    parts = [(b, j) for b in range(bands) for j in range(4)]
    rows = [slice(8 * q, 8 * q + 8) for q in range(8)]
    rhs = tuple(rhs_ref[at, b, rows[2 * j + c], :] for b, j in parts for c in range(2))

    code = graph[i]

    def slot(slot_index, sums):
        sigma, drive = sums
        used = step_to(code, slot_index) != REACH
        s = jnp.where(used, slot_index, 0)
        weight = jnp.where(used, weights[s, pl.ds(row, 8), :], 0.0)
        n = i + step_to(code, s)
        new_sigma, new_drive = [], []
        for b in range(bands):
            for j in range(4):
                k = 4 * b + j
                effective = weight * coupling_ref[at, s, b, 8 * j : 8 * j + 8, :]
                new_sigma.append(sigma[k] + effective)
                for c in range(2):
                    grid = ext_ref[n, b, 16 * j + 8 * c : 16 * j + 8 * c + 8, :]
                    new_drive.append(drive[2 * k + c] + effective * grid)
        return tuple(new_sigma), tuple(new_drive)

    zero = jnp.zeros((8, LANES), f32)
    sums = ((zero,) * len(parts), rhs)
    for s in range(FIRST):
        sums = slot(s, sums)

    def others(_, sums):
        for s in range(FIRST, slots):
            sums = slot(s, sums)
        return sums

    sigma, drive = lax.fori_loop(0, (step_to(code, FIRST) != REACH).astype(jnp.int32), others, sums)
    for k, (b, j) in enumerate(parts):
        first, second = (
            diag_ref[at, b, rows[2 * j + c], :] + sigma[k] for c in range(2)
        )
        cross = cross_ref[at, b, 8 * j : 8 * j + 8, :]
        inverse = 1.0 / (first * second - cross * cross)
        gain, offset = drive[2 * k], drive[2 * k + 1]
        store(
            b,
            j,
            (second * gain - cross * offset) * inverse,
            (first * offset - cross * gain) * inverse,
        )


def edge_sweep(offset_ref, *refs):
    shares, state, (new_ref, near_ref, far_ref, weights, graph) = refs[:4], refs[4:9], refs[9:]
    read_graph(offset_ref, graph)
    spread_weights(shares, False, weights)
    odd = parity()
    last = new_ref.shape[0] - 3 * REACH
    for ref, base in ((far_ref, odd * last), (near_ref, (1 - odd) * last)):

        def step(g, carry, ref=ref, base=base):
            def store(b, j, gain, offset):
                both = jnp.concatenate([gain, offset], axis=0)
                new_ref[base + g + REACH, b, 16 * j : 16 * j + 16, :] = both
                ref[g, b, 16 * j : 16 * j + 16, :] = both.astype(bf16)

            balance(base + g, lax.div(base, 2 * REACH) * REACH + g, *state, weights, graph, store)
            return carry

        lax.fori_loop(0, REACH, step, 0)


def interior_sweep(offset_ref, *refs):
    shares, state, (_, new_ref, weights, graph) = refs[:4], refs[4:9], refs[9:]
    read_graph(offset_ref, graph)
    spread_weights(shares, True, weights)

    def step(i, carry):
        def store(b, j, gain, offset):
            both = jnp.concatenate([gain, offset], axis=0)
            new_ref[i + REACH, b, 16 * j : 16 * j + 16, :] = both

        balance(i, i - REACH, *state, weights, graph, store)
        return carry

    lax.fori_loop(REACH, new_ref.shape[0] - 3 * REACH, step, 0)


def own_columns(ref, at, granules):
    first = lax.axis_index("gran") * granules
    base = pl.multiple_of((first // LANES) * LANES, LANES)
    turn = jnp.bitwise_and(LANES - lax.rem(first, LANES), LANES - 1)
    return pltpu.roll(ref[at + (pl.ds(base, LANES),)], turn, 1)


def last_sweep(interior, offset_ref, *refs):
    shares, state, place_ref = refs[:4], refs[4:9], refs[9]
    weights, graph = refs[-2:]
    if interior:
        solved, windows = refs[10:12]
    else:
        solved, send_ref, windows = refs[12:15]
    granules, bands = solved.shape[:2]
    read_graph(offset_ref, graph)
    if interior:
        windows[...] = jnp.zeros_like(windows)
    spread_weights(shares, interior, weights)

    def step(t, carry):
        i = t if interior else jnp.where(t < REACH, t, t + granules - 2 * REACH)

        def store(b, j, gain, offset):
            solved[i, b, pl.ds(2 * j, 8, stride=8), :] = gain
            solved[i, b, pl.ds(2 * j + 1, 8, stride=8), :] = offset

        balance(i, t - REACH if interior else t, *state, weights, graph, store)
        return carry

    lax.fori_loop(*((REACH, granules - REACH) if interior else (0, 2 * REACH)), step, 0)
    lane = lax.broadcasted_iota(jnp.int32, (8, LANES), 1) // SPAN
    seats = LANES // SPAN
    places = place_ref[...]
    for i in visits(granules, interior):
        for r in range(2):
            owner, rank, top, turn = (places[k, r * granules + i] for k in range(4))
            here = [lane == jnp.bitwise_and(rank + half * (KN // SPAN), seats - 1) for half in (0, 1)]
            for b in range(bands):
                for c in range(2):
                    rows = solved[i, b, pl.ds(2 * top + c, 8, stride=2), :]
                    moved = pltpu.roll(rows, jnp.bitwise_and(turn, LANES - 1), 1)
                    for half in (0, 1):
                        at = 16 * (2 * b + c) + 8 * half
                        pltpu.store(windows.at[owner, at : at + 8, :], moved, mask=here[half])
    if not interior:
        for owner in range(windows.shape[0]):
            for at in range(0, windows.shape[1], 16):
                odd = pltpu.roll(windows[owner, at + 8 : at + 16, :], KN, 1)
                both = jnp.concatenate([windows[owner, at : at + 8, :], odd], axis=0)
                send_ref[owner, at : at + 16, :] = both.astype(bf16)


def earlier(first, second, granules):
    def edge(i):
        return ((i < REACH) | (i >= granules - REACH)).astype(jnp.int32)

    def rank(entry):
        return (edge(entry[1]) * 2 + entry[0]) * granules + entry[1]

    return rank(first) < rank(second)


def spread_columns(row):
    return jnp.transpose(jnp.broadcast_to(row, (LANES, LANES)))


def tile_places(route_ref, window_ref, rows_out, cols_out, place_ref):
    pixels, lanes = rows_out.shape
    senders = lanes // LANES
    granules = route_ref.shape[1] // senders
    own = lax.axis_index("gran")
    lane_row = lax.broadcasted_iota(jnp.int32, (1, LANES), 1)

    def both_routes(rows):
        return jnp.where(lane_row < granules, rows[0:1], pltpu.roll(rows, granules, 1)[1:2])

    routes = own_columns(route_ref, (slice(None),), granules)
    starts = [own_columns(window_ref, (r, slice(None)), granules) for r in range(2)]
    named = both_routes(routes).astype(f32)
    col = lax.broadcasted_iota(jnp.int32, (LANES, LANES), 1)
    row = lax.broadcasted_iota(jnp.int32, (LANES, LANES), 0)
    before = earlier((row // granules, row % granules), (col // granules, col % granules), granules)
    before = before & (row < 2 * granules) & (spread_columns(named) == named)
    rank = jnp.sum(before.astype(f32), axis=0, keepdims=True).astype(jnp.int32)
    knots = [
        jnp.clip(jnp.right_shift(both_routes(jnp.concatenate([s[k : k + 1] for s in starts])), 5) - 1, 0, KN - SPAN)
        for k in range(2)
    ]
    turn = rank * SPAN - knots[1] + LANES
    place_ref[...] = jnp.concatenate(
        [named.astype(jnp.int32), rank, jnp.right_shift(knots[0], 1), turn] * 2, axis=0
    )

    wide = 2 * LANES
    col = lax.broadcasted_iota(jnp.int32, (wide, wide), 1)
    row = lax.broadcasted_iota(jnp.int32, (wide, wide), 0)
    route = [at // LANES for at in (row, col)]
    place = [at % LANES for at in (row, col)]
    before = earlier((route[0], place[0] % granules), (route[1], place[1] % granules), granules)
    before = before & (place[0] // granules == place[1] // granules)
    before = before.astype(f32).astype(bf16)
    seat = (lax.broadcasted_iota(jnp.int32, (LANES, LANES), 1) // SPAN).astype(f32)
    lane = lax.broadcasted_iota(jnp.int32, (8, LANES), 1)
    step = lane % SPAN
    pixel = lax.broadcasted_iota(jnp.int32, (8, LANES), 0).astype(f32) * (1.0 / SP)
    part = LANES // granules
    for t in range(route_ref.shape[1] // LANES):
        at = slice(t * LANES, (t + 1) * LANES)
        hits = [(route_ref[r : r + 1, at] == own).astype(f32) for r in range(2)]
        hits = jnp.broadcast_to(jnp.concatenate(hits, axis=1), (8, wide))
        ranks = jnp.dot(hits.astype(bf16), before, preferred_element_type=f32)
        ranks = jnp.where(hits > 0.5, ranks, -1.0)
        chosen, values = [], []
        for r in range(2):
            chosen.append((spread_columns(ranks[0:1, r * LANES : (r + 1) * LANES]) == seat).astype(f32).astype(bf16))
            sender = lax.broadcasted_iota(jnp.int32, (part, LANES), 0)
            within = lax.broadcasted_iota(jnp.int32, (part, LANES), 1) // granules == sender
            kinds = []
            for k in range(2):
                start = window_ref[r, k : k + 1, at]
                kinds += [jnp.right_shift(start, 5), jnp.bitwise_and(start, SP - 1)]
            kinds.append(jnp.ones((1, LANES), jnp.int32))
            values.append(jnp.concatenate([jnp.where(within, kind, 0).astype(f32) for kind in kinds], axis=0))
        found = jnp.dot(
            jnp.concatenate(values, axis=1).astype(bf16),
            jnp.concatenate(chosen, axis=0),
            preferred_element_type=f32,
        )
        for n in range(part):
            live = found[4 * part + n : 4 * part + n + 1] > 0.5
            for k, ref in ((0, rows_out), (1, cols_out)):
                base = found[2 * k * part + n : 2 * k * part + n + 1]
                rest = found[(2 * k + 1) * part + n : (2 * k + 1) * part + n + 1]
                first = jnp.clip(base.astype(jnp.int32) - 1, 0, KN - SPAN)
                if k == 0:
                    knot = 2 * jnp.right_shift(first, 1) + 2 * (step % 8) + step // 8
                else:
                    knot = first + step
                border = (knot == 0) | (knot == KN - 1)
                cube = jnp.where(border, 1.0, 1.5)
                square = jnp.where(border, -1.5, -2.5)
                single = jnp.where(border, -0.5, 0.0)
                away = jnp.where(live, base + rest * (1.0 / SP) - knot.astype(f32), 4.0 * KN)
                away = away + pixel
                to = pl.ds((t * part + n) * LANES, LANES)
                for q in range(0, pixels, 16):
                    pair = []
                    for p in (q, q + 8):
                        d = jnp.abs(away + p * (1.0 / SP))
                        near = ((cube * d + square) * d + single) * d + 1.0
                        far = ((2.5 - 0.5 * d) * d - 4.0) * d + 2.0
                        pair.append(jnp.where(d <= 1.0, near, jnp.where(d < 2.0, far, 0.0)))
                    ref[q : q + 16, to] = jnp.concatenate(pair, axis=0).astype(bf16)


def compose(route_ref, received_ref, row_ref, col_ref, pixels_ref, solved, out_ref, grids_out, passed, result, sems):
    copies = [pltpu.make_async_copy(solved, grids_out, sems.at[result.shape[0]])]
    copies[0].start()
    senders = received_ref.shape[0]
    bands = result.shape[0]
    lane = lax.broadcasted_iota(jnp.int32, (16, LANES), 1) // SPAN
    masks = [(lane == r).astype(f32).astype(bf16) for r in range(LANES // SPAN)]
    named = (route_ref[...] == lax.axis_index("gran")).astype(f32)
    scale = 1.0 / jnp.sum(named, keepdims=True)

    def sender(n, carry):
        at = pl.ds(pl.multiple_of(n * LANES, LANES), LANES)
        blocks = []
        for k in range(2 * bands):
            window = received_ref[n, 16 * k : 16 * k + 16, :]
            blocks.append(jnp.concatenate([window * mask for mask in masks], axis=0))
        rows = jnp.dot(row_ref[:, at], jnp.concatenate(blocks, axis=1), preferred_element_type=f32)
        for k in range(2 * bands):
            passed[k, :, at] = rows[:, LANES * k : LANES * k + LANES].astype(bf16)
        return carry

    steps = min(8, senders)

    def several(n, carry):
        for k in range(steps):
            sender(n * steps + k, carry)
        return carry

    if senders == steps:
        several(0, 0)
    else:
        lax.fori_loop(0, senders // steps, several, 0)
    for b in range(bands):
        fields = [
            lax.dot_general(
                passed[2 * b + c], col_ref[...], (((1,), (1,)), ((), ())), preferred_element_type=f32
            )
            * scale
            for c in range(2)
        ]
        pixels = pixels_ref[0, b].astype(f32)
        result[b] = (pixels * (1.0 + fields[0]) + fields[1]).astype(bf16)
        copies.append(pltpu.make_async_copy(result.at[b], out_ref.at[0, b], sems.at[b]))
        copies[-1].start()
    for copy in copies:
        copy.wait()


def per_device(
    prior_grids,
    pif_rhs,
    pif_diagonal,
    pif_cross,
    pif_coupling,
    neighbour_offset,
    neighbour_count,
    tile_route,
    tile_window,
    tile_pixels,
):
    granules, bands = prior_grids.shape[:2]
    slots = pif_coupling.shape[1]
    pixel_count = tile_pixels.shape[2]
    device_total = lax.axis_size("gran")
    band_total = lax.axis_size("band")

    def by_lane_tile(array):
        cut = array.reshape(array.shape[:2] + (array.shape[2], 32, LANES)).transpose(0, 1, 3, 2, 4)
        return cut.reshape(array.shape[:2] + (32 * array.shape[2], LANES))

    grids = by_lane_tile(prior_grids)
    rhs = by_lane_tile(pif_rhs)
    diagonal = by_lane_tile(pif_diagonal)
    cross = by_lane_tile(pif_cross.transpose(1, 0, 2).reshape(bands, granules // 8, 8, KN * KN))
    coupling = by_lane_tile(pif_coupling.transpose(0, 2, 1, 3))
    graph = [("v", neighbour_offset.T)]
    tiles = [("v", tile_route.T), ("v", tile_window.transpose(1, 2, 0))]
    edge = (REACH, bands, 64, LANES)
    own = (granules, bands, 64, LANES)
    ext = (granules + 2 * REACH, bands, 64, LANES)
    packed = [("v", (64, LANES), f32), ("v", (64, LANES), bf16)]
    chunks = 4

    near_pairs = [(i, i ^ 1) for i in range(device_total)]
    far_pairs = [
        pair for i in range(1, device_total - 1, 2) for pair in ((i, i + 1), (i + 1, i))
    ]

    def exchange(near, far):
        far = lax.ppermute(far, "gran", far_pairs)
        near = lax.ppermute(near, "gran", near_pairs)
        return near, far

    near, far = call(
        first_edges,
        [("h", grids)],
        [("v", edge, bf16), ("v", edge, bf16)],
        [pltpu.VMEM((2,) + edge, f32), pltpu.SemaphoreType.DMA((2, REACH))],
    )
    near, far = exchange(near, far)
    (extended,) = call(
        arrange_grids,
        [("h", grids)],
        [("v", ext, f32)],
        [pltpu.VMEM(own, f32), pltpu.SemaphoreType.DMA((chunks,))],
    )
    sources = [rhs, diagonal, cross, coupling]

    def arranged(interior, sources):
        part = len(visits(granules, interior))
        some = (part, bands, 64, LANES)
        return call(
            functools.partial(arrange, interior),
            [("v", neighbour_count[None, :])] + [("h", source) for source in sources],
            [
                ("v", some, f32),
                ("v", some, f32),
                ("v", (part, bands, 32, LANES), f32),
                ("v", (part, slots, bands, 32, LANES), f32),
            ],
            [
                pltpu.VMEM(some, f32),
                pltpu.VMEM(some, f32),
                pltpu.VMEM(cross.shape, f32),
                pltpu.VMEM((part,) + coupling.shape[1:], bf16),
                pltpu.VMEM(coupling.shape[1:], f32),
                pltpu.SMEM((part,), jnp.int32),
                pltpu.SemaphoreType.DMA((4, chunks)),
            ],
        )

    gathered = pltpu.VMEM((slots, 64, LANES), f32)
    weights = pltpu.VMEM((slots, 64, LANES), f32)
    scalars = pltpu.SMEM((granules,), jnp.int32)

    def over_band(partial, rounded):
        return [("v", partial)] + [
            ("v", lax.ppermute(rounded, "band", [(i, i ^ flip) for i in range(band_total)]))
            for flip in range(1, band_total)
        ]

    for sweep in range(SWEEPS):
        last = sweep == SWEEPS - 1
        inner, *inner_rounded = call(
            interior_disparities,
            graph + [("v", extended)],
            packed if last else packed[:1],
            [gathered, scalars],
        )
        if sweep == 0:
            inner, *edge_state = lax.optimization_barrier((inner, *arranged(False, sources)))
        if last:
            inner_shares = over_band(inner, *inner_rounded)
        inputs = graph + [("v", near), ("v", far), ("v", extended)]
        inputs += [] if last else [("v", inner)]
        extended, partial, rounded = call(
            edge_disparities,
            inputs,
            [("v", ext, f32)] + packed,
            [gathered, scalars],
            aliases={3: 0},
        )
        shares = over_band(partial, rounded)
        if sweep == 1:
            routes, starts, _ = lax.optimization_barrier((tiles[0][1], tiles[1][1], partial))
            weight_shape = ("v", (pixel_count, device_total * LANES), bf16)
            made = call(
                tile_places,
                [("v", routes), ("v", starts)],
                [weight_shape, weight_shape, ("v", (8, LANES), jnp.int32)],
            )
            partial, row_weights, col_weights, places = lax.optimization_barrier((partial, *made))
            shares[0] = ("v", partial)
        edge_state_now = [("v", extended)] + [("v", array) for array in edge_state]
        if not last:
            inputs = graph + shares + edge_state_now
            updated, near, far = call(
                edge_sweep,
                inputs,
                [("v", ext, f32), ("v", edge, bf16), ("v", edge, bf16)],
                [weights, scalars],
            )
            near, far = exchange(near, far)
            if sweep == 0:
                *later, updated = lax.optimization_barrier((*sources, updated))
                inner_state = [("v", array) for array in arranged(True, later)]
            inputs = graph + shares + [("v", extended)] + inner_state
            (extended,) = call(
                interior_sweep,
                inputs + [("v", updated)],
                [("v", ext, f32)],
                [weights, scalars],
                aliases={len(inputs): 0},
            )
    windows = (device_total, 2 * bands * SPAN, LANES)
    scratch = [weights, scalars]
    inputs = graph + inner_shares + [("v", extended)] + inner_state + [("v", places)]
    balanced, gathered_windows = call(
        functools.partial(last_sweep, True),
        inputs,
        [("v", own, f32), ("v", windows, f32)],
        scratch,
    )
    inputs = graph + shares + edge_state_now + [("v", places)] + [("v", balanced), ("v", gathered_windows)]
    balanced, payload, _ = call(
        functools.partial(last_sweep, False),
        inputs,
        [("v", own, f32), ("v", windows, bf16), ("v", windows, f32)],
        scratch,
        aliases={len(inputs) - 2: 0, len(inputs) - 1: 2},
    )
    received = lax.all_to_all(payload, "gran", split_axis=0, concat_axis=0, tiled=True)
    inputs = [tiles[0], ("v", received), ("v", row_weights), ("v", col_weights), ("v", tile_pixels)]
    corrected, balanced = call(
        compose,
        inputs + [("v", balanced)],
        [("h", tile_pixels.shape, bf16), ("h", own, f32)],
        [
            pltpu.VMEM((2 * bands, pixel_count, device_total * LANES), bf16),
            pltpu.VMEM(tile_pixels.shape[1:], bf16),
            pltpu.SemaphoreType.DMA((bands + 1,)),
        ],
        limit=32,
    )
    balanced = balanced.reshape(granules, bands, 32, 2, LANES).transpose(0, 1, 3, 2, 4)
    return (balanced.reshape(prior_grids.shape), corrected)


def solution(mesh):
    placed = (
        P("gran", "band", None, None),
        P("gran", "band", None, None),
        P("gran", "band", None, None),
        P("gran", "band", None),
        P("gran", None, "band", None),
        P("gran", None),
        P("gran"),
        P(),
        P(),
        P("gran", "band", None, None),
    )
    return jax.shard_map(
        per_device,
        mesh=mesh,
        in_specs=placed,
        out_specs=(P("gran", "band", None, None), P("gran", "band", None, None)),
        check_vma=False,
    )
```

```python
import functools
import jax
import jax.numpy as jnp
from jax import lax
from jax.experimental import pallas as pl
from jax.experimental.pallas import tpu as pltpu
from jax.sharding import PartitionSpec as P

BANDS = 12
KN = 64
PATCH = 8
REACH = 4
SWEEPS = 3
SP = 32
LANES = 128
SPAN = 16
PARTED = 0
FIRST = 3

robust_scale = 0.3

ON_CHIP = pl.BlockSpec(memory_space=pltpu.VMEM)
ANYWHERE = pl.BlockSpec(memory_space=pl.ANY)
f32 = jnp.float32
bf16 = jnp.bfloat16


def call(body, inputs, outputs, scratch=(), aliases=None, limit=16):
    operands = [
        pltpu.with_memory_space_constraint(array, pltpu.VMEM if kind == "v" else pltpu.HBM)
        for kind, array in inputs
    ]
    return pl.pallas_call(
        body,
        in_specs=[ON_CHIP if kind == "v" else ANYWHERE for kind, _ in inputs],
        out_specs=tuple(ON_CHIP if kind == "v" else ANYWHERE for kind, _, _ in outputs),
        out_shape=tuple(
            (pltpu.VMEM if kind == "v" else pltpu.HBM)(shape, dtype)
            for kind, shape, dtype in outputs
        ),
        scratch_shapes=list(scratch),
        input_output_aliases=aliases or {},
        compiler_params=pltpu.CompilerParams(vmem_limit_bytes=limit * 2**20),
    )(*operands)


def parity():
    return lax.rem(lax.axis_index("gran"), 2)


def first_edges(grids_ref, near_ref, far_ref, raw, sems):
    odd = parity()
    last = grids_ref.shape[0] - REACH
    sides = ((far_ref, odd * last), (near_ref, (1 - odd) * last))
    copies = [
        [pltpu.make_async_copy(grids_ref.at[base + g], raw.at[k, g], sems.at[k, g]) for g in range(REACH)]
        for k, (_, base) in enumerate(sides)
    ]
    for copy in copies[0] + copies[1]:
        copy.start()
    for k, (ref, _) in enumerate(sides):
        for g in range(REACH):
            copies[k][g].wait()
            for b in range(ref.shape[1]):
                for j in range(4):
                    both = [raw[k, g, b, pl.ds(2 * j + c, 8, stride=8), :] for c in range(2)]
                    ref[g, b, 16 * j : 16 * j + 16, :] = jnp.concatenate(both, axis=0).astype(bf16)


def arrange_grids(grids_ref, ext_ref, raw, sems):
    granules, bands = grids_ref.shape[:2]
    chunks = sems.shape[0]
    size = granules // chunks
    copies = []
    for n in range(chunks):
        part = pl.ds(n * size, size)
        copies.append(pltpu.make_async_copy(grids_ref.at[part], raw.at[part], sems.at[n]))
        copies[n].start()

    def step(i, carry):
        for b in range(bands):
            for q in range(8):
                ext_ref[i + REACH, b, 8 * q : 8 * q + 8, :] = raw[i, b, pl.ds(q, 8, stride=8), :]
        return carry

    for n in range(chunks):
        copies[n].wait()
        lax.fori_loop(n * size, (n + 1) * size, step, 0)


def visits(granules, interior):
    inner = list(range(REACH, granules - REACH))
    return inner if interior else [i for i in range(granules) if i not in inner]


def arrange(interior, count_ref, rhs_ref, diag_ref, cross_ref, coupling_ref, rhs_out, diag_out, cross_out, coupling_out, rhs_raw, diag_raw, cross_raw, coupling_raw, wide, graph, sems):
    granules, bands = rhs_ref.shape[:2]
    own = visits(granules, interior)
    size = REACH
    chunks = len(own) // size
    copies = []
    for n in range(chunks):
        source, target = pl.ds(own[n * size], size), pl.ds(n * size, size)
        moves = ((coupling_ref, coupling_raw), (diag_ref, diag_raw), (rhs_ref, rhs_raw))
        copies.append(
            [
                pltpu.make_async_copy(here.at[source], there.at[target], sems.at[k, n])
                for k, (here, there) in enumerate(moves)
            ]
        )
        for copy in copies[n]:
            copy.start()
        if n == 0:
            whole = pltpu.make_async_copy(cross_ref, cross_raw, sems.at[3, 0])
            whole.start()
    for i, count in enumerate(visits(granules, interior)):
        graph[i] = count_ref[...][0, count]
    for n in range(chunks):
        for copy in copies[n]:
            copy.wait()
        if n == 0:
            whole.wait()

        def step(g, carry, n=n):
            at = n * size + g
            i = own[n * size] + g
            for b in range(bands):
                wide[b] = coupling_raw[at, b].astype(f32)
                for j in range(4):
                    d = []
                    for c in range(2):
                        rows = pl.ds(2 * j + c, 8, stride=8)
                        to = slice(16 * j + 8 * c, 16 * j + 8 * c + 8)
                        rhs_out[at, b, to, :] = rhs_raw[at, b, rows, :]
                        d.append(diag_raw[at, b, rows, :])
                        diag_out[at, b, to, :] = d[c]
                    pick = cross_raw[b, i // 8, pl.ds(8 * j + i % 8, 8, stride=32), :]
                    cross_out[at, b, 8 * j : 8 * j + 8, :] = pick * jnp.sqrt(d[0] * d[1])

            def slot(s, carry):
                for b in range(bands):
                    for j in range(4):
                        pick = wide[b, pl.ds(8 * j + s, 8, stride=32), :]
                        coupling_out[at, s, b, 8 * j : 8 * j + 8, :] = pick
                return carry

            return lax.fori_loop(0, graph[at], slot, carry)

        lax.fori_loop(0, size, step, 0)


def lane_sums():
    row = lax.broadcasted_iota(jnp.int32, (LANES, LANES), 0)
    col = lax.broadcasted_iota(jnp.int32, (LANES, LANES), 1)
    return ((row % KN) // PATCH == col % PATCH).astype(f32).astype(bf16)


def lane_spread():
    row = lax.broadcasted_iota(jnp.int32, (LANES, LANES), 0)
    col = lax.broadcasted_iota(jnp.int32, (LANES, LANES), 1)
    return ((col % KN) // PATCH == row % PATCH).astype(f32).astype(bf16)


def read_graph(offset_ref, graph):
    slot = lax.broadcasted_iota(jnp.int32, offset_ref.shape, 0)
    codes = jnp.sum(jnp.left_shift(offset_ref[...] + REACH, 4 * slot), axis=0, keepdims=True)
    for i in range(offset_ref.shape[1]):
        graph[i] = codes[0, i]


def step_to(code, s):
    return jnp.bitwise_and(jnp.right_shift(code, 4 * s), 15)


def group_mask(interior, slots):
    row = lax.broadcasted_iota(jnp.int32, (64, LANES), 0) // 32
    lane = lax.broadcasted_iota(jnp.int32, (64, LANES), 1) // PATCH
    return lane - slots * (1 - row if interior else row)


def disparities(interior, offset_ref, ext_ref, gathered, graph):
    bands = ext_ref.shape[1]
    granules = ext_ref.shape[0] - 2 * REACH
    slots = gathered.shape[0]
    gathered[...] = jnp.zeros_like(gathered)
    read_graph(offset_ref, graph)

    def response(g):
        return [
            ext_ref[g, b, 16 * j : 16 * j + 8, :] + ext_ref[g, b, 16 * j + 8 : 16 * j + 16, :]
            for b in range(bands)
            for j in range(4)
        ]

    for i in range(granules):
        if (REACH <= i < granules - REACH) != interior:
            continue
        own = response(i + REACH)
        code = graph[i]

        def slot(s, i=i, own=own, code=code):
            total = None
            for a, o in zip(own, response(i + step_to(code, s))):
                d = a - o
                total = d * d if total is None else total + d * d
            gathered[s, 8 * (i % 8) : 8 * (i % 8) + 8, :] = total

        for s in range(FIRST):
            slot(s)

        @pl.when(step_to(code, FIRST) != REACH)
        def _(slot=slot):
            for s in range(FIRST, slots):
                slot(s)

    sums = jnp.dot(
        gathered[...].reshape(slots * 64, LANES).astype(bf16), lane_sums(), preferred_element_type=f32
    )
    place = group_mask(interior, slots)
    packed = jnp.zeros((64, LANES), f32)
    for s in range(slots):
        packed = jnp.where(place == s, sums[64 * s : 64 * s + 64], packed)
    return packed


def interior_disparities(offset_ref, ext_ref, out_ref, *refs):
    packed = disparities(True, offset_ref, ext_ref, *refs[-2:])
    out_ref[...] = packed
    if len(refs) == 3:
        refs[0][...] = packed.astype(bf16)


def edge_disparities(offset_ref, near_ref, far_ref, *refs):
    ext_ref, out_ref, send_ref, gathered, graph = refs[-5:]
    odd = parity()
    right = ext_ref.shape[0] - REACH
    for ref, base in ((near_ref, (1 - odd) * right), (far_ref, odd * right)):
        for g in range(REACH):
            for b in range(ref.shape[1]):
                if ref.shape[2] == ext_ref.shape[2]:
                    ext_ref[base + g, b] = ref[g, b].astype(f32)
                    continue
                for j in range(4):
                    ext_ref[base + g, b, 16 * j : 16 * j + 8, :] = ref[g, b, 8 * j : 8 * j + 8, :].astype(f32)
                    ext_ref[base + g, b, 16 * j + 8 : 16 * j + 16, :] = jnp.zeros((8, LANES), f32)
    packed = disparities(False, offset_ref, ext_ref, gathered, graph)
    if len(refs) == 7:
        packed = packed + refs[1][...]
    out_ref[...] = packed
    send_ref[...] = packed.astype(bf16)


def spread_weights(shares, interior, weights):
    slots = weights.shape[0]
    total = shares[0][...]
    for share in shares[1:]:
        total = total + share[...].astype(f32)
    robust = 1.0 / (1.0 + total * (1.0 / (robust_scale * BANDS * PATCH * PATCH)))
    high = robust.astype(bf16).astype(f32)
    both = jnp.concatenate([high, robust - high], axis=1)
    place = group_mask(interior, slots)
    place = jnp.concatenate([place, place], axis=1)
    spread = lane_spread()
    spread = jnp.concatenate([spread, spread], axis=0)
    stacked = jnp.concatenate(
        [jnp.where(place == s, both, 0.0).astype(bf16) for s in range(slots)], axis=0
    )
    weights[...] = jnp.dot(stacked, spread, preferred_element_type=f32).reshape(slots, 64, LANES)


def balance(i, at, ext_ref, rhs_ref, diag_ref, cross_ref, coupling_ref, weights, graph, store):
    bands = rhs_ref.shape[1]
    row = pl.multiple_of(lax.rem(i, 8) * 8, 8)
    slots = weights.shape[0]
    parts = [(b, j) for b in range(bands) for j in range(4)]
    rows = [slice(8 * q, 8 * q + 8) for q in range(8)]
    rhs = tuple(rhs_ref[at, b, rows[2 * j + c], :] for b, j in parts for c in range(2))

    code = graph[i]

    def slot(slot_index, sums):
        sigma, drive = sums
        used = step_to(code, slot_index) != REACH
        s = jnp.where(used, slot_index, 0)
        weight = jnp.where(used, weights[s, pl.ds(row, 8), :], 0.0)
        n = i + step_to(code, s)
        new_sigma, new_drive = [], []
        for b in range(bands):
            for j in range(4):
                k = 4 * b + j
                effective = weight * coupling_ref[at, s, b, 8 * j : 8 * j + 8, :]
                new_sigma.append(sigma[k] + effective)
                for c in range(2):
                    grid = ext_ref[n, b, 16 * j + 8 * c : 16 * j + 8 * c + 8, :]
                    new_drive.append(drive[2 * k + c] + effective * grid)
        return tuple(new_sigma), tuple(new_drive)

    zero = jnp.zeros((8, LANES), f32)
    sums = ((zero,) * len(parts), rhs)
    for s in range(FIRST):
        sums = slot(s, sums)

    def others(_, sums):
        for s in range(FIRST, slots):
            sums = slot(s, sums)
        return sums

    sigma, drive = lax.fori_loop(0, (step_to(code, FIRST) != REACH).astype(jnp.int32), others, sums)
    for k, (b, j) in enumerate(parts):
        first, second = (
            diag_ref[at, b, rows[2 * j + c], :] + sigma[k] for c in range(2)
        )
        cross = cross_ref[at, b, 8 * j : 8 * j + 8, :]
        inverse = 1.0 / (first * second - cross * cross)
        gain, offset = drive[2 * k], drive[2 * k + 1]
        store(
            b,
            j,
            (second * gain - cross * offset) * inverse,
            (first * offset - cross * gain) * inverse,
        )


def edge_sweep(split, parted, offset_ref, *refs):
    shares, state, refs = refs[:4], refs[4:9], refs[9:]
    weights, graph = refs[-2:]
    odd = parity()
    if split:
        response_ref, gain_ref, kept_ref = refs[0], refs[1], refs[2]
        refs = refs[3:]
        state = (kept_ref,) + state[1:]
        base = (1 - odd) * (kept_ref.shape[0] - REACH)
        for g in range(REACH):
            for b in range(gain_ref.shape[1]):
                for j in range(4):
                    rows = slice(8 * j, 8 * j + 8)
                    gain = gain_ref[g, b, rows, :].astype(f32)
                    kept_ref[base + g, b, 16 * j : 16 * j + 8, :] = gain
                    offset = response_ref[g, b, rows, :].astype(f32) - gain
                    kept_ref[base + g, b, 16 * j + 8 : 16 * j + 16, :] = offset
    new_ref, far_ref = refs[:2]
    near_refs = refs[2:-2]
    read_graph(offset_ref, graph)
    spread_weights(shares, False, weights)
    last = new_ref.shape[0] - 3 * REACH
    for near, base in ((False, odd * last), (True, (1 - odd) * last)):

        def step(g, carry, near=near, base=base):
            def store(b, j, gain, offset):
                both = jnp.concatenate([gain, offset], axis=0)
                new_ref[base + g + REACH, b, 16 * j : 16 * j + 16, :] = both
                if near and parted:
                    near_refs[0][g, b, 8 * j : 8 * j + 8, :] = (gain + offset).astype(bf16)
                    near_refs[1][g, b, 8 * j : 8 * j + 8, :] = gain.astype(bf16)
                else:
                    ref = near_refs[0] if near else far_ref
                    ref[g, b, 16 * j : 16 * j + 16, :] = both.astype(bf16)

            balance(base + g, lax.div(base, 2 * REACH) * REACH + g, *state, weights, graph, store)
            return carry

        lax.fori_loop(0, REACH, step, 0)


def interior_sweep(offset_ref, *refs):
    shares, state, (_, new_ref, weights, graph) = refs[:4], refs[4:9], refs[9:]
    read_graph(offset_ref, graph)
    spread_weights(shares, True, weights)

    def step(i, carry):
        def store(b, j, gain, offset):
            both = jnp.concatenate([gain, offset], axis=0)
            new_ref[i + REACH, b, 16 * j : 16 * j + 16, :] = both

        balance(i, i - REACH, *state, weights, graph, store)
        return carry

    lax.fori_loop(REACH, new_ref.shape[0] - 3 * REACH, step, 0)


def own_columns(ref, at, granules):
    first = lax.axis_index("gran") * granules
    base = pl.multiple_of((first // LANES) * LANES, LANES)
    turn = jnp.bitwise_and(LANES - lax.rem(first, LANES), LANES - 1)
    return pltpu.roll(ref[at + (pl.ds(base, LANES),)], turn, 1)


def last_sweep(interior, offset_ref, *refs):
    shares, state, place_ref = refs[:4], refs[4:9], refs[9]
    weights, graph = refs[-2:]
    if interior:
        solved, windows = refs[10:12]
    else:
        solved, send_ref, windows = refs[12:15]
    granules, bands = solved.shape[:2]
    read_graph(offset_ref, graph)
    if interior:
        windows[...] = jnp.zeros_like(windows)
    spread_weights(shares, interior, weights)

    def step(t, carry):
        i = t if interior else jnp.where(t < REACH, t, t + granules - 2 * REACH)

        def store(b, j, gain, offset):
            solved[i, b, pl.ds(2 * j, 8, stride=8), :] = gain
            solved[i, b, pl.ds(2 * j + 1, 8, stride=8), :] = offset

        balance(i, t - REACH if interior else t, *state, weights, graph, store)
        return carry

    lax.fori_loop(*((REACH, granules - REACH) if interior else (0, 2 * REACH)), step, 0)
    lane = lax.broadcasted_iota(jnp.int32, (8, LANES), 1) // SPAN
    seats = LANES // SPAN
    places = place_ref[...]
    for i in visits(granules, interior):
        for r in range(2):
            owner, rank, top, turn = (places[k, r * granules + i] for k in range(4))
            here = [lane == jnp.bitwise_and(rank + half * (KN // SPAN), seats - 1) for half in (0, 1)]
            for b in range(bands):
                for c in range(2):
                    rows = solved[i, b, pl.ds(2 * top + c, 8, stride=2), :]
                    moved = pltpu.roll(rows, jnp.bitwise_and(turn, LANES - 1), 1)
                    for half in (0, 1):
                        at = 16 * (2 * b + c) + 8 * half
                        pltpu.store(windows.at[owner, at : at + 8, :], moved, mask=here[half])
    if not interior:
        for owner in range(windows.shape[0]):
            for at in range(0, windows.shape[1], 16):
                odd = pltpu.roll(windows[owner, at + 8 : at + 16, :], KN, 1)
                both = jnp.concatenate([windows[owner, at : at + 8, :], odd], axis=0)
                send_ref[owner, at : at + 16, :] = both.astype(bf16)


def earlier(first, second, granules):
    def edge(i):
        return ((i < REACH) | (i >= granules - REACH)).astype(jnp.int32)

    def rank(entry):
        return (edge(entry[1]) * 2 + entry[0]) * granules + entry[1]

    return rank(first) < rank(second)


def spread_columns(row):
    return jnp.transpose(jnp.broadcast_to(row, (LANES, LANES)))


def tile_places(route_ref, window_ref, rows_out, cols_out, place_ref):
    pixels, lanes = rows_out.shape
    senders = lanes // LANES
    granules = route_ref.shape[1] // senders
    own = lax.axis_index("gran")
    lane_row = lax.broadcasted_iota(jnp.int32, (1, LANES), 1)

    def both_routes(rows):
        return jnp.where(lane_row < granules, rows[0:1], pltpu.roll(rows, granules, 1)[1:2])

    routes = own_columns(route_ref, (slice(None),), granules)
    starts = [own_columns(window_ref, (r, slice(None)), granules) for r in range(2)]
    named = both_routes(routes).astype(f32)
    col = lax.broadcasted_iota(jnp.int32, (LANES, LANES), 1)
    row = lax.broadcasted_iota(jnp.int32, (LANES, LANES), 0)
    before = earlier((row // granules, row % granules), (col // granules, col % granules), granules)
    before = before & (row < 2 * granules) & (spread_columns(named) == named)
    rank = jnp.sum(before.astype(f32), axis=0, keepdims=True).astype(jnp.int32)
    knots = [
        jnp.clip(jnp.right_shift(both_routes(jnp.concatenate([s[k : k + 1] for s in starts])), 5) - 1, 0, KN - SPAN)
        for k in range(2)
    ]
    turn = rank * SPAN - knots[1] + LANES
    place_ref[...] = jnp.concatenate(
        [named.astype(jnp.int32), rank, jnp.right_shift(knots[0], 1), turn] * 2, axis=0
    )

    wide = 2 * LANES
    col = lax.broadcasted_iota(jnp.int32, (wide, wide), 1)
    row = lax.broadcasted_iota(jnp.int32, (wide, wide), 0)
    route = [at // LANES for at in (row, col)]
    place = [at % LANES for at in (row, col)]
    before = earlier((route[0], place[0] % granules), (route[1], place[1] % granules), granules)
    before = before & (place[0] // granules == place[1] // granules)
    before = before.astype(f32).astype(bf16)
    seat = (lax.broadcasted_iota(jnp.int32, (LANES, LANES), 1) // SPAN).astype(f32)
    lane = lax.broadcasted_iota(jnp.int32, (8, LANES), 1)
    step = lane % SPAN
    pixel = lax.broadcasted_iota(jnp.int32, (8, LANES), 0).astype(f32) * (1.0 / SP)
    part = LANES // granules
    for t in range(route_ref.shape[1] // LANES):
        at = slice(t * LANES, (t + 1) * LANES)
        hits = [(route_ref[r : r + 1, at] == own).astype(f32) for r in range(2)]
        hits = jnp.broadcast_to(jnp.concatenate(hits, axis=1), (8, wide))
        ranks = jnp.dot(hits.astype(bf16), before, preferred_element_type=f32)
        ranks = jnp.where(hits > 0.5, ranks, -1.0)
        chosen, values = [], []
        for r in range(2):
            chosen.append((spread_columns(ranks[0:1, r * LANES : (r + 1) * LANES]) == seat).astype(f32).astype(bf16))
            sender = lax.broadcasted_iota(jnp.int32, (part, LANES), 0)
            within = lax.broadcasted_iota(jnp.int32, (part, LANES), 1) // granules == sender
            kinds = []
            for k in range(2):
                start = window_ref[r, k : k + 1, at]
                kinds += [jnp.right_shift(start, 5), jnp.bitwise_and(start, SP - 1)]
            kinds.append(jnp.ones((1, LANES), jnp.int32))
            values.append(jnp.concatenate([jnp.where(within, kind, 0).astype(f32) for kind in kinds], axis=0))
        found = jnp.dot(
            jnp.concatenate(values, axis=1).astype(bf16),
            jnp.concatenate(chosen, axis=0),
            preferred_element_type=f32,
        )
        for n in range(part):
            live = found[4 * part + n : 4 * part + n + 1] > 0.5
            for k, ref in ((0, rows_out), (1, cols_out)):
                base = found[2 * k * part + n : 2 * k * part + n + 1]
                rest = found[(2 * k + 1) * part + n : (2 * k + 1) * part + n + 1]
                first = jnp.clip(base.astype(jnp.int32) - 1, 0, KN - SPAN)
                if k == 0:
                    knot = 2 * jnp.right_shift(first, 1) + 2 * (step % 8) + step // 8
                else:
                    knot = first + step
                border = (knot == 0) | (knot == KN - 1)
                cube = jnp.where(border, 1.0, 1.5)
                square = jnp.where(border, -1.5, -2.5)
                single = jnp.where(border, -0.5, 0.0)
                away = jnp.where(live, base + rest * (1.0 / SP) - knot.astype(f32), 4.0 * KN)
                away = away + pixel
                to = pl.ds((t * part + n) * LANES, LANES)
                for q in range(0, pixels, 16):
                    pair = []
                    for p in (q, q + 8):
                        d = jnp.abs(away + p * (1.0 / SP))
                        near = ((cube * d + square) * d + single) * d + 1.0
                        far = ((2.5 - 0.5 * d) * d - 4.0) * d + 2.0
                        pair.append(jnp.where(d <= 1.0, near, jnp.where(d < 2.0, far, 0.0)))
                    ref[q : q + 16, to] = jnp.concatenate(pair, axis=0).astype(bf16)


def compose(route_ref, received_ref, row_ref, col_ref, pixels_ref, solved, out_ref, grids_out, passed, result, sems):
    copies = [pltpu.make_async_copy(solved, grids_out, sems.at[result.shape[0]])]
    copies[0].start()
    senders = received_ref.shape[0]
    bands = result.shape[0]
    lane = lax.broadcasted_iota(jnp.int32, (16, LANES), 1) // SPAN
    masks = [(lane == r).astype(f32).astype(bf16) for r in range(LANES // SPAN)]
    named = (route_ref[...] == lax.axis_index("gran")).astype(f32)
    scale = 1.0 / jnp.sum(named, keepdims=True)

    def sender(n, carry):
        at = pl.ds(pl.multiple_of(n * LANES, LANES), LANES)
        blocks = []
        for k in range(2 * bands):
            window = received_ref[n, 16 * k : 16 * k + 16, :]
            blocks.append(jnp.concatenate([window * mask for mask in masks], axis=0))
        rows = jnp.dot(row_ref[:, at], jnp.concatenate(blocks, axis=1), preferred_element_type=f32)
        for k in range(2 * bands):
            passed[k, :, at] = rows[:, LANES * k : LANES * k + LANES].astype(bf16)
        return carry

    steps = min(8, senders)

    def several(n, carry):
        for k in range(steps):
            sender(n * steps + k, carry)
        return carry

    if senders == steps:
        several(0, 0)
    else:
        lax.fori_loop(0, senders // steps, several, 0)
    for b in range(bands):
        fields = [
            lax.dot_general(
                passed[2 * b + c], col_ref[...], (((1,), (1,)), ((), ())), preferred_element_type=f32
            )
            * scale
            for c in range(2)
        ]
        pixels = pixels_ref[0, b].astype(f32)
        result[b] = (pixels * (1.0 + fields[0]) + fields[1]).astype(bf16)
        copies.append(pltpu.make_async_copy(result.at[b], out_ref.at[0, b], sems.at[b]))
        copies[-1].start()
    for copy in copies:
        copy.wait()


def per_device(
    prior_grids,
    pif_rhs,
    pif_diagonal,
    pif_cross,
    pif_coupling,
    neighbour_offset,
    neighbour_count,
    tile_route,
    tile_window,
    tile_pixels,
):
    granules, bands = prior_grids.shape[:2]
    slots = pif_coupling.shape[1]
    pixel_count = tile_pixels.shape[2]
    device_total = lax.axis_size("gran")
    band_total = lax.axis_size("band")

    def by_lane_tile(array):
        cut = array.reshape(array.shape[:2] + (array.shape[2], 32, LANES)).transpose(0, 1, 3, 2, 4)
        return cut.reshape(array.shape[:2] + (32 * array.shape[2], LANES))

    grids = by_lane_tile(prior_grids)
    rhs = by_lane_tile(pif_rhs)
    diagonal = by_lane_tile(pif_diagonal)
    cross = by_lane_tile(pif_cross.transpose(1, 0, 2).reshape(bands, granules // 8, 8, KN * KN))
    coupling = by_lane_tile(pif_coupling.transpose(0, 2, 1, 3))
    graph = [("v", neighbour_offset.T)]
    tiles = [("v", tile_route.T), ("v", tile_window.transpose(1, 2, 0))]
    edge = (REACH, bands, 64, LANES)
    own = (granules, bands, 64, LANES)
    ext = (granules + 2 * REACH, bands, 64, LANES)
    packed = [("v", (64, LANES), f32), ("v", (64, LANES), bf16)]
    chunks = 4

    near_pairs = [(i, i ^ 1) for i in range(device_total)]
    far_pairs = [
        pair for i in range(1, device_total - 1, 2) for pair in ((i, i + 1), (i + 1, i))
    ]

    def exchange(near, far):
        far = lax.ppermute(far, "gran", far_pairs)
        near = lax.ppermute(near, "gran", near_pairs)
        return near, far

    near, far = call(
        first_edges,
        [("h", grids)],
        [("v", edge, bf16), ("v", edge, bf16)],
        [pltpu.VMEM((2,) + edge, f32), pltpu.SemaphoreType.DMA((2, REACH))],
    )
    near, far = exchange(near, far)
    (extended,) = call(
        arrange_grids,
        [("h", grids)],
        [("v", ext, f32)],
        [pltpu.VMEM(own, f32), pltpu.SemaphoreType.DMA((chunks,))],
    )
    sources = [rhs, diagonal, cross, coupling]

    def arranged(interior, sources):
        part = len(visits(granules, interior))
        some = (part, bands, 64, LANES)
        return call(
            functools.partial(arrange, interior),
            [("v", neighbour_count[None, :])] + [("h", source) for source in sources],
            [
                ("v", some, f32),
                ("v", some, f32),
                ("v", (part, bands, 32, LANES), f32),
                ("v", (part, slots, bands, 32, LANES), f32),
            ],
            [
                pltpu.VMEM(some, f32),
                pltpu.VMEM(some, f32),
                pltpu.VMEM(cross.shape, f32),
                pltpu.VMEM((part,) + coupling.shape[1:], bf16),
                pltpu.VMEM(coupling.shape[1:], f32),
                pltpu.SMEM((part,), jnp.int32),
                pltpu.SemaphoreType.DMA((4, chunks)),
            ],
        )

    gathered = pltpu.VMEM((slots, 64, LANES), f32)
    weights = pltpu.VMEM((slots, 64, LANES), f32)
    scalars = pltpu.SMEM((granules,), jnp.int32)

    def over_band(partial, rounded):
        return [("v", partial)] + [
            ("v", lax.ppermute(rounded, "band", [(i, i ^ flip) for i in range(band_total)]))
            for flip in range(1, band_total)
        ]

    for sweep in range(SWEEPS):
        last = sweep == SWEEPS - 1
        inner, *inner_rounded = call(
            interior_disparities,
            graph + [("v", extended)],
            packed if last else packed[:1],
            [gathered, scalars],
        )
        if sweep == PARTED + 1:
            inner, *gains = lax.optimization_barrier((inner, *gains))
        if sweep == 0:
            inner, *edge_state = lax.optimization_barrier((inner, *arranged(False, sources)))
        if last:
            inner_shares = over_band(inner, *inner_rounded)
        inputs = graph + [("v", near), ("v", far), ("v", extended)]
        inputs += [] if last else [("v", inner)]
        extended, partial, rounded = call(
            edge_disparities,
            inputs,
            [("v", ext, f32)] + packed,
            [gathered, scalars],
            aliases={3: 0},
        )
        shares = over_band(partial, rounded)
        if sweep == PARTED + 1:
            near_gain = lax.ppermute(gains[0], "gran", near_pairs)
        if sweep == 1:
            routes, starts, _ = lax.optimization_barrier((tiles[0][1], tiles[1][1], partial))
            weight_shape = ("v", (pixel_count, device_total * LANES), bf16)
            made = call(
                tile_places,
                [("v", routes), ("v", starts)],
                [weight_shape, weight_shape, ("v", (8, LANES), jnp.int32)],
            )
            partial, row_weights, col_weights, places = lax.optimization_barrier((partial, *made))
            shares[0] = ("v", partial)
        edge_state_now = [("v", extended)] + [("v", array) for array in edge_state]
        if not last:
            inputs = graph + shares + edge_state_now
            parted = sweep == PARTED
            split = sweep == PARTED + 1
            half = ("v", (REACH, bands, 32, LANES), bf16)
            outputs = [("v", ext, f32), ("v", edge, bf16)] + ([half] * 2 if parted else [("v", edge, bf16)])
            aliases = {}
            if split:
                inputs = inputs + [("v", near), ("v", near_gain)]
                outputs = [("v", ext, f32)] + outputs
                aliases = {len(graph + shares): 0}
            made = call(
                functools.partial(edge_sweep, split, parted),
                inputs,
                outputs,
                [weights, scalars],
                aliases=aliases,
            )
            if split:
                extended, *made = made
            updated, far, near, *gains = made
            near, far = exchange(near, far)
            if sweep == 0:
                *later, updated = lax.optimization_barrier((*sources, updated))
                inner_state = [("v", array) for array in arranged(True, later)]
            inputs = graph + shares + [("v", extended)] + inner_state
            (extended,) = call(
                interior_sweep,
                inputs + [("v", updated)],
                [("v", ext, f32)],
                [weights, scalars],
                aliases={len(inputs): 0},
            )
    windows = (device_total, 2 * bands * SPAN, LANES)
    scratch = [weights, scalars]
    inputs = graph + inner_shares + [("v", extended)] + inner_state + [("v", places)]
    balanced, gathered_windows = call(
        functools.partial(last_sweep, True),
        inputs,
        [("v", own, f32), ("v", windows, f32)],
        scratch,
    )
    inputs = graph + shares + edge_state_now + [("v", places)] + [("v", balanced), ("v", gathered_windows)]
    balanced, payload, _ = call(
        functools.partial(last_sweep, False),
        inputs,
        [("v", own, f32), ("v", windows, bf16), ("v", windows, f32)],
        scratch,
        aliases={len(inputs) - 2: 0, len(inputs) - 1: 2},
    )
    received = lax.all_to_all(payload, "gran", split_axis=0, concat_axis=0, tiled=True)
    inputs = [tiles[0], ("v", received), ("v", row_weights), ("v", col_weights), ("v", tile_pixels)]
    corrected, balanced = call(
        compose,
        inputs + [("v", balanced)],
        [("h", tile_pixels.shape, bf16), ("h", own, f32)],
        [
            pltpu.VMEM((2 * bands, pixel_count, device_total * LANES), bf16),
            pltpu.VMEM(tile_pixels.shape[1:], bf16),
            pltpu.SemaphoreType.DMA((bands + 1,)),
        ],
        limit=32,
    )
    balanced = balanced.reshape(granules, bands, 32, 2, LANES).transpose(0, 1, 3, 2, 4)
    return (balanced.reshape(prior_grids.shape), corrected)


def solution(mesh):
    placed = (
        P("gran", "band", None, None),
        P("gran", "band", None, None),
        P("gran", "band", None, None),
        P("gran", "band", None),
        P("gran", None, "band", None),
        P("gran", None),
        P("gran"),
        P(),
        P(),
        P("gran", "band", None, None),
    )
    return jax.shard_map(
        per_device,
        mesh=mesh,
        in_specs=placed,
        out_specs=(P("gran", "band", None, None), P("gran", "band", None, None)),
        check_vma=False,
    )
```

```python
import functools
import jax
import jax.numpy as jnp
from jax import lax
from jax.experimental import pallas as pl
from jax.experimental.pallas import tpu as pltpu
from jax.sharding import PartitionSpec as P

BANDS = 12
KN = 64
PATCH = 8
REACH = 4
SWEEPS = 3
SP = 32
LANES = 128
SPAN = 16
PARTED = 0
FIRST = 3

robust_scale = 0.3

ON_CHIP = pl.BlockSpec(memory_space=pltpu.VMEM)
ANYWHERE = pl.BlockSpec(memory_space=pl.ANY)
f32 = jnp.float32
bf16 = jnp.bfloat16


def call(body, inputs, outputs, scratch=(), aliases=None, limit=16):
    operands = [
        pltpu.with_memory_space_constraint(array, pltpu.VMEM if kind == "v" else pltpu.HBM)
        for kind, array in inputs
    ]
    return pl.pallas_call(
        body,
        in_specs=[ON_CHIP if kind == "v" else ANYWHERE for kind, _ in inputs],
        out_specs=tuple(ON_CHIP if kind == "v" else ANYWHERE for kind, _, _ in outputs),
        out_shape=tuple(
            (pltpu.VMEM if kind == "v" else pltpu.HBM)(shape, dtype)
            for kind, shape, dtype in outputs
        ),
        scratch_shapes=list(scratch),
        input_output_aliases=aliases or {},
        compiler_params=pltpu.CompilerParams(vmem_limit_bytes=limit * 2**20),
    )(*operands)


def parity():
    return lax.rem(lax.axis_index("gran"), 2)


def first_edges(grids_ref, near_ref, far_ref, raw, sems):
    odd = parity()
    last = grids_ref.shape[0] - REACH
    sides = ((far_ref, odd * last), (near_ref, (1 - odd) * last))
    copies = [
        [pltpu.make_async_copy(grids_ref.at[base + g], raw.at[k, g], sems.at[k, g]) for g in range(REACH)]
        for k, (_, base) in enumerate(sides)
    ]
    for copy in copies[0] + copies[1]:
        copy.start()
    for k, (ref, _) in enumerate(sides):
        for g in range(REACH):
            copies[k][g].wait()
            for b in range(ref.shape[1]):
                for j in range(4):
                    both = [raw[k, g, b, pl.ds(2 * j + c, 8, stride=8), :] for c in range(2)]
                    ref[g, b, 16 * j : 16 * j + 16, :] = jnp.concatenate(both, axis=0).astype(bf16)


def arrange_grids(grids_ref, ext_ref, raw, sems):
    granules, bands = grids_ref.shape[:2]
    chunks = sems.shape[0]
    size = granules // chunks
    copies = []
    for n in range(chunks):
        part = pl.ds(n * size, size)
        copies.append(pltpu.make_async_copy(grids_ref.at[part], raw.at[part], sems.at[n]))
        copies[n].start()

    def step(i, carry):
        for b in range(bands):
            for q in range(8):
                ext_ref[i + REACH, b, 8 * q : 8 * q + 8, :] = raw[i, b, pl.ds(q, 8, stride=8), :]
        return carry

    for n in range(chunks):
        copies[n].wait()
        lax.fori_loop(n * size, (n + 1) * size, step, 0)


def visits(granules, interior):
    inner = list(range(REACH, granules - REACH))
    return inner if interior else [i for i in range(granules) if i not in inner]


def arrange(interior, count_ref, rhs_ref, diag_ref, cross_ref, coupling_ref, rhs_out, diag_out, cross_out, coupling_out, rhs_raw, diag_raw, cross_raw, coupling_raw, wide, graph, sems):
    granules, bands = rhs_ref.shape[:2]
    own = visits(granules, interior)
    size = REACH
    chunks = len(own) // size
    copies = []
    for n in range(chunks):
        source, target = pl.ds(own[n * size], size), pl.ds(n * size, size)
        moves = ((coupling_ref, coupling_raw), (diag_ref, diag_raw), (rhs_ref, rhs_raw))
        copies.append(
            [
                pltpu.make_async_copy(here.at[source], there.at[target], sems.at[k, n])
                for k, (here, there) in enumerate(moves)
            ]
        )
        for copy in copies[n]:
            copy.start()
        if n == 0:
            whole = pltpu.make_async_copy(cross_ref, cross_raw, sems.at[3, 0])
            whole.start()
    for i, count in enumerate(visits(granules, interior)):
        graph[i] = count_ref[...][0, count]
    for n in range(chunks):
        for copy in copies[n]:
            copy.wait()
        if n == 0:
            whole.wait()

        def step(g, carry, n=n):
            at = n * size + g
            i = own[n * size] + g
            for b in range(bands):
                wide[b] = coupling_raw[at, b].astype(f32)
                for j in range(4):
                    d = []
                    for c in range(2):
                        rows = pl.ds(2 * j + c, 8, stride=8)
                        to = slice(16 * j + 8 * c, 16 * j + 8 * c + 8)
                        rhs_out[at, b, to, :] = rhs_raw[at, b, rows, :]
                        d.append(diag_raw[at, b, rows, :])
                        diag_out[at, b, to, :] = d[c]
                    pick = cross_raw[b, i // 8, pl.ds(8 * j + i % 8, 8, stride=32), :]
                    cross_out[at, b, 8 * j : 8 * j + 8, :] = pick * jnp.sqrt(d[0] * d[1])

            def slot(s, carry):
                for b in range(bands):
                    for j in range(4):
                        pick = wide[b, pl.ds(8 * j + s, 8, stride=32), :]
                        coupling_out[at, s, b, 8 * j : 8 * j + 8, :] = pick
                return carry

            return lax.fori_loop(0, graph[at], slot, carry)

        lax.fori_loop(0, size, step, 0)


def lane_sums():
    row = lax.broadcasted_iota(jnp.int32, (LANES, LANES), 0)
    col = lax.broadcasted_iota(jnp.int32, (LANES, LANES), 1)
    return ((row % KN) // PATCH == col % PATCH).astype(f32).astype(bf16)


def lane_spread():
    row = lax.broadcasted_iota(jnp.int32, (LANES, LANES), 0)
    col = lax.broadcasted_iota(jnp.int32, (LANES, LANES), 1)
    return ((col % KN) // PATCH == row % PATCH).astype(f32).astype(bf16)


def read_graph(offset_ref, graph):
    slot = lax.broadcasted_iota(jnp.int32, offset_ref.shape, 0)
    codes = jnp.sum(jnp.left_shift(offset_ref[...] + REACH, 4 * slot), axis=0, keepdims=True)
    for i in range(offset_ref.shape[1]):
        graph[i] = codes[0, i]


def step_to(code, s):
    return jnp.bitwise_and(jnp.right_shift(code, 4 * s), 15)


def group_mask(interior, slots):
    row = lax.broadcasted_iota(jnp.int32, (64, LANES), 0) // 32
    lane = lax.broadcasted_iota(jnp.int32, (64, LANES), 1) // PATCH
    return lane - slots * (1 - row if interior else row)


def disparities(interior, offset_ref, ext_ref, gathered, graph):
    bands = ext_ref.shape[1]
    granules = ext_ref.shape[0] - 2 * REACH
    slots = gathered.shape[0]
    gathered[...] = jnp.zeros_like(gathered)
    read_graph(offset_ref, graph)

    def response(g):
        return [
            ext_ref[g, b, 16 * j : 16 * j + 8, :] + ext_ref[g, b, 16 * j + 8 : 16 * j + 16, :]
            for b in range(bands)
            for j in range(4)
        ]

    for i in range(granules):
        if (REACH <= i < granules - REACH) != interior:
            continue
        own = response(i + REACH)
        code = graph[i]

        def slot(s, i=i, own=own, code=code):
            total = None
            for a, o in zip(own, response(i + step_to(code, s))):
                d = a - o
                total = d * d if total is None else total + d * d
            gathered[s, 8 * (i % 8) : 8 * (i % 8) + 8, :] = total

        for s in range(FIRST):
            slot(s)

        @pl.when(step_to(code, FIRST) != REACH)
        def _(slot=slot):
            for s in range(FIRST, slots):
                slot(s)

    sums = jnp.dot(
        gathered[...].reshape(slots * 64, LANES).astype(bf16), lane_sums(), preferred_element_type=f32
    )
    place = group_mask(interior, slots)
    packed = jnp.zeros((64, LANES), f32)
    for s in range(slots):
        packed = jnp.where(place == s, sums[64 * s : 64 * s + 64], packed)
    return packed


def interior_disparities(offset_ref, ext_ref, out_ref, *refs):
    packed = disparities(True, offset_ref, ext_ref, *refs[-2:])
    out_ref[...] = packed
    if len(refs) == 3:
        refs[0][...] = packed.astype(bf16)


def edge_disparities(offset_ref, near_ref, far_ref, *refs):
    ext_ref, out_ref, send_ref, gathered, graph = refs[-5:]
    odd = parity()
    right = ext_ref.shape[0] - REACH
    for ref, base in ((near_ref, (1 - odd) * right), (far_ref, odd * right)):
        for g in range(REACH):
            for b in range(ref.shape[1]):
                if ref.shape[2] == ext_ref.shape[2]:
                    ext_ref[base + g, b] = ref[g, b].astype(f32)
                    continue
                for j in range(4):
                    ext_ref[base + g, b, 16 * j : 16 * j + 8, :] = ref[g, b, 8 * j : 8 * j + 8, :].astype(f32)
                    ext_ref[base + g, b, 16 * j + 8 : 16 * j + 16, :] = jnp.zeros((8, LANES), f32)
    packed = disparities(False, offset_ref, ext_ref, gathered, graph)
    if len(refs) == 7:
        packed = packed + refs[1][...]
    out_ref[...] = packed
    send_ref[...] = packed.astype(bf16)


def spread_weights(shares, interior, weights):
    slots = weights.shape[0]
    total = shares[0][...]
    for share in shares[1:]:
        total = total + share[...].astype(f32)
    robust = 1.0 / (1.0 + total * (1.0 / (robust_scale * BANDS * PATCH * PATCH)))
    high = robust.astype(bf16).astype(f32)
    both = jnp.concatenate([high, robust - high], axis=1)
    place = group_mask(interior, slots)
    place = jnp.concatenate([place, place], axis=1)
    spread = lane_spread()
    spread = jnp.concatenate([spread, spread], axis=0)
    stacked = jnp.concatenate(
        [jnp.where(place == s, both, 0.0).astype(bf16) for s in range(slots)], axis=0
    )
    weights[...] = jnp.dot(stacked, spread, preferred_element_type=f32).reshape(slots, 64, LANES)


def balance(i, at, ext_ref, rhs_ref, diag_ref, cross_ref, coupling_ref, weights, graph, store):
    bands = rhs_ref.shape[1]
    row = pl.multiple_of(lax.rem(i, 8) * 8, 8)
    slots = weights.shape[0]
    parts = [(b, j) for b in range(bands) for j in range(4)]
    rows = [slice(8 * q, 8 * q + 8) for q in range(8)]
    rhs = tuple(rhs_ref[at, b, rows[2 * j + c], :] for b, j in parts for c in range(2))

    code = graph[i]

    def slot(slot_index, sums):
        sigma, drive = sums
        used = step_to(code, slot_index) != REACH
        s = jnp.where(used, slot_index, 0)
        weight = jnp.where(used, weights[s, pl.ds(row, 8), :], 0.0)
        n = i + step_to(code, s)
        new_sigma, new_drive = [], []
        for b in range(bands):
            for j in range(4):
                k = 4 * b + j
                effective = weight * coupling_ref[at, s, b, 8 * j : 8 * j + 8, :]
                new_sigma.append(sigma[k] + effective)
                for c in range(2):
                    grid = ext_ref[n, b, 16 * j + 8 * c : 16 * j + 8 * c + 8, :]
                    new_drive.append(drive[2 * k + c] + effective * grid)
        return tuple(new_sigma), tuple(new_drive)

    zero = jnp.zeros((8, LANES), f32)
    sums = ((zero,) * len(parts), rhs)
    for s in range(FIRST):
        sums = slot(s, sums)

    def others(_, sums):
        for s in range(FIRST, slots):
            sums = slot(s, sums)
        return sums

    sigma, drive = lax.fori_loop(0, (step_to(code, FIRST) != REACH).astype(jnp.int32), others, sums)
    for k, (b, j) in enumerate(parts):
        first, second = (
            diag_ref[at, b, rows[2 * j + c], :] + sigma[k] for c in range(2)
        )
        cross = cross_ref[at, b, 8 * j : 8 * j + 8, :]
        inverse = 1.0 / (first * second - cross * cross)
        gain, offset = drive[2 * k], drive[2 * k + 1]
        store(
            b,
            j,
            (second * gain - cross * offset) * inverse,
            (first * offset - cross * gain) * inverse,
        )


def edge_sweep(split, parted, offset_ref, *refs):
    shares, state, refs = refs[:4], refs[4:9], refs[9:]
    weights, graph = refs[-2:]
    odd = parity()
    if split:
        response_ref, gain_ref, kept_ref = refs[0], refs[1], refs[2]
        refs = refs[3:]
        state = (kept_ref,) + state[1:]
        base = odd * (kept_ref.shape[0] - REACH)
        for g in range(REACH):
            for b in range(gain_ref.shape[1]):
                for j in range(4):
                    rows = slice(8 * j, 8 * j + 8)
                    gain = gain_ref[g, b, rows, :].astype(f32)
                    kept_ref[base + g, b, 16 * j : 16 * j + 8, :] = gain
                    offset = response_ref[g, b, rows, :].astype(f32) - gain
                    kept_ref[base + g, b, 16 * j + 8 : 16 * j + 16, :] = offset
    new_ref, near_ref = refs[:2]
    far_refs = refs[2:-2]
    read_graph(offset_ref, graph)
    spread_weights(shares, False, weights)
    last = new_ref.shape[0] - 3 * REACH
    for near, base in ((False, odd * last), (True, (1 - odd) * last)):

        def step(g, carry, near=near, base=base):
            def store(b, j, gain, offset):
                both = jnp.concatenate([gain, offset], axis=0)
                new_ref[base + g + REACH, b, 16 * j : 16 * j + 16, :] = both
                if parted and not near:
                    far_refs[0][g, b, 8 * j : 8 * j + 8, :] = (gain + offset).astype(bf16)
                    far_refs[1][g, b, 8 * j : 8 * j + 8, :] = gain.astype(bf16)
                else:
                    ref = near_ref if near else far_refs[0]
                    ref[g, b, 16 * j : 16 * j + 16, :] = both.astype(bf16)

            balance(base + g, lax.div(base, 2 * REACH) * REACH + g, *state, weights, graph, store)
            return carry

        lax.fori_loop(0, REACH, step, 0)


def interior_sweep(offset_ref, *refs):
    shares, state, (_, new_ref, weights, graph) = refs[:4], refs[4:9], refs[9:]
    read_graph(offset_ref, graph)
    spread_weights(shares, True, weights)

    def step(i, carry):
        def store(b, j, gain, offset):
            both = jnp.concatenate([gain, offset], axis=0)
            new_ref[i + REACH, b, 16 * j : 16 * j + 16, :] = both

        balance(i, i - REACH, *state, weights, graph, store)
        return carry

    lax.fori_loop(REACH, new_ref.shape[0] - 3 * REACH, step, 0)


def own_columns(ref, at, granules):
    first = lax.axis_index("gran") * granules
    base = pl.multiple_of((first // LANES) * LANES, LANES)
    turn = jnp.bitwise_and(LANES - lax.rem(first, LANES), LANES - 1)
    return pltpu.roll(ref[at + (pl.ds(base, LANES),)], turn, 1)


def last_sweep(interior, offset_ref, *refs):
    shares, state, place_ref = refs[:4], refs[4:9], refs[9]
    weights, graph = refs[-2:]
    if interior:
        solved, windows = refs[10:12]
    else:
        solved, send_ref, windows = refs[12:15]
    granules, bands = solved.shape[:2]
    read_graph(offset_ref, graph)
    if interior:
        windows[...] = jnp.zeros_like(windows)
    spread_weights(shares, interior, weights)

    def step(t, carry):
        i = t if interior else jnp.where(t < REACH, t, t + granules - 2 * REACH)

        def store(b, j, gain, offset):
            solved[i, b, pl.ds(2 * j, 8, stride=8), :] = gain
            solved[i, b, pl.ds(2 * j + 1, 8, stride=8), :] = offset

        balance(i, t - REACH if interior else t, *state, weights, graph, store)
        return carry

    lax.fori_loop(*((REACH, granules - REACH) if interior else (0, 2 * REACH)), step, 0)
    lane = lax.broadcasted_iota(jnp.int32, (8, LANES), 1) // SPAN
    seats = LANES // SPAN
    places = place_ref[...]
    for i in visits(granules, interior):
        for r in range(2):
            owner, rank, top, turn = (places[k, r * granules + i] for k in range(4))
            here = [lane == jnp.bitwise_and(rank + half * (KN // SPAN), seats - 1) for half in (0, 1)]
            for b in range(bands):
                for c in range(2):
                    rows = solved[i, b, pl.ds(2 * top + c, 8, stride=2), :]
                    moved = pltpu.roll(rows, jnp.bitwise_and(turn, LANES - 1), 1)
                    for half in (0, 1):
                        at = 16 * (2 * b + c) + 8 * half
                        pltpu.store(windows.at[owner, at : at + 8, :], moved, mask=here[half])
    if not interior:
        for owner in range(windows.shape[0]):
            for at in range(0, windows.shape[1], 16):
                odd = pltpu.roll(windows[owner, at + 8 : at + 16, :], KN, 1)
                both = jnp.concatenate([windows[owner, at : at + 8, :], odd], axis=0)
                send_ref[owner, at : at + 16, :] = both.astype(bf16)


def earlier(first, second, granules):
    def edge(i):
        return ((i < REACH) | (i >= granules - REACH)).astype(jnp.int32)

    def rank(entry):
        return (edge(entry[1]) * 2 + entry[0]) * granules + entry[1]

    return rank(first) < rank(second)


def spread_columns(row):
    return jnp.transpose(jnp.broadcast_to(row, (LANES, LANES)))


def tile_places(route_ref, window_ref, rows_out, cols_out, place_ref):
    pixels, lanes = rows_out.shape
    senders = lanes // LANES
    granules = route_ref.shape[1] // senders
    own = lax.axis_index("gran")
    lane_row = lax.broadcasted_iota(jnp.int32, (1, LANES), 1)

    def both_routes(rows):
        return jnp.where(lane_row < granules, rows[0:1], pltpu.roll(rows, granules, 1)[1:2])

    routes = own_columns(route_ref, (slice(None),), granules)
    starts = [own_columns(window_ref, (r, slice(None)), granules) for r in range(2)]
    named = both_routes(routes).astype(f32)
    col = lax.broadcasted_iota(jnp.int32, (LANES, LANES), 1)
    row = lax.broadcasted_iota(jnp.int32, (LANES, LANES), 0)
    before = earlier((row // granules, row % granules), (col // granules, col % granules), granules)
    before = before & (row < 2 * granules) & (spread_columns(named) == named)
    rank = jnp.sum(before.astype(f32), axis=0, keepdims=True).astype(jnp.int32)
    knots = [
        jnp.clip(jnp.right_shift(both_routes(jnp.concatenate([s[k : k + 1] for s in starts])), 5) - 1, 0, KN - SPAN)
        for k in range(2)
    ]
    turn = rank * SPAN - knots[1] + LANES
    place_ref[...] = jnp.concatenate(
        [named.astype(jnp.int32), rank, jnp.right_shift(knots[0], 1), turn] * 2, axis=0
    )

    wide = 2 * LANES
    col = lax.broadcasted_iota(jnp.int32, (wide, wide), 1)
    row = lax.broadcasted_iota(jnp.int32, (wide, wide), 0)
    route = [at // LANES for at in (row, col)]
    place = [at % LANES for at in (row, col)]
    before = earlier((route[0], place[0] % granules), (route[1], place[1] % granules), granules)
    before = before & (place[0] // granules == place[1] // granules)
    before = before.astype(f32).astype(bf16)
    seat = (lax.broadcasted_iota(jnp.int32, (LANES, LANES), 1) // SPAN).astype(f32)
    lane = lax.broadcasted_iota(jnp.int32, (8, LANES), 1)
    step = lane % SPAN
    pixel = lax.broadcasted_iota(jnp.int32, (8, LANES), 0).astype(f32) * (1.0 / SP)
    part = LANES // granules
    for t in range(route_ref.shape[1] // LANES):
        at = slice(t * LANES, (t + 1) * LANES)
        hits = [(route_ref[r : r + 1, at] == own).astype(f32) for r in range(2)]
        hits = jnp.broadcast_to(jnp.concatenate(hits, axis=1), (8, wide))
        ranks = jnp.dot(hits.astype(bf16), before, preferred_element_type=f32)
        ranks = jnp.where(hits > 0.5, ranks, -1.0)
        chosen, values = [], []
        for r in range(2):
            chosen.append((spread_columns(ranks[0:1, r * LANES : (r + 1) * LANES]) == seat).astype(f32).astype(bf16))
            sender = lax.broadcasted_iota(jnp.int32, (part, LANES), 0)
            within = lax.broadcasted_iota(jnp.int32, (part, LANES), 1) // granules == sender
            kinds = []
            for k in range(2):
                start = window_ref[r, k : k + 1, at]
                kinds += [jnp.right_shift(start, 5), jnp.bitwise_and(start, SP - 1)]
            kinds.append(jnp.ones((1, LANES), jnp.int32))
            values.append(jnp.concatenate([jnp.where(within, kind, 0).astype(f32) for kind in kinds], axis=0))
        found = jnp.dot(
            jnp.concatenate(values, axis=1).astype(bf16),
            jnp.concatenate(chosen, axis=0),
            preferred_element_type=f32,
        )
        for n in range(part):
            live = found[4 * part + n : 4 * part + n + 1] > 0.5
            for k, ref in ((0, rows_out), (1, cols_out)):
                base = found[2 * k * part + n : 2 * k * part + n + 1]
                rest = found[(2 * k + 1) * part + n : (2 * k + 1) * part + n + 1]
                first = jnp.clip(base.astype(jnp.int32) - 1, 0, KN - SPAN)
                if k == 0:
                    knot = 2 * jnp.right_shift(first, 1) + 2 * (step % 8) + step // 8
                else:
                    knot = first + step
                border = (knot == 0) | (knot == KN - 1)
                cube = jnp.where(border, 1.0, 1.5)
                square = jnp.where(border, -1.5, -2.5)
                single = jnp.where(border, -0.5, 0.0)
                away = jnp.where(live, base + rest * (1.0 / SP) - knot.astype(f32), 4.0 * KN)
                away = away + pixel
                to = pl.ds((t * part + n) * LANES, LANES)
                for q in range(0, pixels, 16):
                    pair = []
                    for p in (q, q + 8):
                        d = jnp.abs(away + p * (1.0 / SP))
                        near = ((cube * d + square) * d + single) * d + 1.0
                        far = ((2.5 - 0.5 * d) * d - 4.0) * d + 2.0
                        pair.append(jnp.where(d <= 1.0, near, jnp.where(d < 2.0, far, 0.0)))
                    ref[q : q + 16, to] = jnp.concatenate(pair, axis=0).astype(bf16)


def compose(route_ref, received_ref, row_ref, col_ref, pixels_ref, solved, out_ref, grids_out, passed, result, sems):
    copies = [pltpu.make_async_copy(solved, grids_out, sems.at[result.shape[0]])]
    copies[0].start()
    senders = received_ref.shape[0]
    bands = result.shape[0]
    lane = lax.broadcasted_iota(jnp.int32, (16, LANES), 1) // SPAN
    masks = [(lane == r).astype(f32).astype(bf16) for r in range(LANES // SPAN)]
    named = (route_ref[...] == lax.axis_index("gran")).astype(f32)
    scale = 1.0 / jnp.sum(named, keepdims=True)

    def sender(n, carry):
        at = pl.ds(pl.multiple_of(n * LANES, LANES), LANES)
        blocks = []
        for k in range(2 * bands):
            window = received_ref[n, 16 * k : 16 * k + 16, :]
            blocks.append(jnp.concatenate([window * mask for mask in masks], axis=0))
        rows = jnp.dot(row_ref[:, at], jnp.concatenate(blocks, axis=1), preferred_element_type=f32)
        for k in range(2 * bands):
            passed[k, :, at] = rows[:, LANES * k : LANES * k + LANES].astype(bf16)
        return carry

    steps = min(8, senders)

    def several(n, carry):
        for k in range(steps):
            sender(n * steps + k, carry)
        return carry

    if senders == steps:
        several(0, 0)
    else:
        lax.fori_loop(0, senders // steps, several, 0)
    for b in range(bands):
        fields = [
            lax.dot_general(
                passed[2 * b + c], col_ref[...], (((1,), (1,)), ((), ())), preferred_element_type=f32
            )
            * scale
            for c in range(2)
        ]
        pixels = pixels_ref[0, b].astype(f32)
        result[b] = (pixels * (1.0 + fields[0]) + fields[1]).astype(bf16)
        copies.append(pltpu.make_async_copy(result.at[b], out_ref.at[0, b], sems.at[b]))
        copies[-1].start()
    for copy in copies:
        copy.wait()


def per_device(
    prior_grids,
    pif_rhs,
    pif_diagonal,
    pif_cross,
    pif_coupling,
    neighbour_offset,
    neighbour_count,
    tile_route,
    tile_window,
    tile_pixels,
):
    granules, bands = prior_grids.shape[:2]
    slots = pif_coupling.shape[1]
    pixel_count = tile_pixels.shape[2]
    device_total = lax.axis_size("gran")
    band_total = lax.axis_size("band")

    def by_lane_tile(array):
        cut = array.reshape(array.shape[:2] + (array.shape[2], 32, LANES)).transpose(0, 1, 3, 2, 4)
        return cut.reshape(array.shape[:2] + (32 * array.shape[2], LANES))

    grids = by_lane_tile(prior_grids)
    rhs = by_lane_tile(pif_rhs)
    diagonal = by_lane_tile(pif_diagonal)
    cross = by_lane_tile(pif_cross.transpose(1, 0, 2).reshape(bands, granules // 8, 8, KN * KN))
    coupling = by_lane_tile(pif_coupling.transpose(0, 2, 1, 3))
    graph = [("v", neighbour_offset.T)]
    tiles = [("v", tile_route.T), ("v", tile_window.transpose(1, 2, 0))]
    edge = (REACH, bands, 64, LANES)
    own = (granules, bands, 64, LANES)
    ext = (granules + 2 * REACH, bands, 64, LANES)
    packed = [("v", (64, LANES), f32), ("v", (64, LANES), bf16)]
    chunks = 4

    near_pairs = [(i, i ^ 1) for i in range(device_total)]
    far_pairs = [
        pair for i in range(1, device_total - 1, 2) for pair in ((i, i + 1), (i + 1, i))
    ]

    def exchange(near, far):
        far = lax.ppermute(far, "gran", far_pairs)
        near = lax.ppermute(near, "gran", near_pairs)
        return near, far

    near, far = call(
        first_edges,
        [("h", grids)],
        [("v", edge, bf16), ("v", edge, bf16)],
        [pltpu.VMEM((2,) + edge, f32), pltpu.SemaphoreType.DMA((2, REACH))],
    )
    near, far = exchange(near, far)
    (extended,) = call(
        arrange_grids,
        [("h", grids)],
        [("v", ext, f32)],
        [pltpu.VMEM(own, f32), pltpu.SemaphoreType.DMA((chunks,))],
    )
    sources = [rhs, diagonal, cross, coupling]

    def arranged(interior, sources):
        part = len(visits(granules, interior))
        some = (part, bands, 64, LANES)
        return call(
            functools.partial(arrange, interior),
            [("v", neighbour_count[None, :])] + [("h", source) for source in sources],
            [
                ("v", some, f32),
                ("v", some, f32),
                ("v", (part, bands, 32, LANES), f32),
                ("v", (part, slots, bands, 32, LANES), f32),
            ],
            [
                pltpu.VMEM(some, f32),
                pltpu.VMEM(some, f32),
                pltpu.VMEM(cross.shape, f32),
                pltpu.VMEM((part,) + coupling.shape[1:], bf16),
                pltpu.VMEM(coupling.shape[1:], f32),
                pltpu.SMEM((part,), jnp.int32),
                pltpu.SemaphoreType.DMA((4, chunks)),
            ],
        )

    gathered = pltpu.VMEM((slots, 64, LANES), f32)
    weights = pltpu.VMEM((slots, 64, LANES), f32)
    scalars = pltpu.SMEM((granules,), jnp.int32)

    def over_band(partial, rounded):
        return [("v", partial)] + [
            ("v", lax.ppermute(rounded, "band", [(i, i ^ flip) for i in range(band_total)]))
            for flip in range(1, band_total)
        ]

    for sweep in range(SWEEPS):
        last = sweep == SWEEPS - 1
        inner, *inner_rounded = call(
            interior_disparities,
            graph + [("v", extended)],
            packed if last else packed[:1],
            [gathered, scalars],
        )
        if sweep == PARTED + 1:
            inner, *gains = lax.optimization_barrier((inner, *gains))
        if sweep == 0:
            inner, *edge_state = lax.optimization_barrier((inner, *arranged(False, sources)))
        if last:
            inner_shares = over_band(inner, *inner_rounded)
        inputs = graph + [("v", near), ("v", far), ("v", extended)]
        inputs += [] if last else [("v", inner)]
        extended, partial, rounded = call(
            edge_disparities,
            inputs,
            [("v", ext, f32)] + packed,
            [gathered, scalars],
            aliases={3: 0},
        )
        shares = over_band(partial, rounded)
        if sweep == PARTED + 1:
            far_gain = lax.ppermute(gains[0], "gran", far_pairs)
        if sweep == 1:
            routes, starts, _ = lax.optimization_barrier((tiles[0][1], tiles[1][1], partial))
            weight_shape = ("v", (pixel_count, device_total * LANES), bf16)
            made = call(
                tile_places,
                [("v", routes), ("v", starts)],
                [weight_shape, weight_shape, ("v", (8, LANES), jnp.int32)],
            )
            partial, row_weights, col_weights, places = lax.optimization_barrier((partial, *made))
            shares[0] = ("v", partial)
        edge_state_now = [("v", extended)] + [("v", array) for array in edge_state]
        if not last:
            inputs = graph + shares + edge_state_now
            parted = sweep == PARTED
            split = sweep == PARTED + 1
            half = ("v", (REACH, bands, 32, LANES), bf16)
            outputs = [("v", ext, f32), ("v", edge, bf16)] + ([half] * 2 if parted else [("v", edge, bf16)])
            aliases = {}
            if split:
                inputs = inputs + [("v", far), ("v", far_gain)]
                outputs = [("v", ext, f32)] + outputs
                aliases = {len(graph + shares): 0}
            made = call(
                functools.partial(edge_sweep, split, parted),
                inputs,
                outputs,
                [weights, scalars],
                aliases=aliases,
            )
            if split:
                extended, *made = made
            updated, near, far, *gains = made
            near, far = exchange(near, far)
            if sweep == 0:
                *later, updated = lax.optimization_barrier((*sources, updated))
                inner_state = [("v", array) for array in arranged(True, later)]
            inputs = graph + shares + [("v", extended)] + inner_state
            (extended,) = call(
                interior_sweep,
                inputs + [("v", updated)],
                [("v", ext, f32)],
                [weights, scalars],
                aliases={len(inputs): 0},
            )
    windows = (device_total, 2 * bands * SPAN, LANES)
    scratch = [weights, scalars]
    inputs = graph + inner_shares + [("v", extended)] + inner_state + [("v", places)]
    balanced, gathered_windows = call(
        functools.partial(last_sweep, True),
        inputs,
        [("v", own, f32), ("v", windows, f32)],
        scratch,
    )
    inputs = graph + shares + edge_state_now + [("v", places)] + [("v", balanced), ("v", gathered_windows)]
    balanced, payload, _ = call(
        functools.partial(last_sweep, False),
        inputs,
        [("v", own, f32), ("v", windows, bf16), ("v", windows, f32)],
        scratch,
        aliases={len(inputs) - 2: 0, len(inputs) - 1: 2},
    )
    received = lax.all_to_all(payload, "gran", split_axis=0, concat_axis=0, tiled=True)
    inputs = [tiles[0], ("v", received), ("v", row_weights), ("v", col_weights), ("v", tile_pixels)]
    corrected, balanced = call(
        compose,
        inputs + [("v", balanced)],
        [("h", tile_pixels.shape, bf16), ("h", own, f32)],
        [
            pltpu.VMEM((2 * bands, pixel_count, device_total * LANES), bf16),
            pltpu.VMEM(tile_pixels.shape[1:], bf16),
            pltpu.SemaphoreType.DMA((bands + 1,)),
        ],
        limit=32,
    )
    balanced = balanced.reshape(granules, bands, 32, 2, LANES).transpose(0, 1, 3, 2, 4)
    return (balanced.reshape(prior_grids.shape), corrected)


def solution(mesh):
    placed = (
        P("gran", "band", None, None),
        P("gran", "band", None, None),
        P("gran", "band", None, None),
        P("gran", "band", None),
        P("gran", None, "band", None),
        P("gran", None),
        P("gran"),
        P(),
        P(),
        P("gran", "band", None, None),
    )
    return jax.shard_map(
        per_device,
        mesh=mesh,
        in_specs=placed,
        out_specs=(P("gran", "band", None, None), P("gran", "band", None, None)),
        check_vma=False,
    )
```
